128 devices in a mesh: section: 2 (over core), dp: 16 (over z, y), tensor: 4 (over x).
Axes of the slice: x: 4, y: 4, z: 4, core: 2. Of those that a mesh axis runs over, the one named last changes fastest.
Arguments:
- tokens: bfloat16 [32, 384, 1088], P('dp', 'tensor'), may hold values from -6 to 6
- cotangent: bfloat16 [32, 384, 1088], P('dp', 'tensor'), may hold values from -6 to 6
- doc_lengths: int32 [32, 4], P('dp'), may hold values from 1 to 336, 384 in all within a row
- norm_gains: bfloat16 [2, 2, 1088], P('section', None, 'tensor'), may hold values from 0.5 to 1.5
- w_qkv: bfloat16 [2, 1088, 3264], P('section', 'tensor'), may hold values from -0.1875 to 0.1875
- w_out: bfloat16 [2, 1088, 1088], P('section', 'tensor'), may hold values from -0.75 to 0.75
- w_up: bfloat16 [2, 1088, 4352], P('section', None, 'tensor'), may hold values from -0.1875 to 0.1875
- w_down: bfloat16 [2, 4352, 1088], P('section', 'tensor'), may hold values from -0.09375 to 0.09375
Outputs:
- activations: bfloat16 [2, 32, 384, 1088], P('section', 'dp', 'tensor')
- input_grads: bfloat16 [2, 32, 384, 1088], P('section', 'dp', 'tensor')
- grad_gains: float32 [2, 2, 1088], P('section', None, 'tensor')
- grad_qkv: float32 [2, 1088, 3264], P('section', 'tensor')
- grad_out: float32 [2, 1088, 1088], P('section', 'tensor')
- grad_up: float32 [2, 1088, 4352], P('section', None, 'tensor')
- grad_down: float32 [2, 4352, 1088], P('section', 'tensor')
The draws below stay inside these ranges and needn't reach their ends.
Inputs may be any that keep to these rules, and one draw needn't show every extreme that they name: `doc_lengths`: each row holds the lengths of the 4 documents of one sequence, summing to 384; the longest has exactly 336 tokens.
All inputs are finite; a program needn't handle non-finite values.
Results may differ from the reference program's by a relative error of at most 0.035.
Values may be sent and summed in bfloat16 or wider, within the bound.
A program may use at most 192 MiB of HBM per device.

```python
import math
import jax
import jax.numpy as jnp
import numpy as np
from jax import lax

D = 1088
HEAD_DIM = 64
FF = 4352
SEQ = 384
DOCS = 4
LONGEST = 336
BATCH = 32


def shard_levels(own_key, extent, shards, low, largest):
    gain, own = 1.0, jax.random.fold_in(own_key, 6)
    for position, parts in shards:
        steps = jnp.exp(jax.random.uniform(jax.random.fold_in(own, position), (parts,), jnp.float32, low / len(shards), largest / len(shards)))
        gain = gain * jnp.repeat(steps, extent[position] // parts).reshape([-1 if axis == position else 1 for axis in range(len(extent))])
    return gain


def length_profile(amount, total, bound, skew):
    loads = [(1 << 20) // math.isqrt(grade ** skew) + 1 for grade in range(2, amount + 1)]
    spare, given = total - bound - (amount - 1), [1] * (amount - 1)
    while spare > 0:
        free = [i for i in range(amount - 1) if given[i] < bound]
        whole, left = sum([loads[i] for i in free]), spare
        for i in free:
            more = min(bound - given[i], max(1, left * loads[i] // whole), spare)
            given[i] = given[i] + more
            spare = spare - more
    return np.array([bound] + given)


def uneven_parts(stream_key, amount, total, bound, slope):
    if amount == 2:
        one = jax.random.randint(stream_key, (), max(1, total - bound), min(bound, total - 1) + 1)
        return jnp.stack([one, total - one])
    sizes = jnp.asarray(length_profile(amount, total, bound, slope), jnp.int32)
    pairs = (amount - 1) // 2
    donor, taker = sizes[1:1 + 2 * pairs:2], sizes[2:2 + 2 * pairs:2]
    margin = jnp.minimum(donor - 1, bound - taker)
    shifted = jax.random.randint(jax.random.fold_in(stream_key, 1), (pairs,), 0, 1 << 20) % (margin + 1)
    sizes = sizes.at[1:1 + 2 * pairs:2].set(donor - shifted).at[2:2 + 2 * pairs:2].set(taker + shifted)
    return sizes[jax.random.permutation(jax.random.fold_in(stream_key, 2), amount)]


def noise(own_key, extent, spread, most, split=(), kind=jnp.bfloat16):
    values = jax.random.normal(own_key, extent, jnp.float32) * spread
    if len(split) > 0:
        values = shard_levels(own_key, extent, split, -0.22, 0.18) * values
    return jnp.clip(values, min=-most, max=most).astype(kind)


def setup_inputs(seed: int = 0) -> dict:
    keys = jax.random.split(jax.random.key(seed), 9)
    tokens = noise(keys[0], (BATCH, SEQ, D), 1.0, 6.0, ((0, 16), (1, 4)))
    cotangent = noise(keys[1], (BATCH, SEQ, D), 1.0, 6.0, ((0, 16), (1, 4)))
    doc_lengths = jax.vmap(lambda own: uneven_parts(own, DOCS, SEQ, LONGEST, 2))(jax.random.split(keys[2], BATCH)).reshape((BATCH, DOCS)).astype(jnp.int32)
    norm_gains = jnp.clip(1.0 + 0.1 * jax.random.normal(keys[3], (2, 2, D), jnp.float32), 0.5, 1.5).astype(jnp.bfloat16)
    w_qkv = noise(keys[4], (2, D, 3 * D), D ** -0.5, 0.1875, ((0, 2), (1, 4)))
    w_out = noise(keys[5], (2, D, D), (D // 16) ** -0.5, 0.75, ((0, 2), (1, 4)))
    w_up = noise(keys[6], (2, D, FF), D ** -0.5, 0.1875, ((0, 2), (2, 4)))
    w_down = noise(keys[7], (2, FF, D), FF ** -0.5, 0.09375, ((0, 2), (1, 4)))
    return dict(tokens=tokens, cotangent=cotangent, doc_lengths=doc_lengths, norm_gains=norm_gains, w_qkv=w_qkv, w_out=w_out, w_up=w_up, w_down=w_down)


@jax.custom_vjp
def low(v):
    return lax.optimization_barrier(v.astype(jnp.bfloat16)).astype(jnp.float32)

@jax.custom_vjp
def low_back(v):
    return v

def low_keep(v):
    return (low(v), None)

def low_pass(kept, grad):
    return (grad,)

def back_keep(v):
    return (v, None)

def back_low(kept, grad):
    return (low(grad),)
low.defvjp(low_keep, low_pass)
low_back.defvjp(back_keep, back_low)

def norm_rows(values, norm_gain):
    average = lax.optimization_barrier(jnp.mean(values, axis=-1, keepdims=True))
    centered = values - average
    variance = lax.optimization_barrier(jnp.mean(centered * centered, axis=-1, keepdims=True))
    return centered * lax.rsqrt(variance + 1e-05) * norm_gain

def gelu_tanh(values):
    inner = 0.7978845608028654 * (values + 0.044715 * values * values * values)
    return 0.5 * values * (1.0 + jnp.tanh(inner))

def doc_numbers(lengths, places):
    doc_ends = jnp.cumsum(lengths)
    return lax.optimization_barrier(jnp.sum((places[:, None] >= doc_ends[None, :]).astype(jnp.int32), axis=1))

def layer(values, gains, w_qkv, w_out, w_up, w_down, allowed):
    row_total, features = values.shape
    head_count = features // HEAD_DIM
    highest = lax.Precision.HIGHEST
    normed_one = low(norm_rows(values, gains[0]))
    projected = low(low_back(jnp.dot(normed_one, w_qkv, precision=highest)))
    query_heads = projected[:, :features].reshape(row_total, head_count, HEAD_DIM)
    key_heads = projected[:, features:2 * features].reshape(row_total, head_count, HEAD_DIM)
    value_heads = projected[:, 2 * features:].reshape(row_total, head_count, HEAD_DIM)
    scores = low_back(jnp.einsum('qhd,khd->hqk', query_heads, key_heads, precision=highest) * HEAD_DIM ** (-0.5))
    scores = jnp.where(allowed[None], scores, -1e+30)
    row_max = lax.optimization_barrier(jnp.max(scores, axis=-1, keepdims=True))
    raised = jnp.exp(scores - row_max)
    attn_probs = low(raised / lax.optimization_barrier(jnp.sum(raised, axis=-1, keepdims=True)))
    mixed_heads = jnp.einsum('hqk,khd->qhd', attn_probs, value_heads, precision=highest).reshape(row_total, features)
    mixed_heads = low(low_back(mixed_heads))
    middle = values + low_back(jnp.dot(mixed_heads, w_out, precision=highest))
    normed_two = low(norm_rows(middle, gains[1]))
    pre_act = low_back(jnp.dot(normed_two, w_up, precision=highest))
    hidden = low(gelu_tanh(pre_act))
    return middle + low_back(jnp.dot(hidden, w_down, precision=highest))

def reference(tokens, cotangent, doc_lengths, norm_gains, w_qkv, w_out, w_up, w_down):
    weights = tuple((member.astype(jnp.float32) for member in (norm_gains, w_qkv, w_out, w_up, w_down)))
    places = jnp.arange(SEQ, dtype=jnp.int32)
    causal = places[None, :] <= places[:, None]
    section_zero = tuple((member[0] for member in weights))
    section_one = tuple((member[1] for member in weights))

    def one_sequence(totals, inputs):
        seq_in, seq_cot, lengths = inputs
        doc_ids = doc_numbers(lengths, places)
        allowed = causal & (doc_ids[None, :] == doc_ids[:, None])

        def apply_layer(values, gains, qkv_weight, out_weight, up_weight, down_weight):
            return layer(values, gains, qkv_weight, out_weight, up_weight, down_weight, allowed)
        out_zero, back_zero = jax.vjp(apply_layer, seq_in.astype(jnp.float32), *section_zero)
        handed = out_zero.astype(jnp.bfloat16)
        out_one, back_one = jax.vjp(apply_layer, handed.astype(jnp.float32), *section_one)
        grads_one = back_one(seq_cot.astype(jnp.float32))
        returned = grads_one[0].astype(jnp.bfloat16)
        grads_zero = back_zero(returned.astype(jnp.float32))
        updated = tuple((totals[member] + jnp.stack([grads_zero[member + 1], grads_one[member + 1]]) for member in range(5)))
        return (updated, (handed, out_one.astype(jnp.bfloat16), grads_zero[0].astype(jnp.bfloat16), returned))
    start_totals = tuple((jnp.zeros(member.shape, jnp.float32) for member in weights))
    totals, results = lax.scan(one_sequence, start_totals, (tokens, cotangent, doc_lengths))
    handed_all, last_all, first_grads, second_grads = results
    activations = jnp.stack([handed_all, last_all])
    input_grads = jnp.stack([first_grads, second_grads])
    return (activations, input_grads, totals[0], totals[1], totals[2], totals[3], totals[4])
```

```python
import functools
import jax
import jax.numpy as jnp
from jax import lax
from jax.experimental import pallas as pl
from jax.experimental.pallas import tpu as pltpu
from jax.sharding import PartitionSpec as P

HEAD_DIM = 64
LOW = jnp.bfloat16
F32 = jnp.float32
MESH = pl.DeviceIdType.MESH


def dot_nn(left, right):
    return lax.dot_general(left, right, (((1,), (0,)), ((), ())), preferred_element_type=F32)


def dot_nt(left, right):
    return lax.dot_general(left, right, (((1,), (1,)), ((), ())), preferred_element_type=F32)


def dot_tn(left, right):
    return lax.dot_general(left, right, (((0,), (0,)), ((), ())), preferred_element_type=F32)


def places():
    me = lax.axis_index("tensor")
    return me, lax.rem(me + 1, 4), lax.rem(me + 3, 4), lax.rem(me + 2, 4)


def greet(right, left):
    barrier = pltpu.get_barrier_semaphore()
    for neighbour in (left, right):
        pl.semaphore_signal(
            barrier, inc=1, device_id={"tensor": neighbour}, device_id_type=MESH
        )
    pl.semaphore_wait(barrier, 2)


def remote(src, dst, sems, which, target):
    return pltpu.make_async_remote_copy(
        src_ref=src,
        dst_ref=dst,
        send_sem=sems[0].at[which],
        recv_sem=sems[1].at[which],
        device_id={"tensor": target},
        device_id_type=MESH,
    )


class Gather:
    def __init__(self, full, sems):
        self.full, self.sems = full, sems
        self.me, self.right, self.left, self.opposite = places()
        half = full.shape[1] // 2
        self.first, self.second = pl.ds(0, half), pl.ds(half, half)

    def copy(self, block, rows, which, target):
        part = self.full.at[block, rows]
        return remote(part, part, self.sems, which, target)

    def start(self):
        self.copy(self.me, self.first, 0, self.right).start()
        self.copy(self.me, self.second, 1, self.left).start()
        self.copy(self.me, self.second, 2, self.right).start()
        self.copy(self.me, self.first, 3, self.left).start()

    def relay(self):
        self.copy(self.left, self.first, 0, self.right).wait_recv()
        self.copy(self.left, self.first, 4, self.right).start()
        self.copy(self.right, self.second, 1, self.left).wait_recv()
        self.copy(self.right, self.second, 5, self.left).start()

    def wait_left(self):
        self.copy(self.left, self.second, 2, self.right).wait_recv()

    def wait_right(self):
        self.copy(self.right, self.first, 3, self.left).wait_recv()

    def wait_opposite(self):
        self.copy(self.opposite, self.first, 4, self.right).wait_recv()
        self.copy(self.opposite, self.second, 5, self.left).wait_recv()

    def finish(self):
        self.copy(self.me, self.first, 0, self.right).wait_send()
        self.copy(self.me, self.second, 1, self.left).wait_send()
        self.copy(self.me, self.second, 2, self.right).wait_send()
        self.copy(self.me, self.first, 3, self.left).wait_send()
        self.copy(self.left, self.first, 4, self.right).wait_send()
        self.copy(self.right, self.second, 5, self.left).wait_send()


class Scatter:
    def __init__(self, parts, landing, passing, arrived, sems):
        self.parts, self.landing, self.passing, self.arrived = parts, landing, passing, arrived
        self.sems = sems
        self.me, self.right, self.left, self.opposite = places()
        half = parts.shape[1] // 2
        self.first, self.second = pl.ds(0, half), pl.ds(half, half)

    def copy(self, which):
        parts, first, second = self.parts, self.first, self.second
        src, dst = {
            0: lambda: (parts.at[self.opposite, first], self.landing.at[0]),
            1: lambda: (parts.at[self.opposite, second], self.landing.at[1]),
            2: lambda: (parts.at[self.right, second], self.arrived.at[0, second]),
            3: lambda: (parts.at[self.left, first], self.arrived.at[1, first]),
            4: lambda: (self.passing.at[0], self.arrived.at[0, first]),
            5: lambda: (self.passing.at[1], self.arrived.at[1, second]),
        }[which]()
        target = self.left if which in (1, 3, 5) else self.right
        return remote(src, dst, self.sems, which, target)

    def start_near(self):
        self.copy(2).start()
        self.copy(3).start()

    def start_far(self):
        self.copy(0).start()
        self.copy(1).start()

    def relay(self):
        self.copy(0).wait_recv()
        self.passing[0] = (
            self.parts[self.right, self.first].astype(F32) + self.landing[0].astype(F32)
        ).astype(LOW)
        self.copy(4).start()
        self.copy(1).wait_recv()
        self.passing[1] = (
            self.parts[self.left, self.second].astype(F32) + self.landing[1].astype(F32)
        ).astype(LOW)
        self.copy(5).start()

    def result(self):
        for which in (2, 3, 4, 5):
            self.copy(which).wait_recv()
        return (
            self.parts[self.me].astype(F32)
            + self.arrived[0].astype(F32)
            + self.arrived[1].astype(F32)
        )

    def finish(self):
        for which in range(6):
            self.copy(which).wait_send()


def norm_stats(values):
    average = jnp.mean(values, axis=-1, keepdims=True)
    centered = values - average
    variance = jnp.mean(centered * centered, axis=-1, keepdims=True)
    scale = lax.rsqrt(variance + 1e-05)
    return centered * scale, scale


def norm_back(values, gain, grad):
    xhat, scale = norm_stats(values)
    scaled = grad * gain
    part = scale * (
        scaled
        - jnp.mean(scaled, axis=-1, keepdims=True)
        - xhat * jnp.mean(scaled * xhat, axis=-1, keepdims=True)
    )
    return part, jnp.sum(grad * xhat, axis=0, keepdims=True)


def gelu_tanh(values):
    inner = 0.7978845608028654 * (values + 0.044715 * values * values * values)
    return 0.5 * values * (1.0 + jnp.tanh(inner))


def gelu_slope(values):
    square = values * values
    bent = jnp.tanh(0.7978845608028654 * values * (1.0 + 0.044715 * square))
    slope = 0.7978845608028654 * (1.0 + 3.0 * 0.044715 * square)
    return 0.5 * (1.0 + bent) + 0.5 * values * (1.0 - bent * bent) * slope


def pick_copies(layer, mine, theirs, target, sem):
    def start():
        mine_here = lax.axis_index("section") == layer

        @pl.when(mine_here)
        def _():
            pltpu.make_async_copy(mine, target, sem).start()

        @pl.when(jnp.logical_not(mine_here))
        def _():
            pltpu.make_async_copy(theirs, target, sem).start()

    def wait():
        pltpu.make_async_copy(mine, target, sem).wait()

    return start, wait


def pair_columns(features):
    width = 2 * HEAD_DIM
    return [
        (start, min(width, features - start)) for start in range(0, features, width)
    ]


def head_masks(width):
    lanes = lax.broadcasted_iota(jnp.int32, (1, width), 1)
    if width == HEAD_DIM:
        return [None]
    return [lanes < HEAD_DIM, lanes >= HEAD_DIM]


def masked(values, mask):
    return values if mask is None else jnp.where(mask, values, jnp.zeros_like(values))


def attention_weights(layer, mine, theirs, target, sems):
    pairs = []
    for half in range(2):
        pairs.append(
            pick_copies(half, mine, theirs, target.at[pl.ds(2 * half, 2)], sems.at[half])
        )
    return pairs


def forward_kernel(
    layer, features, x_ref, bias_ref, gains_ref, at_mine, at_theirs, up_mine, up_theirs, down_mine,
    down_theirs, y_ref, middle_ref, one_ref, query_ref, key_ref, value_ref, mixed_ref, two_ref,
    act_ref, hidden_ref, at_w, up_w, down_w, weight_sems, parts, landing, passing, arrived,
    key_send, key_recv, value_send, value_recv, two_send, two_recv, sum_send, sum_recv,
):
    me, right, left, opposite = places()
    fetches = attention_weights(layer, at_mine, at_theirs, at_w, weight_sems)
    fetches.append(pick_copies(layer, up_mine, up_theirs, up_w, weight_sems.at[2]))
    fetches.append(pick_copies(layer, down_mine, down_theirs, down_w, weight_sems.at[3]))
    for start, _ in fetches:
        start()
    greet(right, left)
    rows = x_ref.shape[0]
    inputs = x_ref[...].astype(F32)
    xhat, _ = norm_stats(inputs)
    one_ref[...] = (xhat * gains_ref[0:1, :]).astype(LOW)
    normed_one = one_ref[...]
    fetches[0][1]()
    key_ref[me] = dot_nn(normed_one, at_w[1]).astype(LOW)
    keys = Gather(key_ref, (key_send, key_recv))
    keys.start()
    fetches[1][1]()
    value_ref[me] = dot_nn(normed_one, at_w[2]).astype(LOW)
    values = Gather(value_ref, (value_send, value_recv))
    values.start()
    query_ref[...] = dot_nn(normed_one, at_w[0]).astype(LOW)
    keys.relay()
    values.relay()
    keys.wait_left()
    keys.wait_right()
    keys.wait_opposite()
    values.wait_left()
    values.wait_right()
    values.wait_opposite()
    bias = bias_ref[...]
    for begin, width in pair_columns(features):
        columns = pl.ds(begin, width)
        queries = query_ref[:, columns]
        key_block = key_ref[:, :, columns].reshape(4 * rows, width)
        value_block = value_ref[:, :, columns].reshape(4 * rows, width)
        mixed = None
        for mask in head_masks(width):
            scores = dot_nt(masked(queries, mask), key_block) * 0.125 + bias
            raised = jnp.exp(scores - jnp.max(scores, axis=-1, keepdims=True))
            probs = raised * (1.0 / jnp.sum(raised, axis=-1, keepdims=True))
            own = dot_nn(probs.astype(LOW), value_block)
            mixed = own if mixed is None else jnp.where(mask, own, mixed)
        mixed_ref[:, columns] = mixed.astype(LOW)
    middle_ref[...] = x_ref[...].astype(F32) + dot_nn(mixed_ref[...], at_w[3])
    xhat, _ = norm_stats(middle_ref[...])
    two_ref[me] = (xhat * gains_ref[1:2, :]).astype(LOW)
    tokens = Gather(two_ref, (two_send, two_recv))
    tokens.start()
    fetches[2][1]()
    fetches[3][1]()
    sums = Scatter(parts, landing, passing, arrived, (sum_send, sum_recv))

    def feed(block):
        act_ref[block] = dot_nn(two_ref[block], up_w[...])
        hidden_ref[block] = gelu_tanh(act_ref[block]).astype(LOW)
        parts[block] = dot_nn(hidden_ref[block], down_w[...]).astype(LOW)

    feed(me)
    tokens.relay()
    tokens.wait_left()
    feed(left)
    tokens.wait_right()
    feed(right)
    sums.start_near()
    tokens.wait_opposite()
    feed(opposite)
    sums.start_far()
    sums.relay()
    y_ref[...] = (middle_ref[...] + sums.result()).astype(LOW)
    keys.finish()
    values.finish()
    tokens.finish()
    sums.finish()


def scatter_scratch(rows, features):
    return [
        pltpu.VMEM((4, rows, features), LOW),
        pltpu.VMEM((2, rows // 2, features), LOW),
        pltpu.VMEM((2, rows // 2, features), LOW),
        pltpu.VMEM((2, rows, features), LOW),
    ]


def weight_scratch(features, hidden):
    return [
        pltpu.VMEM((4, features, features), LOW),
        pltpu.VMEM((features, hidden), LOW),
        pltpu.VMEM((hidden, features), LOW),
        pltpu.SemaphoreType.DMA((4,)),
    ]


def in_vmem():
    return pl.BlockSpec(memory_space=pltpu.VMEM)


def anywhere():
    return pl.BlockSpec(memory_space=pl.ANY)


def forward_layer(layer, x, bias, gains, attention, feed):
    rows, features = x.shape
    hidden = feed[0].shape[1]
    out_shape = (
        jax.ShapeDtypeStruct((rows, features), LOW),
        jax.ShapeDtypeStruct((rows, features), F32),
        jax.ShapeDtypeStruct((rows, features), LOW),
        jax.ShapeDtypeStruct((rows, features), LOW),
        jax.ShapeDtypeStruct((4, rows, features), LOW),
        jax.ShapeDtypeStruct((4, rows, features), LOW),
        jax.ShapeDtypeStruct((rows, features), LOW),
        jax.ShapeDtypeStruct((4, rows, features), LOW),
        jax.ShapeDtypeStruct((4, rows, hidden), F32),
        jax.ShapeDtypeStruct((4, rows, hidden), LOW),
    )
    return pl.pallas_call(
        functools.partial(forward_kernel, layer, features),
        out_shape=out_shape,
        in_specs=[in_vmem()] * 3 + [anywhere()] * 6,
        out_specs=[in_vmem()] * len(out_shape),
        scratch_shapes=weight_scratch(features, hidden)
        + scatter_scratch(rows, features)
        + [pltpu.SemaphoreType.DMA((6,))] * 8,
        compiler_params=pltpu.CompilerParams(
            collective_id=layer, has_side_effects=True, vmem_limit_bytes=56 * 2**20
        ),
        cost_estimate=pl.CostEstimate(
            flops=3 * 10**9, bytes_accessed=24 * 10**6, transcendentals=10**6
        ),
        name=f"layer_forward_{layer}",
    )(x, bias, gains, *attention, *feed)


def backward_kernel(
    layer, features, x_ref, dy_ref, bias_ref, gains_ref, middle_ref, query_ref, key_ref, value_ref,
    act_ref, at_mine, at_theirs, up_mine, up_theirs, down_mine, down_theirs,
    dx_ref, gain_ref, out_ref, pre_ref, branch_ref, dquery_ref, dkey_ref, dvalue_ref,
    at_w, up_w, down_w, weight_sems, parts, landing, passing, arrived, parts_b, landing_b,
    passing_b, arrived_b, parts_c, landing_c, passing_c, arrived_c, mixed_grad,
    out_send, out_recv, sum_send, sum_recv, key_send, key_recv, value_send, value_recv,
):
    me, right, left, opposite = places()
    fetches = attention_weights(layer, at_mine, at_theirs, at_w, weight_sems)
    fetches.append(pick_copies(layer, up_mine, up_theirs, up_w, weight_sems.at[2]))
    fetches.append(pick_copies(layer, down_mine, down_theirs, down_w, weight_sems.at[3]))
    for which in (3, 2, 1, 0):
        fetches[which][0]()
    rows = x_ref.shape[0]
    out_ref[me] = dy_ref[...]
    greet(right, left)
    grads = Gather(out_ref, (out_send, out_recv))
    grads.start()
    sums = Scatter(parts, landing, passing, arrived, (sum_send, sum_recv))
    fetches[3][1]()
    fetches[2][1]()

    def feed(block):
        hidden_grad = dot_nt(out_ref[block], down_w[...])
        pre_ref[block] = (hidden_grad * gelu_slope(act_ref[block])).astype(LOW)
        parts[block] = dot_nt(pre_ref[block], up_w[...]).astype(LOW)

    feed(me)
    grads.relay()
    grads.wait_left()
    feed(left)
    grads.wait_right()
    feed(right)
    sums.start_near()
    grads.wait_opposite()
    feed(opposite)
    sums.start_far()
    sums.relay()
    middle_part, gain_two = norm_back(middle_ref[...], gains_ref[1:2, :], sums.result())
    gain_ref[1:2, :] = gain_two
    middle_grad = dy_ref[...].astype(F32) + middle_part
    middle_ref_grad = middle_grad
    branch_ref[...] = middle_grad.astype(LOW)
    fetches[1][1]()
    mixed_grad[...] = dot_nt(branch_ref[...], at_w[3]).astype(LOW)
    bias = bias_ref[...]
    for begin, width in pair_columns(features):
        columns = pl.ds(begin, width)
        queries = query_ref[:, columns]
        outer = mixed_grad[:, columns]
        key_block = key_ref[:, :, columns].reshape(4 * rows, width)
        value_block = value_ref[:, :, columns].reshape(4 * rows, width)
        dquery = dkey = dvalue = None
        for mask in head_masks(width):
            query_one, outer_one = masked(queries, mask), masked(outer, mask)
            scores = dot_nt(key_block, query_one) * 0.125 + bias
            raised = jnp.exp(scores - jnp.max(scores, axis=0, keepdims=True))
            probs = raised * (1.0 / jnp.sum(raised, axis=0, keepdims=True))
            probs_grad = dot_nt(value_block, outer_one)
            mean = jnp.sum(probs * probs_grad, axis=0, keepdims=True)
            score_grad = (probs * (probs_grad - mean)).astype(LOW)
            own_query = dot_tn(score_grad, key_block)
            own_key = dot_nn(score_grad, query_one)
            own_value = dot_nn(probs.astype(LOW), outer_one)
            if dquery is None:
                dquery, dkey, dvalue = own_query, own_key, own_value
            else:
                dquery = jnp.where(mask, own_query, dquery)
                dkey, dvalue = dkey + own_key, dvalue + own_value
        dquery_ref[:, columns] = (dquery * 0.125).astype(LOW)
        parts_b[:, :, columns] = (dkey * 0.125).astype(LOW).reshape(4, rows, width)
        parts_c[:, :, columns] = dvalue.astype(LOW).reshape(4, rows, width)
    dkeys = Scatter(parts_b, landing_b, passing_b, arrived_b, (key_send, key_recv))
    dvalues = Scatter(parts_c, landing_c, passing_c, arrived_c, (value_send, value_recv))
    dkeys.start_far()
    dvalues.start_far()
    dkeys.start_near()
    dvalues.start_near()
    fetches[0][1]()
    one_grad = dot_nt(dquery_ref[...], at_w[0])
    dkeys.relay()
    dvalues.relay()
    dkey_ref[...] = dkeys.result().astype(LOW)
    dvalue_ref[...] = dvalues.result().astype(LOW)
    one_grad = one_grad + dot_nt(dkey_ref[...], at_w[1]) + dot_nt(dvalue_ref[...], at_w[2])
    inputs_part, gain_one = norm_back(x_ref[...].astype(F32), gains_ref[0:1, :], one_grad)
    gain_ref[0:1, :] = gain_one
    dx_ref[...] = (middle_ref_grad + inputs_part).astype(LOW)
    grads.finish()
    sums.finish()
    dkeys.finish()
    dvalues.finish()


def backward_layer(layer, x, dy, bias, gains, middle, query, key, value, act, attention, feed):
    rows, features = x.shape
    hidden = feed[0].shape[1]
    out_shape = (
        jax.ShapeDtypeStruct((rows, features), LOW),
        jax.ShapeDtypeStruct((2, features), F32),
        jax.ShapeDtypeStruct((4, rows, features), LOW),
        jax.ShapeDtypeStruct((4, rows, hidden), LOW),
        jax.ShapeDtypeStruct((rows, features), LOW),
        jax.ShapeDtypeStruct((rows, features), LOW),
        jax.ShapeDtypeStruct((rows, features), LOW),
        jax.ShapeDtypeStruct((rows, features), LOW),
    )
    return pl.pallas_call(
        functools.partial(backward_kernel, layer, features),
        out_shape=out_shape,
        in_specs=[in_vmem()] * 9 + [anywhere()] * 6,
        out_specs=[in_vmem()] * len(out_shape),
        scratch_shapes=weight_scratch(features, hidden)
        + scatter_scratch(rows, features) * 3
        + [pltpu.VMEM((rows, features), LOW)]
        + [pltpu.SemaphoreType.DMA((6,))] * 8,
        compiler_params=pltpu.CompilerParams(
            collective_id=2 + layer, has_side_effects=True, vmem_limit_bytes=56 * 2**20
        ),
        cost_estimate=pl.CostEstimate(
            flops=4 * 10**9, bytes_accessed=24 * 10**6, transcendentals=10**6
        ),
        name=f"layer_backward_{layer}",
    )(x, dy, bias, gains, middle, query, key, value, act, *attention, *feed)


def doc_numbers(lengths, positions):
    doc_ends = jnp.cumsum(lengths)
    return jnp.sum((positions[:, None] >= doc_ends[None, :]).astype(jnp.int32), axis=1)


def contract_first(left, right):
    return lax.dot_general(
        left, right, (((0,), (0,)), ((), ())), preferred_element_type=F32
    )


def swapped(block):
    return lax.ppermute(block, "section", [(0, 1), (1, 0)])


def body(tokens, cotangent, doc_lengths, norm_gains, w_qkv, w_out, w_up, w_down):
    batches, rows, features = tokens.shape
    seq_rows = rows * lax.axis_size("tensor")
    section = lax.axis_index("section")
    is_first = section == 0

    def choose(zero_side, one_side):
        return jnp.where(is_first, zero_side, one_side)

    own_tokens = lax.dynamic_index_in_dim(tokens, section, 0, keepdims=False)
    own_cotangent = lax.dynamic_index_in_dim(cotangent, section, 0, keepdims=False)
    lengths = lax.dynamic_index_in_dim(doc_lengths, section, 0, keepdims=False)
    own_places = lax.axis_index("tensor") * rows + jnp.arange(rows, dtype=jnp.int32)
    all_places = jnp.arange(seq_rows, dtype=jnp.int32)
    own_docs = doc_numbers(lengths, own_places)
    all_docs = doc_numbers(lengths, all_places)
    allowed = (all_places[None, :] <= own_places[:, None]) & (
        all_docs[None, :] == own_docs[:, None]
    )
    bias = jnp.where(allowed, 0.0, -1e30).astype(F32)
    bias_turned = bias.T
    gains = lax.all_gather(
        lax.all_gather(norm_gains[0], "tensor", axis=1, tiled=True), "section", axis=0
    ).astype(F32)

    query_key = jnp.stack([w_qkv[0, :, :features], w_qkv[0, :, features : 2 * features]])
    value_out = jnp.stack([w_qkv[0, :, 2 * features :], w_out[0]])
    crossed = swapped(choose(value_out, query_key))
    zero_mine = lax.all_gather(choose(query_key, crossed), "tensor", axis=1, tiled=True)
    zero_theirs = swapped(zero_mine)
    one_mine = lax.all_gather(choose(crossed, value_out), "tensor", axis=1, tiled=True)
    one_theirs = swapped(one_mine)
    attention = ((zero_mine, zero_theirs), (one_mine, one_theirs))
    feed = (w_up[0], swapped(w_up[0]), w_down[0], swapped(w_down[0]))

    inputs = own_tokens
    saved = []
    for layer in range(2):
        results = forward_layer(layer, inputs, bias, gains[layer], attention[layer], feed)
        saved.append((inputs,) + tuple(results))
        inputs = results[0]
    activations = (saved[0][1], saved[1][1])

    grad = own_cotangent
    input_grads = [None, None]
    gain_grads = [None, None]
    feed_sums = [None, None]
    attention_sums = [None, None]
    for layer in (1, 0):
        (x, _, middle, normed_one, query, key, value, mixed, normed_two, act, hidden) = saved[layer]
        (grad, gain_grad, out_all, pre_grad, branch, dquery, dkey, dvalue) = backward_layer(
            layer, x, grad, bias_turned, gains[layer], middle, query, key, value, act,
            attention[layer], feed,
        )
        input_grads[layer] = grad
        gain_grads[layer] = gain_grad

        def flat(block):
            return block.reshape(seq_rows, block.shape[-1])

        up_left, up_right = flat(normed_two), flat(pre_grad)
        down_left, down_right = flat(hidden), flat(out_all)
        mine_left, mine_right = choose(up_left, down_left), choose(up_right, down_right)
        their_left = swapped(choose(down_left, up_left))
        their_right = swapped(choose(down_right, up_right))
        feed_grad = contract_first(mine_left, mine_right) + contract_first(their_left, their_right)
        feed_grad = feed_grad.astype(LOW)
        if layer == 0:
            feed_grad, feed_sums[1] = lax.optimization_barrier((feed_grad, feed_sums[1]))
        feed_sums[layer] = lax.psum(feed_grad, "dp")
        first_left, first_right = jnp.stack([normed_one, normed_one]), jnp.stack([dquery, dkey])
        other_left, other_right = jnp.stack([normed_one, mixed]), jnp.stack([dvalue, branch])
        left = jnp.concatenate(
            [choose(first_left, other_left), swapped(choose(other_left, first_left))], axis=1
        )
        right = jnp.concatenate(
            [choose(first_right, other_right), swapped(choose(other_right, first_right))], axis=1
        )
        attention_grad = lax.dot_general(
            left, right, (((1,), (1,)), ((0,), (0,))), preferred_element_type=F32
        ).astype(LOW)
        part = lax.psum_scatter(attention_grad, "tensor", scatter_dimension=1, tiled=True)
        if layer == 0:
            part, attention_sums[1] = lax.optimization_barrier((part, attention_sums[1]))
        attention_sums[layer] = lax.psum(part, "dp")

    gain_total = lax.psum(jnp.stack(gain_grads), ("section", "dp", "tensor"))
    gain_own = lax.dynamic_index_in_dim(gain_total, section, 0, keepdims=True)
    share = features // lax.axis_size("tensor")
    gain_own = lax.dynamic_slice_in_dim(gain_own, lax.axis_index("tensor") * share, share, 2)
    kept_activation = choose(activations[0], activations[1])
    their_activation = swapped(choose(activations[1], activations[0]))
    kept_grad = choose(input_grads[0], input_grads[1])
    their_grad = swapped(choose(input_grads[1], input_grads[0]))

    def in_order(mine, theirs):
        return jnp.stack([choose(mine, theirs), choose(theirs, mine)])[None]

    feed_kept = choose(feed_sums[0], feed_sums[1])
    feed_other = swapped(choose(feed_sums[1], feed_sums[0]))
    attention_kept = choose(attention_sums[0], attention_sums[1])
    attention_other = swapped(choose(attention_sums[1], attention_sums[0]))
    first_half = choose(attention_kept, attention_other).astype(F32)
    other_half = choose(attention_other, attention_kept).astype(F32)
    grad_qkv = jnp.concatenate([first_half[0], first_half[1], other_half[0]], axis=1)
    return (
        in_order(kept_activation, their_activation),
        in_order(kept_grad, their_grad),
        gain_own,
        grad_qkv[None],
        other_half[1][None],
        choose(feed_kept, feed_other).astype(F32)[None],
        choose(feed_other, feed_kept).astype(F32)[None],
    )


def solution(mesh):
    placed = (
        P("dp", "tensor", None),
        P("dp", "tensor", None),
        P("dp", None),
        P("section", None, "tensor"),
        P("section", "tensor", None),
        P("section", "tensor", None),
        P("section", None, "tensor"),
        P("section", "tensor", None),
    )
    return jax.shard_map(
        body,
        mesh=mesh,
        in_specs=placed,
        out_specs=(
            P("section", "dp", "tensor", None),
            P("section", "dp", "tensor", None),
            P("section", None, "tensor"),
            P("section", "tensor", None),
            P("section", "tensor", None),
            P("section", None, "tensor"),
            P("section", "tensor", None),
        ),
        check_vma=False,
    )
```

```python
import functools
import jax
import jax.numpy as jnp
from jax import lax
from jax.experimental import pallas as pl
from jax.experimental.pallas import tpu as pltpu
from jax.sharding import PartitionSpec as P

HEAD_DIM = 64
LOW = jnp.bfloat16
F32 = jnp.float32
MESH = pl.DeviceIdType.MESH


def dot_nn(left, right):
    return lax.dot_general(left, right, (((1,), (0,)), ((), ())), preferred_element_type=F32)


def dot_nt(left, right):
    return lax.dot_general(left, right, (((1,), (1,)), ((), ())), preferred_element_type=F32)


def dot_tn(left, right):
    return lax.dot_general(left, right, (((0,), (0,)), ((), ())), preferred_element_type=F32)


class Ring:
    def __init__(self, axis):
        whole = lax.axis_index("dp")
        rest = None
        if axis == "x":
            self.me = lax.axis_index("tensor")
        elif axis == "y":
            self.me, rest = lax.rem(whole, 4), lax.div(whole, 4) * 4
        else:
            self.me, rest = lax.div(whole, 4), lax.rem(whole, 4)
        self.right = lax.rem(self.me + 1, 4)
        self.left = lax.rem(self.me + 3, 4)
        self.opposite = lax.rem(self.me + 2, 4)

        def device(place):
            if axis == "x":
                return {"tensor": place}
            if axis == "y":
                return {"dp": rest + place}
            return {"dp": place * 4 + rest}

        self.to_right, self.to_left = device(self.right), device(self.left)


def sibling():
    return {"section": 1 - lax.axis_index("section")}


def greet(*targets):
    barrier = pltpu.get_barrier_semaphore()
    for target in targets:
        pl.semaphore_signal(barrier, inc=1, device_id=target, device_id_type=MESH)
    pl.semaphore_wait(barrier, len(targets))


def remote(src, dst, sems, which, target):
    return pltpu.make_async_remote_copy(
        src_ref=src,
        dst_ref=dst,
        send_sem=sems[0].at[which],
        recv_sem=sems[1].at[which],
        device_id=target,
        device_id_type=MESH,
    )


class Gather:
    def __init__(self, ring, slot, sems, own=None):
        self.ring, self.slot, self.sems = ring, slot, sems
        self.own = own if own is not None else lambda half: slot(ring.me, half)

    def copy(self, which, arriving=False):
        ring = self.ring
        half = (0, 1, 1, 0, 0, 1)[which]
        goes_right = which in (0, 2, 4)
        target = ring.to_right if goes_right else ring.to_left
        if which < 4:
            source_block = ring.left if goes_right else ring.right
            if not arriving:
                return remote(self.own(half), self.slot(ring.me, half), self.sems, which, target)
        else:
            source_block = ring.opposite
            if not arriving:
                handed = self.slot(ring.left if goes_right else ring.right, half)
                return remote(handed, handed, self.sems, which, target)
        part = self.slot(source_block, half)
        return remote(part, part, self.sems, which, target)

    def start(self):
        for which in range(4):
            self.copy(which).start()

    def relay(self):
        for which in (0, 1):
            self.copy(which, arriving=True).wait_recv()
            self.copy(which + 4).start()

    def wait_left(self):
        self.copy(2, arriving=True).wait_recv()

    def wait_right(self):
        self.copy(3, arriving=True).wait_recv()

    def wait_opposite(self):
        self.copy(4, arriving=True).wait_recv()
        self.copy(5, arriving=True).wait_recv()

    def wait_all(self):
        self.wait_left()
        self.wait_right()
        self.wait_opposite()

    def finish(self):
        for which in range(6):
            self.copy(which).wait_send()


class Scatter:
    def __init__(self, ring, part, landing, passing, arrived, sems):
        self.ring, self.part, self.landing, self.passing = ring, part, landing, passing
        self.arrived, self.sems = arrived, sems

    def copy(self, which):
        ring = self.ring
        half = (0, 1, 1, 0, 0, 1)[which]
        goes_right = which in (0, 2, 4)
        if which < 2:
            src, dst = self.part(ring.opposite, half), self.landing(half)
        else:
            dst = self.arrived(0 if goes_right else 1, half)
            if which < 4:
                src = self.part(ring.right if goes_right else ring.left, half)
            else:
                src = self.passing(half)
        return remote(src, dst, self.sems, which, ring.to_right if goes_right else ring.to_left)

    def start_near(self):
        self.copy(2).start()
        self.copy(3).start()

    def start_far(self):
        self.copy(0).start()
        self.copy(1).start()

    def relay(self):
        for half, block in ((0, self.ring.right), (1, self.ring.left)):
            self.copy(half).wait_recv()
            added = self.part(block, half)[...].astype(F32) + self.landing(half)[...].astype(F32)
            self.passing(half)[...] = added.astype(LOW)
            self.copy(half + 4).start()

    def wait(self):
        for which in (2, 3, 4, 5):
            self.copy(which).wait_recv()

    def total(self, half):
        return (
            self.part(self.ring.me, half)[...].astype(F32)
            + self.arrived(0, half)[...].astype(F32)
            + self.arrived(1, half)[...].astype(F32)
        )

    def finish(self):
        for which in range(6):
            self.copy(which).wait_send()


def row_gather(ring, full, sems):
    half = full.shape[1] // 2
    return Gather(ring, lambda block, which: full.at[block, pl.ds(which * half, half)], sems)


def row_scatter(ring, parts, landing, passing, arrived, sems):
    half = parts.shape[1] // 2

    def rows(which):
        return pl.ds(which * half, half)

    return Scatter(
        ring,
        lambda block, which: parts.at[block, rows(which)],
        lambda which: landing.at[which],
        lambda which: passing.at[which],
        lambda side, which: arrived.at[side, rows(which)],
        sems,
    )


def row_total(scatter):
    scatter.wait()
    return jnp.concatenate([scatter.total(0), scatter.total(1)], axis=0)


def norm_stats(values):
    average = jnp.mean(values, axis=-1, keepdims=True)
    centered = values - average
    variance = jnp.mean(centered * centered, axis=-1, keepdims=True)
    scale = lax.rsqrt(variance + 1e-05)
    return centered * scale, scale


def norm_back(values, gain, grad):
    xhat, scale = norm_stats(values)
    scaled = grad * gain
    part = scale * (
        scaled
        - jnp.mean(scaled, axis=-1, keepdims=True)
        - xhat * jnp.mean(scaled * xhat, axis=-1, keepdims=True)
    )
    return part, jnp.sum(grad * xhat, axis=0, keepdims=True)


def gelu_tanh(values):
    inner = 0.7978845608028654 * (values + 0.044715 * values * values * values)
    return 0.5 * values * (1.0 + jnp.tanh(inner))


def gelu_slope(values):
    square = values * values
    bent = jnp.tanh(0.7978845608028654 * values * (1.0 + 0.044715 * square))
    slope = 0.7978845608028654 * (1.0 + 3.0 * 0.044715 * square)
    return 0.5 * (1.0 + bent) + 0.5 * values * (1.0 - bent * bent) * slope


def pick_copies(layer, mine, theirs, target, sem):
    def start():
        mine_here = lax.axis_index("section") == layer

        @pl.when(mine_here)
        def _():
            pltpu.make_async_copy(mine, target, sem).start()

        @pl.when(jnp.logical_not(mine_here))
        def _():
            pltpu.make_async_copy(theirs, target, sem).start()

    def wait():
        pltpu.make_async_copy(mine, target, sem).wait()

    return start, wait


def pair_columns(features):
    width = 2 * HEAD_DIM
    return [
        (start, min(width, features - start)) for start in range(0, features, width)
    ]


def head_masks(width):
    lanes = lax.broadcasted_iota(jnp.int32, (1, width), 1)
    if width == HEAD_DIM:
        return [None]
    return [lanes < HEAD_DIM, lanes >= HEAD_DIM]


def masked(values, mask):
    return values if mask is None else jnp.where(mask, values, jnp.zeros_like(values))


def attention_weights(layer, mine, theirs, target, sems):
    return [
        pick_copies(layer, mine.at[which], theirs.at[which], target.at[which], sems.at[which])
        for which in range(4)
    ]


def forward_kernel(
    layer, features, x_ref, bias_ref, gains_ref, at_mine, at_theirs, up_mine, up_theirs, down_mine,
    down_theirs, y_ref, middle_ref, one_ref, query_ref, key_ref, value_ref, mixed_ref, two_ref,
    act_ref, hidden_ref, at_w, up_w, down_w, weight_sems, parts, landing, passing, arrived,
    key_send, key_recv, value_send, value_recv, two_send, two_recv, sum_send, sum_recv,
):
    ring = Ring("x")
    me = ring.me
    fetches = attention_weights(layer, at_mine, at_theirs, at_w, weight_sems)
    fetches.append(pick_copies(layer, up_mine, up_theirs, up_w, weight_sems.at[4]))
    fetches.append(pick_copies(layer, down_mine, down_theirs, down_w, weight_sems.at[5]))
    for which in (1, 2, 0, 3, 4, 5):
        fetches[which][0]()
    greet(ring.to_right, ring.to_left)
    rows = x_ref.shape[0]
    inputs = x_ref[...].astype(F32)
    xhat, _ = norm_stats(inputs)
    one_ref[...] = (xhat * gains_ref[0:1, :]).astype(LOW)
    normed_one = one_ref[...]
    fetches[1][1]()
    key_ref[me] = dot_nn(normed_one, at_w[1]).astype(LOW)
    keys = row_gather(ring, key_ref, (key_send, key_recv))
    keys.start()
    fetches[2][1]()
    value_ref[me] = dot_nn(normed_one, at_w[2]).astype(LOW)
    values = row_gather(ring, value_ref, (value_send, value_recv))
    values.start()
    fetches[0][1]()
    query_ref[...] = dot_nn(normed_one, at_w[0]).astype(LOW)
    keys.relay()
    values.relay()
    keys.wait_all()
    values.wait_all()
    fetches[3][1]()
    bias = bias_ref[...]
    for begin, width in pair_columns(features):
        columns = pl.ds(begin, width)
        queries = query_ref[:, columns]
        key_block = key_ref[:, :, columns].reshape(4 * rows, width)
        value_block = value_ref[:, :, columns].reshape(4 * rows, width)
        mixed = None
        for mask in head_masks(width):
            scores = dot_nt(masked(queries, mask), key_block) * 0.125 + bias
            raised = jnp.exp(scores - jnp.max(scores, axis=-1, keepdims=True))
            probs = raised * (1.0 / jnp.sum(raised, axis=-1, keepdims=True))
            own = dot_nn(probs.astype(LOW), value_block)
            mixed = own if mixed is None else jnp.where(mask, own, mixed)
        mixed_ref[:, columns] = mixed.astype(LOW)
    middle_ref[...] = x_ref[...].astype(F32) + dot_nn(mixed_ref[...], at_w[3])
    xhat, _ = norm_stats(middle_ref[...])
    two_ref[me] = (xhat * gains_ref[1:2, :]).astype(LOW)
    tokens = row_gather(ring, two_ref, (two_send, two_recv))
    tokens.start()
    fetches[4][1]()
    fetches[5][1]()
    sums = row_scatter(ring, parts, landing, passing, arrived, (sum_send, sum_recv))

    def feed(block):
        act_ref[block] = dot_nn(two_ref[block], up_w[...])
        hidden_ref[block] = gelu_tanh(act_ref[block]).astype(LOW)
        parts[block] = dot_nn(hidden_ref[block], down_w[...]).astype(LOW)

    feed(me)
    tokens.relay()
    tokens.wait_left()
    feed(ring.left)
    tokens.wait_right()
    feed(ring.right)
    sums.start_near()
    tokens.wait_opposite()
    feed(ring.opposite)
    sums.start_far()
    sums.relay()
    y_ref[...] = (middle_ref[...] + row_total(sums)).astype(LOW)
    keys.finish()
    values.finish()
    tokens.finish()
    sums.finish()


def scatter_scratch(rows, features):
    return [
        pltpu.VMEM((4, rows, features), LOW),
        pltpu.VMEM((2, rows // 2, features), LOW),
        pltpu.VMEM((2, rows // 2, features), LOW),
        pltpu.VMEM((2, rows, features), LOW),
    ]


def weight_scratch(features, hidden):
    return [
        pltpu.VMEM((4, features, features), LOW),
        pltpu.VMEM((features, hidden), LOW),
        pltpu.VMEM((hidden, features), LOW),
        pltpu.SemaphoreType.DMA((6,)),
    ]


def in_vmem():
    return pl.BlockSpec(memory_space=pltpu.VMEM)


def anywhere():
    return pl.BlockSpec(memory_space=pl.ANY)


def forward_layer(layer, x, bias, gains, attention, feed):
    rows, features = x.shape
    hidden = feed[0].shape[1]
    out_shape = (
        jax.ShapeDtypeStruct((rows, features), LOW),
        jax.ShapeDtypeStruct((rows, features), F32),
        jax.ShapeDtypeStruct((rows, features), LOW),
        jax.ShapeDtypeStruct((rows, features), LOW),
        jax.ShapeDtypeStruct((4, rows, features), LOW),
        jax.ShapeDtypeStruct((4, rows, features), LOW),
        jax.ShapeDtypeStruct((rows, features), LOW),
        jax.ShapeDtypeStruct((4, rows, features), LOW),
        jax.ShapeDtypeStruct((4, rows, hidden), F32),
        jax.ShapeDtypeStruct((4, rows, hidden), LOW),
    )
    return pl.pallas_call(
        functools.partial(forward_kernel, layer, features),
        out_shape=out_shape,
        in_specs=[in_vmem()] * 3 + [anywhere()] * 6,
        out_specs=[in_vmem()] * len(out_shape),
        scratch_shapes=weight_scratch(features, hidden)
        + scatter_scratch(rows, features)
        + [pltpu.SemaphoreType.DMA((6,))] * 8,
        compiler_params=pltpu.CompilerParams(
            collective_id=layer, has_side_effects=True, vmem_limit_bytes=56 * 2**20
        ),
        cost_estimate=pl.CostEstimate(
            flops=3 * 10**9, bytes_accessed=24 * 10**6, transcendentals=10**6
        ),
        name=f"layer_forward_{layer}",
    )(x, bias, gains, *attention, *feed)


def backward_kernel(
    layer, features, x_ref, dy_ref, bias_ref, gains_ref, middle_ref, query_ref, key_ref, value_ref,
    act_ref, at_mine, at_theirs, up_mine, up_theirs, down_mine, down_theirs,
    dx_ref, gain_ref, out_ref, pre_ref, branch_ref, dquery_ref, dkey_ref, dvalue_ref,
    at_w, up_w, down_w, weight_sems, parts, landing, passing, arrived, parts_b, landing_b,
    passing_b, arrived_b, parts_c, landing_c, passing_c, arrived_c, mixed_grad,
    out_send, out_recv, sum_send, sum_recv, key_send, key_recv, value_send, value_recv,
):
    ring = Ring("x")
    me = ring.me
    fetches = attention_weights(layer, at_mine, at_theirs, at_w, weight_sems)
    fetches.append(pick_copies(layer, up_mine, up_theirs, up_w, weight_sems.at[4]))
    fetches.append(pick_copies(layer, down_mine, down_theirs, down_w, weight_sems.at[5]))
    for which in (5, 4, 3, 0, 1, 2):
        fetches[which][0]()
    rows = x_ref.shape[0]
    out_ref[me] = dy_ref[...]
    greet(ring.to_right, ring.to_left)
    grads = row_gather(ring, out_ref, (out_send, out_recv))
    grads.start()
    sums = row_scatter(ring, parts, landing, passing, arrived, (sum_send, sum_recv))
    fetches[5][1]()
    fetches[4][1]()

    def feed(block):
        hidden_grad = dot_nt(out_ref[block], down_w[...])
        pre_ref[block] = (hidden_grad * gelu_slope(act_ref[block])).astype(LOW)
        parts[block] = dot_nt(pre_ref[block], up_w[...]).astype(LOW)

    feed(me)
    grads.relay()
    grads.wait_left()
    feed(ring.left)
    grads.wait_right()
    feed(ring.right)
    sums.start_near()
    grads.wait_opposite()
    feed(ring.opposite)
    sums.start_far()
    sums.relay()
    middle_part, gain_two = norm_back(middle_ref[...], gains_ref[1:2, :], row_total(sums))
    gain_ref[1:2, :] = gain_two
    middle_grad = dy_ref[...].astype(F32) + middle_part
    middle_ref_grad = middle_grad
    branch_ref[...] = middle_grad.astype(LOW)
    fetches[3][1]()
    mixed_grad[...] = dot_nt(branch_ref[...], at_w[3]).astype(LOW)
    bias = bias_ref[...]
    for begin, width in pair_columns(features):
        columns = pl.ds(begin, width)
        queries = query_ref[:, columns]
        outer = mixed_grad[:, columns]
        key_block = key_ref[:, :, columns].reshape(4 * rows, width)
        value_block = value_ref[:, :, columns].reshape(4 * rows, width)
        dquery = dkey = dvalue = None
        for mask in head_masks(width):
            query_one, outer_one = masked(queries, mask), masked(outer, mask)
            scores = dot_nt(key_block, query_one) * 0.125 + bias
            raised = jnp.exp(scores - jnp.max(scores, axis=0, keepdims=True))
            probs = raised * (1.0 / jnp.sum(raised, axis=0, keepdims=True))
            probs_grad = dot_nt(value_block, outer_one)
            mean = jnp.sum(probs * probs_grad, axis=0, keepdims=True)
            score_grad = (probs * (probs_grad - mean)).astype(LOW)
            own_query = dot_tn(score_grad, key_block)
            own_key = dot_nn(score_grad, query_one)
            own_value = dot_nn(probs.astype(LOW), outer_one)
            if dquery is None:
                dquery, dkey, dvalue = own_query, own_key, own_value
            else:
                dquery = jnp.where(mask, own_query, dquery)
                dkey, dvalue = dkey + own_key, dvalue + own_value
        dquery_ref[:, columns] = (dquery * 0.125).astype(LOW)
        parts_b[:, :, columns] = (dkey * 0.125).astype(LOW).reshape(4, rows, width)
        parts_c[:, :, columns] = dvalue.astype(LOW).reshape(4, rows, width)
    dkeys = row_scatter(ring, parts_b, landing_b, passing_b, arrived_b, (key_send, key_recv))
    dvalues = row_scatter(
        ring, parts_c, landing_c, passing_c, arrived_c, (value_send, value_recv)
    )
    dkeys.start_far()
    dvalues.start_far()
    dkeys.start_near()
    dvalues.start_near()
    for which in (0, 1, 2):
        fetches[which][1]()
    one_grad = dot_nt(dquery_ref[...], at_w[0])
    dkeys.relay()
    dvalues.relay()
    dkey_ref[...] = row_total(dkeys).astype(LOW)
    dvalue_ref[...] = row_total(dvalues).astype(LOW)
    one_grad = one_grad + dot_nt(dkey_ref[...], at_w[1]) + dot_nt(dvalue_ref[...], at_w[2])
    inputs_part, gain_one = norm_back(x_ref[...].astype(F32), gains_ref[0:1, :], one_grad)
    gain_ref[0:1, :] = gain_one
    dx_ref[...] = (middle_ref_grad + inputs_part).astype(LOW)
    grads.finish()
    sums.finish()
    dkeys.finish()
    dvalues.finish()


def backward_layer(layer, x, dy, bias, gains, middle, query, key, value, act, attention, feed):
    rows, features = x.shape
    hidden = feed[0].shape[1]
    out_shape = (
        jax.ShapeDtypeStruct((rows, features), LOW),
        jax.ShapeDtypeStruct((2, features), F32),
        jax.ShapeDtypeStruct((4, rows, features), LOW),
        jax.ShapeDtypeStruct((4, rows, hidden), LOW),
        jax.ShapeDtypeStruct((rows, features), LOW),
        jax.ShapeDtypeStruct((rows, features), LOW),
        jax.ShapeDtypeStruct((rows, features), LOW),
        jax.ShapeDtypeStruct((rows, features), LOW),
    )
    return pl.pallas_call(
        functools.partial(backward_kernel, layer, features),
        out_shape=out_shape,
        in_specs=[in_vmem()] * 9 + [anywhere()] * 6,
        out_specs=[in_vmem()] * len(out_shape),
        scratch_shapes=weight_scratch(features, hidden)
        + scatter_scratch(rows, features) * 3
        + [pltpu.VMEM((rows, features), LOW)]
        + [pltpu.SemaphoreType.DMA((6,))] * 8,
        compiler_params=pltpu.CompilerParams(
            collective_id=2 + layer, has_side_effects=True, vmem_limit_bytes=56 * 2**20
        ),
        cost_estimate=pl.CostEstimate(
            flops=4 * 10**9, bytes_accessed=24 * 10**6, transcendentals=10**6
        ),
        name=f"layer_backward_{layer}",
    )(x, dy, bias, gains, middle, query, key, value, act, *attention, *feed)


X_ROWS, Y_ROWS = 48, 112


def weights_kernel(
    shard_ref, gain_ref, mine_ref, theirs_ref, gain_mine, gain_theirs, local_sems, x_send, x_recv,
    yx_send, yx_recv, zx_send, zx_recv, y_send, y_recv, z_send, z_recv, gain_send, gain_recv,
    pair_send, pair_recv,
):
    x_ring, y_ring, z_ring = Ring("x"), Ring("y"), Ring("z")
    mine_y, mine_z, mine_x = y_ring.me, z_ring.me, x_ring.me
    share = shard_ref.shape[1]
    y_begin, z_begin = X_ROWS, X_ROWS + Y_ROWS
    z_rows = share - z_begin
    all_x, all_y, all_z = pl.ds(0, X_ROWS), pl.ds(y_begin, Y_ROWS), pl.ds(z_begin, z_rows)
    y_half = (pl.ds(y_begin, 64), pl.ds(y_begin + 64, Y_ROWS - 64))
    z_half = (pl.ds(z_begin, 64), pl.ds(z_begin + 64, z_rows - 64))
    pair = sibling()
    greet(
        x_ring.to_right, x_ring.to_left, y_ring.to_right, y_ring.to_left, z_ring.to_right,
        z_ring.to_left, pair,
    )
    locals_ = [
        pltpu.make_async_copy(
            shard_ref.at[mine_y, all_y], mine_ref.at[mine_y, mine_x, all_y], local_sems.at[0]
        ),
        pltpu.make_async_copy(
            shard_ref.at[mine_z, all_z], mine_ref.at[mine_z, mine_x, all_z], local_sems.at[1]
        ),
        pltpu.make_async_copy(
            shard_ref.at[:, all_x], mine_ref.at[:, mine_x, all_x], local_sems.at[2]
        ),
        pltpu.make_async_copy(gain_ref, gain_mine.at[mine_x], local_sems.at[3]),
    ]
    first_y = Gather(
        x_ring,
        lambda block, half: mine_ref.at[mine_y, block, y_half[half]],
        (yx_send, yx_recv),
        lambda half: shard_ref.at[mine_y, y_half[half]],
    )
    first_z = Gather(
        x_ring,
        lambda block, half: mine_ref.at[mine_z, block, z_half[half]],
        (zx_send, zx_recv),
        lambda half: shard_ref.at[mine_z, z_half[half]],
    )
    along_x = Gather(
        x_ring,
        lambda block, half: mine_ref.at[pl.ds(2 * half, 2), block, all_x],
        (x_send, x_recv),
        lambda half: shard_ref.at[pl.ds(2 * half, 2), all_x],
    )
    along_y = Gather(
        y_ring,
        lambda block, half: mine_ref.at[block, pl.ds(2 * half, 2), all_y],
        (y_send, y_recv),
    )
    along_z = Gather(
        z_ring,
        lambda block, half: mine_ref.at[block, pl.ds(2 * half, 2), all_z],
        (z_send, z_recv),
    )

    def gain_copy(which, block, src=None):
        part = gain_mine.at[block]
        target = x_ring.to_left if which == 1 else x_ring.to_right
        return remote(part if src is None else src, part, (gain_send, gain_recv), which, target)

    def hand(which, region):
        return remote(mine_ref.at[region], theirs_ref.at[region], (pair_send, pair_recv), which, pair)

    handed = []

    def hand_on(which, region):
        copy = hand(which, region)
        copy.start()
        handed.append(copy)

    first_y.start()
    first_z.start()
    for copy in locals_:
        copy.start()
    gain_copy(0, mine_x, gain_ref).start()
    gain_copy(1, mine_x, gain_ref).start()
    along_x.start()
    first_y.relay()
    first_z.relay()
    first_y.wait_all()
    locals_[0].wait()
    along_y.start()
    hand_on(0, (mine_y, slice(None), all_y))
    first_z.wait_all()
    locals_[1].wait()
    along_z.start()
    hand_on(1, (mine_z, slice(None), all_z))
    gain_copy(0, x_ring.left).wait_recv()
    gain_copy(2, x_ring.left).start()
    along_x.relay()
    along_y.relay()
    along_z.relay()
    along_x.wait_all()
    locals_[2].wait()
    hand_on(2, (slice(None), slice(None), all_x))
    along_y.wait_left()
    hand_on(3, (y_ring.left, slice(None), all_y))
    along_z.wait_left()
    hand_on(4, (z_ring.left, slice(None), all_z))
    along_y.wait_right()
    hand_on(5, (y_ring.right, slice(None), all_y))
    along_z.wait_right()
    hand_on(6, (z_ring.right, slice(None), all_z))
    gain_copy(1, x_ring.right).wait_recv()
    gain_copy(2, x_ring.opposite).wait_recv()
    locals_[3].wait()
    gains = remote(gain_mine, gain_theirs, (pair_send, pair_recv), 9, pair)
    gains.start()
    along_y.wait_opposite()
    hand_on(7, (y_ring.opposite, slice(None), all_y))
    along_z.wait_opposite()
    hand_on(8, (z_ring.opposite, slice(None), all_z))
    for copy in handed + [gains]:
        copy.wait()
    for which in range(3):
        gain_copy(which, mine_x).wait_send()
    for gather in (first_y, first_z, along_x, along_y, along_z):
        gather.finish()


def gather_weights(shard, gain):
    mats, share, features = shard.shape
    full = jax.ShapeDtypeStruct((mats, 4, share, features), LOW)
    gains = jax.ShapeDtypeStruct((4,) + gain.shape, LOW)
    return pl.pallas_call(
        weights_kernel,
        out_shape=(full, full, gains, gains),
        in_specs=[anywhere()] * 2,
        out_specs=[anywhere()] * 4,
        scratch_shapes=[pltpu.SemaphoreType.DMA((4,))]
        + [pltpu.SemaphoreType.DMA((6,))] * 10
        + [pltpu.SemaphoreType.DMA((3,))] * 2
        + [pltpu.SemaphoreType.DMA((10,))] * 2,
        compiler_params=pltpu.CompilerParams(collective_id=4, has_side_effects=True),
        cost_estimate=pl.CostEstimate(flops=0, bytes_accessed=60 * 10**6, transcendentals=0),
        name="gather_weights",
    )(shard, gain)


class SmallSum:
    def __init__(self, ring, slots, sems):
        self.ring, self.slots, self.sems = ring, slots, sems

    def copy(self, which, block):
        target = self.ring.to_left if which == 1 else self.ring.to_right
        part = self.slots.at[block]
        return remote(part, part, self.sems, which, target)

    def start(self):
        self.copy(0, self.ring.me).start()
        self.copy(1, self.ring.me).start()

    def relay(self):
        self.copy(0, self.ring.left).wait_recv()
        self.copy(2, self.ring.left).start()

    def result(self):
        self.copy(1, self.ring.right).wait_recv()
        self.copy(2, self.ring.opposite).wait_recv()
        return (self.slots[0] + self.slots[1]) + (self.slots[2] + self.slots[3])

    def finish(self):
        for which in range(3):
            self.copy(which, self.ring.me).wait_send()


def gradient_kernel(features, *refs):
    (two_a, two_b, pre_a, pre_b, hid_a, hid_b, out_a, out_b, one_a, one_b, mix_a, mix_b, dq_a, dq_b,
     dk_a, dk_b, dv_a, dv_b, br_a, br_b, y_a, y_b, dx_a, dx_b, gain_in,
     feed_out, feed_other, at_out, at_other, act_out, grad_out, gain_out,
     feed_in, at_left, at_right, at_sum, feed_sum,
     xl, xp, xa, fl, fp, fa, fs, fr, al, ap, aa, as_, ar, ad, gain_pair, gain_x, gain_y, gain_z,
     local_sems, swap_send, swap_recv, x_send, x_recv, f_send, f_recv, fg_send, fg_recv, fh_send,
     fh_recv, a_send, a_recv, ag_send, ag_recv, ah_send, ah_recv, gain_send, gain_recv, end_send,
     end_recv, keep_sems) = refs
    x_ring, y_ring, z_ring = Ring("x"), Ring("y"), Ring("z")
    pair = sibling()
    section = lax.axis_index("section")
    share = features // 4
    greet(
        x_ring.to_right, x_ring.to_left, y_ring.to_right, y_ring.to_left, z_ring.to_right,
        z_ring.to_left, pair,
    )
    layers = (
        (two_a, pre_a, hid_a, out_a, one_a, mix_a, dq_a, dk_a, dv_a, br_a, y_a, dx_a),
        (two_b, pre_b, hid_b, out_b, one_b, mix_b, dq_b, dk_b, dv_b, br_b, y_b, dx_b),
    )

    def both(layer, first):
        (two, pre, hidden, out, one, mixed, dq, dk, dv, branch, _, _) = layers[layer]
        zero = (one, one, dq, dk, two, pre)
        other = (one, mixed, dv, branch, hidden, out)
        own, sent = (zero, other) if first else (other, zero)
        targets = [
            at_left.at[layer, 0], at_left.at[layer, 1], at_right.at[layer, 0],
            at_right.at[layer, 1], feed_in.at[layer, 0], feed_in.at[layer, 1],
        ]
        keeps = [
            pltpu.make_async_copy(ref, target.at[0], local_sems.at[layer * 6 + which])
            for which, (ref, target) in enumerate(zip(own, targets))
        ]
        sends = [
            remote(ref, target.at[1], (swap_send, swap_recv), layer * 6 + which, pair)
            for which, (ref, target) in enumerate(zip(sent, targets))
        ]
        return keeps, sends

    def start_inputs(first):
        for which in range(6):
            for layer in (1, 0):
                for copy in both(layer, first):
                    copy[which].start()

    def last_copies(layer):
        _, _, _, _, _, _, _, _, _, _, y, dx = layers[layer]
        return (
            remote(y, act_out.at[section], (swap_send, swap_recv), 12, pair),
            remote(dx, grad_out.at[section], (swap_send, swap_recv), 13, pair),
        )

    def keep_copies(layer):
        _, _, _, _, _, _, _, _, _, _, y, dx = layers[layer]
        return (
            pltpu.make_async_copy(y, act_out.at[section], keep_sems.at[0]),
            pltpu.make_async_copy(dx, grad_out.at[section], keep_sems.at[1]),
        )

    @pl.when(section == 0)
    def _():
        start_inputs(True)
        for copy in last_copies(1) + keep_copies(0):
            copy.start()

    @pl.when(section == 1)
    def _():
        start_inputs(False)
        for copy in last_copies(0) + keep_copies(1):
            copy.start()

    gain_pair[0] = gain_in[...]
    swap_gain = remote(gain_pair.at[0], gain_pair.at[1], (gain_send, gain_recv), 9, pair)
    swap_gain.start()

    def wait_inputs(layer, whiches):
        keeps, sends = both(layer, True)
        for which in whiches:
            keeps[which].wait()
            sends[which].wait_recv()

    x_sums, f_sums, f_mids, f_ends, a_sums, a_mids, a_ends = [], [], [], [], [], [], []
    f_half = ((0, 144), (144, share - 144))
    a_half = ((0, 80), (80, 64))
    for layer in range(2):

        def x_part(block, half, layer=layer):
            return at_sum.at[layer, half, pl.ds(pl.multiple_of(block * share, 16), share)]

        def pick(ref, layer=layer):
            return lambda half: ref.at[layer, half]

        def pick_side(ref, halves, layer=layer):
            return lambda side, half: ref.at[layer, side, pl.ds(*halves[half])]

        def pick_half(ref, halves, layer=layer):
            return lambda half: ref.at[layer, pl.ds(*halves[half])]

        def pick_slot(ref, halves, layer=layer):
            return lambda block, half: ref.at[layer, block, pl.ds(*halves[half])]

        def sems(send, recv, layer=layer):
            return send.at[layer], recv.at[layer]

        def f_part(block, half, layer=layer):
            begin, size = f_half[half]
            return feed_sum.at[layer, pl.ds(pl.multiple_of(block * share + begin, 16), size)]

        def a_part(block, half, layer=layer):
            begin, size = a_half[half]
            row = lax.rem(block, 2) * 144 + begin
            return ad.at[layer, lax.div(block, 2), pl.ds(pl.multiple_of(row, 16), size)]

        def a_out(block, half, layer=layer):
            begin, size = a_half[half]
            row = lax.rem(block, 2) * 144 + begin
            return at_out.at[layer, lax.div(block, 2), pl.ds(pl.multiple_of(row, 16), size)]

        x_sums.append(
            Scatter(
                x_ring, x_part, pick(xl), pick(xp),
                lambda side, half, layer=layer: xa.at[layer, side, half], sems(x_send, x_recv),
            )
        )
        near, far = (y_ring, z_ring) if layer == 0 else (z_ring, y_ring)
        f_sums.append(
            Scatter(
                near, f_part, pick_half(fl, f_half), pick_half(fp, f_half),
                pick_side(fa, f_half), sems(f_send, f_recv),
            )
        )
        f_mids.append(Gather(far, pick_slot(fs, f_half), sems(fg_send, fg_recv)))
        f_ends.append(
            Gather(near, pick_slot(feed_out, f_half), sems(fh_send, fh_recv), pick_half(fr, f_half))
        )
        a_sums.append(
            Scatter(
                near, a_part, pick_half(al, a_half), pick_half(ap, a_half),
                pick_side(aa, a_half), sems(a_send, a_recv),
            )
        )
        a_mids.append(Gather(far, pick_slot(as_, a_half), sems(ag_send, ag_recv)))
        a_ends.append(Gather(near, a_out, sems(ah_send, ah_recv), pick_half(ar, a_half)))

    chunks = [(begin, min(256, features - begin)) for begin in range(0, features, 256)]

    def attention_products(layer):
        wait_inputs(layer, (0, 1, 2, 3))
        for which in range(2):
            right = at_right[layer, which].reshape(-1, features)
            for begin, size in chunks:
                left = at_left[layer, which, :, :, pl.ds(begin, size)].reshape(-1, size)
                at_sum[layer, which, pl.ds(begin, size)] = dot_tn(left, right).astype(LOW)
        x_sums[layer].start_far()
        x_sums[layer].start_near()

    def feed_products(layer):
        wait_inputs(layer, (4, 5))
        right = feed_in[layer, 1].reshape(-1, features)
        for begin, size in chunks:
            left = feed_in[layer, 0, :, :, :, pl.ds(begin, size)].reshape(-1, size)
            feed_sum[layer, pl.ds(begin, size)] = dot_tn(left, right).astype(LOW)
        f_sums[layer].start_far()
        f_sums[layer].start_near()

    def feed_middle(layer):
        f_sums[layer].wait()
        place = f_mids[layer].ring.me
        for half in range(2):
            fs[layer, place, pl.ds(*f_half[half])] = f_sums[layer].total(half).astype(LOW)
        f_mids[layer].start()

    def four(ref, layer, halves, half):
        rows = pl.ds(*halves[half])
        return (ref[layer, 0, rows].astype(F32) + ref[layer, 1, rows].astype(F32)) + (
            ref[layer, 2, rows].astype(F32) + ref[layer, 3, rows].astype(F32)
        )

    def feed_end(layer):
        f_mids[layer].wait_all()
        for half in range(2):
            fr[layer, pl.ds(*f_half[half])] = four(fs, layer, f_half, half).astype(LOW)
        f_ends[layer].start()
        pltpu.make_async_copy(
            fr.at[layer], feed_out.at[layer, f_ends[layer].ring.me], keep_sems.at[2 + layer]
        ).start()

    def attention_middle(layer):
        x_sums[layer].wait()
        for half in range(2):
            ad[layer, half, pl.ds(0, share)] = x_sums[layer].total(half).astype(LOW)
            ad[layer, half, pl.ds(share, 288 - share)] = jnp.zeros((288 - share, features), LOW)
        a_sums[layer].start_far()
        a_sums[layer].start_near()

    def attention_far(layer):
        a_sums[layer].wait()
        place = a_mids[layer].ring.me
        for half in range(2):
            as_[layer, place, pl.ds(*a_half[half])] = a_sums[layer].total(half).astype(LOW)
        a_mids[layer].start()

    def own_attention(layer):
        block = a_ends[layer].ring.me
        row = pl.multiple_of(lax.rem(block, 2) * 144, 16)
        return pltpu.make_async_copy(
            ar.at[layer], at_out.at[layer, lax.div(block, 2), pl.ds(row, 144)],
            keep_sems.at[4 + layer],
        )

    def attention_end(layer):
        a_mids[layer].wait_all()
        for half in range(2):
            ar[layer, pl.ds(*a_half[half])] = four(as_, layer, a_half, half).astype(LOW)
        a_ends[layer].start()
        own_attention(layer).start()

    attention_products(1)
    attention_products(0)
    feed_products(0)
    feed_products(1)

    swap_gain.wait()
    gain_x[x_ring.me] = gain_pair[0] + gain_pair[1]
    small = [
        SmallSum(ring, slots, (gain_send.at[pl.ds(3 * i, 3)], gain_recv.at[pl.ds(3 * i, 3)]))
        for i, (ring, slots) in enumerate(((x_ring, gain_x), (y_ring, gain_y), (z_ring, gain_z)))
    ]
    small[0].start()
    x_sums[1].relay()
    f_sums[0].relay()
    f_sums[1].relay()
    small[0].relay()
    feed_middle(0)
    feed_middle(1)
    gain_y[y_ring.me] = small[0].result()
    small[1].start()
    f_mids[0].relay()
    f_mids[1].relay()
    x_sums[0].relay()
    small[1].relay()
    attention_middle(1)
    feed_end(0)
    feed_end(1)
    gain_z[z_ring.me] = small[1].result()
    small[2].start()
    a_sums[1].relay()
    f_ends[0].relay()
    f_ends[1].relay()
    small[2].relay()
    attention_far(1)
    attention_middle(0)
    a_mids[1].relay()
    attention_end(1)
    a_sums[0].relay()
    a_ends[1].relay()
    gain_out[...] = small[2].result()

    for layer in range(2):
        f_ends[layer].wait_all()
        pltpu.make_async_copy(
            fr.at[layer], feed_out.at[layer, f_ends[layer].ring.me], keep_sems.at[2 + layer]
        ).wait()
    end_feed = remote(feed_out.at[1 - section], feed_other, (end_send, end_recv), 0, pair)
    end_feed.start()

    attention_far(0)
    a_mids[0].relay()
    attention_end(0)
    a_ends[0].relay()
    for layer in (1, 0):
        a_ends[layer].wait_all()
        own_attention(layer).wait()
    end_attention = remote(at_out.at[1 - section], at_other, (end_send, end_recv), 1, pair)
    end_attention.start()
    for layer in range(2):
        for copy in both(layer, True)[1]:
            copy.wait_send()
        for many in (x_sums, f_sums, f_mids, f_ends, a_sums, a_mids, a_ends):
            many[layer].finish()
    for each in small:
        each.finish()
    for copy in last_copies(0):
        copy.wait()
    for copy in keep_copies(0):
        copy.wait()
    end_feed.wait()
    end_attention.wait()


def sum_gradients(features, rows, operands, gain):
    share = features // 4
    dma = pltpu.SemaphoreType.DMA

    def low(*shape):
        return pltpu.VMEM(shape + (features,), LOW)

    def out(*shape):
        return jax.ShapeDtypeStruct(shape + (features,), LOW)

    return pl.pallas_call(
        functools.partial(gradient_kernel, features),
        out_shape=(
            out(2, 4, share), out(4, share), out(2, 2, 288), out(2, 288), out(2, rows),
            out(2, rows), jax.ShapeDtypeStruct((8, features), F32),
        ),
        in_specs=[anywhere()] * 24 + [in_vmem()],
        out_specs=[anywhere()] * 6 + [in_vmem()],
        scratch_shapes=[
            low(2, 2, 2, 4, rows), low(2, 2, 2, rows), low(2, 2, 2, rows),
            low(2, 2, features), low(2, features),
            low(2, 2, share), low(2, 2, share), low(2, 2, 2, share),
            low(2, share), low(2, share), low(2, 2, share), low(2, 4, share), low(2, share),
            low(2, 144), low(2, 144), low(2, 2, 144), low(2, 4, 144), low(2, 144),
            low(2, 2, 288),
            pltpu.VMEM((2, 8, features), F32),
            pltpu.VMEM((4, 8, features), F32),
            pltpu.VMEM((4, 8, features), F32),
            pltpu.VMEM((4, 8, features), F32),
            dma((12,)), dma((14,)), dma((14,)),
        ]
        + [dma((2, 6))] * 14
        + [dma((10,)), dma((10,)), dma((2,)), dma((2,)), dma((6,))],
        compiler_params=pltpu.CompilerParams(
            collective_id=5, has_side_effects=True, vmem_limit_bytes=60 * 2**20
        ),
        cost_estimate=pl.CostEstimate(
            flops=12 * 10**9, bytes_accessed=60 * 10**6, transcendentals=0
        ),
        name="sum_gradients",
    )(*operands, gain)


def doc_numbers(lengths, positions):
    doc_ends = jnp.cumsum(lengths)
    return jnp.sum((positions[:, None] >= doc_ends[None, :]).astype(jnp.int32), axis=1)


def swapped(block):
    return lax.ppermute(block, "section", [(0, 1), (1, 0)])


def body(tokens, cotangent, doc_lengths, norm_gains, w_qkv, w_out, w_up, w_down):
    batches, rows, features = tokens.shape
    share = w_qkv.shape[1]
    seq_rows = rows * lax.axis_size("tensor")
    section = lax.axis_index("section")
    is_first = section == 0

    def choose(zero_side, one_side):
        return jnp.where(is_first, zero_side, one_side)

    own_tokens = lax.dynamic_index_in_dim(tokens, section, 0, keepdims=False)
    own_cotangent = lax.dynamic_index_in_dim(cotangent, section, 0, keepdims=False)
    lengths = lax.dynamic_index_in_dim(doc_lengths, section, 0, keepdims=False)
    own_places = lax.axis_index("tensor") * rows + jnp.arange(rows, dtype=jnp.int32)
    all_places = jnp.arange(seq_rows, dtype=jnp.int32)
    own_docs = doc_numbers(lengths, own_places)
    all_docs = doc_numbers(lengths, all_places)
    allowed = (all_places[None, :] <= own_places[:, None]) & (
        all_docs[None, :] == own_docs[:, None]
    )
    bias = jnp.where(allowed, 0.0, -1e30).astype(F32)
    bias_turned = bias.T

    feed = (w_up[0], swapped(w_up[0]), w_down[0], swapped(w_down[0]))
    shard = jnp.stack(
        [w_qkv[0, :, :features], w_qkv[0, :, features : 2 * features], w_qkv[0, :, 2 * features :],
         w_out[0]]
    )
    gain_shard = jnp.pad(norm_gains[0], ((0, 14), (0, 0)))
    at_mine, at_theirs, gain_mine, gain_theirs = gather_weights(shard, gain_shard)
    attention = (
        at_mine.reshape(4, features, features), at_theirs.reshape(4, features, features)
    )

    def whole_gains(block):
        return block[:, :2].transpose(1, 0, 2).reshape(2, features).astype(F32)

    gain_mine, gain_theirs = whole_gains(gain_mine), whole_gains(gain_theirs)
    gains = (choose(gain_mine, gain_theirs), choose(gain_theirs, gain_mine))

    inputs = own_tokens
    saved = []
    for layer in range(2):
        results = forward_layer(layer, inputs, bias, gains[layer], attention, feed)
        saved.append((inputs,) + tuple(results))
        inputs = results[0]

    grad = own_cotangent
    pieces = [None, None]
    gain_grads = [None, None]
    for layer in (1, 0):
        (x, y, middle, normed_one, query, key, value, mixed, normed_two, act, hidden) = saved[layer]
        (grad, gain_grads[layer], out_all, pre_grad, branch, dquery, dkey, dvalue) = backward_layer(
            layer, x, grad, bias_turned, gains[layer], middle, query, key, value, act,
            attention, feed,
        )
        pieces[layer] = (
            normed_two, pre_grad, hidden, out_all, normed_one, mixed, dquery, dkey, dvalue, branch,
            y, grad,
        )
    operands = [member[layer] for member in zip(*pieces) for layer in range(2)]
    gain_rows = jnp.concatenate(gain_grads + [jnp.zeros((4, features), F32)], axis=0)
    feed_both, feed_other, at_both, at_other, activations, input_grads, gain_total = sum_gradients(
        features, rows, operands, gain_rows
    )
    gain_own = lax.dynamic_slice(
        gain_total, (2 * section, lax.axis_index("tensor") * share), (2, share)
    )
    feed_kept = lax.dynamic_index_in_dim(feed_both, section, 0, keepdims=False)
    at_kept = lax.dynamic_index_in_dim(at_both, section, 0, keepdims=False)

    def wide(block):
        return block.reshape(features, features).astype(F32)[None]

    first_half = choose(at_kept, at_other)[:, :share].astype(F32)
    other_half = choose(at_other, at_kept)[:, :share].astype(F32)
    grad_qkv = jnp.concatenate([first_half[0], first_half[1], other_half[0]], axis=1)
    return (
        activations[None],
        input_grads[None],
        gain_own[None],
        grad_qkv[None],
        other_half[1][None],
        wide(choose(feed_kept, feed_other)),
        wide(choose(feed_other, feed_kept)),
    )


def solution(mesh):
    placed = (
        P("dp", "tensor", None),
        P("dp", "tensor", None),
        P("dp", None),
        P("section", None, "tensor"),
        P("section", "tensor", None),
        P("section", "tensor", None),
        P("section", None, "tensor"),
        P("section", "tensor", None),
    )
    return jax.shard_map(
        body,
        mesh=mesh,
        in_specs=placed,
        out_specs=(
            P("section", "dp", "tensor", None),
            P("section", "dp", "tensor", None),
            P("section", None, "tensor"),
            P("section", "tensor", None),
            P("section", "tensor", None),
            P("section", None, "tensor"),
            P("section", "tensor", None),
        ),
        check_vma=False,
    )
```

```python
import functools
import jax
import jax.numpy as jnp
from jax import lax
from jax.experimental import pallas as pl
from jax.experimental.pallas import tpu as pltpu
from jax.sharding import PartitionSpec as P

HEAD_DIM = 64
LOW = jnp.bfloat16
F32 = jnp.float32
MESH = pl.DeviceIdType.MESH


def dot_nn(left, right):
    return lax.dot_general(left, right, (((1,), (0,)), ((), ())), preferred_element_type=F32)


def dot_nt(left, right):
    return lax.dot_general(left, right, (((1,), (1,)), ((), ())), preferred_element_type=F32)


def dot_tn(left, right):
    return lax.dot_general(left, right, (((0,), (0,)), ((), ())), preferred_element_type=F32)


class Ring:
    def __init__(self, axis):
        whole = lax.axis_index("dp")
        rest = None
        if axis == "x":
            self.me = lax.axis_index("tensor")
        elif axis == "y":
            self.me, rest = lax.rem(whole, 4), lax.div(whole, 4) * 4
        else:
            self.me, rest = lax.div(whole, 4), lax.rem(whole, 4)
        self.right = lax.rem(self.me + 1, 4)
        self.left = lax.rem(self.me + 3, 4)
        self.opposite = lax.rem(self.me + 2, 4)

        def device(place):
            if axis == "x":
                return {"tensor": place}
            if axis == "y":
                return {"dp": rest + place}
            return {"dp": place * 4 + rest}

        self.to_right, self.to_left = device(self.right), device(self.left)


def sibling():
    return {"section": 1 - lax.axis_index("section")}


def greet(*targets):
    barrier = pltpu.get_barrier_semaphore()
    for target in targets:
        pl.semaphore_signal(barrier, inc=1, device_id=target, device_id_type=MESH)
    pl.semaphore_wait(barrier, len(targets))


def remote(src, dst, sems, which, target):
    return pltpu.make_async_remote_copy(
        src_ref=src,
        dst_ref=dst,
        send_sem=sems[0].at[which],
        recv_sem=sems[1].at[which],
        device_id=target,
        device_id_type=MESH,
    )


class Gather:
    def __init__(self, ring, slot, sems, own=None):
        self.ring, self.slot, self.sems = ring, slot, sems
        self.own = own if own is not None else lambda half: slot(ring.me, half)

    def copy(self, which, arriving=False):
        ring = self.ring
        half = (0, 1, 1, 0, 0, 1)[which]
        goes_right = which in (0, 2, 4)
        target = ring.to_right if goes_right else ring.to_left
        if which < 4:
            source_block = ring.left if goes_right else ring.right
            if not arriving:
                return remote(self.own(half), self.slot(ring.me, half), self.sems, which, target)
        else:
            source_block = ring.opposite
            if not arriving:
                handed = self.slot(ring.left if goes_right else ring.right, half)
                return remote(handed, handed, self.sems, which, target)
        part = self.slot(source_block, half)
        return remote(part, part, self.sems, which, target)

    def start(self):
        for which in range(4):
            self.copy(which).start()

    def relay(self):
        for which in (0, 1):
            self.copy(which, arriving=True).wait_recv()
            self.copy(which + 4).start()

    def wait_left(self):
        self.copy(2, arriving=True).wait_recv()

    def wait_right(self):
        self.copy(3, arriving=True).wait_recv()

    def wait_opposite(self):
        self.copy(4, arriving=True).wait_recv()
        self.copy(5, arriving=True).wait_recv()

    def wait_all(self):
        self.wait_left()
        self.wait_right()
        self.wait_opposite()

    def finish(self):
        for which in range(6):
            self.copy(which).wait_send()


class Scatter:
    def __init__(self, ring, part, landing, passing, arrived, sems):
        self.ring, self.part, self.landing, self.passing = ring, part, landing, passing
        self.arrived, self.sems = arrived, sems

    def copy(self, which):
        ring = self.ring
        half = (0, 1, 1, 0, 0, 1)[which]
        goes_right = which in (0, 2, 4)
        if which < 2:
            src, dst = self.part(ring.opposite, half), self.landing(half)
        else:
            dst = self.arrived(0 if goes_right else 1, half)
            if which < 4:
                src = self.part(ring.right if goes_right else ring.left, half)
            else:
                src = self.passing(half)
        return remote(src, dst, self.sems, which, ring.to_right if goes_right else ring.to_left)

    def start_near(self):
        self.copy(2).start()
        self.copy(3).start()

    def start_far(self):
        self.copy(0).start()
        self.copy(1).start()

    def relay(self):
        for half, block in ((0, self.ring.right), (1, self.ring.left)):
            self.copy(half).wait_recv()
            added = self.part(block, half)[...].astype(F32) + self.landing(half)[...].astype(F32)
            self.passing(half)[...] = added.astype(LOW)
            self.copy(half + 4).start()

    def wait(self):
        for which in (2, 3, 4, 5):
            self.copy(which).wait_recv()

    def total(self, half):
        return (
            self.part(self.ring.me, half)[...].astype(F32)
            + self.arrived(0, half)[...].astype(F32)
            + self.arrived(1, half)[...].astype(F32)
        )

    def finish(self):
        for which in range(6):
            self.copy(which).wait_send()


def row_gather(ring, full, sems):
    half = full.shape[1] // 2
    return Gather(ring, lambda block, which: full.at[block, pl.ds(which * half, half)], sems)


def row_scatter(ring, parts, landing, passing, arrived, sems):
    half = parts.shape[1] // 2

    def rows(which):
        return pl.ds(which * half, half)

    return Scatter(
        ring,
        lambda block, which: parts.at[block, rows(which)],
        lambda which: landing.at[which],
        lambda which: passing.at[which],
        lambda side, which: arrived.at[side, rows(which)],
        sems,
    )


def row_total(scatter):
    scatter.wait()
    return jnp.concatenate([scatter.total(0), scatter.total(1)], axis=0)


def norm_stats(values):
    average = jnp.mean(values, axis=-1, keepdims=True)
    centered = values - average
    variance = jnp.mean(centered * centered, axis=-1, keepdims=True)
    scale = lax.rsqrt(variance + 1e-05)
    return centered * scale, scale


def norm_back(values, gain, grad):
    xhat, scale = norm_stats(values)
    scaled = grad * gain
    part = scale * (
        scaled
        - jnp.mean(scaled, axis=-1, keepdims=True)
        - xhat * jnp.mean(scaled * xhat, axis=-1, keepdims=True)
    )
    return part, jnp.sum(grad * xhat, axis=0, keepdims=True)


def gelu_tanh(values):
    inner = 0.7978845608028654 * (values + 0.044715 * values * values * values)
    return 0.5 * values * (1.0 + jnp.tanh(inner))


def gelu_slope(values):
    square = values * values
    bent = jnp.tanh(0.7978845608028654 * values * (1.0 + 0.044715 * square))
    slope = 0.7978845608028654 * (1.0 + 3.0 * 0.044715 * square)
    return 0.5 * (1.0 + bent) + 0.5 * values * (1.0 - bent * bent) * slope


def pick_copies(layer, mine, theirs, target, sem):
    def start():
        mine_here = lax.axis_index("section") == layer

        @pl.when(mine_here)
        def _():
            pltpu.make_async_copy(mine, target, sem).start()

        @pl.when(jnp.logical_not(mine_here))
        def _():
            pltpu.make_async_copy(theirs, target, sem).start()

    def wait():
        pltpu.make_async_copy(mine, target, sem).wait()

    return start, wait


def pair_columns(features):
    width = 2 * HEAD_DIM
    return [
        (start, min(width, features - start)) for start in range(0, features, width)
    ]


def head_masks(width):
    lanes = lax.broadcasted_iota(jnp.int32, (1, width), 1)
    if width == HEAD_DIM:
        return [None]
    return [lanes < HEAD_DIM, lanes >= HEAD_DIM]


def masked(values, mask):
    return values if mask is None else jnp.where(mask, values, jnp.zeros_like(values))


def attention_weights(layer, mine, theirs, target, sems):
    return [
        pick_copies(layer, mine.at[which], theirs.at[which], target.at[which], sems.at[which])
        for which in range(4)
    ]


def forward_kernel(
    layer, features, x_ref, bias_ref, gains_ref, at_mine, at_theirs, up_mine, up_theirs, down_mine,
    down_theirs, y_ref, middle_ref, one_ref, query_ref, key_ref, value_ref, mixed_ref, two_ref,
    act_ref, hidden_ref, at_w, up_w, down_w, weight_sems, parts, landing, passing, arrived,
    key_send, key_recv, value_send, value_recv, two_send, two_recv, sum_send, sum_recv,
):
    ring = Ring("x")
    me = ring.me
    fetches = attention_weights(layer, at_mine, at_theirs, at_w, weight_sems)
    fetches.append(pick_copies(layer, up_mine, up_theirs, up_w, weight_sems.at[4]))
    fetches.append(pick_copies(layer, down_mine, down_theirs, down_w, weight_sems.at[5]))
    for which in (1, 2, 0, 3, 4, 5):
        fetches[which][0]()
    greet(ring.to_right, ring.to_left)
    rows = x_ref.shape[0]
    inputs = x_ref[...].astype(F32)
    xhat, _ = norm_stats(inputs)
    one_ref[...] = (xhat * gains_ref[0:1, :]).astype(LOW)
    normed_one = one_ref[...]
    fetches[1][1]()
    key_ref[me] = dot_nn(normed_one, at_w[1]).astype(LOW)
    keys = row_gather(ring, key_ref, (key_send, key_recv))
    keys.start()
    fetches[2][1]()
    value_ref[me] = dot_nn(normed_one, at_w[2]).astype(LOW)
    values = row_gather(ring, value_ref, (value_send, value_recv))
    values.start()
    fetches[0][1]()
    query_ref[...] = dot_nn(normed_one, at_w[0]).astype(LOW)
    keys.relay()
    values.relay()
    keys.wait_all()
    values.wait_all()
    fetches[3][1]()
    bias = bias_ref[...]
    for begin, width in pair_columns(features):
        columns = pl.ds(begin, width)
        queries = query_ref[:, columns]
        key_block = key_ref[:, :, columns].reshape(4 * rows, width)
        value_block = value_ref[:, :, columns].reshape(4 * rows, width)
        mixed = None
        for mask in head_masks(width):
            scores = dot_nt(masked(queries, mask), key_block) * 0.125 + bias
            raised = jnp.exp(scores - jnp.max(scores, axis=-1, keepdims=True))
            probs = raised * (1.0 / jnp.sum(raised, axis=-1, keepdims=True))
            own = dot_nn(probs.astype(LOW), value_block)
            mixed = own if mixed is None else jnp.where(mask, own, mixed)
        mixed_ref[:, columns] = mixed.astype(LOW)
    middle_ref[...] = x_ref[...].astype(F32) + dot_nn(mixed_ref[...], at_w[3])
    xhat, _ = norm_stats(middle_ref[...])
    two_ref[me] = (xhat * gains_ref[1:2, :]).astype(LOW)
    tokens = row_gather(ring, two_ref, (two_send, two_recv))
    tokens.start()
    fetches[4][1]()
    fetches[5][1]()
    sums = row_scatter(ring, parts, landing, passing, arrived, (sum_send, sum_recv))

    def feed(block):
        act_ref[block] = dot_nn(two_ref[block], up_w[...])
        hidden_ref[block] = gelu_tanh(act_ref[block]).astype(LOW)
        parts[block] = dot_nn(hidden_ref[block], down_w[...]).astype(LOW)

    feed(me)
    tokens.relay()
    tokens.wait_left()
    feed(ring.left)
    tokens.wait_right()
    feed(ring.right)
    sums.start_near()
    tokens.wait_opposite()
    feed(ring.opposite)
    sums.start_far()
    sums.relay()
    y_ref[...] = (middle_ref[...] + row_total(sums)).astype(LOW)
    keys.finish()
    values.finish()
    tokens.finish()
    sums.finish()


def scatter_scratch(rows, features):
    return [
        pltpu.VMEM((4, rows, features), LOW),
        pltpu.VMEM((2, rows // 2, features), LOW),
        pltpu.VMEM((2, rows // 2, features), LOW),
        pltpu.VMEM((2, rows, features), LOW),
    ]


def weight_scratch(features, hidden):
    return [
        pltpu.VMEM((4, features, features), LOW),
        pltpu.VMEM((features, hidden), LOW),
        pltpu.VMEM((hidden, features), LOW),
        pltpu.SemaphoreType.DMA((6,)),
    ]


def in_vmem():
    return pl.BlockSpec(memory_space=pltpu.VMEM)


def anywhere():
    return pl.BlockSpec(memory_space=pl.ANY)


def forward_layer(layer, x, bias, gains, attention, feed):
    rows, features = x.shape
    hidden = feed[0].shape[1]
    out_shape = (
        jax.ShapeDtypeStruct((rows, features), LOW),
        jax.ShapeDtypeStruct((rows, features), F32),
        jax.ShapeDtypeStruct((rows, features), LOW),
        jax.ShapeDtypeStruct((rows, features), LOW),
        jax.ShapeDtypeStruct((4, rows, features), LOW),
        jax.ShapeDtypeStruct((4, rows, features), LOW),
        jax.ShapeDtypeStruct((rows, features), LOW),
        jax.ShapeDtypeStruct((4, rows, features), LOW),
        jax.ShapeDtypeStruct((4, rows, hidden), F32),
        jax.ShapeDtypeStruct((4, rows, hidden), LOW),
    )
    return pl.pallas_call(
        functools.partial(forward_kernel, layer, features),
        out_shape=out_shape,
        in_specs=[in_vmem()] * 3 + [anywhere()] * 6,
        out_specs=[in_vmem()] * len(out_shape),
        scratch_shapes=weight_scratch(features, hidden)
        + scatter_scratch(rows, features)
        + [pltpu.SemaphoreType.DMA((6,))] * 8,
        compiler_params=pltpu.CompilerParams(
            collective_id=layer, has_side_effects=True, vmem_limit_bytes=56 * 2**20
        ),
        cost_estimate=pl.CostEstimate(
            flops=3 * 10**9, bytes_accessed=24 * 10**6, transcendentals=10**6
        ),
        name=f"layer_forward_{layer}",
    )(x, bias, gains, *attention, *feed)


def backward_kernel(layer, features, *refs):
    take = iter(refs)

    def some(count):
        return [next(take) for _ in range(count)]

    (x_ref, dy_ref, bias_ref, gains_ref, middle_ref, query_ref, key_ref, value_ref, act_ref,
     at_mine, at_theirs, up_mine, up_theirs, down_mine, down_theirs) = some(15)
    operands = some(10) if layer == 0 else None
    (dx_ref, gain_ref, out_ref, pre_ref, branch_ref, dquery_ref, dkey_ref, dvalue_ref) = some(8)
    results = some(4) if layer == 0 else None
    (at_w, up_w, down_w, weight_sems, parts, landing, passing, arrived, parts_b, landing_b,
     passing_b, arrived_b, parts_c, landing_c, passing_c, arrived_c, mixed_grad, kept_grad,
     out_send, out_recv, sum_send, sum_recv, key_send, key_recv, value_send, value_recv) = some(26)
    extra = GradientSum(1, features, operands, results, take) if layer == 0 else None
    ring = Ring("x")
    me = ring.me
    fetches = attention_weights(layer, at_mine, at_theirs, at_w, weight_sems)
    fetches.append(pick_copies(layer, up_mine, up_theirs, up_w, weight_sems.at[4]))
    fetches.append(pick_copies(layer, down_mine, down_theirs, down_w, weight_sems.at[5]))
    for which in (5, 4, 3, 0, 1, 2):
        fetches[which][0]()
    rows = x_ref.shape[0]
    out_ref[me] = dy_ref[...]
    if extra is None:
        greet(ring.to_right, ring.to_left)
    else:
        greet_all()
    grads = row_gather(ring, out_ref, (out_send, out_recv))
    grads.start()
    if extra is not None:
        extra.start_inputs()
    sums = row_scatter(ring, parts, landing, passing, arrived, (sum_send, sum_recv))
    fetches[5][1]()
    fetches[4][1]()

    def feed(block):
        hidden_grad = dot_nt(out_ref[block], down_w[...])
        pre_ref[block] = (hidden_grad * gelu_slope(act_ref[block])).astype(LOW)
        parts[block] = dot_nt(pre_ref[block], up_w[...]).astype(LOW)

    def steps(*names):
        if extra is not None:
            for name in names:
                getattr(extra, name)()

    feed(me)
    grads.relay()
    steps("feed_products")
    grads.wait_left()
    feed(ring.left)
    grads.wait_right()
    feed(ring.right)
    sums.start_near()
    grads.wait_opposite()
    feed(ring.opposite)
    sums.start_far()
    steps("products_0", "feed_relay")
    sums.relay()
    steps("products_1")
    middle_part, gain_two = norm_back(middle_ref[...], gains_ref[1:2, :], row_total(sums))
    gain_ref[1:2, :] = gain_two
    middle_grad = dy_ref[...].astype(F32) + middle_part
    kept_grad[...] = middle_grad
    branch_ref[...] = middle_grad.astype(LOW)
    fetches[3][1]()
    mixed_grad[...] = dot_nt(branch_ref[...], at_w[3]).astype(LOW)
    bias = bias_ref[...]
    dkeys = row_scatter(ring, parts_b, landing_b, passing_b, arrived_b, (key_send, key_recv))
    dvalues = row_scatter(
        ring, parts_c, landing_c, passing_c, arrived_c, (value_send, value_recv)
    )
    for count, (begin, width) in enumerate(pair_columns(features)):
        columns = pl.ds(begin, width)
        queries = query_ref[:, columns]
        outer = mixed_grad[:, columns]
        key_block = key_ref[:, :, columns].reshape(4 * rows, width)
        value_block = value_ref[:, :, columns].reshape(4 * rows, width)
        dquery = dkey = dvalue = None
        for mask in head_masks(width):
            query_one, outer_one = masked(queries, mask), masked(outer, mask)
            scores = dot_nt(key_block, query_one) * 0.125 + bias
            raised = jnp.exp(scores - jnp.max(scores, axis=0, keepdims=True))
            probs = raised * (1.0 / jnp.sum(raised, axis=0, keepdims=True))
            probs_grad = dot_nt(value_block, outer_one)
            mean = jnp.sum(probs * probs_grad, axis=0, keepdims=True)
            score_grad = (probs * (probs_grad - mean)).astype(LOW)
            own_query = dot_tn(score_grad, key_block)
            own_key = dot_nn(score_grad, query_one)
            own_value = dot_nn(probs.astype(LOW), outer_one)
            if dquery is None:
                dquery, dkey, dvalue = own_query, own_key, own_value
            else:
                dquery = jnp.where(mask, own_query, dquery)
                dkey, dvalue = dkey + own_key, dvalue + own_value
        dquery_ref[:, columns] = (dquery * 0.125).astype(LOW)
        parts_b[:, :, columns] = (dkey * 0.125).astype(LOW).reshape(4, rows, width)
        parts_c[:, :, columns] = dvalue.astype(LOW).reshape(4, rows, width)
        if count == 2:
            steps("feed_middle", "x_relay_0")
        if count == 5:
            steps("feed_middle_relay", "x_relay_1")
    dkeys.start_far()
    dvalues.start_far()
    dkeys.start_near()
    dvalues.start_near()
    for which in (0, 1, 2):
        fetches[which][1]()
    one_grad = dot_nt(dquery_ref[...], at_w[0])
    steps("feed_end")
    dkeys.relay()
    dvalues.relay()
    steps("start_0", "feed_end_relay")
    dkey_ref[...] = row_total(dkeys).astype(LOW)
    one_grad = one_grad + dot_nt(dkey_ref[...], at_w[1])
    steps("start_1", "relay_0")
    dvalue_ref[...] = row_total(dvalues).astype(LOW)
    one_grad = one_grad + dot_nt(dvalue_ref[...], at_w[2])
    inputs_part, gain_one = norm_back(x_ref[...].astype(F32), gains_ref[0:1, :], one_grad)
    gain_ref[0:1, :] = gain_one
    dx_ref[...] = (kept_grad[...] + inputs_part).astype(LOW)
    steps("relay_1", "middle_0", "middle_relay_0", "feed_hand", "middle_1", "end_0", "middle_relay_1",
          "end_relay_0", "end_1", "end_relay_1", "hand", "finish")
    grads.finish()
    sums.finish()
    dkeys.finish()
    dvalues.finish()


def greet_all():
    rings = [Ring(axis) for axis in ("x", "y", "z")]
    greet(
        *[ring.to_right for ring in rings], *[ring.to_left for ring in rings], sibling()
    )


def backward_layer(layer, x, dy, bias, gains, middle, query, key, value, act, attention, feed,
                   operands=()):
    rows, features = x.shape
    hidden = feed[0].shape[1]
    out_shape = (
        jax.ShapeDtypeStruct((rows, features), LOW),
        jax.ShapeDtypeStruct((2, features), F32),
        jax.ShapeDtypeStruct((4, rows, features), LOW),
        jax.ShapeDtypeStruct((4, rows, hidden), LOW),
        jax.ShapeDtypeStruct((rows, features), LOW),
        jax.ShapeDtypeStruct((rows, features), LOW),
        jax.ShapeDtypeStruct((rows, features), LOW),
        jax.ShapeDtypeStruct((rows, features), LOW),
    )
    sums = gradient_outputs(features) if layer == 0 else ()
    return pl.pallas_call(
        functools.partial(backward_kernel, layer, features),
        out_shape=out_shape + sums,
        in_specs=[in_vmem()] * 9 + [anywhere()] * (6 + len(operands)),
        out_specs=[in_vmem()] * len(out_shape) + [anywhere()] * len(sums),
        scratch_shapes=weight_scratch(features, hidden)
        + scatter_scratch(rows, features) * 3
        + [pltpu.VMEM((rows, features), LOW), pltpu.VMEM((rows, features), F32)]
        + [pltpu.SemaphoreType.DMA((6,))] * 8
        + (gradient_scratch(features, rows) if layer == 0 else []),
        compiler_params=pltpu.CompilerParams(
            collective_id=2 + layer, has_side_effects=True, vmem_limit_bytes=62 * 2**20
        ),
        cost_estimate=pl.CostEstimate(
            flops=4 * 10**9, bytes_accessed=24 * 10**6, transcendentals=10**6
        ),
        name=f"layer_backward_{layer}",
    )(x, dy, bias, gains, middle, query, key, value, act, *attention, *feed, *operands)


X_ROWS, Y_ROWS = 96, 96


def weights_kernel(
    shard_ref, gain_ref, mine_ref, theirs_ref, gain_mine, gain_theirs, local_sems, x_send, x_recv,
    yx_send, yx_recv, zx_send, zx_recv, y_send, y_recv, z_send, z_recv, gain_send, gain_recv,
    pair_send, pair_recv,
):
    x_ring, y_ring, z_ring = Ring("x"), Ring("y"), Ring("z")
    mine_y, mine_z, mine_x = y_ring.me, z_ring.me, x_ring.me
    share = shard_ref.shape[1]
    y_begin, z_begin = X_ROWS, X_ROWS + Y_ROWS
    z_rows = share - z_begin
    all_x, all_y, all_z = pl.ds(0, X_ROWS), pl.ds(y_begin, Y_ROWS), pl.ds(z_begin, z_rows)
    y_half = (pl.ds(y_begin, 48), pl.ds(y_begin + 48, Y_ROWS - 48))
    z_half = (pl.ds(z_begin, 48), pl.ds(z_begin + 48, z_rows - 48))
    pair = sibling()
    greet(
        x_ring.to_right, x_ring.to_left, y_ring.to_right, y_ring.to_left, z_ring.to_right,
        z_ring.to_left, pair,
    )
    locals_ = [
        pltpu.make_async_copy(
            shard_ref.at[mine_y, all_y], mine_ref.at[mine_y, mine_x, all_y], local_sems.at[0]
        ),
        pltpu.make_async_copy(
            shard_ref.at[mine_z, all_z], mine_ref.at[mine_z, mine_x, all_z], local_sems.at[1]
        ),
        pltpu.make_async_copy(
            shard_ref.at[:, all_x], mine_ref.at[:, mine_x, all_x], local_sems.at[2]
        ),
        pltpu.make_async_copy(gain_ref, gain_mine.at[mine_x], local_sems.at[3]),
    ]
    first_y = Gather(
        x_ring,
        lambda block, half: mine_ref.at[mine_y, block, y_half[half]],
        (yx_send, yx_recv),
        lambda half: shard_ref.at[mine_y, y_half[half]],
    )
    first_z = Gather(
        x_ring,
        lambda block, half: mine_ref.at[mine_z, block, z_half[half]],
        (zx_send, zx_recv),
        lambda half: shard_ref.at[mine_z, z_half[half]],
    )
    along_x = Gather(
        x_ring,
        lambda block, half: mine_ref.at[pl.ds(2 * half, 2), block, all_x],
        (x_send, x_recv),
        lambda half: shard_ref.at[pl.ds(2 * half, 2), all_x],
    )
    along_y = Gather(
        y_ring,
        lambda block, half: mine_ref.at[block, pl.ds(2 * half, 2), all_y],
        (y_send, y_recv),
    )
    along_z = Gather(
        z_ring,
        lambda block, half: mine_ref.at[block, pl.ds(2 * half, 2), all_z],
        (z_send, z_recv),
    )

    def gain_copy(which, block, src=None):
        part = gain_mine.at[block]
        target = x_ring.to_left if which == 1 else x_ring.to_right
        return remote(part if src is None else src, part, (gain_send, gain_recv), which, target)

    def hand(which, region):
        return remote(mine_ref.at[region], theirs_ref.at[region], (pair_send, pair_recv), which, pair)

    handed = []

    def hand_on(which, region):
        copy = hand(which, region)
        copy.start()
        handed.append(copy)

    first_y.start()
    first_z.start()
    for copy in locals_:
        copy.start()
    gain_copy(0, mine_x, gain_ref).start()
    gain_copy(1, mine_x, gain_ref).start()
    first_y.relay()
    first_z.relay()
    along_x.start()
    first_y.wait_all()
    locals_[0].wait()
    along_y.start()
    hand_on(0, (mine_y, slice(None), all_y))
    first_z.wait_all()
    locals_[1].wait()
    along_z.start()
    hand_on(1, (mine_z, slice(None), all_z))
    gain_copy(0, x_ring.left).wait_recv()
    gain_copy(2, x_ring.left).start()
    along_x.relay()
    along_y.relay()
    along_z.relay()
    along_x.wait_all()
    locals_[2].wait()
    hand_on(2, (slice(None), slice(None), all_x))
    along_y.wait_left()
    hand_on(3, (y_ring.left, slice(None), all_y))
    along_z.wait_left()
    hand_on(4, (z_ring.left, slice(None), all_z))
    along_y.wait_right()
    hand_on(5, (y_ring.right, slice(None), all_y))
    along_z.wait_right()
    hand_on(6, (z_ring.right, slice(None), all_z))
    gain_copy(1, x_ring.right).wait_recv()
    gain_copy(2, x_ring.opposite).wait_recv()
    locals_[3].wait()
    gains = remote(gain_mine, gain_theirs, (pair_send, pair_recv), 9, pair)
    gains.start()
    along_y.wait_opposite()
    hand_on(7, (y_ring.opposite, slice(None), all_y))
    along_z.wait_opposite()
    hand_on(8, (z_ring.opposite, slice(None), all_z))
    for copy in handed + [gains]:
        copy.wait()
    for which in range(3):
        gain_copy(which, mine_x).wait_send()
    for gather in (first_y, first_z, along_x, along_y, along_z):
        gather.finish()


def gather_weights(shard, gain):
    mats, share, features = shard.shape
    full = jax.ShapeDtypeStruct((mats, 4, share, features), LOW)
    gains = jax.ShapeDtypeStruct((4,) + gain.shape, LOW)
    return pl.pallas_call(
        weights_kernel,
        out_shape=(full, full, gains, gains),
        in_specs=[anywhere()] * 2,
        out_specs=[anywhere()] * 4,
        scratch_shapes=[pltpu.SemaphoreType.DMA((4,))]
        + [pltpu.SemaphoreType.DMA((6,))] * 10
        + [pltpu.SemaphoreType.DMA((3,))] * 2
        + [pltpu.SemaphoreType.DMA((10,))] * 2,
        compiler_params=pltpu.CompilerParams(collective_id=4, has_side_effects=True),
        cost_estimate=pl.CostEstimate(flops=0, bytes_accessed=60 * 10**6, transcendentals=0),
        name="gather_weights",
    )(shard, gain)


class SmallSum:
    def __init__(self, ring, slots, sems):
        self.ring, self.slots, self.sems = ring, slots, sems

    def copy(self, which, block):
        target = self.ring.to_left if which == 1 else self.ring.to_right
        part = self.slots.at[block]
        return remote(part, part, self.sems, which, target)

    def start(self):
        self.copy(0, self.ring.me).start()
        self.copy(1, self.ring.me).start()

    def relay(self):
        self.copy(0, self.ring.left).wait_recv()
        self.copy(2, self.ring.left).start()

    def result(self):
        self.copy(1, self.ring.right).wait_recv()
        self.copy(2, self.ring.opposite).wait_recv()
        return (self.slots[0] + self.slots[1]) + (self.slots[2] + self.slots[3])

    def finish(self):
        for which in range(3):
            self.copy(which, self.ring.me).wait_send()


class PlaneSum:
    def __init__(self, near, far, source, out, size, first, scratch, sems, keep):
        self.landing, self.passing, self.arrived, self.mid, self.done = scratch
        self.out, self.size, self.near, self.far, self.keep = out, size, near, far, keep
        self.halves = ((0, first), (first, size - first))

        def rows(block, half):
            begin, count = self.halves[half]
            return pl.ds(pl.multiple_of(block * size + begin, 16), count)

        def half_rows(half):
            return pl.ds(*self.halves[half])

        self.half_rows = half_rows
        self.scatter = Scatter(
            near,
            lambda block, half: source.at[rows(block, half)],
            lambda half: self.landing.at[half_rows(half)],
            lambda half: self.passing.at[half_rows(half)],
            lambda side, half: self.arrived.at[side, half_rows(half)],
            sems[0],
        )
        self.gather = Gather(far, lambda block, half: self.mid.at[block, half_rows(half)], sems[1])
        self.spread = Gather(
            near,
            lambda block, half: out.at[rows(block, half)],
            sems[2],
            lambda half: self.done.at[half_rows(half)],
        )

    def start(self):
        self.scatter.start_far()
        self.scatter.start_near()

    def relay(self):
        self.scatter.relay()

    def middle(self):
        self.scatter.wait()
        for half in range(2):
            self.mid[self.far.me, self.half_rows(half)] = self.scatter.total(half).astype(LOW)
        self.gather.start()

    def middle_relay(self):
        self.gather.relay()

    def own(self):
        place = pl.ds(pl.multiple_of(self.near.me * self.size, 16), self.size)
        return pltpu.make_async_copy(self.done, self.out.at[place], self.keep)

    def end(self):
        self.gather.wait_all()
        four = [self.mid[block].astype(F32) for block in range(4)]
        self.done[...] = ((four[0] + four[1]) + (four[2] + four[3])).astype(LOW)
        self.spread.start()
        self.own().start()

    def end_relay(self):
        self.spread.relay()

    def wait(self):
        self.spread.wait_all()
        self.own().wait()

    def finish(self):
        self.scatter.finish()
        self.gather.finish()
        self.spread.finish()


FEED_BLOCK, AT_BLOCK = 144, 80


def gradient_outputs(features):
    feed = jax.ShapeDtypeStruct((2, 4 * FEED_BLOCK, features), LOW)
    attention = jax.ShapeDtypeStruct((2, 4 * AT_BLOCK, features), LOW)
    return (feed, feed, attention, attention)


def gradient_scratch(features, rows):
    share = features // 4
    dma = pltpu.SemaphoreType.DMA

    def low(*shape):
        return pltpu.VMEM(shape + (features,), LOW)

    def plane(size):
        return [low(size), low(size), low(2, size), low(4, size), low(size)] + [dma((6,))] * 6

    return (
        [low(2, 2, 4, rows), low(2, 2, rows), low(2, 2, rows), low(2, features),
         low(2, 4 * FEED_BLOCK), low(2, 4 * AT_BLOCK)]
        + ([low(share), low(share), low(2, share)] + [dma((6,))] * 2) * 2
        + plane(FEED_BLOCK) * 2
        + plane(AT_BLOCK) * 2
        + [dma((6,)), dma((6,)), dma((6,)), dma((4,)), dma((2,)), dma((2,))]
    )


class GradientSum:
    def __init__(self, layer, features, operands, results, take):
        self.layer, self.features = layer, features
        self.operands = operands
        self.feed_out, self.feed_other, self.at_out, self.at_other = results
        (self.feed_in, self.at_left, self.at_right, self.at_sum, self.feed_sum,
         self.at_kept) = [next(take) for _ in range(6)]
        self.pair, self.section = sibling(), lax.axis_index("section")
        x_ring, y_ring, z_ring = Ring("x"), Ring("y"), Ring("z")
        share = features // 4
        self.share = share
        self.across = []
        for which in range(2):
            landing, passing, arrived, send, recv = [next(take) for _ in range(5)]
            halves = ((0, 144), (144, share - 144))

            def part(block, half, which=which, halves=halves):
                begin, count = halves[half]
                row = pl.multiple_of(block * share + begin, 16)
                return self.at_sum.at[which, pl.ds(row, count)]

            def cut(ref, halves=halves):
                return lambda half: ref.at[pl.ds(*halves[half])]

            self.across.append(
                Scatter(
                    x_ring, part, cut(landing), cut(passing),
                    lambda side, half, arrived=arrived, halves=halves: arrived.at[
                        side, pl.ds(*halves[half])
                    ],
                    (send, recv),
                )
            )
        self.halves = halves
        planes = []
        for which in range(4):
            scratch = [next(take) for _ in range(5)]
            sems = [next(take) for _ in range(6)]
            planes.append((scratch, [tuple(sems[i : i + 2]) for i in (0, 2, 4)]))
        (self.local_sems, swap_send, swap_recv, keep, end_send, end_recv) = [
            next(take) for _ in range(6)
        ]
        self.swap, self.end_sems = (swap_send, swap_recv), (end_send, end_recv)
        orders = ((y_ring, z_ring), (z_ring, y_ring))
        self.feed, self.attention = [], []
        for which in range(2):
            self.feed.append(
                PlaneSum(
                    *orders[which], self.feed_sum.at[which], self.feed_out.at[which], FEED_BLOCK,
                    80, *planes[which], keep.at[which],
                )
            )
            self.attention.append(
                PlaneSum(
                    *orders[which], self.at_kept.at[which], self.at_out.at[which], AT_BLOCK, 48,
                    *planes[2 + which], keep.at[2 + which],
                )
            )

    def inputs(self, first):
        two, pre, hidden, out, one, mixed, dq, dk, dv, branch = self.operands
        zero = (two, pre, one, one, dq, dk)
        other = (hidden, out, one, mixed, dv, branch)
        own, sent = (zero, other) if first else (other, zero)
        targets = (
            self.feed_in.at[0], self.feed_in.at[1], self.at_left.at[0], self.at_left.at[1],
            self.at_right.at[0], self.at_right.at[1],
        )

        def keep(which):
            return pltpu.make_async_copy(
                own[which], targets[which].at[0], self.local_sems.at[which]
            )

        def send(which):
            return remote(sent[which], targets[which].at[1], self.swap, which, self.pair)

        return keep, send

    def start_inputs(self):
        for first in (True, False):

            @pl.when(self.section == (0 if first else 1))
            def _(first=first):
                keep, send = self.inputs(first)
                for which in range(6):
                    send(which).start()
                for which in range(6):
                    keep(which).start()

    def wait_inputs(self, whiches):
        keep, send = self.inputs(True)
        for which in whiches:
            keep(which).wait()
            send(which).wait_recv()

    def feed_products(self):
        self.wait_inputs((0, 1))
        features, whole = self.features, 4 * FEED_BLOCK
        right = self.feed_in[1].reshape(-1, features)
        for begin in range(0, features, 256):
            count = min(256, features - begin)
            left = self.feed_in[0, :, :, :, pl.ds(begin, count)].reshape(-1, count)
            product = dot_tn(left, right).astype(LOW)
            first = max(0, min(count, whole - begin))
            if first:
                self.feed_sum[0, pl.ds(begin, first)] = product[:first]
            if first < count:
                self.feed_sum[1, pl.ds(begin + first - whole, count - first)] = product[first:]
        spare = 2 * whole - features
        self.feed_sum[1, pl.ds(whole - spare, spare)] = jnp.zeros((spare, features), LOW)
        for plane in self.feed:
            plane.start()

    def products(self, which):
        self.wait_inputs((2 + which, 4 + which))
        features = self.features
        right = self.at_right[which].reshape(-1, features)
        for begin in range(0, features, 256):
            count = min(256, features - begin)
            left = self.at_left[which, :, :, pl.ds(begin, count)].reshape(-1, count)
            self.at_sum[which, pl.ds(begin, count)] = dot_tn(left, right).astype(LOW)
        self.across[which].start_far()
        self.across[which].start_near()

    def products_0(self):
        self.products(0)

    def products_1(self):
        self.products(1)

    def feed_relay(self):
        for plane in self.feed:
            plane.relay()

    def feed_middle(self):
        for plane in self.feed:
            plane.middle()

    def feed_middle_relay(self):
        for plane in self.feed:
            plane.middle_relay()

    def feed_end(self):
        for plane in self.feed:
            plane.end()

    def feed_end_relay(self):
        for plane in self.feed:
            plane.end_relay()

    def x_relay_0(self):
        self.across[0].relay()

    def x_relay_1(self):
        self.across[1].relay()

    def attention_start(self, which):
        across = self.across[which]
        across.wait()
        for half in range(2):
            self.at_kept[which, pl.ds(*self.halves[half])] = across.total(half).astype(LOW)
        spare = 4 * AT_BLOCK - self.share
        self.at_kept[which, pl.ds(self.share, spare)] = jnp.zeros((spare, self.features), LOW)
        self.attention[which].start()

    def start_0(self):
        self.attention_start(0)

    def start_1(self):
        self.attention_start(1)

    def relay_0(self):
        self.attention[0].relay()

    def relay_1(self):
        self.attention[1].relay()

    def middle_0(self):
        self.attention[0].middle()

    def middle_1(self):
        self.attention[1].middle()

    def middle_relay_0(self):
        self.attention[0].middle_relay()

    def middle_relay_1(self):
        self.attention[1].middle_relay()

    def end_0(self):
        self.attention[0].end()

    def end_1(self):
        self.attention[1].end()

    def end_relay_0(self):
        self.attention[0].end_relay()

    def end_relay_1(self):
        self.attention[1].end_relay()

    def ends(self, which):
        src, dst = ((self.feed_out, self.feed_other), (self.at_out, self.at_other))[which]
        return remote(src, dst, self.end_sems, which, self.pair)

    def give(self, which):
        @pl.when(self.section != self.layer)
        def _():
            self.ends(which).start()

    def feed_hand(self):
        for plane in self.feed:
            plane.wait()
        self.give(0)

    def hand(self):
        for plane in self.attention:
            plane.wait()
        self.give(1)

    def finish(self):
        _, send = self.inputs(True)
        for which in range(6):
            send(which).wait_send()
        for each in self.across + self.feed + self.attention:
            each.finish()

        @pl.when(self.section != self.layer)
        def _():
            self.ends(0).wait_send()
            self.ends(1).wait_send()

        @pl.when(self.section == self.layer)
        def _():
            self.ends(0).wait_recv()
            self.ends(1).wait_recv()


def gradient_kernel(features, *refs):
    take = iter(refs)

    def some(count):
        return [next(take) for _ in range(count)]

    operands = some(10)
    y_a, y_b, dx_a, dx_b, gain_in = some(5)
    results = some(4)
    act_out, grad_out, gain_out = some(3)
    sums = GradientSum(0, features, operands, results, take)
    (gain_pair, gain_x, gain_y, gain_z, gain_send, gain_recv, last_send, last_recv,
     keep_sems) = some(9)
    x_ring, y_ring, z_ring = Ring("x"), Ring("y"), Ring("z")
    pair, section = sibling(), lax.axis_index("section")
    greet_all()
    sums.start_inputs()

    def last_copies(y, dx):
        return (
            remote(y, act_out.at[section], (last_send, last_recv), 0, pair),
            remote(dx, grad_out.at[section], (last_send, last_recv), 1, pair),
        )

    def keep_copies(y, dx):
        return (
            pltpu.make_async_copy(y, act_out.at[section], keep_sems.at[0]),
            pltpu.make_async_copy(dx, grad_out.at[section], keep_sems.at[1]),
        )

    @pl.when(section == 0)
    def _():
        for copy in last_copies(y_b, dx_b) + keep_copies(y_a, dx_a):
            copy.start()

    @pl.when(section == 1)
    def _():
        for copy in last_copies(y_a, dx_a) + keep_copies(y_b, dx_b):
            copy.start()

    gain_pair[0] = gain_in[...]
    swap_gain = remote(gain_pair.at[0], gain_pair.at[1], (gain_send, gain_recv), 9, pair)
    swap_gain.start()
    sums.products_0()
    sums.products_1()
    sums.feed_products()
    swap_gain.wait()
    gain_x[x_ring.me] = gain_pair[0] + gain_pair[1]
    small = [
        SmallSum(ring, slots, (gain_send.at[pl.ds(3 * i, 3)], gain_recv.at[pl.ds(3 * i, 3)]))
        for i, (ring, slots) in enumerate(((x_ring, gain_x), (y_ring, gain_y), (z_ring, gain_z)))
    ]
    small[0].start()
    sums.x_relay_0()
    sums.x_relay_1()
    sums.feed_relay()
    small[0].relay()
    sums.start_0()
    sums.feed_middle()
    gain_y[y_ring.me] = small[0].result()
    small[1].start()
    sums.relay_0()
    sums.feed_middle_relay()
    small[1].relay()
    sums.start_1()
    sums.middle_0()
    sums.feed_end()
    gain_z[z_ring.me] = small[1].result()
    small[2].start()
    sums.relay_1()
    sums.middle_relay_0()
    sums.feed_end_relay()
    small[2].relay()
    sums.middle_1()
    sums.end_0()
    sums.middle_relay_1()
    gain_out[...] = small[2].result()
    sums.end_relay_0()
    sums.end_1()
    sums.feed_hand()
    sums.end_relay_1()
    sums.hand()
    sums.finish()
    for each in small:
        each.finish()
    for copy in last_copies(y_a, dx_a) + keep_copies(y_a, dx_a):
        copy.wait()


def sum_gradients(features, rows, operands, last, gain):
    dma = pltpu.SemaphoreType.DMA
    small = [pltpu.VMEM((4, 8, features), F32)] * 3
    return pl.pallas_call(
        functools.partial(gradient_kernel, features),
        out_shape=gradient_outputs(features)
        + (
            jax.ShapeDtypeStruct((2, rows, features), LOW),
            jax.ShapeDtypeStruct((2, rows, features), LOW),
            jax.ShapeDtypeStruct((8, features), F32),
        ),
        in_specs=[anywhere()] * 14 + [in_vmem()],
        out_specs=[anywhere()] * 6 + [in_vmem()],
        scratch_shapes=gradient_scratch(features, rows)
        + [pltpu.VMEM((2, 8, features), F32)]
        + small
        + [dma((10,)), dma((10,)), dma((2,)), dma((2,)), dma((2,))],
        compiler_params=pltpu.CompilerParams(
            collective_id=5, has_side_effects=True, vmem_limit_bytes=60 * 2**20
        ),
        cost_estimate=pl.CostEstimate(
            flops=6 * 10**9, bytes_accessed=60 * 10**6, transcendentals=0
        ),
        name="sum_gradients",
    )(*operands, *last, gain)


def doc_numbers(lengths, positions):
    doc_ends = jnp.cumsum(lengths)
    return jnp.sum((positions[:, None] >= doc_ends[None, :]).astype(jnp.int32), axis=1)


def swapped(block):
    return lax.ppermute(block, "section", [(0, 1), (1, 0)])


def body(tokens, cotangent, doc_lengths, norm_gains, w_qkv, w_out, w_up, w_down):
    batches, rows, features = tokens.shape
    share = w_qkv.shape[1]
    seq_rows = rows * lax.axis_size("tensor")
    section = lax.axis_index("section")
    is_first = section == 0

    def choose(zero_side, one_side):
        return jnp.where(is_first, zero_side, one_side)

    own_tokens = lax.dynamic_index_in_dim(tokens, section, 0, keepdims=False)
    own_cotangent = lax.dynamic_index_in_dim(cotangent, section, 0, keepdims=False)
    lengths = lax.dynamic_index_in_dim(doc_lengths, section, 0, keepdims=False)
    own_places = lax.axis_index("tensor") * rows + jnp.arange(rows, dtype=jnp.int32)
    all_places = jnp.arange(seq_rows, dtype=jnp.int32)
    own_docs = doc_numbers(lengths, own_places)
    all_docs = doc_numbers(lengths, all_places)
    allowed = (all_places[None, :] <= own_places[:, None]) & (
        all_docs[None, :] == own_docs[:, None]
    )
    bias = jnp.where(allowed, 0.0, -1e30).astype(F32)
    bias_turned = bias.T

    feed = (w_up[0], swapped(w_up[0]), w_down[0], swapped(w_down[0]))
    shard = jnp.stack(
        [w_qkv[0, :, :features], w_qkv[0, :, features : 2 * features], w_qkv[0, :, 2 * features :],
         w_out[0]]
    )
    gain_shard = jnp.pad(norm_gains[0], ((0, 14), (0, 0)))
    at_mine, at_theirs, gain_mine, gain_theirs = gather_weights(shard, gain_shard)
    attention = (
        at_mine.reshape(4, features, features), at_theirs.reshape(4, features, features)
    )

    def whole_gains(block):
        return block[:, :2].transpose(1, 0, 2).reshape(2, features).astype(F32)

    gain_mine, gain_theirs = whole_gains(gain_mine), whole_gains(gain_theirs)
    gains = (choose(gain_mine, gain_theirs), choose(gain_theirs, gain_mine))

    inputs = own_tokens
    saved = []
    for layer in range(2):
        results = forward_layer(layer, inputs, bias, gains[layer], attention, feed)
        saved.append((inputs,) + tuple(results))
        inputs = results[0]

    grad = own_cotangent
    gain_grads, input_grads, operands = [None, None], [None, None], ()
    for layer in (1, 0):
        (x, _, middle, normed_one, query, key, value, mixed, normed_two, act, hidden) = saved[layer]
        results = backward_layer(
            layer, x, grad, bias_turned, gains[layer], middle, query, key, value, act,
            attention, feed, operands,
        )
        (grad, gain_grads[layer], out_all, pre_grad, branch, dquery, dkey, dvalue) = results[:8]
        input_grads[layer] = grad
        operands = (
            normed_two, pre_grad, hidden, out_all, normed_one, mixed, dquery, dkey, dvalue, branch,
        )
    sums_one = results[8:]
    gain_rows = jnp.concatenate(gain_grads + [jnp.zeros((4, features), F32)], axis=0)
    *sums_zero, activations, input_grads, gain_total = sum_gradients(
        features, rows, operands, (saved[0][1], saved[1][1], *input_grads), gain_rows
    )
    gain_own = lax.dynamic_slice(
        gain_total, (2 * section, lax.axis_index("tensor") * share), (2, share)
    )

    def whole(block):
        return block.reshape(-1, features)[:features].astype(F32)[None]

    first_half = choose(sums_zero[2], sums_one[3])[:, :share].astype(F32)
    other_half = choose(sums_zero[3], sums_one[2])[:, :share].astype(F32)
    grad_qkv = jnp.concatenate([first_half[0], first_half[1], other_half[0]], axis=1)
    return (
        activations[None],
        input_grads[None],
        gain_own[None],
        grad_qkv[None],
        other_half[1][None],
        whole(choose(sums_zero[0], sums_one[1])),
        whole(choose(sums_zero[1], sums_one[0])),
    )


def solution(mesh):
    placed = (
        P("dp", "tensor", None),
        P("dp", "tensor", None),
        P("dp", None),
        P("section", None, "tensor"),
        P("section", "tensor", None),
        P("section", "tensor", None),
        P("section", None, "tensor"),
        P("section", "tensor", None),
    )
    return jax.shard_map(
        body,
        mesh=mesh,
        in_specs=placed,
        out_specs=(
            P("section", "dp", "tensor", None),
            P("section", "dp", "tensor", None),
            P("section", None, "tensor"),
            P("section", "tensor", None),
            P("section", "tensor", None),
            P("section", None, "tensor"),
            P("section", "tensor", None),
        ),
        check_vma=False,
    )
```

```python
import functools
import jax
import jax.numpy as jnp
from jax import lax
from jax.experimental import pallas as pl
from jax.experimental.pallas import tpu as pltpu
from jax.sharding import PartitionSpec as P

HEAD_DIM = 64
LOW = jnp.bfloat16
F32 = jnp.float32
MESH = pl.DeviceIdType.MESH


def dot_nn(left, right):
    return lax.dot_general(left, right, (((1,), (0,)), ((), ())), preferred_element_type=F32)


def dot_nt(left, right):
    return lax.dot_general(left, right, (((1,), (1,)), ((), ())), preferred_element_type=F32)


def dot_tn(left, right):
    return lax.dot_general(left, right, (((0,), (0,)), ((), ())), preferred_element_type=F32)


class Ring:
    def __init__(self, axis):
        whole = lax.axis_index("dp")
        rest = None
        if axis == "x":
            self.me = lax.axis_index("tensor")
        elif axis == "y":
            self.me, rest = lax.rem(whole, 4), lax.div(whole, 4) * 4
        else:
            self.me, rest = lax.div(whole, 4), lax.rem(whole, 4)
        self.right = lax.rem(self.me + 1, 4)
        self.left = lax.rem(self.me + 3, 4)
        self.opposite = lax.rem(self.me + 2, 4)

        def device(place):
            if axis == "x":
                return {"tensor": place}
            if axis == "y":
                return {"dp": rest + place}
            return {"dp": place * 4 + rest}

        self.to_right, self.to_left = device(self.right), device(self.left)


def sibling():
    return {"section": 1 - lax.axis_index("section")}


def greet(*targets):
    barrier = pltpu.get_barrier_semaphore()
    for target in targets:
        pl.semaphore_signal(barrier, inc=1, device_id=target, device_id_type=MESH)
    pl.semaphore_wait(barrier, len(targets))


def remote(src, dst, sems, which, target):
    return pltpu.make_async_remote_copy(
        src_ref=src,
        dst_ref=dst,
        send_sem=sems[0].at[which],
        recv_sem=sems[1].at[which],
        device_id=target,
        device_id_type=MESH,
    )


class Gather:
    def __init__(self, ring, slot, sems, own=None):
        self.ring, self.slot, self.sems = ring, slot, sems
        self.own = own if own is not None else lambda half: slot(ring.me, half)

    def copy(self, which, arriving=False):
        ring = self.ring
        half = (0, 1, 1, 0, 0, 1)[which]
        goes_right = which in (0, 2, 4)
        target = ring.to_right if goes_right else ring.to_left
        if which < 4:
            source_block = ring.left if goes_right else ring.right
            if not arriving:
                return remote(self.own(half), self.slot(ring.me, half), self.sems, which, target)
        else:
            source_block = ring.opposite
            if not arriving:
                handed = self.slot(ring.left if goes_right else ring.right, half)
                return remote(handed, handed, self.sems, which, target)
        part = self.slot(source_block, half)
        return remote(part, part, self.sems, which, target)

    def start(self):
        for which in range(4):
            self.copy(which).start()

    def relay(self):
        for which in (0, 1):
            self.copy(which, arriving=True).wait_recv()
            self.copy(which + 4).start()

    def wait_left(self):
        self.copy(2, arriving=True).wait_recv()

    def wait_right(self):
        self.copy(3, arriving=True).wait_recv()

    def wait_opposite(self):
        self.copy(4, arriving=True).wait_recv()
        self.copy(5, arriving=True).wait_recv()

    def wait_all(self):
        self.wait_left()
        self.wait_right()
        self.wait_opposite()

    def finish(self):
        for which in range(6):
            self.copy(which).wait_send()


class Scatter:
    def __init__(self, ring, part, landing, passing, arrived, sems):
        self.ring, self.part, self.landing, self.passing = ring, part, landing, passing
        self.arrived, self.sems = arrived, sems

    def copy(self, which):
        ring = self.ring
        half = (0, 1, 1, 0, 0, 1)[which]
        goes_right = which in (0, 2, 4)
        if which < 2:
            src, dst = self.part(ring.opposite, half), self.landing(half)
        else:
            dst = self.arrived(0 if goes_right else 1, half)
            if which < 4:
                src = self.part(ring.right if goes_right else ring.left, half)
            else:
                src = self.passing(half)
        return remote(src, dst, self.sems, which, ring.to_right if goes_right else ring.to_left)

    def start_near(self):
        self.copy(2).start()
        self.copy(3).start()

    def start_far(self):
        self.copy(0).start()
        self.copy(1).start()

    def relay(self):
        for half, block in ((0, self.ring.right), (1, self.ring.left)):
            self.copy(half).wait_recv()
            added = self.part(block, half)[...].astype(F32) + self.landing(half)[...].astype(F32)
            self.passing(half)[...] = added.astype(LOW)
            self.copy(half + 4).start()

    def wait(self):
        for which in (2, 3, 4, 5):
            self.copy(which).wait_recv()

    def total(self, half):
        return (
            self.part(self.ring.me, half)[...].astype(F32)
            + self.arrived(0, half)[...].astype(F32)
            + self.arrived(1, half)[...].astype(F32)
        )

    def finish(self):
        for which in range(6):
            self.copy(which).wait_send()


def row_gather(ring, full, sems):
    half = full.shape[1] // 2
    return Gather(ring, lambda block, which: full.at[block, pl.ds(which * half, half)], sems)


def row_scatter(ring, parts, landing, passing, arrived, sems):
    half = parts.shape[1] // 2

    def rows(which):
        return pl.ds(which * half, half)

    return Scatter(
        ring,
        lambda block, which: parts.at[block, rows(which)],
        lambda which: landing.at[which],
        lambda which: passing.at[which],
        lambda side, which: arrived.at[side, rows(which)],
        sems,
    )


def row_total(scatter):
    scatter.wait()
    return jnp.concatenate([scatter.total(0), scatter.total(1)], axis=0)


def norm_stats(values):
    average = jnp.mean(values, axis=-1, keepdims=True)
    centered = values - average
    variance = jnp.mean(centered * centered, axis=-1, keepdims=True)
    scale = lax.rsqrt(variance + 1e-05)
    return centered * scale, scale


def norm_back(values, gain, grad):
    xhat, scale = norm_stats(values)
    scaled = grad * gain
    part = scale * (
        scaled
        - jnp.mean(scaled, axis=-1, keepdims=True)
        - xhat * jnp.mean(scaled * xhat, axis=-1, keepdims=True)
    )
    return part, jnp.sum(grad * xhat, axis=0, keepdims=True)


def gelu_tanh(values):
    inner = 0.7978845608028654 * (values + 0.044715 * values * values * values)
    return 0.5 * values * (1.0 + jnp.tanh(inner))


def gelu_slope(values):
    square = values * values
    bent = jnp.tanh(0.7978845608028654 * values * (1.0 + 0.044715 * square))
    slope = 0.7978845608028654 * (1.0 + 3.0 * 0.044715 * square)
    return 0.5 * (1.0 + bent) + 0.5 * values * (1.0 - bent * bent) * slope


def pick_copies(layer, mine, theirs, target, sem):
    def start():
        mine_here = lax.axis_index("section") == layer

        @pl.when(mine_here)
        def _():
            pltpu.make_async_copy(mine, target, sem).start()

        @pl.when(jnp.logical_not(mine_here))
        def _():
            pltpu.make_async_copy(theirs, target, sem).start()

    def wait():
        pltpu.make_async_copy(mine, target, sem).wait()

    return start, wait


def pair_columns(features):
    width = 2 * HEAD_DIM
    return [
        (start, min(width, features - start)) for start in range(0, features, width)
    ]


def head_masks(width):
    lanes = lax.broadcasted_iota(jnp.int32, (1, width), 1)
    if width == HEAD_DIM:
        return [None]
    return [lanes < HEAD_DIM, lanes >= HEAD_DIM]


def masked(values, mask):
    return values if mask is None else jnp.where(mask, values, jnp.zeros_like(values))


def attention_weights(layer, mine, theirs, target, sems):
    return [
        pick_copies(layer, mine.at[which], theirs.at[which], target.at[which], sems.at[which])
        for which in range(4)
    ]


def forward_kernel(
    layer, features, x_ref, bias_ref, gains_ref, at_mine, at_theirs, up_mine, up_theirs, down_mine,
    down_theirs, y_ref, middle_ref, one_ref, query_ref, key_ref, value_ref, mixed_ref, two_ref,
    act_ref, hidden_ref, at_w, up_w, down_w, weight_sems, parts, landing, passing, arrived,
    key_send, key_recv, value_send, value_recv, two_send, two_recv, sum_send, sum_recv,
):
    ring = Ring("x")
    me = ring.me
    fetches = attention_weights(layer, at_mine, at_theirs, at_w, weight_sems)
    fetches.append(pick_copies(layer, up_mine, up_theirs, up_w, weight_sems.at[4]))
    fetches.append(pick_copies(layer, down_mine, down_theirs, down_w, weight_sems.at[5]))
    for which in (1, 2, 0, 3, 4, 5):
        fetches[which][0]()
    greet(ring.to_right, ring.to_left)
    rows = x_ref.shape[0]
    inputs = x_ref[...].astype(F32)
    xhat, _ = norm_stats(inputs)
    one_ref[...] = (xhat * gains_ref[0:1, :]).astype(LOW)
    normed_one = one_ref[...]
    fetches[1][1]()
    key_ref[me] = dot_nn(normed_one, at_w[1]).astype(LOW)
    keys = row_gather(ring, key_ref, (key_send, key_recv))
    keys.start()
    fetches[2][1]()
    value_ref[me] = dot_nn(normed_one, at_w[2]).astype(LOW)
    values = row_gather(ring, value_ref, (value_send, value_recv))
    values.start()
    fetches[0][1]()
    query_ref[...] = dot_nn(normed_one, at_w[0]).astype(LOW)
    keys.relay()
    values.relay()
    keys.wait_all()
    values.wait_all()
    fetches[3][1]()
    bias = bias_ref[...]
    for begin, width in pair_columns(features):
        columns = pl.ds(begin, width)
        queries = query_ref[:, columns]
        key_block = key_ref[:, :, columns].reshape(4 * rows, width)
        value_block = value_ref[:, :, columns].reshape(4 * rows, width)
        mixed = None
        for mask in head_masks(width):
            scores = dot_nt(masked(queries, mask), key_block) * 0.125 + bias
            raised = jnp.exp(scores - jnp.max(scores, axis=-1, keepdims=True))
            probs = raised * (1.0 / jnp.sum(raised, axis=-1, keepdims=True))
            own = dot_nn(probs.astype(LOW), value_block)
            mixed = own if mixed is None else jnp.where(mask, own, mixed)
        mixed_ref[:, columns] = mixed.astype(LOW)
    middle_ref[...] = x_ref[...].astype(F32) + dot_nn(mixed_ref[...], at_w[3])
    xhat, _ = norm_stats(middle_ref[...])
    two_ref[me] = (xhat * gains_ref[1:2, :]).astype(LOW)
    tokens = row_gather(ring, two_ref, (two_send, two_recv))
    tokens.start()
    fetches[4][1]()
    fetches[5][1]()
    sums = row_scatter(ring, parts, landing, passing, arrived, (sum_send, sum_recv))

    def feed(block):
        act_ref[block] = dot_nn(two_ref[block], up_w[...])
        hidden_ref[block] = gelu_tanh(act_ref[block]).astype(LOW)
        parts[block] = dot_nn(hidden_ref[block], down_w[...]).astype(LOW)

    feed(me)
    tokens.relay()
    tokens.wait_left()
    feed(ring.left)
    tokens.wait_right()
    feed(ring.right)
    sums.start_near()
    tokens.wait_opposite()
    feed(ring.opposite)
    sums.start_far()
    sums.relay()
    y_ref[...] = (middle_ref[...] + row_total(sums)).astype(LOW)
    keys.finish()
    values.finish()
    tokens.finish()
    sums.finish()


def scatter_scratch(rows, features):
    return [
        pltpu.VMEM((4, rows, features), LOW),
        pltpu.VMEM((2, rows // 2, features), LOW),
        pltpu.VMEM((2, rows // 2, features), LOW),
        pltpu.VMEM((2, rows, features), LOW),
    ]


def weight_scratch(features, hidden):
    return [
        pltpu.VMEM((4, features, features), LOW),
        pltpu.VMEM((features, hidden), LOW),
        pltpu.VMEM((hidden, features), LOW),
        pltpu.SemaphoreType.DMA((6,)),
    ]


def in_vmem():
    return pl.BlockSpec(memory_space=pltpu.VMEM)


def anywhere():
    return pl.BlockSpec(memory_space=pl.ANY)


def forward_layer(layer, x, bias, gains, attention, feed):
    rows, features = x.shape
    hidden = feed[0].shape[1]
    out_shape = (
        jax.ShapeDtypeStruct((rows, features), LOW),
        jax.ShapeDtypeStruct((rows, features), F32),
        jax.ShapeDtypeStruct((rows, features), LOW),
        jax.ShapeDtypeStruct((rows, features), LOW),
        jax.ShapeDtypeStruct((4, rows, features), LOW),
        jax.ShapeDtypeStruct((4, rows, features), LOW),
        jax.ShapeDtypeStruct((rows, features), LOW),
        jax.ShapeDtypeStruct((4, rows, features), LOW),
        jax.ShapeDtypeStruct((4, rows, hidden), F32),
        jax.ShapeDtypeStruct((4, rows, hidden), LOW),
    )
    return pl.pallas_call(
        functools.partial(forward_kernel, layer, features),
        out_shape=out_shape,
        in_specs=[in_vmem()] * 3 + [anywhere()] * 6,
        out_specs=[in_vmem()] * len(out_shape),
        scratch_shapes=weight_scratch(features, hidden)
        + scatter_scratch(rows, features)
        + [pltpu.SemaphoreType.DMA((6,))] * 8,
        compiler_params=pltpu.CompilerParams(
            collective_id=layer, has_side_effects=True, vmem_limit_bytes=56 * 2**20
        ),
        cost_estimate=pl.CostEstimate(
            flops=3 * 10**9, bytes_accessed=24 * 10**6, transcendentals=10**6
        ),
        name=f"layer_forward_{layer}",
    )(x, bias, gains, *attention, *feed)


def backward_kernel(layer, features, *refs):
    take = iter(refs)

    def some(count):
        return [next(take) for _ in range(count)]

    (x_ref, dy_ref, bias_ref, gains_ref, middle_ref, query_ref, key_ref, value_ref, act_ref,
     at_mine, at_theirs, up_mine, up_theirs, down_mine, down_theirs) = some(15)
    operands = some(10) if layer == 0 else None
    (dx_ref, gain_ref, out_ref, pre_ref, branch_ref, dquery_ref, dkey_ref, dvalue_ref) = some(8)
    results = some(3) if layer == 0 else None
    (at_w, up_w, down_w, weight_sems, parts, landing, passing, arrived, parts_b, landing_b,
     passing_b, arrived_b, parts_c, landing_c, passing_c, arrived_c, mixed_grad, kept_grad,
     out_send, out_recv, sum_send, sum_recv, key_send, key_recv, value_send, value_recv) = some(26)
    extra = GradientSum(1, features, operands, results, take) if layer == 0 else None
    ring = Ring("x")
    me = ring.me
    fetches = attention_weights(layer, at_mine, at_theirs, at_w, weight_sems)
    fetches.append(pick_copies(layer, up_mine, up_theirs, up_w, weight_sems.at[4]))
    fetches.append(pick_copies(layer, down_mine, down_theirs, down_w, weight_sems.at[5]))
    for which in (5, 4, 3, 0, 1, 2):
        fetches[which][0]()
    rows = x_ref.shape[0]
    out_ref[me] = dy_ref[...]
    if extra is None:
        greet(ring.to_right, ring.to_left)
    else:
        greet_all()
    grads = row_gather(ring, out_ref, (out_send, out_recv))
    grads.start()
    if extra is not None:
        extra.start_inputs()
    sums = row_scatter(ring, parts, landing, passing, arrived, (sum_send, sum_recv))
    fetches[5][1]()
    fetches[4][1]()

    def feed(block):
        hidden_grad = dot_nt(out_ref[block], down_w[...])
        pre_ref[block] = (hidden_grad * gelu_slope(act_ref[block])).astype(LOW)
        parts[block] = dot_nt(pre_ref[block], up_w[...]).astype(LOW)

    def steps(*names):
        if extra is not None:
            for name in names:
                getattr(extra, name)()

    feed(me)
    grads.relay()
    steps("feed_products")
    grads.wait_left()
    feed(ring.left)
    grads.wait_right()
    feed(ring.right)
    sums.start_near()
    grads.wait_opposite()
    feed(ring.opposite)
    sums.start_far()
    steps("products_0", "feed_relay")
    sums.relay()
    steps("products_1")
    middle_part, gain_two = norm_back(middle_ref[...], gains_ref[1:2, :], row_total(sums))
    gain_ref[1:2, :] = gain_two
    middle_grad = dy_ref[...].astype(F32) + middle_part
    kept_grad[...] = middle_grad
    branch_ref[...] = middle_grad.astype(LOW)
    fetches[3][1]()
    mixed_grad[...] = dot_nt(branch_ref[...], at_w[3]).astype(LOW)
    bias = bias_ref[...]
    dkeys = row_scatter(ring, parts_b, landing_b, passing_b, arrived_b, (key_send, key_recv))
    dvalues = row_scatter(
        ring, parts_c, landing_c, passing_c, arrived_c, (value_send, value_recv)
    )
    for count, (begin, width) in enumerate(pair_columns(features)):
        columns = pl.ds(begin, width)
        queries = query_ref[:, columns]
        outer = mixed_grad[:, columns]
        key_block = key_ref[:, :, columns].reshape(4 * rows, width)
        value_block = value_ref[:, :, columns].reshape(4 * rows, width)
        dquery = dkey = dvalue = None
        for mask in head_masks(width):
            query_one, outer_one = masked(queries, mask), masked(outer, mask)
            scores = dot_nt(key_block, query_one) * 0.125 + bias
            raised = jnp.exp(scores - jnp.max(scores, axis=0, keepdims=True))
            probs = raised * (1.0 / jnp.sum(raised, axis=0, keepdims=True))
            probs_grad = dot_nt(value_block, outer_one)
            mean = jnp.sum(probs * probs_grad, axis=0, keepdims=True)
            score_grad = (probs * (probs_grad - mean)).astype(LOW)
            own_query = dot_tn(score_grad, key_block)
            own_key = dot_nn(score_grad, query_one)
            own_value = dot_nn(probs.astype(LOW), outer_one)
            if dquery is None:
                dquery, dkey, dvalue = own_query, own_key, own_value
            else:
                dquery = jnp.where(mask, own_query, dquery)
                dkey, dvalue = dkey + own_key, dvalue + own_value
        dquery_ref[:, columns] = (dquery * 0.125).astype(LOW)
        parts_b[:, :, columns] = (dkey * 0.125).astype(LOW).reshape(4, rows, width)
        parts_c[:, :, columns] = dvalue.astype(LOW).reshape(4, rows, width)
        if count == 2:
            steps("feed_middle", "x_relay_0")
        if count == 5:
            steps("feed_middle_relay", "x_relay_1")
    dkeys.start_far()
    dvalues.start_far()
    dkeys.start_near()
    dvalues.start_near()
    for which in (0, 1, 2):
        fetches[which][1]()
    one_grad = dot_nt(dquery_ref[...], at_w[0])
    steps("feed_end")
    dkeys.relay()
    dvalues.relay()
    steps("feed_end_relay")
    dkey_ref[...] = row_total(dkeys).astype(LOW)
    one_grad = one_grad + dot_nt(dkey_ref[...], at_w[1])
    steps("keep_0")
    dvalue_ref[...] = row_total(dvalues).astype(LOW)
    one_grad = one_grad + dot_nt(dvalue_ref[...], at_w[2])
    inputs_part, gain_one = norm_back(x_ref[...].astype(F32), gains_ref[0:1, :], one_grad)
    gain_ref[0:1, :] = gain_one
    dx_ref[...] = (kept_grad[...] + inputs_part).astype(LOW)
    steps("feed_hand", "keep_1", "finish")
    grads.finish()
    sums.finish()
    dkeys.finish()
    dvalues.finish()


def greet_all():
    rings = [Ring(axis) for axis in ("x", "y", "z")]
    greet(
        *[ring.to_right for ring in rings], *[ring.to_left for ring in rings], sibling()
    )


def backward_layer(layer, x, dy, bias, gains, middle, query, key, value, act, attention, feed,
                   operands=()):
    rows, features = x.shape
    hidden = feed[0].shape[1]
    out_shape = (
        jax.ShapeDtypeStruct((rows, features), LOW),
        jax.ShapeDtypeStruct((2, features), F32),
        jax.ShapeDtypeStruct((4, rows, features), LOW),
        jax.ShapeDtypeStruct((4, rows, hidden), LOW),
        jax.ShapeDtypeStruct((rows, features), LOW),
        jax.ShapeDtypeStruct((rows, features), LOW),
        jax.ShapeDtypeStruct((rows, features), LOW),
        jax.ShapeDtypeStruct((rows, features), LOW),
    )
    sums = feed_outputs(features) + kept_output(features) if layer == 0 else ()
    return pl.pallas_call(
        functools.partial(backward_kernel, layer, features),
        out_shape=out_shape + sums,
        in_specs=[in_vmem()] * 9 + [anywhere()] * (6 + len(operands)),
        out_specs=[in_vmem()] * len(out_shape) + [anywhere()] * 2 * (len(sums) // 3)
        + [in_vmem()] * (len(sums) // 3),
        scratch_shapes=weight_scratch(features, hidden)
        + scatter_scratch(rows, features) * 3
        + [pltpu.VMEM((rows, features), LOW), pltpu.VMEM((rows, features), F32)]
        + [pltpu.SemaphoreType.DMA((6,))] * 8
        + (gradient_scratch(features, rows) if layer == 0 else []),
        compiler_params=pltpu.CompilerParams(
            collective_id=2 + layer, has_side_effects=True, vmem_limit_bytes=62 * 2**20
        ),
        cost_estimate=pl.CostEstimate(
            flops=4 * 10**9, bytes_accessed=24 * 10**6, transcendentals=10**6
        ),
        name=f"layer_backward_{layer}",
    )(x, dy, bias, gains, middle, query, key, value, act, *attention, *feed, *operands)


X_ROWS, Y_ROWS = 96, 96


def weights_kernel(
    shard_ref, gain_ref, mine_ref, theirs_ref, gain_mine, gain_theirs, local_sems, x_send, x_recv,
    yx_send, yx_recv, zx_send, zx_recv, y_send, y_recv, z_send, z_recv, gain_send, gain_recv,
    pair_send, pair_recv,
):
    x_ring, y_ring, z_ring = Ring("x"), Ring("y"), Ring("z")
    mine_y, mine_z, mine_x = y_ring.me, z_ring.me, x_ring.me
    share = shard_ref.shape[1]
    y_begin, z_begin = X_ROWS, X_ROWS + Y_ROWS
    z_rows = share - z_begin
    all_x, all_y, all_z = pl.ds(0, X_ROWS), pl.ds(y_begin, Y_ROWS), pl.ds(z_begin, z_rows)
    y_half = (pl.ds(y_begin, 48), pl.ds(y_begin + 48, Y_ROWS - 48))
    z_half = (pl.ds(z_begin, 48), pl.ds(z_begin + 48, z_rows - 48))
    pair = sibling()
    greet(
        x_ring.to_right, x_ring.to_left, y_ring.to_right, y_ring.to_left, z_ring.to_right,
        z_ring.to_left, pair,
    )
    locals_ = [
        pltpu.make_async_copy(
            shard_ref.at[mine_y, all_y], mine_ref.at[mine_y, mine_x, all_y], local_sems.at[0]
        ),
        pltpu.make_async_copy(
            shard_ref.at[mine_z, all_z], mine_ref.at[mine_z, mine_x, all_z], local_sems.at[1]
        ),
        pltpu.make_async_copy(
            shard_ref.at[:, all_x], mine_ref.at[:, mine_x, all_x], local_sems.at[2]
        ),
        pltpu.make_async_copy(gain_ref, gain_mine.at[mine_x], local_sems.at[3]),
    ]
    first_y = Gather(
        x_ring,
        lambda block, half: mine_ref.at[mine_y, block, y_half[half]],
        (yx_send, yx_recv),
        lambda half: shard_ref.at[mine_y, y_half[half]],
    )
    first_z = Gather(
        x_ring,
        lambda block, half: mine_ref.at[mine_z, block, z_half[half]],
        (zx_send, zx_recv),
        lambda half: shard_ref.at[mine_z, z_half[half]],
    )
    along_x = Gather(
        x_ring,
        lambda block, half: mine_ref.at[pl.ds(2 * half, 2), block, all_x],
        (x_send, x_recv),
        lambda half: shard_ref.at[pl.ds(2 * half, 2), all_x],
    )
    along_y = Gather(
        y_ring,
        lambda block, half: mine_ref.at[block, pl.ds(2 * half, 2), all_y],
        (y_send, y_recv),
    )
    along_z = Gather(
        z_ring,
        lambda block, half: mine_ref.at[block, pl.ds(2 * half, 2), all_z],
        (z_send, z_recv),
    )

    def gain_copy(which, block, src=None):
        part = gain_mine.at[block]
        target = x_ring.to_left if which == 1 else x_ring.to_right
        return remote(part if src is None else src, part, (gain_send, gain_recv), which, target)

    def hand(which, region):
        return remote(mine_ref.at[region], theirs_ref.at[region], (pair_send, pair_recv), which, pair)

    handed = []

    def hand_on(which, region):
        copy = hand(which, region)
        copy.start()
        handed.append(copy)

    first_y.start()
    first_z.start()
    for copy in locals_:
        copy.start()
    gain_copy(0, mine_x, gain_ref).start()
    gain_copy(1, mine_x, gain_ref).start()
    first_y.relay()
    first_z.relay()
    along_x.start()
    first_y.wait_all()
    locals_[0].wait()
    along_y.start()
    hand_on(0, (mine_y, slice(None), all_y))
    first_z.wait_all()
    locals_[1].wait()
    along_z.start()
    hand_on(1, (mine_z, slice(None), all_z))
    gain_copy(0, x_ring.left).wait_recv()
    gain_copy(2, x_ring.left).start()
    along_x.relay()
    along_y.relay()
    along_z.relay()
    along_x.wait_all()
    locals_[2].wait()
    hand_on(2, (slice(None), slice(None), all_x))
    along_y.wait_left()
    hand_on(3, (y_ring.left, slice(None), all_y))
    along_z.wait_left()
    hand_on(4, (z_ring.left, slice(None), all_z))
    along_y.wait_right()
    hand_on(5, (y_ring.right, slice(None), all_y))
    along_z.wait_right()
    hand_on(6, (z_ring.right, slice(None), all_z))
    gain_copy(1, x_ring.right).wait_recv()
    gain_copy(2, x_ring.opposite).wait_recv()
    locals_[3].wait()
    gains = remote(gain_mine, gain_theirs, (pair_send, pair_recv), 9, pair)
    gains.start()
    along_y.wait_opposite()
    hand_on(7, (y_ring.opposite, slice(None), all_y))
    along_z.wait_opposite()
    hand_on(8, (z_ring.opposite, slice(None), all_z))
    for copy in handed + [gains]:
        copy.wait()
    for which in range(3):
        gain_copy(which, mine_x).wait_send()
    for gather in (first_y, first_z, along_x, along_y, along_z):
        gather.finish()


def gather_weights(shard, gain):
    mats, share, features = shard.shape
    full = jax.ShapeDtypeStruct((mats, 4, share, features), LOW)
    gains = jax.ShapeDtypeStruct((4,) + gain.shape, LOW)
    return pl.pallas_call(
        weights_kernel,
        out_shape=(full, full, gains, gains),
        in_specs=[anywhere()] * 2,
        out_specs=[anywhere()] * 4,
        scratch_shapes=[pltpu.SemaphoreType.DMA((4,))]
        + [pltpu.SemaphoreType.DMA((6,))] * 10
        + [pltpu.SemaphoreType.DMA((3,))] * 2
        + [pltpu.SemaphoreType.DMA((10,))] * 2,
        compiler_params=pltpu.CompilerParams(collective_id=4, has_side_effects=True),
        cost_estimate=pl.CostEstimate(flops=0, bytes_accessed=60 * 10**6, transcendentals=0),
        name="gather_weights",
    )(shard, gain)


class SmallSum:
    def __init__(self, ring, slots, sems):
        self.ring, self.slots, self.sems = ring, slots, sems

    def copy(self, which, block):
        target = self.ring.to_left if which == 1 else self.ring.to_right
        part = self.slots.at[block]
        return remote(part, part, self.sems, which, target)

    def start(self):
        self.copy(0, self.ring.me).start()
        self.copy(1, self.ring.me).start()

    def relay(self):
        self.copy(0, self.ring.left).wait_recv()
        self.copy(2, self.ring.left).start()

    def result(self):
        self.copy(1, self.ring.right).wait_recv()
        self.copy(2, self.ring.opposite).wait_recv()
        return (self.slots[0] + self.slots[1]) + (self.slots[2] + self.slots[3])

    def finish(self):
        for which in range(3):
            self.copy(which, self.ring.me).wait_send()


class PlaneSum:
    def __init__(self, near, far, source, out, size, first, scratch, sems, keep):
        self.landing, self.passing, self.arrived, self.mid, self.done = scratch
        self.out, self.size, self.near, self.far, self.keep = out, size, near, far, keep
        self.halves = ((0, first), (first, size - first))

        def rows(block, half):
            begin, count = self.halves[half]
            return pl.ds(pl.multiple_of(block * size + begin, 16), count)

        def half_rows(half):
            return pl.ds(*self.halves[half])

        self.half_rows = half_rows
        self.scatter = Scatter(
            near,
            lambda block, half: source.at[rows(block, half)],
            lambda half: self.landing.at[half_rows(half)],
            lambda half: self.passing.at[half_rows(half)],
            lambda side, half: self.arrived.at[side, half_rows(half)],
            sems[0],
        )
        self.gather = Gather(far, lambda block, half: self.mid.at[block, half_rows(half)], sems[1])
        self.spread = Gather(
            near,
            lambda block, half: out.at[rows(block, half)],
            sems[2],
            lambda half: self.done.at[half_rows(half)],
        )

    def start(self):
        self.scatter.start_far()
        self.scatter.start_near()

    def relay(self):
        self.scatter.relay()

    def middle(self):
        self.scatter.wait()
        for half in range(2):
            self.mid[self.far.me, self.half_rows(half)] = self.scatter.total(half).astype(LOW)
        self.gather.start()

    def middle_relay(self):
        self.gather.relay()

    def own(self):
        place = pl.ds(pl.multiple_of(self.near.me * self.size, 16), self.size)
        return pltpu.make_async_copy(self.done, self.out.at[place], self.keep)

    def end(self):
        self.gather.wait_all()
        four = [self.mid[block].astype(F32) for block in range(4)]
        self.done[...] = ((four[0] + four[1]) + (four[2] + four[3])).astype(LOW)
        self.spread.start()
        self.own().start()

    def end_relay(self):
        self.spread.relay()

    def wait(self):
        self.spread.wait_all()
        self.own().wait()

    def finish(self):
        self.scatter.finish()
        self.gather.finish()
        self.spread.finish()


FEED_BLOCK, AT_BLOCK = 144, 80


def feed_outputs(features):
    return (jax.ShapeDtypeStruct((2, 4 * FEED_BLOCK, features), LOW),) * 2


def kept_output(features):
    return (jax.ShapeDtypeStruct((2, 4 * AT_BLOCK, features), LOW),)


def plane_scratch(size, features):
    dma = pltpu.SemaphoreType.DMA

    def low(*shape):
        return pltpu.VMEM(shape + (features,), LOW)

    return [low(size), low(size), low(2, size), low(4, size), low(size)] + [dma((6,))] * 6


def gradient_scratch(features, rows):
    share = features // 4
    dma = pltpu.SemaphoreType.DMA

    def low(*shape):
        return pltpu.VMEM(shape + (features,), LOW)

    return (
        [low(2, 2, 4, rows), low(2, 2, rows), low(2, 2, rows), low(2, features),
         low(2, 4 * FEED_BLOCK)]
        + ([low(share), low(share), low(2, share)] + [dma((6,))] * 2) * 2
        + plane_scratch(FEED_BLOCK, features) * 2
        + [dma((6,)), dma((6,)), dma((6,)), dma((2,)), dma((1,)), dma((1,))]
    )


def attention_scratch(features):
    dma = pltpu.SemaphoreType.DMA
    return plane_scratch(AT_BLOCK, features) * 2 + [dma((2,)), dma((1,)), dma((1,))]


def take_planes(take):
    planes = []
    for _ in range(2):
        scratch = [next(take) for _ in range(5)]
        sems = [next(take) for _ in range(6)]
        planes.append((scratch, [tuple(sems[i : i + 2]) for i in (0, 2, 4)]))
    return planes


def hand_over(layer, src, dst, sems):
    section = lax.axis_index("section")
    copy = functools.partial(remote, src, dst, sems, 0, sibling())

    def start():
        @pl.when(section != layer)
        def _():
            copy().start()

    def wait():
        @pl.when(section != layer)
        def _():
            copy().wait_send()

        @pl.when(section == layer)
        def _():
            copy().wait_recv()

    return start, wait


class AttentionSum:
    def __init__(self, layer, kept, results, take):
        out, other = results
        planes = take_planes(take)
        keep, send, recv = [next(take) for _ in range(3)]
        y_ring, z_ring = Ring("y"), Ring("z")
        orders = ((y_ring, z_ring), (z_ring, y_ring))
        self.planes = [
            PlaneSum(
                *orders[which], kept.at[which], out.at[which], AT_BLOCK, 48, *planes[which],
                keep.at[which],
            )
            for which in range(2)
        ]
        self.give, self.wait_given = hand_over(layer, out, other, (send, recv))

    def hand(self):
        for plane in self.planes:
            plane.wait()
        self.give()

    def finish(self):
        for plane in self.planes:
            plane.finish()
        self.wait_given()


class GradientSum:
    def __init__(self, layer, features, operands, results, take):
        self.layer, self.features = layer, features
        self.operands = operands
        self.feed_out, self.feed_other, self.at_kept = results
        (self.feed_in, self.at_left, self.at_right, self.at_sum, self.feed_sum) = [
            next(take) for _ in range(5)
        ]
        self.pair, self.section = sibling(), lax.axis_index("section")
        x_ring, y_ring, z_ring = Ring("x"), Ring("y"), Ring("z")
        share = features // 4
        self.share = share
        self.across = []
        for which in range(2):
            landing, passing, arrived, send, recv = [next(take) for _ in range(5)]
            halves = ((0, 144), (144, share - 144))

            def part(block, half, which=which, halves=halves):
                begin, count = halves[half]
                row = pl.multiple_of(block * share + begin, 16)
                return self.at_sum.at[which, pl.ds(row, count)]

            def cut(ref, halves=halves):
                return lambda half: ref.at[pl.ds(*halves[half])]

            self.across.append(
                Scatter(
                    x_ring, part, cut(landing), cut(passing),
                    lambda side, half, arrived=arrived, halves=halves: arrived.at[
                        side, pl.ds(*halves[half])
                    ],
                    (send, recv),
                )
            )
        self.halves = halves
        planes = take_planes(take)
        (self.local_sems, swap_send, swap_recv, keep, end_send, end_recv) = [
            next(take) for _ in range(6)
        ]
        self.swap, self.end_sems = (swap_send, swap_recv), (end_send, end_recv)
        orders = ((y_ring, z_ring), (z_ring, y_ring))
        self.feed = [
            PlaneSum(
                *orders[which], self.feed_sum.at[which], self.feed_out.at[which], FEED_BLOCK, 80,
                *planes[which], keep.at[which],
            )
            for which in range(2)
        ]

    def inputs(self, first):
        two, pre, hidden, out, one, mixed, dq, dk, dv, branch = self.operands
        zero = (two, pre, one, one, dq, dk)
        other = (hidden, out, one, mixed, dv, branch)
        own, sent = (zero, other) if first else (other, zero)
        targets = (
            self.feed_in.at[0], self.feed_in.at[1], self.at_left.at[0], self.at_left.at[1],
            self.at_right.at[0], self.at_right.at[1],
        )

        def keep(which):
            return pltpu.make_async_copy(
                own[which], targets[which].at[0], self.local_sems.at[which]
            )

        def send(which):
            return remote(sent[which], targets[which].at[1], self.swap, which, self.pair)

        return keep, send

    def start_inputs(self):
        for first in (True, False):

            @pl.when(self.section == (0 if first else 1))
            def _(first=first):
                keep, send = self.inputs(first)
                for which in range(6):
                    send(which).start()
                for which in range(6):
                    keep(which).start()

    def wait_inputs(self, whiches):
        keep, send = self.inputs(True)
        for which in whiches:
            keep(which).wait()
            send(which).wait_recv()

    def feed_products(self):
        self.wait_inputs((0, 1))
        features, whole = self.features, 4 * FEED_BLOCK
        right = self.feed_in[1].reshape(-1, features)
        for begin in range(0, features, 256):
            count = min(256, features - begin)
            left = self.feed_in[0, :, :, :, pl.ds(begin, count)].reshape(-1, count)
            product = dot_tn(left, right).astype(LOW)
            first = max(0, min(count, whole - begin))
            if first:
                self.feed_sum[0, pl.ds(begin, first)] = product[:first]
            if first < count:
                self.feed_sum[1, pl.ds(begin + first - whole, count - first)] = product[first:]
        spare = 2 * whole - features
        self.feed_sum[1, pl.ds(whole - spare, spare)] = jnp.zeros((spare, features), LOW)
        for plane in self.feed:
            plane.start()

    def products(self, which):
        self.wait_inputs((2 + which, 4 + which))
        features = self.features
        right = self.at_right[which].reshape(-1, features)
        for begin in range(0, features, 256):
            count = min(256, features - begin)
            left = self.at_left[which, :, :, pl.ds(begin, count)].reshape(-1, count)
            self.at_sum[which, pl.ds(begin, count)] = dot_tn(left, right).astype(LOW)
        self.across[which].start_far()

    def products_0(self):
        self.products(0)

    def products_1(self):
        self.products(1)

    def feed_relay(self):
        for plane in self.feed:
            plane.relay()

    def feed_middle(self):
        for plane in self.feed:
            plane.middle()

    def feed_middle_relay(self):
        for plane in self.feed:
            plane.middle_relay()

    def feed_end(self):
        for plane in self.feed:
            plane.end()

    def feed_end_relay(self):
        for plane in self.feed:
            plane.end_relay()

    def x_relay_0(self):
        self.across[0].relay()
        self.across[0].start_near()

    def x_relay_1(self):
        self.across[1].relay()
        self.across[1].start_near()

    def keep(self, which):
        across = self.across[which]
        across.wait()
        for half in range(2):
            self.at_kept[which, pl.ds(*self.halves[half])] = across.total(half).astype(LOW)
        spare = 4 * AT_BLOCK - self.share
        self.at_kept[which, pl.ds(self.share, spare)] = jnp.zeros((spare, self.features), LOW)

    def keep_0(self):
        self.keep(0)

    def keep_1(self):
        self.keep(1)

    def feed_hand(self):
        for plane in self.feed:
            plane.wait()
        hand_over(self.layer, self.feed_out, self.feed_other, self.end_sems)[0]()

    def finish(self):
        _, send = self.inputs(True)
        for which in range(6):
            send(which).wait_send()
        for each in self.across + self.feed:
            each.finish()
        hand_over(self.layer, self.feed_out, self.feed_other, self.end_sems)[1]()


def gradient_kernel(features, *refs):
    take = iter(refs)

    def some(count):
        return [next(take) for _ in range(count)]

    operands = some(10)
    y_a, y_b, dx_a, dx_b, gain_in, kept_one = some(6)
    feed_results, at_zero, at_one = some(2), some(2), some(2)
    act_out, grad_out, gain_out = some(3)
    (kept_zero,) = some(1)
    sums = GradientSum(0, features, operands, feed_results + [kept_zero], take)
    zero = AttentionSum(0, kept_zero, at_zero, take)
    one = AttentionSum(1, kept_one, at_one, take)
    (gain_pair, gain_x, gain_y, gain_z, gain_send, gain_recv, last_send, last_recv,
     keep_sems) = some(9)
    x_ring, y_ring, z_ring = Ring("x"), Ring("y"), Ring("z")
    pair, section = sibling(), lax.axis_index("section")
    greet_all()
    sums.start_inputs()

    def last_copies(y, dx):
        return (
            remote(y, act_out.at[section], (last_send, last_recv), 0, pair),
            remote(dx, grad_out.at[section], (last_send, last_recv), 1, pair),
        )

    def keep_copies(y, dx):
        return (
            pltpu.make_async_copy(y, act_out.at[section], keep_sems.at[0]),
            pltpu.make_async_copy(dx, grad_out.at[section], keep_sems.at[1]),
        )

    @pl.when(section == 0)
    def _():
        for copy in last_copies(y_b, dx_b) + keep_copies(y_a, dx_a):
            copy.start()

    @pl.when(section == 1)
    def _():
        for copy in last_copies(y_a, dx_a) + keep_copies(y_b, dx_b):
            copy.start()

    gain_pair[0] = gain_in[...]
    swap_gain = remote(gain_pair.at[0], gain_pair.at[1], (gain_send, gain_recv), 9, pair)
    swap_gain.start()
    for plane in one.planes:
        plane.start()
    sums.products_0()
    sums.products_1()
    sums.feed_products()
    swap_gain.wait()
    gain_x[x_ring.me] = gain_pair[0] + gain_pair[1]
    small = [
        SmallSum(ring, slots, (gain_send.at[pl.ds(3 * i, 3)], gain_recv.at[pl.ds(3 * i, 3)]))
        for i, (ring, slots) in enumerate(((x_ring, gain_x), (y_ring, gain_y), (z_ring, gain_z)))
    ]
    small[0].start()
    sums.x_relay_0()
    for plane in one.planes:
        plane.relay()
    sums.x_relay_1()
    sums.feed_relay()
    small[0].relay()
    for plane in one.planes:
        plane.middle()
    sums.feed_middle()
    gain_y[y_ring.me] = small[0].result()
    small[1].start()
    for plane in one.planes:
        plane.middle_relay()
    sums.keep_0()
    zero.planes[0].start()
    sums.feed_middle_relay()
    small[1].relay()
    for plane in one.planes:
        plane.end()
    sums.feed_end()
    zero.planes[0].relay()
    sums.keep_1()
    zero.planes[1].start()
    for plane in one.planes:
        plane.end_relay()
    gain_z[z_ring.me] = small[1].result()
    small[2].start()
    sums.feed_end_relay()
    zero.planes[0].middle()
    zero.planes[1].relay()
    small[2].relay()
    one.hand()
    zero.planes[0].middle_relay()
    zero.planes[1].middle()
    gain_out[...] = small[2].result()
    zero.planes[0].end()
    zero.planes[1].middle_relay()
    sums.feed_hand()
    zero.planes[0].end_relay()
    zero.planes[1].end()
    zero.planes[1].end_relay()
    zero.hand()
    zero.finish()
    one.finish()
    sums.finish()
    for each in small:
        each.finish()
    for copy in last_copies(y_a, dx_a) + keep_copies(y_a, dx_a):
        copy.wait()


def sum_gradients(features, rows, operands, last, gain, kept):
    dma = pltpu.SemaphoreType.DMA
    small = [pltpu.VMEM((4, 8, features), F32)] * 3
    return pl.pallas_call(
        functools.partial(gradient_kernel, features),
        out_shape=feed_outputs(features)
        + kept_output(features) * 4
        + (
            jax.ShapeDtypeStruct((2, rows, features), LOW),
            jax.ShapeDtypeStruct((2, rows, features), LOW),
            jax.ShapeDtypeStruct((8, features), F32),
        ),
        in_specs=[anywhere()] * 14 + [in_vmem()] * 2,
        out_specs=[anywhere()] * 8 + [in_vmem()],
        scratch_shapes=[pltpu.VMEM((2, 4 * AT_BLOCK, features), LOW)]
        + gradient_scratch(features, rows)
        + attention_scratch(features) * 2
        + [pltpu.VMEM((2, 8, features), F32)]
        + small
        + [dma((10,)), dma((10,)), dma((2,)), dma((2,)), dma((2,))],
        compiler_params=pltpu.CompilerParams(
            collective_id=5, has_side_effects=True, vmem_limit_bytes=60 * 2**20
        ),
        cost_estimate=pl.CostEstimate(
            flops=6 * 10**9, bytes_accessed=60 * 10**6, transcendentals=0
        ),
        name="sum_gradients",
    )(*operands, *last, gain, kept)


def doc_numbers(lengths, positions):
    doc_ends = jnp.cumsum(lengths)
    return jnp.sum((positions[:, None] >= doc_ends[None, :]).astype(jnp.int32), axis=1)


def swapped(block):
    return lax.ppermute(block, "section", [(0, 1), (1, 0)])


def body(tokens, cotangent, doc_lengths, norm_gains, w_qkv, w_out, w_up, w_down):
    batches, rows, features = tokens.shape
    share = w_qkv.shape[1]
    seq_rows = rows * lax.axis_size("tensor")
    section = lax.axis_index("section")
    is_first = section == 0

    def choose(zero_side, one_side):
        return jnp.where(is_first, zero_side, one_side)

    own_tokens = lax.dynamic_index_in_dim(tokens, section, 0, keepdims=False)
    own_cotangent = lax.dynamic_index_in_dim(cotangent, section, 0, keepdims=False)
    lengths = lax.dynamic_index_in_dim(doc_lengths, section, 0, keepdims=False)
    own_places = lax.axis_index("tensor") * rows + jnp.arange(rows, dtype=jnp.int32)
    all_places = jnp.arange(seq_rows, dtype=jnp.int32)
    own_docs = doc_numbers(lengths, own_places)
    all_docs = doc_numbers(lengths, all_places)
    allowed = (all_places[None, :] <= own_places[:, None]) & (
        all_docs[None, :] == own_docs[:, None]
    )
    bias = jnp.where(allowed, 0.0, -1e30).astype(F32)
    bias_turned = bias.T

    feed = (w_up[0], swapped(w_up[0]), w_down[0], swapped(w_down[0]))
    shard = jnp.stack(
        [w_qkv[0, :, :features], w_qkv[0, :, features : 2 * features], w_qkv[0, :, 2 * features :],
         w_out[0]]
    )
    gain_shard = jnp.pad(norm_gains[0], ((0, 14), (0, 0)))
    at_mine, at_theirs, gain_mine, gain_theirs = gather_weights(shard, gain_shard)
    attention = (
        at_mine.reshape(4, features, features), at_theirs.reshape(4, features, features)
    )

    def whole_gains(block):
        return block[:, :2].transpose(1, 0, 2).reshape(2, features).astype(F32)

    gain_mine, gain_theirs = whole_gains(gain_mine), whole_gains(gain_theirs)
    gains = (choose(gain_mine, gain_theirs), choose(gain_theirs, gain_mine))

    inputs = own_tokens
    saved = []
    for layer in range(2):
        results = forward_layer(layer, inputs, bias, gains[layer], attention, feed)
        saved.append((inputs,) + tuple(results))
        inputs = results[0]

    grad = own_cotangent
    gain_grads, input_grads, operands = [None, None], [None, None], ()
    for layer in (1, 0):
        (x, _, middle, normed_one, query, key, value, mixed, normed_two, act, hidden) = saved[layer]
        results = backward_layer(
            layer, x, grad, bias_turned, gains[layer], middle, query, key, value, act,
            attention, feed, operands,
        )
        (grad, gain_grads[layer], out_all, pre_grad, branch, dquery, dkey, dvalue) = results[:8]
        input_grads[layer] = grad
        operands = (
            normed_two, pre_grad, hidden, out_all, normed_one, mixed, dquery, dkey, dvalue, branch,
        )
    feed_one, feed_one_given, kept_one = results[8:]
    gain_rows = jnp.concatenate(gain_grads + [jnp.zeros((4, features), F32)], axis=0)
    (feed_zero, feed_zero_given, at_zero, at_zero_given, at_one, at_one_given, activations,
     input_grads, gain_total) = sum_gradients(
        features, rows, operands, (saved[0][1], saved[1][1], *input_grads), gain_rows, kept_one
    )
    gain_own = lax.dynamic_slice(
        gain_total, (2 * section, lax.axis_index("tensor") * share), (2, share)
    )

    def whole(block):
        return block.reshape(-1, features)[:features].astype(F32)[None]

    first_half = choose(at_zero, at_one_given)[:, :share].astype(F32)
    other_half = choose(at_zero_given, at_one)[:, :share].astype(F32)
    grad_qkv = jnp.concatenate([first_half[0], first_half[1], other_half[0]], axis=1)
    return (
        activations[None],
        input_grads[None],
        gain_own[None],
        grad_qkv[None],
        other_half[1][None],
        whole(choose(feed_zero, feed_one_given)),
        whole(choose(feed_zero_given, feed_one)),
    )


def solution(mesh):
    placed = (
        P("dp", "tensor", None),
        P("dp", "tensor", None),
        P("dp", None),
        P("section", None, "tensor"),
        P("section", "tensor", None),
        P("section", "tensor", None),
        P("section", None, "tensor"),
        P("section", "tensor", None),
    )
    return jax.shard_map(
        body,
        mesh=mesh,
        in_specs=placed,
        out_specs=(
            P("section", "dp", "tensor", None),
            P("section", "dp", "tensor", None),
            P("section", None, "tensor"),
            P("section", "tensor", None),
            P("section", "tensor", None),
            P("section", None, "tensor"),
            P("section", "tensor", None),
        ),
        check_vma=False,
    )
```

```python
import functools
import jax
import jax.numpy as jnp
from jax import lax
from jax.experimental import pallas as pl
from jax.experimental.pallas import tpu as pltpu
from jax.sharding import PartitionSpec as P

HEAD_DIM = 64
LOW = jnp.bfloat16
F32 = jnp.float32
MESH = pl.DeviceIdType.MESH


def dot_nn(left, right):
    return lax.dot_general(left, right, (((1,), (0,)), ((), ())), preferred_element_type=F32)


def dot_nt(left, right):
    return lax.dot_general(left, right, (((1,), (1,)), ((), ())), preferred_element_type=F32)


def dot_tn(left, right):
    return lax.dot_general(left, right, (((0,), (0,)), ((), ())), preferred_element_type=F32)


class Ring:
    def __init__(self, axis):
        whole = lax.axis_index("dp")
        rest = None
        if axis == "x":
            self.me = lax.axis_index("tensor")
        elif axis == "y":
            self.me, rest = lax.rem(whole, 4), lax.div(whole, 4) * 4
        else:
            self.me, rest = lax.div(whole, 4), lax.rem(whole, 4)
        self.right = lax.rem(self.me + 1, 4)
        self.left = lax.rem(self.me + 3, 4)
        self.opposite = lax.rem(self.me + 2, 4)

        def device(place):
            if axis == "x":
                return {"tensor": place}
            if axis == "y":
                return {"dp": rest + place}
            return {"dp": place * 4 + rest}

        self.to_right, self.to_left = device(self.right), device(self.left)
        self.to_opposite = device(self.opposite)


def sibling():
    return {"section": 1 - lax.axis_index("section")}


def greet(*targets):
    barrier = pltpu.get_barrier_semaphore()
    for target in targets:
        pl.semaphore_signal(barrier, inc=1, device_id=target, device_id_type=MESH)
    pl.semaphore_wait(barrier, len(targets))


def remote(src, dst, sems, which, target):
    return pltpu.make_async_remote_copy(
        src_ref=src,
        dst_ref=dst,
        send_sem=sems[0].at[which],
        recv_sem=sems[1].at[which],
        device_id=target,
        device_id_type=MESH,
    )


class Gather:
    def __init__(self, ring, slot, sems, own=None):
        self.ring, self.slot, self.sems = ring, slot, sems
        self.own = own if own is not None else lambda half: slot(ring.me, half)

    def copy(self, which, arriving=False):
        ring = self.ring
        half = (0, 1, 1, 0, 0, 1)[which]
        goes_right = which in (0, 2, 4)
        target = ring.to_right if goes_right else ring.to_left
        if which < 4:
            source_block = ring.left if goes_right else ring.right
            if not arriving:
                return remote(self.own(half), self.slot(ring.me, half), self.sems, which, target)
        else:
            source_block = ring.opposite
            if not arriving:
                handed = self.slot(ring.left if goes_right else ring.right, half)
                return remote(handed, handed, self.sems, which, target)
        part = self.slot(source_block, half)
        return remote(part, part, self.sems, which, target)

    def start(self):
        for which in range(4):
            self.copy(which).start()

    def relay(self):
        for which in (0, 1):
            self.copy(which, arriving=True).wait_recv()
            self.copy(which + 4).start()

    def wait_left(self):
        self.copy(2, arriving=True).wait_recv()

    def wait_right(self):
        self.copy(3, arriving=True).wait_recv()

    def wait_opposite(self):
        self.copy(4, arriving=True).wait_recv()
        self.copy(5, arriving=True).wait_recv()

    def wait_all(self):
        self.wait_left()
        self.wait_right()
        self.wait_opposite()

    def finish(self):
        for which in range(6):
            self.copy(which).wait_send()


class Scatter:
    def __init__(self, ring, part, landing, passing, arrived, sems):
        self.ring, self.part, self.landing, self.passing = ring, part, landing, passing
        self.arrived, self.sems = arrived, sems

    def copy(self, which):
        ring = self.ring
        half = (0, 1, 1, 0, 0, 1)[which]
        goes_right = which in (0, 2, 4)
        if which < 2:
            src, dst = self.part(ring.opposite, half), self.landing(half)
        else:
            dst = self.arrived(0 if goes_right else 1, half)
            if which < 4:
                src = self.part(ring.right if goes_right else ring.left, half)
            else:
                src = self.passing(half)
        return remote(src, dst, self.sems, which, ring.to_right if goes_right else ring.to_left)

    def start_near(self):
        self.copy(2).start()
        self.copy(3).start()

    def start_far(self):
        self.copy(0).start()
        self.copy(1).start()

    def relay(self):
        for half, block in ((0, self.ring.right), (1, self.ring.left)):
            self.copy(half).wait_recv()
            added = self.part(block, half)[...].astype(F32) + self.landing(half)[...].astype(F32)
            self.passing(half)[...] = added.astype(LOW)
            self.copy(half + 4).start()

    def wait(self):
        for which in (2, 3, 4, 5):
            self.copy(which).wait_recv()

    def total(self, half):
        return (
            self.part(self.ring.me, half)[...].astype(F32)
            + self.arrived(0, half)[...].astype(F32)
            + self.arrived(1, half)[...].astype(F32)
        )

    def finish(self):
        for which in range(6):
            self.copy(which).wait_send()


class DirectGather:
    def __init__(self, ring, slot, sems, own=None):
        self.ring, self.slot, self.sems = ring, slot, sems
        self.own = own if own is not None else lambda half: slot(ring.me, half)

    def copy(self, which):
        target = (self.ring.to_right, self.ring.to_left, self.ring.to_opposite)[which]
        return remote(self.own(None), self.slot(self.ring.me, None), self.sems, which, target)

    def start(self):
        for which in (2, 0, 1):
            self.copy(which).start()

    def relay(self):
        pass

    def wait_all(self):
        for which, block in enumerate((self.ring.left, self.ring.right, self.ring.opposite)):
            part = self.slot(block, None)
            remote(part, part, self.sems, which, self.ring.to_right).wait_recv()

    def finish(self):
        for which in range(3):
            self.copy(which).wait_send()


class DirectScatter:
    def __init__(self, ring, part, arrived, sems):
        self.ring, self.part, self.arrived, self.sems = ring, part, arrived, sems

    def copy(self, which):
        ring = self.ring
        block = (ring.right, ring.left, ring.opposite)[which]
        target = (ring.to_right, ring.to_left, ring.to_opposite)[which]
        return remote(self.part(block, None), self.arrived(which), self.sems, which, target)

    def start_far(self):
        self.copy(2).start()

    def start_near(self):
        self.copy(0).start()
        self.copy(1).start()

    def relay(self):
        pass

    def wait(self):
        for which in range(3):
            self.copy(which).wait_recv()

    def whole(self):
        near = self.arrived(0)[...].astype(F32) + self.arrived(1)[...].astype(F32)
        own = self.part(self.ring.me, None)[...].astype(F32)
        return (own + near) + self.arrived(2)[...].astype(F32)

    def finish(self):
        for which in range(3):
            self.copy(which).wait_send()


def row_gather(ring, full, sems, columns=slice(None)):
    half = full.shape[1] // 2
    return Gather(
        ring, lambda block, which: full.at[block, pl.ds(which * half, half), columns], sems
    )


def row_scatter(ring, parts, landing, passing, arrived, sems, columns=slice(None)):
    half = parts.shape[1] // 2

    def rows(which):
        return pl.ds(which * half, half)

    return Scatter(
        ring,
        lambda block, which: parts.at[block, rows(which), columns],
        lambda which: landing.at[which, :, columns],
        lambda which: passing.at[which, :, columns],
        lambda side, which: arrived.at[side, rows(which), columns],
        sems,
    )


def row_total(scatter):
    scatter.wait()
    return jnp.concatenate([scatter.total(0), scatter.total(1)], axis=0)


def head_groups(features):
    pairs = pair_columns(features)
    middle = (len(pairs) + 1) // 2
    begin = pairs[middle][0]
    return (
        (pl.ds(0, begin), pairs[:middle]),
        (pl.ds(begin, features - begin), pairs[middle:]),
    )


def norm_stats(values):
    average = jnp.mean(values, axis=-1, keepdims=True)
    centered = values - average
    variance = jnp.mean(centered * centered, axis=-1, keepdims=True)
    scale = lax.rsqrt(variance + 1e-05)
    return centered * scale, scale


def norm_back(values, gain, grad):
    xhat, scale = norm_stats(values)
    scaled = grad * gain
    part = scale * (
        scaled
        - jnp.mean(scaled, axis=-1, keepdims=True)
        - xhat * jnp.mean(scaled * xhat, axis=-1, keepdims=True)
    )
    return part, jnp.sum(grad * xhat, axis=0, keepdims=True)


def gelu_tanh(values):
    inner = 0.7978845608028654 * (values + 0.044715 * values * values * values)
    return 0.5 * values * (1.0 + jnp.tanh(inner))


def gelu_slope(values):
    square = values * values
    bent = jnp.tanh(0.7978845608028654 * values * (1.0 + 0.044715 * square))
    slope = 0.7978845608028654 * (1.0 + 3.0 * 0.044715 * square)
    return 0.5 * (1.0 + bent) + 0.5 * values * (1.0 - bent * bent) * slope


def pick_copies(layer, mine, theirs, target, sem):
    def start():
        mine_here = lax.axis_index("section") == layer

        @pl.when(mine_here)
        def _():
            pltpu.make_async_copy(mine, target, sem).start()

        @pl.when(jnp.logical_not(mine_here))
        def _():
            pltpu.make_async_copy(theirs, target, sem).start()

    def wait():
        pltpu.make_async_copy(mine, target, sem).wait()

    return start, wait


def pair_columns(features):
    width = 2 * HEAD_DIM
    return [
        (start, min(width, features - start)) for start in range(0, features, width)
    ]


def head_masks(width):
    lanes = lax.broadcasted_iota(jnp.int32, (1, width), 1)
    if width == HEAD_DIM:
        return [None]
    return [lanes < HEAD_DIM, lanes >= HEAD_DIM]


def masked(values, mask):
    return values if mask is None else jnp.where(mask, values, jnp.zeros_like(values))


def attention_weights(layer, mine, theirs, target, sems):
    return [
        pick_copies(layer, mine.at[which], theirs.at[which], target.at[which], sems.at[which])
        for which in range(4)
    ]


def forward_kernel(
    layer, features, x_ref, bias_ref, gains_ref, at_mine, at_theirs, up_mine, up_theirs, down_mine,
    down_theirs, y_ref, middle_ref, one_ref, query_ref, key_ref, value_ref, mixed_ref, two_ref,
    act_ref, hidden_ref, at_w, up_w, down_w, weight_sems, parts, landing, passing, arrived,
    key_send, key_recv, value_send, value_recv, two_send, two_recv, sum_send, sum_recv,
):
    ring = Ring("x")
    me = ring.me
    fetches = attention_weights(layer, at_mine, at_theirs, at_w, weight_sems)
    fetches.append(pick_copies(layer, up_mine, up_theirs, up_w, weight_sems.at[4]))
    fetches.append(pick_copies(layer, down_mine, down_theirs, down_w, weight_sems.at[5]))
    for which in (1, 2, 0, 3, 4, 5):
        fetches[which][0]()
    greet(ring.to_right, ring.to_left)
    rows = x_ref.shape[0]
    inputs = x_ref[...].astype(F32)
    xhat, _ = norm_stats(inputs)
    one_ref[...] = (xhat * gains_ref[0:1, :]).astype(LOW)
    normed_one = one_ref[...]
    groups = head_groups(features)
    keys, values = [], []
    fetches[1][1]()
    fetches[2][1]()
    for which, (columns, _) in enumerate(groups):
        key_ref[me, :, columns] = dot_nn(normed_one, at_w[1, :, columns]).astype(LOW)
        keys.append(
            row_gather(ring, key_ref, (key_send.at[which], key_recv.at[which]), columns)
        )
        if which == 0:
            keys[0].start()
        value_ref[me, :, columns] = dot_nn(normed_one, at_w[2, :, columns]).astype(LOW)
        values.append(
            row_gather(ring, value_ref, (value_send.at[which], value_recv.at[which]), columns)
        )
        if which == 0:
            values[0].start()
    fetches[0][1]()
    query_ref[...] = dot_nn(normed_one, at_w[0]).astype(LOW)
    keys[0].relay()
    values[0].relay()
    keys[1].start()
    values[1].start()
    bias = bias_ref[...]

    def attend(begin, width):
        columns = pl.ds(begin, width)
        queries = query_ref[:, columns]
        key_block = key_ref[:, :, columns].reshape(4 * rows, width)
        value_block = value_ref[:, :, columns].reshape(4 * rows, width)
        mixed = None
        for mask in head_masks(width):
            scores = dot_nt(masked(queries, mask), key_block) * 0.125 + bias
            raised = jnp.exp(scores - jnp.max(scores, axis=-1, keepdims=True))
            probs = raised * (1.0 / jnp.sum(raised, axis=-1, keepdims=True))
            own = dot_nn(probs.astype(LOW), value_block)
            mixed = own if mixed is None else jnp.where(mask, own, mixed)
        mixed_ref[:, columns] = mixed.astype(LOW)

    for which, (_, pairs) in enumerate(groups):
        keys[which].wait_all()
        values[which].wait_all()
        for count, (begin, width) in enumerate(pairs):
            attend(begin, width)
            if which == 0 and count == 2:
                keys[1].relay()
                values[1].relay()
    fetches[3][1]()
    middle_ref[...] = x_ref[...].astype(F32) + dot_nn(mixed_ref[...], at_w[3])
    xhat, _ = norm_stats(middle_ref[...])
    two_ref[me] = (xhat * gains_ref[1:2, :]).astype(LOW)
    tokens = row_gather(ring, two_ref, (two_send, two_recv))
    tokens.start()
    fetches[4][1]()
    fetches[5][1]()
    sums = row_scatter(ring, parts, landing, passing, arrived, (sum_send, sum_recv))

    def feed(block):
        act_ref[block] = dot_nn(two_ref[block], up_w[...])
        hidden_ref[block] = gelu_tanh(act_ref[block]).astype(LOW)
        parts[block] = dot_nn(hidden_ref[block], down_w[...]).astype(LOW)

    feed(me)
    tokens.relay()
    tokens.wait_left()
    feed(ring.left)
    tokens.wait_right()
    feed(ring.right)
    sums.start_near()
    tokens.wait_opposite()
    feed(ring.opposite)
    sums.start_far()
    sums.relay()
    y_ref[...] = (middle_ref[...] + row_total(sums)).astype(LOW)
    for gather in keys + values:
        gather.finish()
    tokens.finish()
    sums.finish()


def scatter_scratch(rows, features):
    return [
        pltpu.VMEM((4, rows, features), LOW),
        pltpu.VMEM((2, rows // 2, features), LOW),
        pltpu.VMEM((2, rows // 2, features), LOW),
        pltpu.VMEM((2, rows, features), LOW),
    ]


def weight_scratch(features, hidden):
    return [
        pltpu.VMEM((4, features, features), LOW),
        pltpu.VMEM((features, hidden), LOW),
        pltpu.VMEM((hidden, features), LOW),
        pltpu.SemaphoreType.DMA((6,)),
    ]


def in_vmem():
    return pl.BlockSpec(memory_space=pltpu.VMEM)


def anywhere():
    return pl.BlockSpec(memory_space=pl.ANY)


def forward_layer(layer, x, bias, gains, attention, feed):
    rows, features = x.shape
    hidden = feed[0].shape[1]
    out_shape = (
        jax.ShapeDtypeStruct((rows, features), LOW),
        jax.ShapeDtypeStruct((rows, features), F32),
        jax.ShapeDtypeStruct((rows, features), LOW),
        jax.ShapeDtypeStruct((rows, features), LOW),
        jax.ShapeDtypeStruct((4, rows, features), LOW),
        jax.ShapeDtypeStruct((4, rows, features), LOW),
        jax.ShapeDtypeStruct((rows, features), LOW),
        jax.ShapeDtypeStruct((4, rows, features), LOW),
        jax.ShapeDtypeStruct((4, rows, hidden), F32),
        jax.ShapeDtypeStruct((4, rows, hidden), LOW),
    )
    return pl.pallas_call(
        functools.partial(forward_kernel, layer, features),
        out_shape=out_shape,
        in_specs=[in_vmem()] * 3 + [anywhere()] * 6,
        out_specs=[in_vmem()] * len(out_shape),
        scratch_shapes=weight_scratch(features, hidden)
        + scatter_scratch(rows, features)
        + [pltpu.SemaphoreType.DMA((2, 6))] * 4
        + [pltpu.SemaphoreType.DMA((6,))] * 4,
        compiler_params=pltpu.CompilerParams(
            collective_id=layer, has_side_effects=True, vmem_limit_bytes=56 * 2**20
        ),
        cost_estimate=pl.CostEstimate(
            flops=3 * 10**9, bytes_accessed=24 * 10**6, transcendentals=10**6
        ),
        name=f"layer_forward_{layer}",
    )(x, bias, gains, *attention, *feed)


def backward_kernel(layer, features, *refs):
    take = iter(refs)

    def some(count):
        return [next(take) for _ in range(count)]

    (x_ref, dy_ref, bias_ref, gains_ref, middle_ref, query_ref, key_ref, value_ref, act_ref,
     at_mine, at_theirs, up_mine, up_theirs, down_mine, down_theirs) = some(15)
    operands = some(10) if layer == 0 else None
    (dx_ref, gain_ref, out_ref, pre_ref, branch_ref, dquery_ref, dkey_ref, dvalue_ref) = some(8)
    results = some(3) if layer == 0 else None
    (at_w, up_w, down_w, weight_sems, parts, landing, passing, arrived, parts_b, landing_b,
     passing_b, arrived_b, parts_c, landing_c, passing_c, arrived_c, mixed_grad, kept_grad,
     out_send, out_recv, sum_send, sum_recv, key_send, key_recv, value_send, value_recv) = some(26)
    extra = GradientSum(1, features, operands, results, take) if layer == 0 else None
    ring = Ring("x")
    me = ring.me
    fetches = attention_weights(layer, at_mine, at_theirs, at_w, weight_sems)
    fetches.append(pick_copies(layer, up_mine, up_theirs, up_w, weight_sems.at[4]))
    fetches.append(pick_copies(layer, down_mine, down_theirs, down_w, weight_sems.at[5]))
    for which in (5, 4, 3, 0, 1, 2):
        fetches[which][0]()
    rows = x_ref.shape[0]
    out_ref[me] = dy_ref[...]
    if extra is None:
        greet(ring.to_right, ring.to_left)
    else:
        greet_all()
    grads = row_gather(ring, out_ref, (out_send, out_recv))
    grads.start()
    if extra is not None:
        extra.start_inputs((0, 1, 2, 4, 3, 5))
    sums = row_scatter(ring, parts, landing, passing, arrived, (sum_send, sum_recv))
    fetches[5][1]()
    fetches[4][1]()

    def feed(block):
        hidden_grad = dot_nt(out_ref[block], down_w[...])
        pre_ref[block] = (hidden_grad * gelu_slope(act_ref[block])).astype(LOW)
        parts[block] = dot_nt(pre_ref[block], up_w[...]).astype(LOW)

    def steps(*names):
        if extra is not None:
            for name in names:
                getattr(extra, name)()

    feed(me)
    grads.relay()
    steps("feed_products")
    grads.wait_left()
    feed(ring.left)
    grads.wait_right()
    feed(ring.right)
    sums.start_near()
    grads.wait_opposite()
    feed(ring.opposite)
    sums.start_far()
    steps("products_0", "feed_relay")
    sums.relay()
    steps("products_1")
    middle_part, gain_two = norm_back(middle_ref[...], gains_ref[1:2, :], row_total(sums))
    gain_ref[1:2, :] = gain_two
    middle_grad = dy_ref[...].astype(F32) + middle_part
    kept_grad[...] = middle_grad
    branch_ref[...] = middle_grad.astype(LOW)
    fetches[3][1]()
    mixed_grad[...] = dot_nt(branch_ref[...], at_w[3]).astype(LOW)
    bias = bias_ref[...]
    groups = head_groups(features)
    dkeys = [
        row_scatter(ring, parts_b, landing_b, passing_b, arrived_b,
                    (key_send.at[which], key_recv.at[which]), columns)
        for which, (columns, _) in enumerate(groups)
    ]
    dvalues = [
        row_scatter(ring, parts_c, landing_c, passing_c, arrived_c,
                    (value_send.at[which], value_recv.at[which]), columns)
        for which, (columns, _) in enumerate(groups)
    ]

    def send_pair(which):
        for scatter in (dkeys[which], dvalues[which]):
            scatter.start_far()
        for scatter in (dkeys[which], dvalues[which]):
            scatter.start_near()

    def relay_pair(which):
        for scatter in (dkeys[which], dvalues[which]):
            scatter.relay()

    for count, (begin, width) in enumerate(pair_columns(features)):
        columns = pl.ds(begin, width)
        queries = query_ref[:, columns]
        outer = mixed_grad[:, columns]
        key_block = key_ref[:, :, columns].reshape(4 * rows, width)
        value_block = value_ref[:, :, columns].reshape(4 * rows, width)
        dquery = dkey = dvalue = None
        for mask in head_masks(width):
            query_one, outer_one = masked(queries, mask), masked(outer, mask)
            scores = dot_nt(key_block, query_one) * 0.125 + bias
            raised = jnp.exp(scores - jnp.max(scores, axis=0, keepdims=True))
            probs = raised * (1.0 / jnp.sum(raised, axis=0, keepdims=True))
            probs_grad = dot_nt(value_block, outer_one)
            mean = jnp.sum(probs * probs_grad, axis=0, keepdims=True)
            score_grad = (probs * (probs_grad - mean)).astype(LOW)
            own_query = dot_tn(score_grad, key_block)
            own_key = dot_nn(score_grad, query_one)
            own_value = dot_nn(probs.astype(LOW), outer_one)
            if dquery is None:
                dquery, dkey, dvalue = own_query, own_key, own_value
            else:
                dquery = jnp.where(mask, own_query, dquery)
                dkey, dvalue = dkey + own_key, dvalue + own_value
        dquery_ref[:, columns] = (dquery * 0.125).astype(LOW)
        parts_b[:, :, columns] = (dkey * 0.125).astype(LOW).reshape(4, rows, width)
        parts_c[:, :, columns] = dvalue.astype(LOW).reshape(4, rows, width)
        if begin + width == groups[0][0].size:
            send_pair(0)
        if count == 2:
            steps("feed_middle", "x_relay_0")
        if count == 5:
            steps("feed_middle_relay")
    relay_pair(0)
    send_pair(1)
    for which in (0, 1, 2):
        fetches[which][1]()
    one_grad = dot_nt(dquery_ref[...], at_w[0])
    steps("feed_end")
    relay_pair(1)
    steps("x_relay_1", "feed_end_relay")
    for which, (columns, _) in enumerate(groups):
        dkey_ref[:, columns] = row_total(dkeys[which]).astype(LOW)
    one_grad = one_grad + dot_nt(dkey_ref[...], at_w[1])
    steps("keep_0")
    for which, (columns, _) in enumerate(groups):
        dvalue_ref[:, columns] = row_total(dvalues[which]).astype(LOW)
    one_grad = one_grad + dot_nt(dvalue_ref[...], at_w[2])
    inputs_part, gain_one = norm_back(x_ref[...].astype(F32), gains_ref[0:1, :], one_grad)
    gain_ref[0:1, :] = gain_one
    dx_ref[...] = (kept_grad[...] + inputs_part).astype(LOW)
    steps("feed_hand", "keep_1", "finish")
    grads.finish()
    sums.finish()
    for scatter in dkeys + dvalues:
        scatter.finish()


def greet_all(far=False):
    rings = [Ring(axis) for axis in ("x", "y", "z")]
    greet(
        *[ring.to_right for ring in rings], *[ring.to_left for ring in rings], sibling(),
        *[ring.to_opposite for ring in rings[1:] if far],
    )


def backward_layer(layer, x, dy, bias, gains, middle, query, key, value, act, attention, feed,
                   operands=()):
    rows, features = x.shape
    hidden = feed[0].shape[1]
    out_shape = (
        jax.ShapeDtypeStruct((rows, features), LOW),
        jax.ShapeDtypeStruct((2, features), F32),
        jax.ShapeDtypeStruct((4, rows, features), LOW),
        jax.ShapeDtypeStruct((4, rows, hidden), LOW),
        jax.ShapeDtypeStruct((rows, features), LOW),
        jax.ShapeDtypeStruct((rows, features), LOW),
        jax.ShapeDtypeStruct((rows, features), LOW),
        jax.ShapeDtypeStruct((rows, features), LOW),
    )
    sums = feed_outputs(features) + kept_output(features) if layer == 0 else ()
    return pl.pallas_call(
        functools.partial(backward_kernel, layer, features),
        out_shape=out_shape + sums,
        in_specs=[in_vmem()] * 9 + [anywhere()] * (6 + len(operands)),
        out_specs=[in_vmem()] * len(out_shape) + [anywhere()] * 2 * (len(sums) // 3)
        + [in_vmem()] * (len(sums) // 3),
        scratch_shapes=weight_scratch(features, hidden)
        + scatter_scratch(rows, features) * 3
        + [pltpu.VMEM((rows, features), LOW), pltpu.VMEM((rows, features), F32)]
        + [pltpu.SemaphoreType.DMA((6,))] * 4
        + [pltpu.SemaphoreType.DMA((2, 6))] * 4
        + (gradient_scratch(features, rows) if layer == 0 else []),
        compiler_params=pltpu.CompilerParams(
            collective_id=2 + layer, has_side_effects=True, vmem_limit_bytes=62 * 2**20
        ),
        cost_estimate=pl.CostEstimate(
            flops=4 * 10**9, bytes_accessed=24 * 10**6, transcendentals=10**6
        ),
        name=f"layer_backward_{layer}",
    )(x, dy, bias, gains, middle, query, key, value, act, *attention, *feed, *operands)


X_ROWS, Y_ROWS = 96, 96


def weights_kernel(
    shard_ref, gain_ref, mine_ref, theirs_ref, gain_mine, gain_theirs, local_sems, x_send, x_recv,
    yx_send, yx_recv, zx_send, zx_recv, y_send, y_recv, z_send, z_recv, gain_send, gain_recv,
    pair_send, pair_recv,
):
    x_ring, y_ring, z_ring = Ring("x"), Ring("y"), Ring("z")
    mine_y, mine_z, mine_x = y_ring.me, z_ring.me, x_ring.me
    share = shard_ref.shape[1]
    y_begin, z_begin = X_ROWS, X_ROWS + Y_ROWS
    z_rows = share - z_begin
    all_x, all_y, all_z = pl.ds(0, X_ROWS), pl.ds(y_begin, Y_ROWS), pl.ds(z_begin, z_rows)
    y_half = (pl.ds(y_begin, 48), pl.ds(y_begin + 48, Y_ROWS - 48))
    z_half = (pl.ds(z_begin, 48), pl.ds(z_begin + 48, z_rows - 48))
    pair = sibling()
    greet(
        x_ring.to_right, x_ring.to_left, y_ring.to_right, y_ring.to_left, z_ring.to_right,
        z_ring.to_left, pair,
    )
    locals_ = [
        pltpu.make_async_copy(
            shard_ref.at[mine_y, all_y], mine_ref.at[mine_y, mine_x, all_y], local_sems.at[0]
        ),
        pltpu.make_async_copy(
            shard_ref.at[mine_z, all_z], mine_ref.at[mine_z, mine_x, all_z], local_sems.at[1]
        ),
        pltpu.make_async_copy(
            shard_ref.at[:, all_x], mine_ref.at[:, mine_x, all_x], local_sems.at[2]
        ),
        pltpu.make_async_copy(gain_ref, gain_mine.at[mine_x], local_sems.at[3]),
    ]
    first_y = Gather(
        x_ring,
        lambda block, half: mine_ref.at[mine_y, block, y_half[half]],
        (yx_send, yx_recv),
        lambda half: shard_ref.at[mine_y, y_half[half]],
    )
    first_z = Gather(
        x_ring,
        lambda block, half: mine_ref.at[mine_z, block, z_half[half]],
        (zx_send, zx_recv),
        lambda half: shard_ref.at[mine_z, z_half[half]],
    )
    along_x = Gather(
        x_ring,
        lambda block, half: mine_ref.at[pl.ds(2 * half, 2), block, all_x],
        (x_send, x_recv),
        lambda half: shard_ref.at[pl.ds(2 * half, 2), all_x],
    )
    along_y = Gather(
        y_ring,
        lambda block, half: mine_ref.at[block, pl.ds(2 * half, 2), all_y],
        (y_send, y_recv),
    )
    along_z = Gather(
        z_ring,
        lambda block, half: mine_ref.at[block, pl.ds(2 * half, 2), all_z],
        (z_send, z_recv),
    )

    def gain_copy(which, block, src=None):
        part = gain_mine.at[block]
        target = x_ring.to_left if which == 1 else x_ring.to_right
        return remote(part if src is None else src, part, (gain_send, gain_recv), which, target)

    def hand(which, region):
        return remote(mine_ref.at[region], theirs_ref.at[region], (pair_send, pair_recv), which, pair)

    handed = []

    def hand_on(which, region):
        copy = hand(which, region)
        copy.start()
        handed.append(copy)

    first_y.start()
    first_z.start()
    for copy in locals_:
        copy.start()
    gain_copy(0, mine_x, gain_ref).start()
    gain_copy(1, mine_x, gain_ref).start()
    first_y.relay()
    first_z.relay()
    along_x.start()
    first_y.wait_all()
    locals_[0].wait()
    along_y.start()
    hand_on(0, (mine_y, slice(None), all_y))
    first_z.wait_all()
    locals_[1].wait()
    along_z.start()
    hand_on(1, (mine_z, slice(None), all_z))
    gain_copy(0, x_ring.left).wait_recv()
    gain_copy(2, x_ring.left).start()
    along_x.relay()
    along_y.relay()
    along_z.relay()
    along_x.wait_all()
    locals_[2].wait()
    hand_on(2, (slice(None), slice(None), all_x))
    along_y.wait_left()
    hand_on(3, (y_ring.left, slice(None), all_y))
    along_z.wait_left()
    hand_on(4, (z_ring.left, slice(None), all_z))
    along_y.wait_right()
    hand_on(5, (y_ring.right, slice(None), all_y))
    along_z.wait_right()
    hand_on(6, (z_ring.right, slice(None), all_z))
    gain_copy(1, x_ring.right).wait_recv()
    gain_copy(2, x_ring.opposite).wait_recv()
    locals_[3].wait()
    gains = remote(gain_mine, gain_theirs, (pair_send, pair_recv), 9, pair)
    gains.start()
    along_y.wait_opposite()
    hand_on(7, (y_ring.opposite, slice(None), all_y))
    along_z.wait_opposite()
    hand_on(8, (z_ring.opposite, slice(None), all_z))
    for copy in handed + [gains]:
        copy.wait()
    for which in range(3):
        gain_copy(which, mine_x).wait_send()
    for gather in (first_y, first_z, along_x, along_y, along_z):
        gather.finish()


def gather_weights(shard, gain):
    mats, share, features = shard.shape
    full = jax.ShapeDtypeStruct((mats, 4, share, features), LOW)
    gains = jax.ShapeDtypeStruct((4,) + gain.shape, LOW)
    return pl.pallas_call(
        weights_kernel,
        out_shape=(full, full, gains, gains),
        in_specs=[anywhere()] * 2,
        out_specs=[anywhere()] * 4,
        scratch_shapes=[pltpu.SemaphoreType.DMA((4,))]
        + [pltpu.SemaphoreType.DMA((6,))] * 10
        + [pltpu.SemaphoreType.DMA((3,))] * 2
        + [pltpu.SemaphoreType.DMA((10,))] * 2,
        compiler_params=pltpu.CompilerParams(collective_id=4, has_side_effects=True),
        cost_estimate=pl.CostEstimate(flops=0, bytes_accessed=60 * 10**6, transcendentals=0),
        name="gather_weights",
    )(shard, gain)


class SmallSum:
    def __init__(self, ring, slots, sems):
        self.ring, self.slots, self.sems = ring, slots, sems

    def copy(self, which, block):
        target = self.ring.to_left if which == 1 else self.ring.to_right
        part = self.slots.at[block]
        return remote(part, part, self.sems, which, target)

    def start(self):
        self.copy(0, self.ring.me).start()
        self.copy(1, self.ring.me).start()

    def relay(self):
        self.copy(0, self.ring.left).wait_recv()
        self.copy(2, self.ring.left).start()

    def result(self):
        self.copy(1, self.ring.right).wait_recv()
        self.copy(2, self.ring.opposite).wait_recv()
        return (self.slots[0] + self.slots[1]) + (self.slots[2] + self.slots[3])

    def finish(self):
        for which in range(3):
            self.copy(which, self.ring.me).wait_send()


class PlaneSum:
    def __init__(self, near, far, source, out, size, first, scratch, sems, keep, direct=False):
        if direct:
            self.arrived, self.mid, self.done = scratch
        else:
            self.landing, self.passing, self.arrived, self.mid, self.done = scratch
        self.direct = direct
        self.out, self.size, self.near, self.far, self.keep = out, size, near, far, keep
        self.halves = ((0, first), (first, size - first))

        def rows(block, half):
            begin, count = (0, size) if half is None else self.halves[half]
            return pl.ds(pl.multiple_of(block * size + begin, 16), count)

        def half_rows(half):
            return pl.ds(0, size) if half is None else pl.ds(*self.halves[half])

        self.half_rows = half_rows
        def part(block, half):
            return source.at[rows(block, half)]

        if direct:
            self.scatter = DirectScatter(near, part, lambda side: self.arrived.at[side], sems[0])
        else:
            self.scatter = Scatter(
                near,
                part,
                lambda half: self.landing.at[half_rows(half)],
                lambda half: self.passing.at[half_rows(half)],
                lambda side, half: self.arrived.at[side, half_rows(half)],
                sems[0],
            )
        kind = DirectGather if direct else Gather
        self.gather = kind(far, lambda block, half: self.mid.at[block, half_rows(half)], sems[1])
        self.spread = kind(
            near,
            lambda block, half: out.at[rows(block, half)],
            sems[2],
            lambda half: self.done.at[half_rows(half)],
        )

    def start(self):
        self.scatter.start_far()
        self.scatter.start_near()

    def relay(self):
        self.scatter.relay()

    def middle(self):
        self.scatter.wait()
        if self.direct:
            self.mid[self.far.me] = self.scatter.whole().astype(LOW)
        else:
            for half in range(2):
                self.mid[self.far.me, self.half_rows(half)] = self.scatter.total(half).astype(LOW)
        self.gather.start()

    def middle_relay(self):
        self.gather.relay()

    def own(self):
        place = pl.ds(pl.multiple_of(self.near.me * self.size, 16), self.size)
        return pltpu.make_async_copy(self.done, self.out.at[place], self.keep)

    def end(self):
        self.gather.wait_all()
        four = [self.mid[block].astype(F32) for block in range(4)]
        self.done[...] = ((four[0] + four[1]) + (four[2] + four[3])).astype(LOW)
        self.spread.start()
        self.own().start()

    def end_relay(self):
        self.spread.relay()

    def wait(self):
        self.spread.wait_all()
        self.own().wait()

    def finish(self):
        self.scatter.finish()
        self.gather.finish()
        self.spread.finish()


FEED_BLOCK, AT_BLOCK = 144, 80


def feed_outputs(features):
    return (jax.ShapeDtypeStruct((2, 4 * FEED_BLOCK, features), LOW),) * 2


def kept_output(features):
    return (jax.ShapeDtypeStruct((2, 4 * AT_BLOCK, features), LOW),)


def plane_scratch(size, features, direct=False):
    dma = pltpu.SemaphoreType.DMA

    def low(*shape):
        return pltpu.VMEM(shape + (features,), LOW)

    if direct:
        return [low(3, size), low(4, size), low(size)] + [dma((3,))] * 6
    return [low(size), low(size), low(2, size), low(4, size), low(size)] + [dma((6,))] * 6


def gradient_scratch(features, rows):
    share = features // 4
    dma = pltpu.SemaphoreType.DMA

    def low(*shape):
        return pltpu.VMEM(shape + (features,), LOW)

    return (
        [low(2, 2, 4, rows), low(2, 2, rows), low(2, 2, rows), low(2, features),
         low(2, 4 * FEED_BLOCK)]
        + ([low(share), low(share), low(2, share)] + [dma((6,))] * 2) * 2
        + plane_scratch(FEED_BLOCK, features) * 2
        + [dma((6,)), dma((6,)), dma((6,)), dma((2,)), dma((1,)), dma((1,))]
    )


def attention_scratch(features, direct):
    dma = pltpu.SemaphoreType.DMA
    return plane_scratch(AT_BLOCK, features, direct) * 2 + [dma((2,))] * 3


def take_planes(take, direct=False):
    planes = []
    for _ in range(2):
        scratch = [next(take) for _ in range(3 if direct else 5)]
        sems = [next(take) for _ in range(6)]
        planes.append((scratch, [tuple(sems[i : i + 2]) for i in (0, 2, 4)]))
    return planes


def hand_over(layer, src, dst, sems, which=0):
    section = lax.axis_index("section")
    copy = functools.partial(remote, src, dst, sems, which, sibling())

    def start():
        @pl.when(section != layer)
        def _():
            copy().start()

    def wait():
        @pl.when(section != layer)
        def _():
            copy().wait_send()

        @pl.when(section == layer)
        def _():
            copy().wait_recv()

    return start, wait


class AttentionSum:
    def __init__(self, layer, kept, results, take, direct):
        out, other = results
        planes = take_planes(take, direct)
        keep, send, recv = [next(take) for _ in range(3)]
        y_ring, z_ring = Ring("y"), Ring("z")
        orders = ((y_ring, z_ring), (z_ring, y_ring))
        self.planes = [
            PlaneSum(
                *orders[which], kept.at[which], out.at[which], AT_BLOCK, 48, *planes[which],
                keep.at[which], direct,
            )
            for which in range(2)
        ]
        self.given = [
            hand_over(layer, out.at[which], other.at[which], (send, recv), which)
            for which in range(2)
        ]

    def hand(self, which):
        self.planes[which].wait()
        self.given[which][0]()

    def finish(self):
        for which in range(2):
            self.planes[which].finish()
            self.given[which][1]()


class GradientSum:
    def __init__(self, layer, features, operands, results, take):
        self.layer, self.features = layer, features
        self.operands = operands
        self.feed_out, self.feed_other, self.at_kept = results
        (self.feed_in, self.at_left, self.at_right, self.at_sum, self.feed_sum) = [
            next(take) for _ in range(5)
        ]
        self.pair, self.section = sibling(), lax.axis_index("section")
        x_ring, y_ring, z_ring = Ring("x"), Ring("y"), Ring("z")
        share = features // 4
        self.share = share
        self.across = []
        for which in range(2):
            landing, passing, arrived, send, recv = [next(take) for _ in range(5)]
            halves = ((0, 144), (144, share - 144))

            def part(block, half, which=which, halves=halves):
                begin, count = halves[half]
                row = pl.multiple_of(block * share + begin, 16)
                return self.at_sum.at[which, pl.ds(row, count)]

            def cut(ref, halves=halves):
                return lambda half: ref.at[pl.ds(*halves[half])]

            self.across.append(
                Scatter(
                    x_ring, part, cut(landing), cut(passing),
                    lambda side, half, arrived=arrived, halves=halves: arrived.at[
                        side, pl.ds(*halves[half])
                    ],
                    (send, recv),
                )
            )
        self.halves = halves
        planes = take_planes(take)
        (self.local_sems, swap_send, swap_recv, keep, end_send, end_recv) = [
            next(take) for _ in range(6)
        ]
        self.swap, self.end_sems = (swap_send, swap_recv), (end_send, end_recv)
        orders = ((y_ring, z_ring), (z_ring, y_ring))
        self.feed = [
            PlaneSum(
                *orders[which], self.feed_sum.at[which], self.feed_out.at[which], FEED_BLOCK, 80,
                *planes[which], keep.at[which],
            )
            for which in range(2)
        ]

    def inputs(self, first):
        two, pre, hidden, out, one, mixed, dq, dk, dv, branch = self.operands
        zero = (two, pre, one, one, dq, dk)
        other = (hidden, out, one, mixed, dv, branch)
        own, sent = (zero, other) if first else (other, zero)
        targets = (
            self.feed_in.at[0], self.feed_in.at[1], self.at_left.at[0], self.at_left.at[1],
            self.at_right.at[0], self.at_right.at[1],
        )

        def keep(which):
            return pltpu.make_async_copy(
                own[which], targets[which].at[0], self.local_sems.at[which]
            )

        def send(which):
            return remote(sent[which], targets[which].at[1], self.swap, which, self.pair)

        return keep, send

    def start_inputs(self, order):
        for first in (True, False):

            @pl.when(self.section == (0 if first else 1))
            def _(first=first):
                keep, send = self.inputs(first)
                for which in order:
                    send(which).start()
                for which in order:
                    keep(which).start()

    def wait_inputs(self, whiches):
        keep, send = self.inputs(True)
        for which in whiches:
            keep(which).wait()
            send(which).wait_recv()

    def feed_products(self):
        self.wait_inputs((0, 1))
        features, whole = self.features, 4 * FEED_BLOCK
        right = self.feed_in[1].reshape(-1, features)
        for begin in range(0, features, 256):
            count = min(256, features - begin)
            left = self.feed_in[0, :, :, :, pl.ds(begin, count)].reshape(-1, count)
            product = dot_tn(left, right).astype(LOW)
            first = max(0, min(count, whole - begin))
            if first:
                self.feed_sum[0, pl.ds(begin, first)] = product[:first]
            if first < count:
                self.feed_sum[1, pl.ds(begin + first - whole, count - first)] = product[first:]
        spare = 2 * whole - features
        self.feed_sum[1, pl.ds(whole - spare, spare)] = jnp.zeros((spare, features), LOW)
        for plane in self.feed:
            plane.start()

    def products(self, which):
        self.wait_inputs((2 + which, 4 + which))
        features = self.features
        right = self.at_right[which].reshape(-1, features)
        for begin in range(0, features, 256):
            count = min(256, features - begin)
            left = self.at_left[which, :, :, pl.ds(begin, count)].reshape(-1, count)
            self.at_sum[which, pl.ds(begin, count)] = dot_tn(left, right).astype(LOW)
        self.across[which].start_far()

    def products_0(self):
        self.products(0)

    def products_1(self):
        self.products(1)

    def feed_relay(self):
        for plane in self.feed:
            plane.relay()

    def feed_middle(self):
        for plane in self.feed:
            plane.middle()

    def feed_middle_relay(self):
        for plane in self.feed:
            plane.middle_relay()

    def feed_end(self):
        for plane in self.feed:
            plane.end()

    def feed_end_relay(self):
        for plane in self.feed:
            plane.end_relay()

    def x_relay_0(self):
        self.across[0].relay()
        self.across[0].start_near()

    def x_relay_1(self):
        self.across[1].relay()
        self.across[1].start_near()

    def keep(self, which):
        across = self.across[which]
        across.wait()
        for half in range(2):
            self.at_kept[which, pl.ds(*self.halves[half])] = across.total(half).astype(LOW)
        spare = 4 * AT_BLOCK - self.share
        self.at_kept[which, pl.ds(self.share, spare)] = jnp.zeros((spare, self.features), LOW)

    def keep_0(self):
        self.keep(0)

    def keep_1(self):
        self.keep(1)

    def feed_hand(self):
        for plane in self.feed:
            plane.wait()
        hand_over(self.layer, self.feed_out, self.feed_other, self.end_sems)[0]()

    def finish(self):
        _, send = self.inputs(True)
        for which in range(6):
            send(which).wait_send()
        for each in self.across + self.feed:
            each.finish()
        hand_over(self.layer, self.feed_out, self.feed_other, self.end_sems)[1]()


def gradient_kernel(features, *refs):
    take = iter(refs)

    def some(count):
        return [next(take) for _ in range(count)]

    operands = some(10)
    y_a, y_b, dx_a, dx_b, gain_in, kept_one = some(6)
    feed_results, at_zero, at_one = some(2), some(2), some(2)
    act_out, grad_out, gain_out = some(3)
    (kept_zero,) = some(1)
    sums = GradientSum(0, features, operands, feed_results + [kept_zero], take)
    zero = AttentionSum(0, kept_zero, at_zero, take, True)
    one = AttentionSum(1, kept_one, at_one, take, False)
    (gain_pair, gain_x, gain_y, gain_z, gain_send, gain_recv, last_send, last_recv,
     keep_sems) = some(9)
    x_ring, y_ring, z_ring = Ring("x"), Ring("y"), Ring("z")
    pair, section = sibling(), lax.axis_index("section")
    greet_all(far=True)
    sums.start_inputs((2, 4, 3, 5, 0, 1))

    def last_copies(y, dx):
        return (
            remote(y, act_out.at[section], (last_send, last_recv), 0, pair),
            remote(dx, grad_out.at[section], (last_send, last_recv), 1, pair),
        )

    def keep_copies(y, dx):
        return (
            pltpu.make_async_copy(y, act_out.at[section], keep_sems.at[0]),
            pltpu.make_async_copy(dx, grad_out.at[section], keep_sems.at[1]),
        )

    @pl.when(section == 0)
    def _():
        for copy in last_copies(y_b, dx_b) + keep_copies(y_a, dx_a):
            copy.start()

    @pl.when(section == 1)
    def _():
        for copy in last_copies(y_a, dx_a) + keep_copies(y_b, dx_b):
            copy.start()

    gain_pair[0] = gain_in[...]
    swap_gain = remote(gain_pair.at[0], gain_pair.at[1], (gain_send, gain_recv), 9, pair)
    swap_gain.start()
    for plane in one.planes:
        plane.start()
    sums.products_0()
    sums.products_1()
    sums.feed_products()
    swap_gain.wait()
    gain_x[x_ring.me] = gain_pair[0] + gain_pair[1]
    small = [
        SmallSum(ring, slots, (gain_send.at[pl.ds(3 * i, 3)], gain_recv.at[pl.ds(3 * i, 3)]))
        for i, (ring, slots) in enumerate(((x_ring, gain_x), (y_ring, gain_y), (z_ring, gain_z)))
    ]
    small[0].start()
    sums.x_relay_0()
    for plane in one.planes:
        plane.relay()
    sums.feed_relay()
    small[0].relay()
    for plane in one.planes:
        plane.middle()
    sums.feed_middle()
    gain_y[y_ring.me] = small[0].result()
    small[1].start()
    for plane in one.planes:
        plane.middle_relay()
    sums.keep_0()
    sums.x_relay_1()
    zero.planes[0].start()
    sums.feed_middle_relay()
    small[1].relay()
    for plane in one.planes:
        plane.end()
    zero.planes[0].middle()
    sums.feed_end()
    gain_z[z_ring.me] = small[1].result()
    small[2].start()
    for plane in one.planes:
        plane.end_relay()
    zero.planes[0].end()
    sums.feed_end_relay()
    small[2].relay()
    sums.keep_1()
    zero.planes[1].start()
    one.hand(0)
    one.hand(1)
    gain_out[...] = small[2].result()
    zero.hand(0)
    zero.planes[1].middle()
    sums.feed_hand()
    zero.planes[1].end()
    zero.hand(1)
    zero.finish()
    one.finish()
    sums.finish()
    for each in small:
        each.finish()
    for copy in last_copies(y_a, dx_a) + keep_copies(y_a, dx_a):
        copy.wait()


def sum_gradients(features, rows, operands, last, gain, kept):
    dma = pltpu.SemaphoreType.DMA
    small = [pltpu.VMEM((4, 8, features), F32)] * 3
    return pl.pallas_call(
        functools.partial(gradient_kernel, features),
        out_shape=feed_outputs(features)
        + kept_output(features) * 4
        + (
            jax.ShapeDtypeStruct((2, rows, features), LOW),
            jax.ShapeDtypeStruct((2, rows, features), LOW),
            jax.ShapeDtypeStruct((8, features), F32),
        ),
        in_specs=[anywhere()] * 14 + [in_vmem()] * 2,
        out_specs=[anywhere()] * 8 + [in_vmem()],
        scratch_shapes=[pltpu.VMEM((2, 4 * AT_BLOCK, features), LOW)]
        + gradient_scratch(features, rows)
        + attention_scratch(features, True)
        + attention_scratch(features, False)
        + [pltpu.VMEM((2, 8, features), F32)]
        + small
        + [dma((10,)), dma((10,)), dma((2,)), dma((2,)), dma((2,))],
        compiler_params=pltpu.CompilerParams(
            collective_id=5, has_side_effects=True, vmem_limit_bytes=60 * 2**20
        ),
        cost_estimate=pl.CostEstimate(
            flops=6 * 10**9, bytes_accessed=60 * 10**6, transcendentals=0
        ),
        name="sum_gradients",
    )(*operands, *last, gain, kept)


def doc_numbers(lengths, positions):
    doc_ends = jnp.cumsum(lengths)
    return jnp.sum((positions[:, None] >= doc_ends[None, :]).astype(jnp.int32), axis=1)


def swapped(block):
    return lax.ppermute(block, "section", [(0, 1), (1, 0)])


def body(tokens, cotangent, doc_lengths, norm_gains, w_qkv, w_out, w_up, w_down):
    batches, rows, features = tokens.shape
    share = w_qkv.shape[1]
    seq_rows = rows * lax.axis_size("tensor")
    section = lax.axis_index("section")
    is_first = section == 0

    def choose(zero_side, one_side):
        return jnp.where(is_first, zero_side, one_side)

    own_tokens = lax.dynamic_index_in_dim(tokens, section, 0, keepdims=False)
    own_cotangent = lax.dynamic_index_in_dim(cotangent, section, 0, keepdims=False)
    lengths = lax.dynamic_index_in_dim(doc_lengths, section, 0, keepdims=False)
    own_places = lax.axis_index("tensor") * rows + jnp.arange(rows, dtype=jnp.int32)
    all_places = jnp.arange(seq_rows, dtype=jnp.int32)
    own_docs = doc_numbers(lengths, own_places)
    all_docs = doc_numbers(lengths, all_places)
    allowed = (all_places[None, :] <= own_places[:, None]) & (
        all_docs[None, :] == own_docs[:, None]
    )
    bias = jnp.where(allowed, 0.0, -1e30).astype(F32)
    bias_turned = bias.T

    feed = (w_up[0], swapped(w_up[0]), w_down[0], swapped(w_down[0]))
    shard = jnp.stack(
        [w_qkv[0, :, :features], w_qkv[0, :, features : 2 * features], w_qkv[0, :, 2 * features :],
         w_out[0]]
    )
    gain_shard = jnp.pad(norm_gains[0], ((0, 14), (0, 0)))
    at_mine, at_theirs, gain_mine, gain_theirs = gather_weights(shard, gain_shard)
    attention = (
        at_mine.reshape(4, features, features), at_theirs.reshape(4, features, features)
    )

    def whole_gains(block):
        return block[:, :2].transpose(1, 0, 2).reshape(2, features).astype(F32)

    gain_mine, gain_theirs = whole_gains(gain_mine), whole_gains(gain_theirs)
    gains = (choose(gain_mine, gain_theirs), choose(gain_theirs, gain_mine))

    inputs = own_tokens
    saved = []
    for layer in range(2):
        results = forward_layer(layer, inputs, bias, gains[layer], attention, feed)
        saved.append((inputs,) + tuple(results))
        inputs = results[0]

    grad = own_cotangent
    gain_grads, input_grads, operands = [None, None], [None, None], ()
    for layer in (1, 0):
        (x, _, middle, normed_one, query, key, value, mixed, normed_two, act, hidden) = saved[layer]
        results = backward_layer(
            layer, x, grad, bias_turned, gains[layer], middle, query, key, value, act,
            attention, feed, operands,
        )
        (grad, gain_grads[layer], out_all, pre_grad, branch, dquery, dkey, dvalue) = results[:8]
        input_grads[layer] = grad
        operands = (
            normed_two, pre_grad, hidden, out_all, normed_one, mixed, dquery, dkey, dvalue, branch,
        )
    feed_one, feed_one_given, kept_one = results[8:]
    gain_rows = jnp.concatenate(gain_grads + [jnp.zeros((4, features), F32)], axis=0)
    (feed_zero, feed_zero_given, at_zero, at_zero_given, at_one, at_one_given, activations,
     input_grads, gain_total) = sum_gradients(
        features, rows, operands, (saved[0][1], saved[1][1], *input_grads), gain_rows, kept_one
    )
    gain_own = lax.dynamic_slice(
        gain_total, (2 * section, lax.axis_index("tensor") * share), (2, share)
    )

    def whole(block):
        return block.reshape(-1, features)[:features].astype(F32)[None]

    first_half = choose(at_zero, at_one_given)[:, :share].astype(F32)
    other_half = choose(at_zero_given, at_one)[:, :share].astype(F32)
    grad_qkv = jnp.concatenate([first_half[0], first_half[1], other_half[0]], axis=1)
    return (
        activations[None],
        input_grads[None],
        gain_own[None],
        grad_qkv[None],
        other_half[1][None],
        whole(choose(feed_zero, feed_one_given)),
        whole(choose(feed_zero_given, feed_one)),
    )


def solution(mesh):
    placed = (
        P("dp", "tensor", None),
        P("dp", "tensor", None),
        P("dp", None),
        P("section", None, "tensor"),
        P("section", "tensor", None),
        P("section", "tensor", None),
        P("section", None, "tensor"),
        P("section", "tensor", None),
    )
    return jax.shard_map(
        body,
        mesh=mesh,
        in_specs=placed,
        out_specs=(
            P("section", "dp", "tensor", None),
            P("section", "dp", "tensor", None),
            P("section", None, "tensor"),
            P("section", "tensor", None),
            P("section", "tensor", None),
            P("section", None, "tensor"),
            P("section", "tensor", None),
        ),
        check_vma=False,
    )
```

```python
import functools
import jax
import jax.numpy as jnp
from jax import lax
from jax.experimental import pallas as pl
from jax.experimental.pallas import tpu as pltpu
from jax.sharding import PartitionSpec as P

HEAD_DIM = 64
LOW = jnp.bfloat16
F32 = jnp.float32
MESH = pl.DeviceIdType.MESH


def dot_nn(left, right):
    return lax.dot_general(left, right, (((1,), (0,)), ((), ())), preferred_element_type=F32)


def dot_nt(left, right):
    return lax.dot_general(left, right, (((1,), (1,)), ((), ())), preferred_element_type=F32)


def dot_tn(left, right):
    return lax.dot_general(left, right, (((0,), (0,)), ((), ())), preferred_element_type=F32)


class Ring:
    def __init__(self, axis):
        whole = lax.axis_index("dp")
        rest = None
        if axis == "x":
            self.me = lax.axis_index("tensor")
        elif axis == "y":
            self.me, rest = lax.rem(whole, 4), lax.div(whole, 4) * 4
        else:
            self.me, rest = lax.div(whole, 4), lax.rem(whole, 4)
        self.right = lax.rem(self.me + 1, 4)
        self.left = lax.rem(self.me + 3, 4)
        self.opposite = lax.rem(self.me + 2, 4)

        def device(place):
            if axis == "x":
                return {"tensor": place}
            if axis == "y":
                return {"dp": rest + place}
            return {"dp": place * 4 + rest}

        self.to_right, self.to_left = device(self.right), device(self.left)
        self.to_opposite = device(self.opposite)


def sibling():
    return {"section": 1 - lax.axis_index("section")}


def greet(*targets):
    barrier = pltpu.get_barrier_semaphore()
    for target in targets:
        pl.semaphore_signal(barrier, inc=1, device_id=target, device_id_type=MESH)
    pl.semaphore_wait(barrier, len(targets))


def remote(src, dst, sems, which, target):
    return pltpu.make_async_remote_copy(
        src_ref=src,
        dst_ref=dst,
        send_sem=sems[0].at[which],
        recv_sem=sems[1].at[which],
        device_id=target,
        device_id_type=MESH,
    )


class Gather:
    def __init__(self, ring, slot, sems, own=None):
        self.ring, self.slot, self.sems = ring, slot, sems
        self.own = own if own is not None else lambda half: slot(ring.me, half)

    def copy(self, which, arriving=False):
        ring = self.ring
        half = (0, 1, 1, 0, 0, 1)[which]
        goes_right = which in (0, 2, 4)
        target = ring.to_right if goes_right else ring.to_left
        if which < 4:
            source_block = ring.left if goes_right else ring.right
            if not arriving:
                return remote(self.own(half), self.slot(ring.me, half), self.sems, which, target)
        else:
            source_block = ring.opposite
            if not arriving:
                handed = self.slot(ring.left if goes_right else ring.right, half)
                return remote(handed, handed, self.sems, which, target)
        part = self.slot(source_block, half)
        return remote(part, part, self.sems, which, target)

    def start(self):
        for which in range(4):
            self.copy(which).start()

    def relay(self):
        for which in (0, 1):
            self.copy(which, arriving=True).wait_recv()
            self.copy(which + 4).start()

    def wait_left(self):
        self.copy(2, arriving=True).wait_recv()

    def wait_right(self):
        self.copy(3, arriving=True).wait_recv()

    def wait_opposite(self):
        self.copy(4, arriving=True).wait_recv()
        self.copy(5, arriving=True).wait_recv()

    def wait_all(self):
        self.wait_left()
        self.wait_right()
        self.wait_opposite()

    def finish(self):
        for which in range(6):
            self.copy(which).wait_send()


class Scatter:
    def __init__(self, ring, part, landing, passing, arrived, sems):
        self.ring, self.part, self.landing, self.passing = ring, part, landing, passing
        self.arrived, self.sems = arrived, sems

    def copy(self, which):
        ring = self.ring
        half = (0, 1, 1, 0, 0, 1)[which]
        goes_right = which in (0, 2, 4)
        if which < 2:
            src, dst = self.part(ring.opposite, half), self.landing(half)
        else:
            dst = self.arrived(0 if goes_right else 1, half)
            if which < 4:
                src = self.part(ring.right if goes_right else ring.left, half)
            else:
                src = self.passing(half)
        return remote(src, dst, self.sems, which, ring.to_right if goes_right else ring.to_left)

    def start_near(self):
        self.copy(2).start()
        self.copy(3).start()

    def start_far(self):
        self.copy(0).start()
        self.copy(1).start()

    def relay(self):
        for half, block in ((0, self.ring.right), (1, self.ring.left)):
            self.copy(half).wait_recv()
            added = self.part(block, half)[...].astype(F32) + self.landing(half)[...].astype(F32)
            self.passing(half)[...] = added.astype(LOW)
            self.copy(half + 4).start()

    def wait(self):
        for which in (2, 3, 4, 5):
            self.copy(which).wait_recv()

    def total(self, half):
        return (
            self.part(self.ring.me, half)[...].astype(F32)
            + self.arrived(0, half)[...].astype(F32)
            + self.arrived(1, half)[...].astype(F32)
        )

    def finish(self):
        for which in range(6):
            self.copy(which).wait_send()


class DirectGather:
    def __init__(self, ring, slot, sems, own=None):
        self.ring, self.slot, self.sems = ring, slot, sems
        self.own = own if own is not None else lambda half: slot(ring.me, half)

    def copy(self, which):
        target = (self.ring.to_right, self.ring.to_left, self.ring.to_opposite)[which]
        return remote(self.own(None), self.slot(self.ring.me, None), self.sems, which, target)

    def start(self):
        for which in (2, 0, 1):
            self.copy(which).start()

    def relay(self):
        pass

    def wait_all(self):
        for which, block in enumerate((self.ring.left, self.ring.right, self.ring.opposite)):
            part = self.slot(block, None)
            remote(part, part, self.sems, which, self.ring.to_right).wait_recv()

    def finish(self):
        for which in range(3):
            self.copy(which).wait_send()


class DirectScatter:
    def __init__(self, ring, part, arrived, sems):
        self.ring, self.part, self.arrived, self.sems = ring, part, arrived, sems

    def copy(self, which):
        ring = self.ring
        block = (ring.right, ring.left, ring.opposite)[which]
        target = (ring.to_right, ring.to_left, ring.to_opposite)[which]
        return remote(self.part(block, None), self.arrived(which), self.sems, which, target)

    def start_far(self):
        self.copy(2).start()

    def start_near(self):
        self.copy(0).start()
        self.copy(1).start()

    def relay(self):
        pass

    def wait(self):
        for which in range(3):
            self.copy(which).wait_recv()

    def whole(self):
        near = self.arrived(0)[...].astype(F32) + self.arrived(1)[...].astype(F32)
        own = self.part(self.ring.me, None)[...].astype(F32)
        return (own + near) + self.arrived(2)[...].astype(F32)

    def finish(self):
        for which in range(3):
            self.copy(which).wait_send()


def row_gather(ring, full, sems, columns=slice(None)):
    half = full.shape[1] // 2
    return Gather(
        ring, lambda block, which: full.at[block, pl.ds(which * half, half), columns], sems
    )


def row_scatter(ring, parts, landing, passing, arrived, sems, columns=slice(None)):
    half = parts.shape[1] // 2

    def rows(which):
        return pl.ds(which * half, half)

    return Scatter(
        ring,
        lambda block, which: parts.at[block, rows(which), columns],
        lambda which: landing.at[which, :, columns],
        lambda which: passing.at[which, :, columns],
        lambda side, which: arrived.at[side, rows(which), columns],
        sems,
    )


def row_total(scatter):
    scatter.wait()
    return jnp.concatenate([scatter.total(0), scatter.total(1)], axis=0)


def head_groups(features):
    pairs = pair_columns(features)
    middle = (len(pairs) + 1) // 2
    begin = pairs[middle][0]
    return (
        (pl.ds(0, begin), pairs[:middle]),
        (pl.ds(begin, features - begin), pairs[middle:]),
    )


def norm_stats(values):
    average = jnp.mean(values, axis=-1, keepdims=True)
    centered = values - average
    variance = jnp.mean(centered * centered, axis=-1, keepdims=True)
    scale = lax.rsqrt(variance + 1e-05)
    return centered * scale, scale


def norm_back(values, gain, grad):
    xhat, scale = norm_stats(values)
    scaled = grad * gain
    part = scale * (
        scaled
        - jnp.mean(scaled, axis=-1, keepdims=True)
        - xhat * jnp.mean(scaled * xhat, axis=-1, keepdims=True)
    )
    return part, jnp.sum(grad * xhat, axis=0, keepdims=True)


def gelu_tanh(values):
    inner = 0.7978845608028654 * (values + 0.044715 * values * values * values)
    return 0.5 * values * (1.0 + jnp.tanh(inner))


def gelu_slope(values):
    square = values * values
    bent = jnp.tanh(0.7978845608028654 * values * (1.0 + 0.044715 * square))
    slope = 0.7978845608028654 * (1.0 + 3.0 * 0.044715 * square)
    return 0.5 * (1.0 + bent) + 0.5 * values * (1.0 - bent * bent) * slope


def pick_copies(layer, mine, theirs, target, sem):
    def start():
        mine_here = lax.axis_index("section") == layer

        @pl.when(mine_here)
        def _():
            pltpu.make_async_copy(mine, target, sem).start()

        @pl.when(jnp.logical_not(mine_here))
        def _():
            pltpu.make_async_copy(theirs, target, sem).start()

    def wait():
        pltpu.make_async_copy(mine, target, sem).wait()

    return start, wait


def pair_columns(features):
    width = 2 * HEAD_DIM
    return [
        (start, min(width, features - start)) for start in range(0, features, width)
    ]


def head_masks(width):
    lanes = lax.broadcasted_iota(jnp.int32, (1, width), 1)
    if width == HEAD_DIM:
        return [None]
    return [lanes < HEAD_DIM, lanes >= HEAD_DIM]


def masked(values, mask):
    return values if mask is None else jnp.where(mask, values, jnp.zeros_like(values))


def attention_weights(layer, mine, theirs, target, sems):
    return [
        pick_copies(layer, mine.at[which], theirs.at[which], target.at[which], sems.at[which])
        for which in range(4)
    ]


def forward_kernel(
    layer, features, x_ref, bias_ref, gains_ref, at_mine, at_theirs, up_mine, up_theirs, down_mine,
    down_theirs, y_ref, middle_ref, one_ref, query_ref, key_ref, value_ref, mixed_ref, two_ref,
    act_ref, hidden_ref, at_w, up_w, down_w, weight_sems, parts, landing, passing, arrived,
    key_send, key_recv, value_send, value_recv, two_send, two_recv, sum_send, sum_recv,
):
    ring = Ring("x")
    me = ring.me
    fetches = attention_weights(layer, at_mine, at_theirs, at_w, weight_sems)
    fetches.append(pick_copies(layer, up_mine, up_theirs, up_w, weight_sems.at[4]))
    fetches.append(pick_copies(layer, down_mine, down_theirs, down_w, weight_sems.at[5]))
    for which in (1, 2, 0, 3, 4, 5):
        fetches[which][0]()
    greet(ring.to_right, ring.to_left)
    rows = x_ref.shape[0]
    inputs = x_ref[...].astype(F32)
    xhat, _ = norm_stats(inputs)
    one_ref[...] = (xhat * gains_ref[0:1, :]).astype(LOW)
    normed_one = one_ref[...]
    groups = head_groups(features)
    keys, values = [], []
    fetches[1][1]()
    fetches[2][1]()
    for which, (columns, _) in enumerate(groups):
        key_ref[me, :, columns] = dot_nn(normed_one, at_w[1, :, columns]).astype(LOW)
        keys.append(
            row_gather(ring, key_ref, (key_send.at[which], key_recv.at[which]), columns)
        )
        if which == 0:
            keys[0].start()
        value_ref[me, :, columns] = dot_nn(normed_one, at_w[2, :, columns]).astype(LOW)
        values.append(
            row_gather(ring, value_ref, (value_send.at[which], value_recv.at[which]), columns)
        )
        if which == 0:
            values[0].start()
    fetches[0][1]()
    query_ref[...] = dot_nn(normed_one, at_w[0]).astype(LOW)
    keys[0].relay()
    values[0].relay()
    keys[1].start()
    values[1].start()
    bias = bias_ref[...]

    def attend(begin, width):
        columns = pl.ds(begin, width)
        queries = query_ref[:, columns]
        key_block = key_ref[:, :, columns].reshape(4 * rows, width)
        value_block = value_ref[:, :, columns].reshape(4 * rows, width)
        mixed = None
        for mask in head_masks(width):
            scores = dot_nt(masked(queries, mask), key_block) * 0.125 + bias
            raised = jnp.exp(scores - jnp.max(scores, axis=-1, keepdims=True))
            probs = raised * (1.0 / jnp.sum(raised, axis=-1, keepdims=True))
            own = dot_nn(probs.astype(LOW), value_block)
            mixed = own if mixed is None else jnp.where(mask, own, mixed)
        mixed_ref[:, columns] = mixed.astype(LOW)

    for which, (_, pairs) in enumerate(groups):
        keys[which].wait_all()
        values[which].wait_all()
        for count, (begin, width) in enumerate(pairs):
            attend(begin, width)
            if which == 0 and count == 2:
                keys[1].relay()
                values[1].relay()
    fetches[3][1]()
    middle_ref[...] = x_ref[...].astype(F32) + dot_nn(mixed_ref[...], at_w[3])
    xhat, _ = norm_stats(middle_ref[...])
    two_ref[me] = (xhat * gains_ref[1:2, :]).astype(LOW)
    tokens = row_gather(ring, two_ref, (two_send, two_recv))
    tokens.start()
    fetches[4][1]()
    fetches[5][1]()
    sums = row_scatter(ring, parts, landing, passing, arrived, (sum_send, sum_recv))

    def feed(block):
        act_ref[block] = dot_nn(two_ref[block], up_w[...])
        hidden_ref[block] = gelu_tanh(act_ref[block]).astype(LOW)
        parts[block] = dot_nn(hidden_ref[block], down_w[...]).astype(LOW)

    feed(me)
    tokens.relay()
    tokens.wait_left()
    feed(ring.left)
    tokens.wait_right()
    feed(ring.right)
    sums.start_near()
    tokens.wait_opposite()
    feed(ring.opposite)
    sums.start_far()
    sums.relay()
    y_ref[...] = (middle_ref[...] + row_total(sums)).astype(LOW)
    for gather in keys + values:
        gather.finish()
    tokens.finish()
    sums.finish()


def scatter_scratch(rows, features):
    return [
        pltpu.VMEM((4, rows, features), LOW),
        pltpu.VMEM((2, rows // 2, features), LOW),
        pltpu.VMEM((2, rows // 2, features), LOW),
        pltpu.VMEM((2, rows, features), LOW),
    ]


def weight_scratch(features, hidden, matrices=4):
    shape = (features, features) if matrices == 1 else (matrices, features, features)
    return [
        pltpu.VMEM(shape, LOW),
        pltpu.VMEM((features, hidden), LOW),
        pltpu.VMEM((hidden, features), LOW),
        pltpu.SemaphoreType.DMA((6,)),
    ]


def in_vmem():
    return pl.BlockSpec(memory_space=pltpu.VMEM)


def anywhere():
    return pl.BlockSpec(memory_space=pl.ANY)


def forward_layer(layer, x, bias, gains, attention, feed):
    rows, features = x.shape
    hidden = feed[0].shape[1]
    out_shape = (
        jax.ShapeDtypeStruct((rows, features), LOW),
        jax.ShapeDtypeStruct((rows, features), F32),
        jax.ShapeDtypeStruct((rows, features), LOW),
        jax.ShapeDtypeStruct((rows, features), LOW),
        jax.ShapeDtypeStruct((4, rows, features), LOW),
        jax.ShapeDtypeStruct((4, rows, features), LOW),
        jax.ShapeDtypeStruct((rows, features), LOW),
        jax.ShapeDtypeStruct((4, rows, features), LOW),
        jax.ShapeDtypeStruct((4, rows, hidden), F32),
        jax.ShapeDtypeStruct((4, rows, hidden), LOW),
    )
    return pl.pallas_call(
        functools.partial(forward_kernel, layer, features),
        out_shape=out_shape,
        in_specs=[in_vmem()] * 3 + [anywhere()] * 6,
        out_specs=[in_vmem()] * len(out_shape),
        scratch_shapes=weight_scratch(features, hidden)
        + scatter_scratch(rows, features)
        + [pltpu.SemaphoreType.DMA((2, 6))] * 4
        + [pltpu.SemaphoreType.DMA((6,))] * 4,
        compiler_params=pltpu.CompilerParams(
            collective_id=layer, has_side_effects=True, vmem_limit_bytes=56 * 2**20
        ),
        cost_estimate=pl.CostEstimate(
            flops=3 * 10**9, bytes_accessed=24 * 10**6, transcendentals=10**6
        ),
        name=f"layer_forward_{layer}",
    )(x, bias, gains, *attention, *feed)


def backward_kernel(layer, features, *refs):
    take = iter(refs)

    def some(count):
        return [next(take) for _ in range(count)]

    (x_ref, dy_ref, bias_ref, gains_ref, middle_ref, query_ref, key_ref, value_ref, act_ref,
     at_mine, at_theirs, up_mine, up_theirs, down_mine, down_theirs) = some(15)
    operands = some(12) if layer == 0 else None
    (dx_ref, gain_ref, out_ref, pre_ref, branch_ref, dquery_ref, dkey_ref, dvalue_ref) = some(8)
    results = some(4) if layer == 0 else None
    (at_w, up_w, down_w, weight_sems, parts, landing, passing, arrived, parts_b, landing_b,
     passing_b, arrived_b, parts_c, landing_c, passing_c, arrived_c, mixed_grad, kept_grad,
     out_send, out_recv, sum_send, sum_recv, key_send, key_recv, value_send, value_recv) = some(26)
    extra = layer == 0
    if extra:
        (two, pre, hidden, out_all, one, mixed, dq, dk, dv, branch, two_own, hidden_own) = operands
        feed_out, feed_given, feed_own_out, kept = results
        feed_one = FeedSum(features, (two, pre, hidden, out_all), feed_out, take)
        feed_own = FeedSum(
            features, (two_own, pre_ref, hidden_own, out_ref), feed_own_out, take
        )
        across = AcrossSum(features, (one, mixed, dq, dk, dv, branch), kept, take)
        given = hand_over(1, feed_out, feed_given, feed_one.end_sems)
    ring = Ring("x")
    me = ring.me
    fetches = [
        pick_copies(layer, at_mine.at[which], at_theirs.at[which], target, weight_sems.at[which])
        for which, target in enumerate((up_w, down_w, at_w, at_w))
    ]
    fetches.append(pick_copies(layer, up_mine, up_theirs, up_w, weight_sems.at[4]))
    fetches.append(pick_copies(layer, down_mine, down_theirs, down_w, weight_sems.at[5]))
    for which in (5, 4, 3):
        fetches[which][0]()
    rows = x_ref.shape[0]
    out_ref[me] = dy_ref[...]
    if not extra:
        greet(ring.to_right, ring.to_left)
    else:
        greet_all()
    grads = row_gather(ring, out_ref, (out_send, out_recv))
    grads.start()
    if extra:
        feed_one.inputs.start()
        across.inputs.start()
    sums = row_scatter(ring, parts, landing, passing, arrived, (sum_send, sum_recv))
    fetches[5][1]()
    fetches[4][1]()

    def feed(block):
        hidden_grad = dot_nt(out_ref[block], down_w[...])
        pre_ref[block] = (hidden_grad * gelu_slope(act_ref[block])).astype(LOW)
        parts[block] = dot_nt(pre_ref[block], up_w[...]).astype(LOW)

    feed(me)
    grads.relay()
    if extra:
        feed_one.products()
    grads.wait_left()
    feed(ring.left)
    grads.wait_right()
    feed(ring.right)
    sums.start_near()
    grads.wait_opposite()
    feed(ring.opposite)
    sums.start_far()
    for which in (0, 1):
        fetches[which][0]()
    if extra:
        feed_own.inputs.start()
        across.products(0)
        feed_one.run("relay")
    sums.relay()
    if extra:
        across.products(1)
    middle_part, gain_two = norm_back(middle_ref[...], gains_ref[1:2, :], row_total(sums))
    gain_ref[1:2, :] = gain_two
    middle_grad = dy_ref[...].astype(F32) + middle_part
    kept_grad[...] = middle_grad
    branch_ref[...] = middle_grad.astype(LOW)
    fetches[3][1]()
    mixed_grad[...] = dot_nt(branch_ref[...], at_w[...]).astype(LOW)
    fetches[2][0]()
    bias = bias_ref[...]
    groups = head_groups(features)
    dkeys = [
        row_scatter(ring, parts_b, landing_b, passing_b, arrived_b,
                    (key_send.at[which], key_recv.at[which]), columns)
        for which, (columns, _) in enumerate(groups)
    ]
    dvalues = [
        row_scatter(ring, parts_c, landing_c, passing_c, arrived_c,
                    (value_send.at[which], value_recv.at[which]), columns)
        for which, (columns, _) in enumerate(groups)
    ]

    def send_pair(which):
        for scatter in (dkeys[which], dvalues[which]):
            scatter.start_far()
        for scatter in (dkeys[which], dvalues[which]):
            scatter.start_near()

    def relay_pair(which):
        for scatter in (dkeys[which], dvalues[which]):
            scatter.relay()

    for count, (begin, width) in enumerate(pair_columns(features)):
        columns = pl.ds(begin, width)
        queries = query_ref[:, columns]
        outer = mixed_grad[:, columns]
        key_block = key_ref[:, :, columns].reshape(4 * rows, width)
        value_block = value_ref[:, :, columns].reshape(4 * rows, width)
        dquery = dkey = dvalue = None
        for mask in head_masks(width):
            query_one, outer_one = masked(queries, mask), masked(outer, mask)
            scores = dot_nt(key_block, query_one) * 0.125 + bias
            raised = jnp.exp(scores - jnp.max(scores, axis=0, keepdims=True))
            probs = raised * (1.0 / jnp.sum(raised, axis=0, keepdims=True))
            probs_grad = dot_nt(value_block, outer_one)
            mean = jnp.sum(probs * probs_grad, axis=0, keepdims=True)
            score_grad = (probs * (probs_grad - mean)).astype(LOW)
            own_query = dot_tn(score_grad, key_block)
            own_key = dot_nn(score_grad, query_one)
            own_value = dot_nn(probs.astype(LOW), outer_one)
            if dquery is None:
                dquery, dkey, dvalue = own_query, own_key, own_value
            else:
                dquery = jnp.where(mask, own_query, dquery)
                dkey, dvalue = dkey + own_key, dvalue + own_value
        dquery_ref[:, columns] = (dquery * 0.125).astype(LOW)
        parts_b[:, :, columns] = (dkey * 0.125).astype(LOW).reshape(4, rows, width)
        parts_c[:, :, columns] = dvalue.astype(LOW).reshape(4, rows, width)
        if begin + width == groups[0][0].size:
            send_pair(0)
        if extra and count == 1:
            feed_one.run("middle")
            across.relay(0)
        if extra and count == 4:
            feed_own.products()
            feed_one.run("middle_relay")
        if extra and count == 7:
            feed_own.run("relay")
    relay_pair(0)
    send_pair(1)
    for which in (0, 1, 2):
        fetches[which][1]()
    one_grad = dot_nt(dquery_ref[...], up_w[...])
    if extra:
        feed_one.run("end")
    relay_pair(1)
    if extra:
        across.relay(1)
        feed_own.run("middle")
        feed_one.run("end_relay")
    for which, (columns, _) in enumerate(groups):
        dkey_ref[:, columns] = row_total(dkeys[which]).astype(LOW)
    one_grad = one_grad + dot_nt(dkey_ref[...], down_w[...])
    if extra:
        across.keep(0)
        feed_own.run("middle_relay")
    for which, (columns, _) in enumerate(groups):
        dvalue_ref[:, columns] = row_total(dvalues[which]).astype(LOW)
    one_grad = one_grad + dot_nt(dvalue_ref[...], at_w[...])
    inputs_part, gain_one = norm_back(x_ref[...].astype(F32), gains_ref[0:1, :], one_grad)
    gain_ref[0:1, :] = gain_one
    dx_ref[...] = (kept_grad[...] + inputs_part).astype(LOW)
    if extra:
        feed_one.run("wait")
        given[0]()
        feed_own.run("end")
        across.keep(1)
        feed_own.run("end_relay")
        feed_one.finish()
        across.finish()
        given[1]()
        feed_own.run("wait")
        feed_own.finish()
    grads.finish()
    sums.finish()
    for scatter in dkeys + dvalues:
        scatter.finish()


def greet_all(far=False):
    rings = [Ring(axis) for axis in ("x", "y", "z")]
    greet(
        *[ring.to_right for ring in rings], *[ring.to_left for ring in rings], sibling(),
        *[ring.to_opposite for ring in rings[1:] if far],
    )


def backward_layer(layer, x, dy, bias, gains, middle, query, key, value, act, attention, feed,
                   operands=()):
    rows, features = x.shape
    hidden = feed[0].shape[1]
    out_shape = (
        jax.ShapeDtypeStruct((rows, features), LOW),
        jax.ShapeDtypeStruct((2, features), F32),
        jax.ShapeDtypeStruct((4, rows, features), LOW),
        jax.ShapeDtypeStruct((4, rows, hidden), LOW),
        jax.ShapeDtypeStruct((rows, features), LOW),
        jax.ShapeDtypeStruct((rows, features), LOW),
        jax.ShapeDtypeStruct((rows, features), LOW),
        jax.ShapeDtypeStruct((rows, features), LOW),
    )
    sums = feed_output(features) * 3 + kept_output(features) if layer == 0 else ()
    return pl.pallas_call(
        functools.partial(backward_kernel, layer, features),
        out_shape=out_shape + sums,
        in_specs=[in_vmem()] * 9 + [anywhere()] * (6 + len(operands)),
        out_specs=[in_vmem()] * len(out_shape) + [anywhere()] * 3 * (len(sums) // 4)
        + [in_vmem()] * (len(sums) // 4),
        scratch_shapes=weight_scratch(features, hidden, 1)
        + scatter_scratch(rows, features) * 3
        + [pltpu.VMEM((rows, features), LOW), pltpu.VMEM((rows, features), F32)]
        + [pltpu.SemaphoreType.DMA((6,))] * 4
        + [pltpu.SemaphoreType.DMA((2, 6))] * 4
        + (
            feed_scratch(features, rows) * 2 + across_scratch(features, rows)
            if layer == 0
            else []
        ),
        compiler_params=pltpu.CompilerParams(
            collective_id=2 + layer, has_side_effects=True, vmem_limit_bytes=62 * 2**20
        ),
        cost_estimate=pl.CostEstimate(
            flops=4 * 10**9, bytes_accessed=24 * 10**6, transcendentals=10**6
        ),
        name=f"layer_backward_{layer}",
    )(x, dy, bias, gains, middle, query, key, value, act, *attention, *feed, *operands)


X_ROWS, Y_ROWS = 96, 96


def weights_kernel(
    shard_ref, gain_ref, mine_ref, theirs_ref, gain_mine, gain_theirs, local_sems, x_send, x_recv,
    yx_send, yx_recv, zx_send, zx_recv, y_send, y_recv, z_send, z_recv, gain_send, gain_recv,
    pair_send, pair_recv,
):
    x_ring, y_ring, z_ring = Ring("x"), Ring("y"), Ring("z")
    mine_y, mine_z, mine_x = y_ring.me, z_ring.me, x_ring.me
    share = shard_ref.shape[1]
    y_begin, z_begin = X_ROWS, X_ROWS + Y_ROWS
    z_rows = share - z_begin
    all_x, all_y, all_z = pl.ds(0, X_ROWS), pl.ds(y_begin, Y_ROWS), pl.ds(z_begin, z_rows)
    y_half = (pl.ds(y_begin, 48), pl.ds(y_begin + 48, Y_ROWS - 48))
    z_half = (pl.ds(z_begin, 48), pl.ds(z_begin + 48, z_rows - 48))
    pair = sibling()
    greet(
        x_ring.to_right, x_ring.to_left, y_ring.to_right, y_ring.to_left, z_ring.to_right,
        z_ring.to_left, pair,
    )
    locals_ = [
        pltpu.make_async_copy(
            shard_ref.at[mine_y, all_y], mine_ref.at[mine_y, mine_x, all_y], local_sems.at[0]
        ),
        pltpu.make_async_copy(
            shard_ref.at[mine_z, all_z], mine_ref.at[mine_z, mine_x, all_z], local_sems.at[1]
        ),
        pltpu.make_async_copy(
            shard_ref.at[:, all_x], mine_ref.at[:, mine_x, all_x], local_sems.at[2]
        ),
        pltpu.make_async_copy(gain_ref, gain_mine.at[mine_x], local_sems.at[3]),
    ]
    first_y = Gather(
        x_ring,
        lambda block, half: mine_ref.at[mine_y, block, y_half[half]],
        (yx_send, yx_recv),
        lambda half: shard_ref.at[mine_y, y_half[half]],
    )
    first_z = Gather(
        x_ring,
        lambda block, half: mine_ref.at[mine_z, block, z_half[half]],
        (zx_send, zx_recv),
        lambda half: shard_ref.at[mine_z, z_half[half]],
    )
    along_x = Gather(
        x_ring,
        lambda block, half: mine_ref.at[pl.ds(2 * half, 2), block, all_x],
        (x_send, x_recv),
        lambda half: shard_ref.at[pl.ds(2 * half, 2), all_x],
    )
    along_y = Gather(
        y_ring,
        lambda block, half: mine_ref.at[block, pl.ds(2 * half, 2), all_y],
        (y_send, y_recv),
    )
    along_z = Gather(
        z_ring,
        lambda block, half: mine_ref.at[block, pl.ds(2 * half, 2), all_z],
        (z_send, z_recv),
    )

    def gain_copy(which, block, src=None):
        part = gain_mine.at[block]
        target = x_ring.to_left if which == 1 else x_ring.to_right
        return remote(part if src is None else src, part, (gain_send, gain_recv), which, target)

    def hand(which, region):
        return remote(mine_ref.at[region], theirs_ref.at[region], (pair_send, pair_recv), which, pair)

    handed = []

    def hand_on(which, region):
        copy = hand(which, region)
        copy.start()
        handed.append(copy)

    first_y.start()
    first_z.start()
    for copy in locals_:
        copy.start()
    gain_copy(0, mine_x, gain_ref).start()
    gain_copy(1, mine_x, gain_ref).start()
    first_y.relay()
    first_z.relay()
    along_x.start()
    first_y.wait_all()
    locals_[0].wait()
    along_y.start()
    hand_on(0, (mine_y, slice(None), all_y))
    first_z.wait_all()
    locals_[1].wait()
    along_z.start()
    hand_on(1, (mine_z, slice(None), all_z))
    gain_copy(0, x_ring.left).wait_recv()
    gain_copy(2, x_ring.left).start()
    along_x.relay()
    along_y.relay()
    along_z.relay()
    along_x.wait_all()
    locals_[2].wait()
    hand_on(2, (slice(None), slice(None), all_x))
    along_y.wait_left()
    hand_on(3, (y_ring.left, slice(None), all_y))
    along_z.wait_left()
    hand_on(4, (z_ring.left, slice(None), all_z))
    along_y.wait_right()
    hand_on(5, (y_ring.right, slice(None), all_y))
    along_z.wait_right()
    hand_on(6, (z_ring.right, slice(None), all_z))
    gain_copy(1, x_ring.right).wait_recv()
    gain_copy(2, x_ring.opposite).wait_recv()
    locals_[3].wait()
    gains = remote(gain_mine, gain_theirs, (pair_send, pair_recv), 9, pair)
    gains.start()
    along_y.wait_opposite()
    hand_on(7, (y_ring.opposite, slice(None), all_y))
    along_z.wait_opposite()
    hand_on(8, (z_ring.opposite, slice(None), all_z))
    for copy in handed + [gains]:
        copy.wait()
    for which in range(3):
        gain_copy(which, mine_x).wait_send()
    for gather in (first_y, first_z, along_x, along_y, along_z):
        gather.finish()


def gather_weights(shard, gain):
    mats, share, features = shard.shape
    full = jax.ShapeDtypeStruct((mats, 4, share, features), LOW)
    gains = jax.ShapeDtypeStruct((4,) + gain.shape, LOW)
    return pl.pallas_call(
        weights_kernel,
        out_shape=(full, full, gains, gains),
        in_specs=[anywhere()] * 2,
        out_specs=[anywhere()] * 4,
        scratch_shapes=[pltpu.SemaphoreType.DMA((4,))]
        + [pltpu.SemaphoreType.DMA((6,))] * 10
        + [pltpu.SemaphoreType.DMA((3,))] * 2
        + [pltpu.SemaphoreType.DMA((10,))] * 2,
        compiler_params=pltpu.CompilerParams(collective_id=4, has_side_effects=True),
        cost_estimate=pl.CostEstimate(flops=0, bytes_accessed=60 * 10**6, transcendentals=0),
        name="gather_weights",
    )(shard, gain)


class SmallSum:
    def __init__(self, ring, slots, sems):
        self.ring, self.slots, self.sems = ring, slots, sems

    def copy(self, which, block):
        target = self.ring.to_left if which == 1 else self.ring.to_right
        part = self.slots.at[block]
        return remote(part, part, self.sems, which, target)

    def start(self):
        self.copy(0, self.ring.me).start()
        self.copy(1, self.ring.me).start()

    def relay(self):
        self.copy(0, self.ring.left).wait_recv()
        self.copy(2, self.ring.left).start()

    def result(self):
        self.copy(1, self.ring.right).wait_recv()
        self.copy(2, self.ring.opposite).wait_recv()
        return (self.slots[0] + self.slots[1]) + (self.slots[2] + self.slots[3])

    def finish(self):
        for which in range(3):
            self.copy(which, self.ring.me).wait_send()


class PlaneSum:
    def __init__(self, near, far, source, out, size, first, scratch, sems, keep, direct=False,
                 base=0):
        if direct:
            self.arrived, self.mid, self.done = scratch
        else:
            self.landing, self.passing, self.arrived, self.mid, self.done = scratch
        self.direct, self.base = direct, base
        self.out, self.size, self.near, self.far, self.keep = out, size, near, far, keep
        self.halves = ((0, first), (first, size - first))

        def rows(block, half):
            begin, count = (0, size) if half is None else self.halves[half]
            return pl.ds(pl.multiple_of(base + block * size + begin, 16), count)

        def half_rows(half):
            return pl.ds(0, size) if half is None else pl.ds(*self.halves[half])

        self.half_rows = half_rows
        def part(block, half):
            return source.at[rows(block, half)]

        if direct:
            self.scatter = DirectScatter(near, part, lambda side: self.arrived.at[side], sems[0])
        else:
            self.scatter = Scatter(
                near,
                part,
                lambda half: self.landing.at[half_rows(half)],
                lambda half: self.passing.at[half_rows(half)],
                lambda side, half: self.arrived.at[side, half_rows(half)],
                sems[0],
            )
        kind = DirectGather if direct else Gather
        self.gather = kind(far, lambda block, half: self.mid.at[block, half_rows(half)], sems[1])
        self.spread = kind(
            near,
            lambda block, half: out.at[rows(block, half)],
            sems[2],
            lambda half: self.done.at[half_rows(half)],
        )

    def start(self):
        self.scatter.start_far()
        self.scatter.start_near()

    def relay(self):
        self.scatter.relay()

    def middle(self):
        self.scatter.wait()
        if self.direct:
            self.mid[self.far.me] = self.scatter.whole().astype(LOW)
        else:
            for half in range(2):
                self.mid[self.far.me, self.half_rows(half)] = self.scatter.total(half).astype(LOW)
        self.gather.start()

    def middle_relay(self):
        self.gather.relay()

    def own(self):
        place = pl.ds(
            pl.multiple_of(self.base + self.near.me * self.size, 16), self.size
        )
        return pltpu.make_async_copy(self.done, self.out.at[place], self.keep)

    def end(self):
        self.gather.wait_all()
        four = [self.mid[block].astype(F32) for block in range(4)]
        self.done[...] = ((four[0] + four[1]) + (four[2] + four[3])).astype(LOW)
        self.spread.start()
        self.own().start()

    def end_relay(self):
        self.spread.relay()

    def wait(self):
        self.spread.wait_all()
        self.own().wait()

    def finish(self):
        self.scatter.finish()
        self.gather.finish()
        self.spread.finish()


FEED_BLOCK, AT_BLOCK = 144, 80


def feed_output(features):
    return (jax.ShapeDtypeStruct((2, 4 * FEED_BLOCK, features), LOW),)


def kept_output(features):
    return (jax.ShapeDtypeStruct((2, 4 * AT_BLOCK, features), LOW),)


def plane_scratch(size, features, direct=False):
    dma = pltpu.SemaphoreType.DMA

    def low(*shape):
        return pltpu.VMEM(shape + (features,), LOW)

    if direct:
        return [low(3, size), low(4, size), low(size)] + [dma((3,))] * 6
    return [low(size), low(size), low(2, size), low(4, size), low(size)] + [dma((6,))] * 6


def feed_scratch(features, rows):
    dma = pltpu.SemaphoreType.DMA
    return (
        [pltpu.VMEM((2, 2, 4, rows, features), LOW), pltpu.VMEM((2, 4 * FEED_BLOCK, features), LOW)]
        + plane_scratch(FEED_BLOCK, features) * 2
        + [dma((2,)), dma((2,)), dma((2,)), dma((2,)), dma((1,)), dma((1,))]
    )


def across_scratch(features, rows):
    share = features // 4
    dma = pltpu.SemaphoreType.DMA

    def low(*shape):
        return pltpu.VMEM(shape + (features,), LOW)

    return (
        [low(2, 2, rows), low(2, 2, rows), low(2, features)]
        + ([low(share), low(share), low(2, share)] + [dma((6,))] * 2) * 2
        + [dma((4,)), dma((4,)), dma((4,))]
    )


WIDE_PIECES = ((0, 0, 80, 48, 0), (1, 0, 80, 48, 1))
FINE_PIECES = ((0, 0, 48, 32, 0), (0, 192, 32, 16, 1), (1, 0, 48, 32, 1), (1, 192, 32, 16, 0))


def attention_scratch(features, pieces, direct):
    dma = pltpu.SemaphoreType.DMA
    scratch = []
    for piece in pieces:
        scratch += plane_scratch(piece[2], features, direct)
    return scratch + [dma((len(pieces),)), dma((2,)), dma((2,))]


def take_planes(take, count, direct=False):
    planes = []
    for _ in range(count):
        scratch = [next(take) for _ in range(3 if direct else 5)]
        sems = [next(take) for _ in range(6)]
        planes.append((scratch, [tuple(sems[i : i + 2]) for i in (0, 2, 4)]))
    return planes


def hand_over(layer, src, dst, sems, which=0):
    section = lax.axis_index("section")
    copy = functools.partial(remote, src, dst, sems, which, sibling())

    def start():
        @pl.when(section != layer)
        def _():
            copy().start()

    def wait():
        @pl.when(section != layer)
        def _():
            copy().wait_send()

        @pl.when(section == layer)
        def _():
            copy().wait_recv()

    return start, wait


class SwappedInputs:
    def __init__(self, zero, other, targets, local_sems, swap):
        self.zero, self.other, self.targets = zero, other, targets
        self.local_sems, self.swap, self.pair = local_sems, swap, sibling()

    def copies(self, first, which):
        own, sent = (self.zero, self.other) if first else (self.other, self.zero)
        target = self.targets[which]
        return (
            lambda: pltpu.make_async_copy(own[which], target.at[0], self.local_sems.at[which]),
            lambda: remote(sent[which], target.at[1], self.swap, which, self.pair),
        )

    def start(self):
        section = lax.axis_index("section")
        for first in (True, False):

            @pl.when(section == (0 if first else 1))
            def _(first=first):
                for which in range(len(self.targets)):
                    self.copies(first, which)[1]().start()
                for which in range(len(self.targets)):
                    self.copies(first, which)[0]().start()

    def wait(self, whiches):
        for which in whiches:
            keep, send = self.copies(True, which)
            keep().wait()
            send().wait_recv()

    def finish(self):
        for which in range(len(self.targets)):
            self.copies(True, which)[1]().wait_send()


class AttentionSum:
    def __init__(self, layer, kept, results, take, pieces, direct):
        out, other = results
        planes = take_planes(take, len(pieces), direct)
        keep, send, recv = [next(take) for _ in range(3)]
        y_ring, z_ring = Ring("y"), Ring("z")
        orders = ((y_ring, z_ring), (z_ring, y_ring))
        self.pieces = pieces
        self.planes = [
            PlaneSum(
                *orders[order], kept.at[matrix], out.at[matrix], size, first, *planes[which],
                keep.at[which], direct, base,
            )
            for which, (matrix, base, size, first, order) in enumerate(pieces)
        ]
        self.given = [
            hand_over(layer, out.at[which], other.at[which], (send, recv), which)
            for which in range(2)
        ]

    def run(self, name, matrix=None):
        for plane, piece in zip(self.planes, self.pieces):
            if matrix is None or piece[0] == matrix:
                getattr(plane, name)()

    def hand(self, matrix):
        self.run("wait", matrix)
        self.given[matrix][0]()

    def finish(self):
        self.run("finish")
        for given in self.given:
            given[1]()


class FeedSum:
    def __init__(self, features, operands, out, take):
        two, pre, hidden, out_all = operands
        self.features = features
        self.feed_in, self.feed_sum = next(take), next(take)
        planes = take_planes(take, 2)
        local_sems, swap_send, swap_recv, keep, end_send, end_recv = [
            next(take) for _ in range(6)
        ]
        self.end_sems = (end_send, end_recv)
        self.inputs = SwappedInputs(
            (two, pre), (hidden, out_all), (self.feed_in.at[0], self.feed_in.at[1]), local_sems,
            (swap_send, swap_recv),
        )
        y_ring, z_ring = Ring("y"), Ring("z")
        orders = ((y_ring, z_ring), (z_ring, y_ring))
        self.planes = [
            PlaneSum(
                *orders[which], self.feed_sum.at[which], out.at[which], FEED_BLOCK, 80,
                *planes[which], keep.at[which],
            )
            for which in range(2)
        ]

    def products(self):
        self.inputs.wait((0, 1))
        features, whole = self.features, 4 * FEED_BLOCK
        right = self.feed_in[1].reshape(-1, features)
        for begin in range(0, features, 256):
            count = min(256, features - begin)
            left = self.feed_in[0, :, :, :, pl.ds(begin, count)].reshape(-1, count)
            product = dot_tn(left, right).astype(LOW)
            first = max(0, min(count, whole - begin))
            if first:
                self.feed_sum[0, pl.ds(begin, first)] = product[:first]
            if first < count:
                self.feed_sum[1, pl.ds(begin + first - whole, count - first)] = product[first:]
        spare = 2 * whole - features
        self.feed_sum[1, pl.ds(whole - spare, spare)] = jnp.zeros((spare, features), LOW)
        self.run("start")

    def run(self, name):
        for plane in self.planes:
            getattr(plane, name)()

    def finish(self):
        self.inputs.finish()
        self.run("finish")


class AcrossSum:
    def __init__(self, features, operands, kept, take):
        one, mixed, dq, dk, dv, branch = operands
        self.features, self.share, self.kept = features, features // 4, kept
        share = self.share
        self.at_left, self.at_right, self.at_sum = [next(take) for _ in range(3)]
        self.halves = halves = ((0, 144), (144, share - 144))
        x_ring = Ring("x")
        self.across = []
        for which in range(2):
            landing, passing, arrived, send, recv = [next(take) for _ in range(5)]

            def part(block, half, which=which):
                begin, count = halves[half]
                row = pl.multiple_of(block * share + begin, 16)
                return self.at_sum.at[which, pl.ds(row, count)]

            def cut(ref):
                return lambda half: ref.at[pl.ds(*halves[half])]

            self.across.append(
                Scatter(
                    x_ring, part, cut(landing), cut(passing),
                    lambda side, half, arrived=arrived: arrived.at[side, pl.ds(*halves[half])],
                    (send, recv),
                )
            )
        local_sems, swap_send, swap_recv = [next(take) for _ in range(3)]
        self.inputs = SwappedInputs(
            (one, dq, one, dk),
            (one, dv, mixed, branch),
            (self.at_left.at[0], self.at_right.at[0], self.at_left.at[1], self.at_right.at[1]),
            local_sems,
            (swap_send, swap_recv),
        )

    def products(self, which):
        self.inputs.wait((2 * which, 2 * which + 1))
        features = self.features
        right = self.at_right[which].reshape(-1, features)
        for begin in range(0, features, 256):
            count = min(256, features - begin)
            left = self.at_left[which, :, :, pl.ds(begin, count)].reshape(-1, count)
            self.at_sum[which, pl.ds(begin, count)] = dot_tn(left, right).astype(LOW)
        self.across[which].start_far()

    def relay(self, which):
        self.across[which].relay()
        self.across[which].start_near()

    def keep(self, which):
        across = self.across[which]
        across.wait()
        for half in range(2):
            self.kept[which, pl.ds(*self.halves[half])] = across.total(half).astype(LOW)
        spare = 4 * AT_BLOCK - self.share
        self.kept[which, pl.ds(self.share, spare)] = jnp.zeros((spare, self.features), LOW)

    def finish(self):
        self.inputs.finish()
        for across in self.across:
            across.finish()


def gradient_kernel(features, *refs):
    take = iter(refs)

    def some(count):
        return [next(take) for _ in range(count)]

    operands = some(6)
    y_a, y_b, dx_a, dx_b, feed_zero, gain_in, kept_one = some(7)
    (feed_given,), at_zero, at_one = some(1), some(2), some(2)
    act_out, grad_out, gain_out = some(3)
    (kept_zero,) = some(1)
    sums = AcrossSum(features, operands, kept_zero, take)
    zero = AttentionSum(0, kept_zero, at_zero, take, FINE_PIECES, True)
    one = AttentionSum(1, kept_one, at_one, take, WIDE_PIECES, False)
    (gain_pair, gain_x, gain_y, gain_z, gain_send, gain_recv, last_send, last_recv, keep_sems,
     feed_send, feed_recv) = some(11)
    x_ring, y_ring, z_ring = Ring("x"), Ring("y"), Ring("z")
    pair, section = sibling(), lax.axis_index("section")
    greet_all(far=True)
    sums.inputs.start()
    feed = hand_over(0, feed_zero, feed_given, (feed_send, feed_recv))

    def last_copies(y, dx):
        return (
            remote(y, act_out.at[section], (last_send, last_recv), 0, pair),
            remote(dx, grad_out.at[section], (last_send, last_recv), 1, pair),
        )

    def keep_copies(y, dx):
        return (
            pltpu.make_async_copy(y, act_out.at[section], keep_sems.at[0]),
            pltpu.make_async_copy(dx, grad_out.at[section], keep_sems.at[1]),
        )

    @pl.when(section == 0)
    def _():
        for copy in last_copies(y_b, dx_b) + keep_copies(y_a, dx_a):
            copy.start()

    @pl.when(section == 1)
    def _():
        for copy in last_copies(y_a, dx_a) + keep_copies(y_b, dx_b):
            copy.start()

    gain_pair[0] = gain_in[...]
    swap_gain = remote(gain_pair.at[0], gain_pair.at[1], (gain_send, gain_recv), 9, pair)
    swap_gain.start()
    one.run("start")
    sums.products(0)
    sums.products(1)
    feed[0]()
    swap_gain.wait()
    gain_x[x_ring.me] = gain_pair[0] + gain_pair[1]
    small = [
        SmallSum(ring, slots, (gain_send.at[pl.ds(3 * i, 3)], gain_recv.at[pl.ds(3 * i, 3)]))
        for i, (ring, slots) in enumerate(((x_ring, gain_x), (y_ring, gain_y), (z_ring, gain_z)))
    ]
    small[0].start()
    one.run("relay")
    sums.relay(0)
    small[0].relay()
    one.run("middle")
    gain_y[y_ring.me] = small[0].result()
    small[1].start()
    one.run("middle_relay")
    small[1].relay()
    sums.keep(0)
    sums.relay(1)
    zero.run("start", 0)
    one.run("end")
    gain_z[z_ring.me] = small[1].result()
    small[2].start()
    zero.run("middle", 0)
    one.run("end_relay")
    small[2].relay()
    zero.run("end", 0)
    gain_out[...] = small[2].result()
    sums.keep(1)
    zero.run("start", 1)
    one.hand(0)
    one.hand(1)
    zero.hand(0)
    zero.run("middle", 1)
    zero.run("end", 1)
    zero.hand(1)
    zero.finish()
    one.finish()
    sums.finish()
    feed[1]()
    for each in small:
        each.finish()
    for copy in last_copies(y_a, dx_a) + keep_copies(y_a, dx_a):
        copy.wait()


def sum_gradients(features, rows, operands, last, gain, kept):
    dma = pltpu.SemaphoreType.DMA
    small = [pltpu.VMEM((4, 8, features), F32)] * 3
    return pl.pallas_call(
        functools.partial(gradient_kernel, features),
        out_shape=feed_output(features)
        + kept_output(features) * 4
        + (
            jax.ShapeDtypeStruct((2, rows, features), LOW),
            jax.ShapeDtypeStruct((2, rows, features), LOW),
            jax.ShapeDtypeStruct((8, features), F32),
        ),
        in_specs=[anywhere()] * 11 + [in_vmem()] * 2,
        out_specs=[anywhere()] * 7 + [in_vmem()],
        scratch_shapes=[pltpu.VMEM((2, 4 * AT_BLOCK, features), LOW)]
        + across_scratch(features, rows)
        + attention_scratch(features, FINE_PIECES, True)
        + attention_scratch(features, WIDE_PIECES, False)
        + [pltpu.VMEM((2, 8, features), F32)]
        + small
        + [dma((10,)), dma((10,)), dma((2,)), dma((2,)), dma((2,)), dma((1,)), dma((1,))],
        compiler_params=pltpu.CompilerParams(
            collective_id=5, has_side_effects=True, vmem_limit_bytes=60 * 2**20
        ),
        cost_estimate=pl.CostEstimate(
            flops=3 * 10**9, bytes_accessed=60 * 10**6, transcendentals=0
        ),
        name="sum_gradients",
    )(*operands, *last, gain, kept)


def doc_numbers(lengths, positions):
    doc_ends = jnp.cumsum(lengths)
    return jnp.sum((positions[:, None] >= doc_ends[None, :]).astype(jnp.int32), axis=1)


def swapped(block):
    return lax.ppermute(block, "section", [(0, 1), (1, 0)])


def body(tokens, cotangent, doc_lengths, norm_gains, w_qkv, w_out, w_up, w_down):
    batches, rows, features = tokens.shape
    share = w_qkv.shape[1]
    seq_rows = rows * lax.axis_size("tensor")
    section = lax.axis_index("section")
    is_first = section == 0

    def choose(zero_side, one_side):
        return jnp.where(is_first, zero_side, one_side)

    own_tokens = lax.dynamic_index_in_dim(tokens, section, 0, keepdims=False)
    own_cotangent = lax.dynamic_index_in_dim(cotangent, section, 0, keepdims=False)
    lengths = lax.dynamic_index_in_dim(doc_lengths, section, 0, keepdims=False)
    own_places = lax.axis_index("tensor") * rows + jnp.arange(rows, dtype=jnp.int32)
    all_places = jnp.arange(seq_rows, dtype=jnp.int32)
    own_docs = doc_numbers(lengths, own_places)
    all_docs = doc_numbers(lengths, all_places)
    allowed = (all_places[None, :] <= own_places[:, None]) & (
        all_docs[None, :] == own_docs[:, None]
    )
    bias = jnp.where(allowed, 0.0, -1e30).astype(F32)
    bias_turned = bias.T

    feed = (w_up[0], swapped(w_up[0]), w_down[0], swapped(w_down[0]))
    shard = jnp.stack(
        [w_qkv[0, :, :features], w_qkv[0, :, features : 2 * features], w_qkv[0, :, 2 * features :],
         w_out[0]]
    )
    gain_shard = jnp.pad(norm_gains[0], ((0, 14), (0, 0)))
    at_mine, at_theirs, gain_mine, gain_theirs = gather_weights(shard, gain_shard)
    attention = (
        at_mine.reshape(4, features, features), at_theirs.reshape(4, features, features)
    )

    def whole_gains(block):
        return block[:, :2].transpose(1, 0, 2).reshape(2, features).astype(F32)

    gain_mine, gain_theirs = whole_gains(gain_mine), whole_gains(gain_theirs)
    gains = (choose(gain_mine, gain_theirs), choose(gain_theirs, gain_mine))

    inputs = own_tokens
    saved = []
    for layer in range(2):
        results = forward_layer(layer, inputs, bias, gains[layer], attention, feed)
        saved.append((inputs,) + tuple(results))
        inputs = results[0]

    grad = own_cotangent
    gain_grads, input_grads, operands = [None, None], [None, None], ()
    for layer in (1, 0):
        (x, _, middle, normed_one, query, key, value, mixed, normed_two, act, hidden) = saved[layer]
        results = backward_layer(
            layer, x, grad, bias_turned, gains[layer], middle, query, key, value, act,
            attention, feed, operands + (saved[0][8], saved[0][10]) if layer == 0 else (),
        )
        (grad, gain_grads[layer], out_all, pre_grad, branch, dquery, dkey, dvalue) = results[:8]
        input_grads[layer] = grad
        operands = (
            normed_two, pre_grad, hidden, out_all, normed_one, mixed, dquery, dkey, dvalue, branch,
        )
    feed_one, feed_one_given, feed_zero, kept_one = results[8:]
    gain_rows = jnp.concatenate(gain_grads + [jnp.zeros((4, features), F32)], axis=0)
    (feed_zero_given, at_zero, at_zero_given, at_one, at_one_given, activations, input_grads,
     gain_total) = sum_gradients(
        features, rows, operands[4:], (saved[0][1], saved[1][1], *input_grads, feed_zero),
        gain_rows, kept_one,
    )
    gain_own = lax.dynamic_slice(
        gain_total, (2 * section, lax.axis_index("tensor") * share), (2, share)
    )

    def whole(block):
        return block.reshape(-1, features)[:features].astype(F32)[None]

    first_half = choose(at_zero, at_one_given)[:, :share].astype(F32)
    other_half = choose(at_zero_given, at_one)[:, :share].astype(F32)
    grad_qkv = jnp.concatenate([first_half[0], first_half[1], other_half[0]], axis=1)
    return (
        activations[None],
        input_grads[None],
        gain_own[None],
        grad_qkv[None],
        other_half[1][None],
        whole(choose(feed_zero, feed_one_given)),
        whole(choose(feed_zero_given, feed_one)),
    )


def solution(mesh):
    placed = (
        P("dp", "tensor", None),
        P("dp", "tensor", None),
        P("dp", None),
        P("section", None, "tensor"),
        P("section", "tensor", None),
        P("section", "tensor", None),
        P("section", None, "tensor"),
        P("section", "tensor", None),
    )
    return jax.shard_map(
        body,
        mesh=mesh,
        in_specs=placed,
        out_specs=(
            P("section", "dp", "tensor", None),
            P("section", "dp", "tensor", None),
            P("section", None, "tensor"),
            P("section", "tensor", None),
            P("section", "tensor", None),
            P("section", None, "tensor"),
            P("section", "tensor", None),
        ),
        check_vma=False,
    )
```

```python
import functools
import jax
import jax.numpy as jnp
from jax import lax
from jax.experimental import pallas as pl
from jax.experimental.pallas import tpu as pltpu
from jax.sharding import PartitionSpec as P

HEAD_DIM = 64
LOW = jnp.bfloat16
F32 = jnp.float32
MESH = pl.DeviceIdType.MESH


def dot_nn(left, right):
    return lax.dot_general(left, right, (((1,), (0,)), ((), ())), preferred_element_type=F32)


def dot_nt(left, right):
    return lax.dot_general(left, right, (((1,), (1,)), ((), ())), preferred_element_type=F32)


def dot_tn(left, right):
    return lax.dot_general(left, right, (((0,), (0,)), ((), ())), preferred_element_type=F32)


class Ring:
    def __init__(self, axis):
        whole = lax.axis_index("dp")
        rest = None
        if axis == "x":
            self.me = lax.axis_index("tensor")
        elif axis == "y":
            self.me, rest = lax.rem(whole, 4), lax.div(whole, 4) * 4
        else:
            self.me, rest = lax.div(whole, 4), lax.rem(whole, 4)
        self.right = lax.rem(self.me + 1, 4)
        self.left = lax.rem(self.me + 3, 4)
        self.opposite = lax.rem(self.me + 2, 4)

        def device(place):
            if axis == "x":
                return {"tensor": place}
            if axis == "y":
                return {"dp": rest + place}
            return {"dp": place * 4 + rest}

        self.to_right, self.to_left = device(self.right), device(self.left)
        self.to_opposite = device(self.opposite)


def sibling():
    return {"section": 1 - lax.axis_index("section")}


def greet(*targets):
    barrier = pltpu.get_barrier_semaphore()
    for target in targets:
        pl.semaphore_signal(barrier, inc=1, device_id=target, device_id_type=MESH)
    pl.semaphore_wait(barrier, len(targets))


def remote(src, dst, sems, which, target):
    return pltpu.make_async_remote_copy(
        src_ref=src,
        dst_ref=dst,
        send_sem=sems[0].at[which],
        recv_sem=sems[1].at[which],
        device_id=target,
        device_id_type=MESH,
    )


class Gather:
    def __init__(self, ring, slot, sems, own=None):
        self.ring, self.slot, self.sems = ring, slot, sems
        self.own = own if own is not None else lambda half: slot(ring.me, half)

    def copy(self, which, arriving=False):
        ring = self.ring
        half = (0, 1, 1, 0, 0, 1)[which]
        goes_right = which in (0, 2, 4)
        target = ring.to_right if goes_right else ring.to_left
        if which < 4:
            source_block = ring.left if goes_right else ring.right
            if not arriving:
                return remote(self.own(half), self.slot(ring.me, half), self.sems, which, target)
        else:
            source_block = ring.opposite
            if not arriving:
                handed = self.slot(ring.left if goes_right else ring.right, half)
                return remote(handed, handed, self.sems, which, target)
        part = self.slot(source_block, half)
        return remote(part, part, self.sems, which, target)

    def start(self):
        for which in range(4):
            self.copy(which).start()

    def relay(self):
        for which in (0, 1):
            self.copy(which, arriving=True).wait_recv()
            self.copy(which + 4).start()

    def wait_left(self):
        self.copy(2, arriving=True).wait_recv()

    def wait_right(self):
        self.copy(3, arriving=True).wait_recv()

    def wait_opposite(self):
        self.copy(4, arriving=True).wait_recv()
        self.copy(5, arriving=True).wait_recv()

    def wait_all(self):
        self.wait_left()
        self.wait_right()
        self.wait_opposite()

    def finish(self):
        for which in range(6):
            self.copy(which).wait_send()


class Scatter:
    def __init__(self, ring, part, landing, passing, arrived, sems):
        self.ring, self.part, self.landing, self.passing = ring, part, landing, passing
        self.arrived, self.sems = arrived, sems

    def copy(self, which):
        ring = self.ring
        half = (0, 1, 1, 0, 0, 1)[which]
        goes_right = which in (0, 2, 4)
        if which < 2:
            src, dst = self.part(ring.opposite, half), self.landing(half)
        else:
            dst = self.arrived(0 if goes_right else 1, half)
            if which < 4:
                src = self.part(ring.right if goes_right else ring.left, half)
            else:
                src = self.passing(half)
        return remote(src, dst, self.sems, which, ring.to_right if goes_right else ring.to_left)

    def start_near(self):
        self.copy(2).start()
        self.copy(3).start()

    def start_far(self):
        self.copy(0).start()
        self.copy(1).start()

    def relay(self):
        for half, block in ((0, self.ring.right), (1, self.ring.left)):
            self.copy(half).wait_recv()
            added = self.part(block, half)[...].astype(F32) + self.landing(half)[...].astype(F32)
            self.passing(half)[...] = added.astype(LOW)
            self.copy(half + 4).start()

    def wait(self):
        for which in (2, 3, 4, 5):
            self.copy(which).wait_recv()

    def total(self, half):
        return (
            self.part(self.ring.me, half)[...].astype(F32)
            + self.arrived(0, half)[...].astype(F32)
            + self.arrived(1, half)[...].astype(F32)
        )

    def finish(self):
        for which in range(6):
            self.copy(which).wait_send()


class DirectGather:
    def __init__(self, ring, slot, sems, own=None):
        self.ring, self.slot, self.sems = ring, slot, sems
        self.own = own if own is not None else lambda half: slot(ring.me, half)

    def copy(self, which):
        target = (self.ring.to_right, self.ring.to_left, self.ring.to_opposite)[which]
        return remote(self.own(None), self.slot(self.ring.me, None), self.sems, which, target)

    def start(self):
        for which in (2, 0, 1):
            self.copy(which).start()

    def relay(self):
        pass

    def wait_all(self):
        for which, block in enumerate((self.ring.left, self.ring.right, self.ring.opposite)):
            part = self.slot(block, None)
            remote(part, part, self.sems, which, self.ring.to_right).wait_recv()

    def finish(self):
        for which in range(3):
            self.copy(which).wait_send()


class DirectScatter:
    def __init__(self, ring, part, arrived, sems):
        self.ring, self.part, self.arrived, self.sems = ring, part, arrived, sems

    def copy(self, which):
        ring = self.ring
        block = (ring.right, ring.left, ring.opposite)[which]
        target = (ring.to_right, ring.to_left, ring.to_opposite)[which]
        return remote(self.part(block, None), self.arrived(which), self.sems, which, target)

    def start_far(self):
        self.copy(2).start()

    def start_near(self):
        self.copy(0).start()
        self.copy(1).start()

    def relay(self):
        pass

    def wait(self):
        for which in range(3):
            self.copy(which).wait_recv()

    def whole(self):
        near = self.arrived(0)[...].astype(F32) + self.arrived(1)[...].astype(F32)
        own = self.part(self.ring.me, None)[...].astype(F32)
        return (own + near) + self.arrived(2)[...].astype(F32)

    def finish(self):
        for which in range(3):
            self.copy(which).wait_send()


def row_gather(ring, full, sems, columns=slice(None)):
    half = full.shape[1] // 2
    return Gather(
        ring, lambda block, which: full.at[block, pl.ds(which * half, half), columns], sems
    )


def row_scatter(ring, parts, landing, passing, arrived, sems, columns=slice(None)):
    half = parts.shape[1] // 2

    def rows(which):
        return pl.ds(which * half, half)

    return Scatter(
        ring,
        lambda block, which: parts.at[block, rows(which), columns],
        lambda which: landing.at[which, :, columns],
        lambda which: passing.at[which, :, columns],
        lambda side, which: arrived.at[side, rows(which), columns],
        sems,
    )


def row_total(scatter):
    scatter.wait()
    return jnp.concatenate([scatter.total(0), scatter.total(1)], axis=0)


def head_groups(features):
    pairs = pair_columns(features)
    middle = (len(pairs) + 1) // 2
    begin = pairs[middle][0]
    return (
        (pl.ds(0, begin), pairs[:middle]),
        (pl.ds(begin, features - begin), pairs[middle:]),
    )


def norm_stats(values):
    average = jnp.mean(values, axis=-1, keepdims=True)
    centered = values - average
    variance = jnp.mean(centered * centered, axis=-1, keepdims=True)
    scale = lax.rsqrt(variance + 1e-05)
    return centered * scale, scale


def norm_back(values, gain, grad):
    xhat, scale = norm_stats(values)
    scaled = grad * gain
    part = scale * (
        scaled
        - jnp.mean(scaled, axis=-1, keepdims=True)
        - xhat * jnp.mean(scaled * xhat, axis=-1, keepdims=True)
    )
    return part, jnp.sum(grad * xhat, axis=0, keepdims=True)


def gelu_tanh(values):
    inner = 0.7978845608028654 * (values + 0.044715 * values * values * values)
    return 0.5 * values * (1.0 + jnp.tanh(inner))


def gelu_slope(values):
    square = values * values
    bent = jnp.tanh(0.7978845608028654 * values * (1.0 + 0.044715 * square))
    slope = 0.7978845608028654 * (1.0 + 3.0 * 0.044715 * square)
    return 0.5 * (1.0 + bent) + 0.5 * values * (1.0 - bent * bent) * slope


def pick_copies(layer, mine, theirs, target, sem):
    def start():
        mine_here = lax.axis_index("section") == layer

        @pl.when(mine_here)
        def _():
            pltpu.make_async_copy(mine, target, sem).start()

        @pl.when(jnp.logical_not(mine_here))
        def _():
            pltpu.make_async_copy(theirs, target, sem).start()

    def wait():
        pltpu.make_async_copy(mine, target, sem).wait()

    return start, wait


def pair_columns(features):
    width = 2 * HEAD_DIM
    return [
        (start, min(width, features - start)) for start in range(0, features, width)
    ]


def head_masks(width):
    lanes = lax.broadcasted_iota(jnp.int32, (1, width), 1)
    if width == HEAD_DIM:
        return [None]
    return [lanes < HEAD_DIM, lanes >= HEAD_DIM]


def masked(values, mask):
    return values if mask is None else jnp.where(mask, values, jnp.zeros_like(values))


def plain_copy(src, target, sem):
    copy = functools.partial(pltpu.make_async_copy, src, target, sem)
    return lambda: copy().start(), lambda: copy().wait()


def forward_kernel(layer, features, *refs):
    take = iter(refs)

    def some(count):
        return [next(take) for _ in range(count)]

    (x_ref, bias_ref, gains_ref, at_full, up_mine, up_theirs, down_mine, down_theirs) = some(8)
    shard_ref = next(take) if layer == 0 else None
    (y_ref, middle_ref, one_ref, query_ref, key_ref, value_ref, mixed_ref, two_ref, act_ref,
     hidden_ref) = some(10)
    next_ref = next(take) if layer == 0 else None
    (at_w, up_w, down_w, weight_sems_, parts, landing, passing, arrived,
     key_send, key_recv, value_send, value_recv, two_send, two_recv, sum_send, sum_recv) = some(16)
    ring = Ring("x")
    me = ring.me
    fetches = [
        plain_copy(at_full.at[which], at_w.at[which], weight_sems_.at[which]) for which in range(4)
    ]
    fetches.append(pick_copies(layer, up_mine, up_theirs, up_w, weight_sems_.at[4]))
    fetches.append(pick_copies(layer, down_mine, down_theirs, down_w, weight_sems_.at[5]))
    for which in (1, 2, 0, 3, 4, 5):
        fetches[which][0]()
    if layer == 0:
        following = WeightGather(1, shard_ref, next_ref, (0, 144, 80, 64), some(13))
        greet_all()
    else:
        greet(ring.to_right, ring.to_left)

    def steps(*names):
        if layer == 0:
            following.steps(*names)

    rows = x_ref.shape[0]
    inputs = x_ref[...].astype(F32)
    xhat, _ = norm_stats(inputs)
    one_ref[...] = (xhat * gains_ref[0:1, :]).astype(LOW)
    normed_one = one_ref[...]
    groups = head_groups(features)
    keys, values = [], []
    fetches[1][1]()
    fetches[2][1]()
    for which, (columns, _) in enumerate(groups):
        key_ref[me, :, columns] = dot_nn(normed_one, at_w[1, :, columns]).astype(LOW)
        keys.append(
            row_gather(ring, key_ref, (key_send.at[which], key_recv.at[which]), columns)
        )
        if which == 0:
            keys[0].start()
        value_ref[me, :, columns] = dot_nn(normed_one, at_w[2, :, columns]).astype(LOW)
        values.append(
            row_gather(ring, value_ref, (value_send.at[which], value_recv.at[which]), columns)
        )
        if which == 0:
            values[0].start()
            steps("start")
    fetches[0][1]()
    query_ref[...] = dot_nn(normed_one, at_w[0]).astype(LOW)
    keys[0].relay()
    values[0].relay()
    keys[1].start()
    values[1].start()
    steps("first_relay")
    bias = bias_ref[...]

    def attend(begin, width):
        columns = pl.ds(begin, width)
        queries = query_ref[:, columns]
        key_block = key_ref[:, :, columns].reshape(4 * rows, width)
        value_block = value_ref[:, :, columns].reshape(4 * rows, width)
        mixed = None
        for mask in head_masks(width):
            scores = dot_nt(masked(queries, mask), key_block) * 0.125 + bias
            raised = jnp.exp(scores - jnp.max(scores, axis=-1, keepdims=True))
            probs = raised * (1.0 / jnp.sum(raised, axis=-1, keepdims=True))
            own = dot_nn(probs.astype(LOW), value_block)
            mixed = own if mixed is None else jnp.where(mask, own, mixed)
        mixed_ref[:, columns] = mixed.astype(LOW)

    for which, (_, pairs) in enumerate(groups):
        keys[which].wait_all()
        values[which].wait_all()
        for count, (begin, width) in enumerate(pairs):
            attend(begin, width)
            if which == 0 and count == 2:
                keys[1].relay()
                values[1].relay()
                steps("second")
    fetches[3][1]()
    middle_ref[...] = x_ref[...].astype(F32) + dot_nn(mixed_ref[...], at_w[3])
    xhat, _ = norm_stats(middle_ref[...])
    two_ref[me] = (xhat * gains_ref[1:2, :]).astype(LOW)
    tokens = row_gather(ring, two_ref, (two_send, two_recv))
    tokens.start()
    fetches[4][1]()
    fetches[5][1]()
    sums = row_scatter(ring, parts, landing, passing, arrived, (sum_send, sum_recv))

    def feed(block):
        act_ref[block] = dot_nn(two_ref[block], up_w[...])
        hidden_ref[block] = gelu_tanh(act_ref[block]).astype(LOW)
        parts[block] = dot_nn(hidden_ref[block], down_w[...]).astype(LOW)

    feed(me)
    tokens.relay()
    tokens.wait_left()
    feed(ring.left)
    tokens.wait_right()
    feed(ring.right)
    sums.start_near()
    tokens.wait_opposite()
    feed(ring.opposite)
    sums.start_far()
    sums.relay()
    steps("second_relay")
    y_ref[...] = (middle_ref[...] + row_total(sums)).astype(LOW)
    for gather in keys + values:
        gather.finish()
    tokens.finish()
    sums.finish()
    if layer == 0:
        following.end()


def scatter_scratch(rows, features):
    return [
        pltpu.VMEM((4, rows, features), LOW),
        pltpu.VMEM((2, rows // 2, features), LOW),
        pltpu.VMEM((2, rows // 2, features), LOW),
        pltpu.VMEM((2, rows, features), LOW),
    ]


def weight_scratch(features, hidden, matrices=4):
    shape = (features, features) if matrices == 1 else (matrices, features, features)
    return [
        pltpu.VMEM(shape, LOW),
        pltpu.VMEM((features, hidden), LOW),
        pltpu.VMEM((hidden, features), LOW),
        pltpu.SemaphoreType.DMA((6,)),
    ]


def in_vmem():
    return pl.BlockSpec(memory_space=pltpu.VMEM)


def anywhere():
    return pl.BlockSpec(memory_space=pl.ANY)


def forward_layer(layer, x, bias, gains, attention, feed, shard=()):
    rows, features = x.shape
    hidden = feed[0].shape[1]
    out_shape = (
        jax.ShapeDtypeStruct((rows, features), LOW),
        jax.ShapeDtypeStruct((rows, features), F32),
        jax.ShapeDtypeStruct((rows, features), LOW),
        jax.ShapeDtypeStruct((rows, features), LOW),
        jax.ShapeDtypeStruct((4, rows, features), LOW),
        jax.ShapeDtypeStruct((4, rows, features), LOW),
        jax.ShapeDtypeStruct((rows, features), LOW),
        jax.ShapeDtypeStruct((4, rows, features), LOW),
        jax.ShapeDtypeStruct((4, rows, hidden), F32),
        jax.ShapeDtypeStruct((4, rows, hidden), LOW),
    )
    following = (
        (jax.ShapeDtypeStruct((4, 4, features // 4, features), LOW),) if layer == 0 else ()
    )
    return pl.pallas_call(
        functools.partial(forward_kernel, layer, features),
        out_shape=out_shape + following,
        in_specs=[in_vmem()] * 3 + [anywhere()] * (5 + len(shard)),
        out_specs=[in_vmem()] * len(out_shape) + [anywhere()] * len(following),
        scratch_shapes=weight_scratch(features, hidden)
        + scatter_scratch(rows, features)
        + [pltpu.SemaphoreType.DMA((2, 6))] * 4
        + [pltpu.SemaphoreType.DMA((6,))] * 4
        + (weight_sems() if layer == 0 else []),
        compiler_params=pltpu.CompilerParams(
            collective_id=layer, has_side_effects=True, vmem_limit_bytes=56 * 2**20
        ),
        cost_estimate=pl.CostEstimate(
            flops=3 * 10**9, bytes_accessed=24 * 10**6, transcendentals=10**6
        ),
        name=f"layer_forward_{layer}",
    )(x, bias, gains, attention, *feed, *shard)


def backward_kernel(layer, features, *refs):
    take = iter(refs)

    def some(count):
        return [next(take) for _ in range(count)]

    (x_ref, dy_ref, bias_ref, gains_ref, middle_ref, query_ref, key_ref, value_ref, act_ref,
     at_full, up_mine, up_theirs, down_mine, down_theirs) = some(14)
    operands = some(12) if layer == 0 else None
    (dx_ref, gain_ref, out_ref, pre_ref, branch_ref, dquery_ref, dkey_ref, dvalue_ref) = some(8)
    results = some(4) if layer == 0 else None
    (at_w, up_w, down_w, weight_sems, parts, landing, passing, arrived, parts_b, landing_b,
     passing_b, arrived_b, parts_c, landing_c, passing_c, arrived_c, mixed_grad, kept_grad,
     out_send, out_recv, sum_send, sum_recv, key_send, key_recv, value_send, value_recv) = some(26)
    extra = layer == 0
    if extra:
        (two, pre, hidden, out_all, one, mixed, dq, dk, dv, branch, two_own, hidden_own) = operands
        feed_out, feed_given, feed_own_out, kept = results
        feed_one = FeedSum(features, (two, pre, hidden, out_all), feed_out, take)
        feed_own = FeedSum(
            features, (two_own, pre_ref, hidden_own, out_ref), feed_own_out, take
        )
        across = AcrossSum(features, (one, mixed, dq, dk, dv, branch), kept, take)
        given = hand_over(1, feed_out, feed_given, feed_one.end_sems)
    ring = Ring("x")
    me = ring.me
    fetches = [
        plain_copy(at_full.at[which], target, weight_sems.at[which])
        for which, target in enumerate((up_w, down_w, at_w, at_w))
    ]
    fetches.append(pick_copies(layer, up_mine, up_theirs, up_w, weight_sems.at[4]))
    fetches.append(pick_copies(layer, down_mine, down_theirs, down_w, weight_sems.at[5]))
    for which in (5, 4, 3):
        fetches[which][0]()
    rows = x_ref.shape[0]
    out_ref[me] = dy_ref[...]
    if not extra:
        greet(ring.to_right, ring.to_left)
    else:
        greet_all()
    grads = row_gather(ring, out_ref, (out_send, out_recv))
    grads.start()
    if extra:
        across.inputs.start()
        feed_one.inputs.start()
    sums = row_scatter(ring, parts, landing, passing, arrived, (sum_send, sum_recv))
    fetches[5][1]()
    fetches[4][1]()

    def feed(block):
        hidden_grad = dot_nt(out_ref[block], down_w[...])
        pre_ref[block] = (hidden_grad * gelu_slope(act_ref[block])).astype(LOW)
        parts[block] = dot_nt(pre_ref[block], up_w[...]).astype(LOW)

    feed(me)
    grads.relay()
    if extra:
        across.products(0)
        feed_one.products()
    grads.wait_left()
    feed(ring.left)
    grads.wait_right()
    feed(ring.right)
    sums.start_near()
    grads.wait_opposite()
    feed(ring.opposite)
    sums.start_far()
    for which in (0, 1):
        fetches[which][0]()
    if extra:
        feed_own.inputs.start()
        feed_one.run("relay")
    sums.relay()
    if extra:
        across.products(1)
    middle_part, gain_two = norm_back(middle_ref[...], gains_ref[1:2, :], row_total(sums))
    gain_ref[1:2, :] = gain_two
    middle_grad = dy_ref[...].astype(F32) + middle_part
    kept_grad[...] = middle_grad
    branch_ref[...] = middle_grad.astype(LOW)
    fetches[3][1]()
    mixed_grad[...] = dot_nt(branch_ref[...], at_w[...]).astype(LOW)
    fetches[2][0]()
    bias = bias_ref[...]
    groups = head_groups(features)
    dkeys = [
        row_scatter(ring, parts_b, landing_b, passing_b, arrived_b,
                    (key_send.at[which], key_recv.at[which]), columns)
        for which, (columns, _) in enumerate(groups)
    ]
    dvalues = [
        row_scatter(ring, parts_c, landing_c, passing_c, arrived_c,
                    (value_send.at[which], value_recv.at[which]), columns)
        for which, (columns, _) in enumerate(groups)
    ]

    def send_pair(which):
        for scatter in (dkeys[which], dvalues[which]):
            scatter.start_far()
        for scatter in (dkeys[which], dvalues[which]):
            scatter.start_near()

    def relay_pair(which):
        for scatter in (dkeys[which], dvalues[which]):
            scatter.relay()

    for count, (begin, width) in enumerate(pair_columns(features)):
        columns = pl.ds(begin, width)
        queries = query_ref[:, columns]
        outer = mixed_grad[:, columns]
        key_block = key_ref[:, :, columns].reshape(4 * rows, width)
        value_block = value_ref[:, :, columns].reshape(4 * rows, width)
        dquery = dkey = dvalue = None
        for mask in head_masks(width):
            query_one, outer_one = masked(queries, mask), masked(outer, mask)
            scores = dot_nt(key_block, query_one) * 0.125 + bias
            raised = jnp.exp(scores - jnp.max(scores, axis=0, keepdims=True))
            probs = raised * (1.0 / jnp.sum(raised, axis=0, keepdims=True))
            probs_grad = dot_nt(value_block, outer_one)
            mean = jnp.sum(probs * probs_grad, axis=0, keepdims=True)
            score_grad = (probs * (probs_grad - mean)).astype(LOW)
            own_query = dot_tn(score_grad, key_block)
            own_key = dot_nn(score_grad, query_one)
            own_value = dot_nn(probs.astype(LOW), outer_one)
            if dquery is None:
                dquery, dkey, dvalue = own_query, own_key, own_value
            else:
                dquery = jnp.where(mask, own_query, dquery)
                dkey, dvalue = dkey + own_key, dvalue + own_value
        dquery_ref[:, columns] = (dquery * 0.125).astype(LOW)
        parts_b[:, :, columns] = (dkey * 0.125).astype(LOW).reshape(4, rows, width)
        parts_c[:, :, columns] = dvalue.astype(LOW).reshape(4, rows, width)
        if begin + width == groups[0][0].size:
            send_pair(0)
        if extra and count == 1:
            feed_one.run("middle")
            across.relay(0)
        if extra and count == 4:
            feed_own.products()
            feed_one.run("middle_relay")
        if extra and count == 7:
            feed_own.run("relay")
    relay_pair(0)
    send_pair(1)
    for which in (0, 1, 2):
        fetches[which][1]()
    one_grad = dot_nt(dquery_ref[...], up_w[...])
    if extra:
        feed_one.run("end")
    relay_pair(1)
    if extra:
        across.relay(1)
        feed_own.run("middle")
        feed_one.run("end_relay")
    for which, (columns, _) in enumerate(groups):
        dkey_ref[:, columns] = row_total(dkeys[which]).astype(LOW)
    one_grad = one_grad + dot_nt(dkey_ref[...], down_w[...])
    if extra:
        across.keep(0)
        feed_own.run("middle_relay")
    for which, (columns, _) in enumerate(groups):
        dvalue_ref[:, columns] = row_total(dvalues[which]).astype(LOW)
    one_grad = one_grad + dot_nt(dvalue_ref[...], at_w[...])
    inputs_part, gain_one = norm_back(x_ref[...].astype(F32), gains_ref[0:1, :], one_grad)
    gain_ref[0:1, :] = gain_one
    dx_ref[...] = (kept_grad[...] + inputs_part).astype(LOW)
    if extra:
        feed_one.run("wait")
        given[0]()
        feed_own.run("end")
        across.keep(1)
        feed_own.run("end_relay")
        feed_one.finish()
        across.finish()
        given[1]()
        feed_own.run("wait")
        feed_own.finish()
    grads.finish()
    sums.finish()
    for scatter in dkeys + dvalues:
        scatter.finish()


def greet_all(far=False):
    rings = [Ring(axis) for axis in ("x", "y", "z")]
    greet(
        *[ring.to_right for ring in rings], *[ring.to_left for ring in rings], sibling(),
        *[ring.to_opposite for ring in rings[1:] if far],
    )


def backward_layer(layer, x, dy, bias, gains, middle, query, key, value, act, attention, feed,
                   operands=()):
    rows, features = x.shape
    hidden = feed[0].shape[1]
    out_shape = (
        jax.ShapeDtypeStruct((rows, features), LOW),
        jax.ShapeDtypeStruct((2, features), F32),
        jax.ShapeDtypeStruct((4, rows, features), LOW),
        jax.ShapeDtypeStruct((4, rows, hidden), LOW),
        jax.ShapeDtypeStruct((rows, features), LOW),
        jax.ShapeDtypeStruct((rows, features), LOW),
        jax.ShapeDtypeStruct((rows, features), LOW),
        jax.ShapeDtypeStruct((rows, features), LOW),
    )
    sums = feed_output(features) * 3 + kept_output(features) if layer == 0 else ()
    return pl.pallas_call(
        functools.partial(backward_kernel, layer, features),
        out_shape=out_shape + sums,
        in_specs=[in_vmem()] * 9 + [anywhere()] * (5 + len(operands)),
        out_specs=[in_vmem()] * len(out_shape) + [anywhere()] * 3 * (len(sums) // 4)
        + [in_vmem()] * (len(sums) // 4),
        scratch_shapes=weight_scratch(features, hidden, 1)
        + scatter_scratch(rows, features) * 3
        + [pltpu.VMEM((rows, features), LOW), pltpu.VMEM((rows, features), F32)]
        + [pltpu.SemaphoreType.DMA((6,))] * 4
        + [pltpu.SemaphoreType.DMA((2, 6))] * 4
        + (
            feed_scratch(features, rows) * 2 + across_scratch(features, rows)
            if layer == 0
            else []
        ),
        compiler_params=pltpu.CompilerParams(
            collective_id=2 + layer, has_side_effects=True, vmem_limit_bytes=62 * 2**20
        ),
        cost_estimate=pl.CostEstimate(
            flops=4 * 10**9, bytes_accessed=24 * 10**6, transcendentals=10**6
        ),
        name=f"layer_backward_{layer}",
    )(x, dy, bias, gains, middle, query, key, value, act, attention, *feed, *operands)


class WeightGather:
    def __init__(self, layer, shard, full, split, sems):
        self.layer, self.full = layer, full
        self.owner = lax.axis_index("section") == layer
        local_sems, pair_sems = sems[0], sems[11:13]
        rings = [tuple(sems[which : which + 2]) for which in (1, 3, 5, 7, 9)]
        x_ring, y_ring, z_ring = Ring("x"), Ring("y"), Ring("z")
        self.y_ring, self.z_ring = y_ring, z_ring
        x_rows, y_rows, y_first, z_first = split
        z_rows = shard.shape[1] - x_rows - y_rows
        z_begin = x_rows + y_rows
        self.with_x = x_rows > 0
        all_x, all_y, all_z = pl.ds(0, x_rows), pl.ds(x_rows, y_rows), pl.ds(z_begin, z_rows)
        self.all_x, self.all_y, self.all_z = all_x, all_y, all_z
        y_half = (pl.ds(x_rows, y_first), pl.ds(x_rows + y_first, y_rows - y_first))
        z_half = (pl.ds(z_begin, z_first), pl.ds(z_begin + z_first, z_rows - z_first))
        me_x, me_y, me_z = x_ring.me, y_ring.me, z_ring.me
        self.pair, self.pair_sems = sibling(), pair_sems

        def local(which):
            src, dst = (
                lambda: (shard.at[me_y, all_y], full.at[me_y, me_x, all_y]),
                lambda: (shard.at[me_z, all_z], full.at[me_z, me_x, all_z]),
                lambda: (shard.at[:, all_x], full.at[:, me_x, all_x]),
            )[which]()
            return pltpu.make_async_copy(src, dst, local_sems.at[which])

        self.local = local
        self.first_y = Gather(
            x_ring,
            lambda block, half: full.at[me_y, block, y_half[half]],
            rings[0],
            lambda half: shard.at[me_y, y_half[half]],
        )
        self.first_z = Gather(
            x_ring,
            lambda block, half: full.at[me_z, block, z_half[half]],
            rings[1],
            lambda half: shard.at[me_z, z_half[half]],
        )
        self.along_x = Gather(
            x_ring,
            lambda block, half: full.at[pl.ds(2 * half, 2), block, all_x],
            rings[2],
            lambda half: shard.at[pl.ds(2 * half, 2), all_x],
        )
        self.along_y = Gather(
            y_ring, lambda block, half: full.at[block, pl.ds(2 * half, 2), all_y], rings[3]
        )
        self.along_z = Gather(
            z_ring, lambda block, half: full.at[block, pl.ds(2 * half, 2), all_z], rings[4]
        )

    def hand(self, which):
        y_ring, z_ring = self.y_ring, self.z_ring
        if which == 2:
            region = (slice(None), slice(None), self.all_x)
        elif which in (0, 3, 5, 7):
            block = {0: y_ring.me, 3: y_ring.left, 5: y_ring.right, 7: y_ring.opposite}[which]
            region = (block, slice(None), self.all_y)
        else:
            block = {1: z_ring.me, 4: z_ring.left, 6: z_ring.right, 8: z_ring.opposite}[which]
            region = (block, slice(None), self.all_z)
        part = self.full.at[region]
        return remote(part, part, self.pair_sems, which, self.pair)

    def handed(self):
        return [which for which in range(9) if which != 2 or self.with_x]

    def start(self):
        self.first_y.start()
        self.first_z.start()
        for which in (0, 1, 2) if self.with_x else (0, 1):
            self.local(which).start()

    def first_relay(self):
        self.first_y.relay()
        self.first_z.relay()
        if self.with_x:
            self.along_x.start()

    def second(self):
        self.first_y.wait_all()
        self.local(0).wait()
        self.along_y.start()
        self.hand(0).start()
        self.first_z.wait_all()
        self.local(1).wait()
        self.along_z.start()
        self.hand(1).start()

    def second_relay(self):
        if self.with_x:
            self.along_x.relay()
        self.along_y.relay()
        self.along_z.relay()

    def last(self):
        if self.with_x:
            self.along_x.wait_all()
            self.local(2).wait()
            self.hand(2).start()
        for which, (gather, wait) in enumerate(
            (gather, wait)
            for wait in ("wait_left", "wait_right", "wait_opposite")
            for gather in (self.along_y, self.along_z)
        ):
            getattr(gather, wait)()
            self.hand(3 + which).start()

    def finish(self):
        for which in self.handed():
            self.hand(which).wait_send()
        for gather in (self.first_y, self.first_z, self.along_y, self.along_z):
            gather.finish()
        if self.with_x:
            self.along_x.finish()

    def receive(self):
        for which in self.handed():
            self.hand(which).wait_recv()

    def steps(self, *names):
        @pl.when(self.owner)
        def _():
            for name in names:
                getattr(self, name)()

    def end(self):
        self.steps("last", "finish")

        @pl.when(jnp.logical_not(self.owner))
        def _():
            self.receive()


def weight_sems():
    dma = pltpu.SemaphoreType.DMA
    return [dma((3,))] + [dma((6,))] * 10 + [dma((9,))] * 2


def weights_kernel(shard_ref, gain_ref, full_ref, gain_mine, gain_theirs, *sems):
    gain_local, gain_send, gain_recv = sems[13:]
    weights = WeightGather(0, shard_ref, full_ref, (96, 96, 48, 48), sems[:13])
    x_ring = Ring("x")
    mine_x, pair = x_ring.me, sibling()
    greet_all()

    def gain_copy(which, block, src=None):
        part = gain_mine.at[block]
        target = x_ring.to_left if which == 1 else x_ring.to_right
        return remote(part if src is None else src, part, (gain_send, gain_recv), which, target)

    gain_keep = pltpu.make_async_copy(gain_ref, gain_mine.at[mine_x], gain_local.at[0])
    weights.steps("start")
    gain_keep.start()
    gain_copy(0, mine_x, gain_ref).start()
    gain_copy(1, mine_x, gain_ref).start()
    weights.steps("first_relay")
    gain_copy(0, x_ring.left).wait_recv()
    gain_copy(2, x_ring.left).start()
    weights.steps("second")
    gain_copy(1, x_ring.right).wait_recv()
    gain_copy(2, x_ring.opposite).wait_recv()
    gain_keep.wait()
    gains = remote(gain_mine, gain_theirs, (gain_send, gain_recv), 3, pair)
    gains.start()
    weights.steps("second_relay")
    weights.end()
    gains.wait()
    for which in range(3):
        gain_copy(which, mine_x).wait_send()


def gather_weights(shard, gain):
    mats, share, features = shard.shape
    gains = jax.ShapeDtypeStruct((4,) + gain.shape, LOW)
    dma = pltpu.SemaphoreType.DMA
    return pl.pallas_call(
        weights_kernel,
        out_shape=(jax.ShapeDtypeStruct((mats, 4, share, features), LOW), gains, gains),
        in_specs=[anywhere()] * 2,
        out_specs=[anywhere()] * 3,
        scratch_shapes=weight_sems() + [dma((1,)), dma((4,)), dma((4,))],
        compiler_params=pltpu.CompilerParams(collective_id=4, has_side_effects=True),
        cost_estimate=pl.CostEstimate(flops=0, bytes_accessed=30 * 10**6, transcendentals=0),
        name="gather_weights",
    )(shard, gain)


class SmallSum:
    def __init__(self, ring, slots, sems):
        self.ring, self.slots, self.sems = ring, slots, sems

    def copy(self, which, block):
        target = self.ring.to_left if which == 1 else self.ring.to_right
        part = self.slots.at[block]
        return remote(part, part, self.sems, which, target)

    def start(self):
        self.copy(0, self.ring.me).start()
        self.copy(1, self.ring.me).start()

    def relay(self):
        self.copy(0, self.ring.left).wait_recv()
        self.copy(2, self.ring.left).start()

    def result(self):
        self.copy(1, self.ring.right).wait_recv()
        self.copy(2, self.ring.opposite).wait_recv()
        return (self.slots[0] + self.slots[1]) + (self.slots[2] + self.slots[3])

    def finish(self):
        for which in range(3):
            self.copy(which, self.ring.me).wait_send()


class PlaneSum:
    def __init__(self, near, far, source, out, size, first, scratch, sems, keep, direct=False,
                 base=0):
        if direct:
            self.arrived, self.mid, self.done = scratch
        else:
            self.landing, self.passing, self.arrived, self.mid, self.done = scratch
        self.direct, self.base = direct, base
        self.out, self.size, self.near, self.far, self.keep = out, size, near, far, keep
        self.halves = ((0, first), (first, size - first))

        def rows(block, half):
            begin, count = (0, size) if half is None else self.halves[half]
            return pl.ds(pl.multiple_of(base + block * size + begin, 16), count)

        def half_rows(half):
            return pl.ds(0, size) if half is None else pl.ds(*self.halves[half])

        self.half_rows = half_rows
        def part(block, half):
            return source.at[rows(block, half)]

        if direct:
            self.scatter = DirectScatter(near, part, lambda side: self.arrived.at[side], sems[0])
        else:
            self.scatter = Scatter(
                near,
                part,
                lambda half: self.landing.at[half_rows(half)],
                lambda half: self.passing.at[half_rows(half)],
                lambda side, half: self.arrived.at[side, half_rows(half)],
                sems[0],
            )
        kind = DirectGather if direct else Gather
        self.gather = kind(far, lambda block, half: self.mid.at[block, half_rows(half)], sems[1])
        self.spread = kind(
            near,
            lambda block, half: out.at[rows(block, half)],
            sems[2],
            lambda half: self.done.at[half_rows(half)],
        )

    def start(self):
        self.scatter.start_far()
        self.scatter.start_near()

    def relay(self):
        self.scatter.relay()

    def middle(self):
        self.scatter.wait()
        if self.direct:
            self.mid[self.far.me] = self.scatter.whole().astype(LOW)
        else:
            for half in range(2):
                self.mid[self.far.me, self.half_rows(half)] = self.scatter.total(half).astype(LOW)
        self.gather.start()

    def middle_relay(self):
        self.gather.relay()

    def own(self):
        place = pl.ds(
            pl.multiple_of(self.base + self.near.me * self.size, 16), self.size
        )
        return pltpu.make_async_copy(self.done, self.out.at[place], self.keep)

    def end(self):
        self.gather.wait_all()
        four = [self.mid[block].astype(F32) for block in range(4)]
        self.done[...] = ((four[0] + four[1]) + (four[2] + four[3])).astype(LOW)
        self.spread.start()
        self.own().start()

    def end_relay(self):
        self.spread.relay()

    def wait(self):
        self.spread.wait_all()
        self.own().wait()

    def finish(self):
        self.scatter.finish()
        self.gather.finish()
        self.spread.finish()


FEED_BLOCK, AT_BLOCK = 144, 80


def feed_output(features):
    return (jax.ShapeDtypeStruct((2, 4 * FEED_BLOCK, features), LOW),)


def kept_output(features):
    return (jax.ShapeDtypeStruct((2, 4 * AT_BLOCK, features), LOW),)


def plane_scratch(size, features, direct=False):
    dma = pltpu.SemaphoreType.DMA

    def low(*shape):
        return pltpu.VMEM(shape + (features,), LOW)

    if direct:
        return [low(3, size), low(4, size), low(size)] + [dma((3,))] * 6
    return [low(size), low(size), low(2, size), low(4, size), low(size)] + [dma((6,))] * 6


def feed_scratch(features, rows):
    dma = pltpu.SemaphoreType.DMA
    return (
        [pltpu.VMEM((2, 2, 4, rows, features), LOW), pltpu.VMEM((2, 4 * FEED_BLOCK, features), LOW)]
        + plane_scratch(FEED_BLOCK, features) * 2
        + [dma((2,)), dma((2,)), dma((2,)), dma((2,)), dma((1,)), dma((1,))]
    )


def across_scratch(features, rows):
    share = features // 4
    dma = pltpu.SemaphoreType.DMA

    def low(*shape):
        return pltpu.VMEM(shape + (features,), LOW)

    return (
        [low(2, 2, rows), low(2, 2, rows), low(2, features)]
        + ([low(share), low(share), low(2, share)] + [dma((6,))] * 2) * 2
        + [dma((4,)), dma((4,)), dma((4,))]
    )


WIDE_PIECES = ((0, 0, 80, 48, 0), (1, 0, 80, 48, 1))
FINE_PIECES = ((0, 0, 48, 32, 0), (0, 192, 32, 16, 1), (1, 0, 48, 32, 1), (1, 192, 32, 16, 0))


def attention_scratch(features, pieces, direct):
    dma = pltpu.SemaphoreType.DMA
    scratch = []
    for piece in pieces:
        scratch += plane_scratch(piece[2], features, direct)
    return scratch + [dma((len(pieces),)), dma((2,)), dma((2,))]


def take_planes(take, count, direct=False):
    planes = []
    for _ in range(count):
        scratch = [next(take) for _ in range(3 if direct else 5)]
        sems = [next(take) for _ in range(6)]
        planes.append((scratch, [tuple(sems[i : i + 2]) for i in (0, 2, 4)]))
    return planes


def hand_over(layer, src, dst, sems, which=0):
    section = lax.axis_index("section")
    copy = functools.partial(remote, src, dst, sems, which, sibling())

    def start():
        @pl.when(section != layer)
        def _():
            copy().start()

    def wait():
        @pl.when(section != layer)
        def _():
            copy().wait_send()

        @pl.when(section == layer)
        def _():
            copy().wait_recv()

    return start, wait


class SwappedInputs:
    def __init__(self, zero, other, targets, local_sems, swap):
        self.zero, self.other, self.targets = zero, other, targets
        self.local_sems, self.swap, self.pair = local_sems, swap, sibling()

    def copies(self, first, which):
        own, sent = (self.zero, self.other) if first else (self.other, self.zero)
        target = self.targets[which]
        return (
            lambda: pltpu.make_async_copy(own[which], target.at[0], self.local_sems.at[which]),
            lambda: remote(sent[which], target.at[1], self.swap, which, self.pair),
        )

    def start(self):
        section = lax.axis_index("section")
        for first in (True, False):

            @pl.when(section == (0 if first else 1))
            def _(first=first):
                for which in range(len(self.targets)):
                    self.copies(first, which)[1]().start()
                for which in range(len(self.targets)):
                    self.copies(first, which)[0]().start()

    def wait(self, whiches):
        for which in whiches:
            keep, send = self.copies(True, which)
            keep().wait()
            send().wait_recv()

    def finish(self):
        for which in range(len(self.targets)):
            self.copies(True, which)[1]().wait_send()


class AttentionSum:
    def __init__(self, layer, kept, results, take, pieces, direct):
        out, other = results
        planes = take_planes(take, len(pieces), direct)
        keep, send, recv = [next(take) for _ in range(3)]
        y_ring, z_ring = Ring("y"), Ring("z")
        orders = ((y_ring, z_ring), (z_ring, y_ring))
        self.pieces = pieces
        self.planes = [
            PlaneSum(
                *orders[order], kept.at[matrix], out.at[matrix], size, first, *planes[which],
                keep.at[which], direct, base,
            )
            for which, (matrix, base, size, first, order) in enumerate(pieces)
        ]
        self.given = [
            hand_over(layer, out.at[which], other.at[which], (send, recv), which)
            for which in range(2)
        ]

    def run(self, name, matrix=None):
        for plane, piece in zip(self.planes, self.pieces):
            if matrix is None or piece[0] == matrix:
                getattr(plane, name)()

    def hand(self, matrix):
        self.run("wait", matrix)
        self.given[matrix][0]()

    def finish(self):
        self.run("finish")
        for given in self.given:
            given[1]()


class FeedSum:
    def __init__(self, features, operands, out, take):
        two, pre, hidden, out_all = operands
        self.features = features
        self.feed_in, self.feed_sum = next(take), next(take)
        planes = take_planes(take, 2)
        local_sems, swap_send, swap_recv, keep, end_send, end_recv = [
            next(take) for _ in range(6)
        ]
        self.end_sems = (end_send, end_recv)
        self.inputs = SwappedInputs(
            (two, pre), (hidden, out_all), (self.feed_in.at[0], self.feed_in.at[1]), local_sems,
            (swap_send, swap_recv),
        )
        y_ring, z_ring = Ring("y"), Ring("z")
        orders = ((y_ring, z_ring), (z_ring, y_ring))
        self.planes = [
            PlaneSum(
                *orders[which], self.feed_sum.at[which], out.at[which], FEED_BLOCK, 80,
                *planes[which], keep.at[which],
            )
            for which in range(2)
        ]

    def products(self):
        self.inputs.wait((0, 1))
        features, whole = self.features, 4 * FEED_BLOCK
        right = self.feed_in[1].reshape(-1, features)
        for begin in range(0, features, 256):
            count = min(256, features - begin)
            left = self.feed_in[0, :, :, :, pl.ds(begin, count)].reshape(-1, count)
            product = dot_tn(left, right).astype(LOW)
            first = max(0, min(count, whole - begin))
            if first:
                self.feed_sum[0, pl.ds(begin, first)] = product[:first]
            if first < count:
                self.feed_sum[1, pl.ds(begin + first - whole, count - first)] = product[first:]
        spare = 2 * whole - features
        self.feed_sum[1, pl.ds(whole - spare, spare)] = jnp.zeros((spare, features), LOW)
        self.run("start")

    def run(self, name):
        for plane in self.planes:
            getattr(plane, name)()

    def finish(self):
        self.inputs.finish()
        self.run("finish")


class AcrossSum:
    def __init__(self, features, operands, kept, take):
        one, mixed, dq, dk, dv, branch = operands
        self.features, self.share, self.kept = features, features // 4, kept
        share = self.share
        self.at_left, self.at_right, self.at_sum = [next(take) for _ in range(3)]
        self.halves = halves = ((0, 144), (144, share - 144))
        x_ring = Ring("x")
        self.across = []
        for which in range(2):
            landing, passing, arrived, send, recv = [next(take) for _ in range(5)]

            def part(block, half, which=which):
                begin, count = halves[half]
                row = pl.multiple_of(block * share + begin, 16)
                return self.at_sum.at[which, pl.ds(row, count)]

            def cut(ref):
                return lambda half: ref.at[pl.ds(*halves[half])]

            self.across.append(
                Scatter(
                    x_ring, part, cut(landing), cut(passing),
                    lambda side, half, arrived=arrived: arrived.at[side, pl.ds(*halves[half])],
                    (send, recv),
                )
            )
        local_sems, swap_send, swap_recv = [next(take) for _ in range(3)]
        self.inputs = SwappedInputs(
            (one, dq, one, dk),
            (one, dv, mixed, branch),
            (self.at_left.at[0], self.at_right.at[0], self.at_left.at[1], self.at_right.at[1]),
            local_sems,
            (swap_send, swap_recv),
        )

    def products(self, which):
        self.inputs.wait((2 * which, 2 * which + 1))
        features = self.features
        right = self.at_right[which].reshape(-1, features)
        for begin in range(0, features, 256):
            count = min(256, features - begin)
            left = self.at_left[which, :, :, pl.ds(begin, count)].reshape(-1, count)
            self.at_sum[which, pl.ds(begin, count)] = dot_tn(left, right).astype(LOW)
        self.across[which].start_far()

    def relay(self, which):
        self.across[which].relay()
        self.across[which].start_near()

    def keep(self, which):
        across = self.across[which]
        across.wait()
        for half in range(2):
            self.kept[which, pl.ds(*self.halves[half])] = across.total(half).astype(LOW)
        spare = 4 * AT_BLOCK - self.share
        self.kept[which, pl.ds(self.share, spare)] = jnp.zeros((spare, self.features), LOW)

    def finish(self):
        self.inputs.finish()
        for across in self.across:
            across.finish()


def gradient_kernel(features, *refs):
    take = iter(refs)

    def some(count):
        return [next(take) for _ in range(count)]

    operands = some(6)
    y_a, y_b, dx_a, dx_b, feed_zero, gain_in, kept_one = some(7)
    (feed_given,), at_zero, at_one = some(1), some(2), some(2)
    act_out, grad_out, gain_out = some(3)
    (kept_zero,) = some(1)
    sums = AcrossSum(features, operands, kept_zero, take)
    zero = AttentionSum(0, kept_zero, at_zero, take, FINE_PIECES, True)
    one = AttentionSum(1, kept_one, at_one, take, WIDE_PIECES, False)
    (gain_pair, gain_x, gain_y, gain_z, gain_send, gain_recv, last_send, last_recv, keep_sems,
     feed_send, feed_recv) = some(11)
    x_ring, y_ring, z_ring = Ring("x"), Ring("y"), Ring("z")
    pair, section = sibling(), lax.axis_index("section")
    greet_all(far=True)
    sums.inputs.start()
    feed = hand_over(0, feed_zero, feed_given, (feed_send, feed_recv))

    def last_copies(y, dx):
        return (
            remote(y, act_out.at[section], (last_send, last_recv), 0, pair),
            remote(dx, grad_out.at[section], (last_send, last_recv), 1, pair),
        )

    def keep_copies(y, dx):
        return (
            pltpu.make_async_copy(y, act_out.at[section], keep_sems.at[0]),
            pltpu.make_async_copy(dx, grad_out.at[section], keep_sems.at[1]),
        )

    @pl.when(section == 0)
    def _():
        for copy in last_copies(y_b, dx_b) + keep_copies(y_a, dx_a):
            copy.start()

    @pl.when(section == 1)
    def _():
        for copy in last_copies(y_a, dx_a) + keep_copies(y_b, dx_b):
            copy.start()

    gain_pair[0] = gain_in[...]
    swap_gain = remote(gain_pair.at[0], gain_pair.at[1], (gain_send, gain_recv), 9, pair)
    swap_gain.start()
    one.run("start")
    sums.products(0)
    sums.products(1)
    feed[0]()
    swap_gain.wait()
    gain_x[x_ring.me] = gain_pair[0] + gain_pair[1]
    small = [
        SmallSum(ring, slots, (gain_send.at[pl.ds(3 * i, 3)], gain_recv.at[pl.ds(3 * i, 3)]))
        for i, (ring, slots) in enumerate(((x_ring, gain_x), (y_ring, gain_y), (z_ring, gain_z)))
    ]
    small[0].start()
    one.run("relay")
    sums.relay(0)
    small[0].relay()
    one.run("middle")
    gain_y[y_ring.me] = small[0].result()
    small[1].start()
    one.run("middle_relay")
    small[1].relay()
    sums.keep(0)
    sums.relay(1)
    zero.run("start", 0)
    one.run("end")
    gain_z[z_ring.me] = small[1].result()
    small[2].start()
    zero.run("middle", 0)
    one.run("end_relay")
    small[2].relay()
    zero.run("end", 0)
    gain_out[...] = small[2].result()
    sums.keep(1)
    zero.run("start", 1)
    one.hand(0)
    one.hand(1)
    zero.hand(0)
    zero.run("middle", 1)
    zero.run("end", 1)
    zero.hand(1)
    zero.finish()
    one.finish()
    sums.finish()
    feed[1]()
    for each in small:
        each.finish()
    for copy in last_copies(y_a, dx_a) + keep_copies(y_a, dx_a):
        copy.wait()


def sum_gradients(features, rows, operands, last, gain, kept):
    dma = pltpu.SemaphoreType.DMA
    small = [pltpu.VMEM((4, 8, features), F32)] * 3
    return pl.pallas_call(
        functools.partial(gradient_kernel, features),
        out_shape=feed_output(features)
        + kept_output(features) * 4
        + (
            jax.ShapeDtypeStruct((2, rows, features), LOW),
            jax.ShapeDtypeStruct((2, rows, features), LOW),
            jax.ShapeDtypeStruct((8, features), F32),
        ),
        in_specs=[anywhere()] * 11 + [in_vmem()] * 2,
        out_specs=[anywhere()] * 7 + [in_vmem()],
        scratch_shapes=[pltpu.VMEM((2, 4 * AT_BLOCK, features), LOW)]
        + across_scratch(features, rows)
        + attention_scratch(features, FINE_PIECES, True)
        + attention_scratch(features, WIDE_PIECES, False)
        + [pltpu.VMEM((2, 8, features), F32)]
        + small
        + [dma((10,)), dma((10,)), dma((2,)), dma((2,)), dma((2,)), dma((1,)), dma((1,))],
        compiler_params=pltpu.CompilerParams(
            collective_id=5, has_side_effects=True, vmem_limit_bytes=60 * 2**20
        ),
        cost_estimate=pl.CostEstimate(
            flops=3 * 10**9, bytes_accessed=60 * 10**6, transcendentals=0
        ),
        name="sum_gradients",
    )(*operands, *last, gain, kept)


def doc_numbers(lengths, positions):
    doc_ends = jnp.cumsum(lengths)
    return jnp.sum((positions[:, None] >= doc_ends[None, :]).astype(jnp.int32), axis=1)


def swapped(block):
    return lax.ppermute(block, "section", [(0, 1), (1, 0)])


def body(tokens, cotangent, doc_lengths, norm_gains, w_qkv, w_out, w_up, w_down):
    batches, rows, features = tokens.shape
    share = w_qkv.shape[1]
    seq_rows = rows * lax.axis_size("tensor")
    section = lax.axis_index("section")
    is_first = section == 0

    def choose(zero_side, one_side):
        return jnp.where(is_first, zero_side, one_side)

    own_tokens = lax.dynamic_index_in_dim(tokens, section, 0, keepdims=False)
    own_cotangent = lax.dynamic_index_in_dim(cotangent, section, 0, keepdims=False)
    lengths = lax.dynamic_index_in_dim(doc_lengths, section, 0, keepdims=False)
    own_places = lax.axis_index("tensor") * rows + jnp.arange(rows, dtype=jnp.int32)
    all_places = jnp.arange(seq_rows, dtype=jnp.int32)
    own_docs = doc_numbers(lengths, own_places)
    all_docs = doc_numbers(lengths, all_places)
    allowed = (all_places[None, :] <= own_places[:, None]) & (
        all_docs[None, :] == own_docs[:, None]
    )
    bias = jnp.where(allowed, 0.0, -1e30).astype(F32)
    bias_turned = bias.T

    feed = (w_up[0], swapped(w_up[0]), w_down[0], swapped(w_down[0]))
    shard = jnp.stack(
        [w_qkv[0, :, :features], w_qkv[0, :, features : 2 * features], w_qkv[0, :, 2 * features :],
         w_out[0]]
    )
    gain_shard = jnp.pad(norm_gains[0], ((0, 14), (0, 0)))
    at_zero, gain_mine, gain_theirs = gather_weights(shard, gain_shard)
    attention = [at_zero.reshape(4, features, features), None]

    def whole_gains(block):
        return block[:, :2].transpose(1, 0, 2).reshape(2, features).astype(F32)

    gain_mine, gain_theirs = whole_gains(gain_mine), whole_gains(gain_theirs)
    gains = (choose(gain_mine, gain_theirs), choose(gain_theirs, gain_mine))

    inputs = own_tokens
    saved = []
    for layer in range(2):
        results = forward_layer(
            layer, inputs, bias, gains[layer], attention[layer], feed,
            (shard,) if layer == 0 else (),
        )
        if layer == 0:
            attention[1] = results[10].reshape(4, features, features)
        saved.append((inputs,) + tuple(results[:10]))
        inputs = results[0]

    grad = own_cotangent
    gain_grads, input_grads, operands = [None, None], [None, None], ()
    for layer in (1, 0):
        (x, _, middle, normed_one, query, key, value, mixed, normed_two, act, hidden) = saved[layer]
        results = backward_layer(
            layer, x, grad, bias_turned, gains[layer], middle, query, key, value, act,
            attention[layer], feed, operands + (saved[0][8], saved[0][10]) if layer == 0 else (),
        )
        (grad, gain_grads[layer], out_all, pre_grad, branch, dquery, dkey, dvalue) = results[:8]
        input_grads[layer] = grad
        operands = (
            normed_two, pre_grad, hidden, out_all, normed_one, mixed, dquery, dkey, dvalue, branch,
        )
    feed_one, feed_one_given, feed_zero, kept_one = results[8:]
    gain_rows = jnp.concatenate(gain_grads + [jnp.zeros((4, features), F32)], axis=0)
    (feed_zero_given, at_zero, at_zero_given, at_one, at_one_given, activations, input_grads,
     gain_total) = sum_gradients(
        features, rows, operands[4:], (saved[0][1], saved[1][1], *input_grads, feed_zero),
        gain_rows, kept_one,
    )
    gain_own = lax.dynamic_slice(
        gain_total, (2 * section, lax.axis_index("tensor") * share), (2, share)
    )

    def whole(block):
        return block.reshape(-1, features)[:features].astype(F32)[None]

    first_half = choose(at_zero, at_one_given)[:, :share].astype(F32)
    other_half = choose(at_zero_given, at_one)[:, :share].astype(F32)
    grad_qkv = jnp.concatenate([first_half[0], first_half[1], other_half[0]], axis=1)
    return (
        activations[None],
        input_grads[None],
        gain_own[None],
        grad_qkv[None],
        other_half[1][None],
        whole(choose(feed_zero, feed_one_given)),
        whole(choose(feed_zero_given, feed_one)),
    )


def solution(mesh):
    placed = (
        P("dp", "tensor", None),
        P("dp", "tensor", None),
        P("dp", None),
        P("section", None, "tensor"),
        P("section", "tensor", None),
        P("section", "tensor", None),
        P("section", None, "tensor"),
        P("section", "tensor", None),
    )
    return jax.shard_map(
        body,
        mesh=mesh,
        in_specs=placed,
        out_specs=(
            P("section", "dp", "tensor", None),
            P("section", "dp", "tensor", None),
            P("section", None, "tensor"),
            P("section", "tensor", None),
            P("section", "tensor", None),
            P("section", None, "tensor"),
            P("section", "tensor", None),
        ),
        check_vma=False,
    )
```

```python
import functools
import jax
import jax.numpy as jnp
from jax import lax
from jax.experimental import pallas as pl
from jax.experimental.pallas import tpu as pltpu
from jax.sharding import PartitionSpec as P

HEAD_DIM = 64
LOW = jnp.bfloat16
F32 = jnp.float32
MESH = pl.DeviceIdType.MESH


def dot_nn(left, right):
    return lax.dot_general(left, right, (((1,), (0,)), ((), ())), preferred_element_type=F32)


def dot_nt(left, right):
    return lax.dot_general(left, right, (((1,), (1,)), ((), ())), preferred_element_type=F32)


def dot_tn(left, right):
    return lax.dot_general(left, right, (((0,), (0,)), ((), ())), preferred_element_type=F32)


class Ring:
    def __init__(self, axis):
        whole = lax.axis_index("dp")
        rest = None
        if axis == "x":
            self.me = lax.axis_index("tensor")
        elif axis == "y":
            self.me, rest = lax.rem(whole, 4), lax.div(whole, 4) * 4
        else:
            self.me, rest = lax.div(whole, 4), lax.rem(whole, 4)
        self.right = lax.rem(self.me + 1, 4)
        self.left = lax.rem(self.me + 3, 4)
        self.opposite = lax.rem(self.me + 2, 4)

        def device(place):
            if axis == "x":
                return {"tensor": place}
            if axis == "y":
                return {"dp": rest + place}
            return {"dp": place * 4 + rest}

        self.to_right, self.to_left = device(self.right), device(self.left)
        self.to_opposite = device(self.opposite)


def sibling():
    return {"section": 1 - lax.axis_index("section")}


def greet(*targets):
    barrier = pltpu.get_barrier_semaphore()
    for target in targets:
        pl.semaphore_signal(barrier, inc=1, device_id=target, device_id_type=MESH)
    pl.semaphore_wait(barrier, len(targets))


def remote(src, dst, sems, which, target):
    return pltpu.make_async_remote_copy(
        src_ref=src,
        dst_ref=dst,
        send_sem=sems[0].at[which],
        recv_sem=sems[1].at[which],
        device_id=target,
        device_id_type=MESH,
    )


class Gather:
    def __init__(self, ring, slot, sems, own=None):
        self.ring, self.slot, self.sems = ring, slot, sems
        self.own = own if own is not None else lambda half: slot(ring.me, half)

    def copy(self, which, arriving=False):
        ring = self.ring
        half = (0, 1, 1, 0, 0, 1)[which]
        goes_right = which in (0, 2, 4)
        target = ring.to_right if goes_right else ring.to_left
        if which < 4:
            source_block = ring.left if goes_right else ring.right
            if not arriving:
                return remote(self.own(half), self.slot(ring.me, half), self.sems, which, target)
        else:
            source_block = ring.opposite
            if not arriving:
                handed = self.slot(ring.left if goes_right else ring.right, half)
                return remote(handed, handed, self.sems, which, target)
        part = self.slot(source_block, half)
        return remote(part, part, self.sems, which, target)

    def start(self):
        for which in range(4):
            self.copy(which).start()

    def relay(self):
        for which in (0, 1):
            self.copy(which, arriving=True).wait_recv()
            self.copy(which + 4).start()

    def wait_left(self):
        self.copy(2, arriving=True).wait_recv()

    def wait_right(self):
        self.copy(3, arriving=True).wait_recv()

    def wait_opposite(self):
        self.copy(4, arriving=True).wait_recv()
        self.copy(5, arriving=True).wait_recv()

    def wait_all(self):
        self.wait_left()
        self.wait_right()
        self.wait_opposite()

    def finish(self):
        for which in range(6):
            self.copy(which).wait_send()


class Scatter:
    def __init__(self, ring, part, landing, passing, arrived, sems):
        self.ring, self.part, self.landing, self.passing = ring, part, landing, passing
        self.arrived, self.sems = arrived, sems

    def copy(self, which):
        ring = self.ring
        half = (0, 1, 1, 0, 0, 1)[which]
        goes_right = which in (0, 2, 4)
        if which < 2:
            src, dst = self.part(ring.opposite, half), self.landing(half)
        else:
            dst = self.arrived(0 if goes_right else 1, half)
            if which < 4:
                src = self.part(ring.right if goes_right else ring.left, half)
            else:
                src = self.passing(half)
        return remote(src, dst, self.sems, which, ring.to_right if goes_right else ring.to_left)

    def start_near(self):
        self.copy(2).start()
        self.copy(3).start()

    def start_far(self):
        self.copy(0).start()
        self.copy(1).start()

    def relay(self):
        for half, block in ((0, self.ring.right), (1, self.ring.left)):
            self.copy(half).wait_recv()
            added = self.part(block, half)[...].astype(F32) + self.landing(half)[...].astype(F32)
            self.passing(half)[...] = added.astype(LOW)
            self.copy(half + 4).start()

    def wait(self):
        for which in (2, 3, 4, 5):
            self.copy(which).wait_recv()

    def total(self, half):
        return (
            self.part(self.ring.me, half)[...].astype(F32)
            + self.arrived(0, half)[...].astype(F32)
            + self.arrived(1, half)[...].astype(F32)
        )

    def finish(self):
        for which in range(6):
            self.copy(which).wait_send()


class DirectGather:
    def __init__(self, ring, slot, sems, own=None):
        self.ring, self.slot, self.sems = ring, slot, sems
        self.own = own if own is not None else lambda half: slot(ring.me, half)

    def copy(self, which):
        target = (self.ring.to_right, self.ring.to_left, self.ring.to_opposite)[which]
        return remote(self.own(None), self.slot(self.ring.me, None), self.sems, which, target)

    def start(self):
        for which in (2, 0, 1):
            self.copy(which).start()

    def relay(self):
        pass

    def wait_all(self):
        for which, block in enumerate((self.ring.left, self.ring.right, self.ring.opposite)):
            part = self.slot(block, None)
            remote(part, part, self.sems, which, self.ring.to_right).wait_recv()

    def finish(self):
        for which in range(3):
            self.copy(which).wait_send()


class DirectScatter:
    def __init__(self, ring, part, arrived, sems):
        self.ring, self.part, self.arrived, self.sems = ring, part, arrived, sems

    def copy(self, which):
        ring = self.ring
        block = (ring.right, ring.left, ring.opposite)[which]
        target = (ring.to_right, ring.to_left, ring.to_opposite)[which]
        return remote(self.part(block, None), self.arrived(which), self.sems, which, target)

    def start_far(self):
        self.copy(2).start()

    def start_near(self):
        self.copy(0).start()
        self.copy(1).start()

    def relay(self):
        pass

    def wait(self):
        for which in range(3):
            self.copy(which).wait_recv()

    def whole(self):
        near = self.arrived(0)[...].astype(F32) + self.arrived(1)[...].astype(F32)
        own = self.part(self.ring.me, None)[...].astype(F32)
        return (own + near) + self.arrived(2)[...].astype(F32)

    def finish(self):
        for which in range(3):
            self.copy(which).wait_send()


def row_gather(ring, full, sems, columns=slice(None)):
    half = full.shape[1] // 2
    return Gather(
        ring, lambda block, which: full.at[block, pl.ds(which * half, half), columns], sems
    )


def row_scatter(ring, parts, landing, passing, arrived, sems, columns=slice(None)):
    half = parts.shape[1] // 2

    def rows(which):
        return pl.ds(which * half, half)

    return Scatter(
        ring,
        lambda block, which: parts.at[block, rows(which), columns],
        lambda which: landing.at[which, :, columns],
        lambda which: passing.at[which, :, columns],
        lambda side, which: arrived.at[side, rows(which), columns],
        sems,
    )


def row_total(scatter):
    scatter.wait()
    return jnp.concatenate([scatter.total(0), scatter.total(1)], axis=0)


def head_groups(features):
    pairs = pair_columns(features)
    middle = (len(pairs) + 1) // 2
    begin = pairs[middle][0]
    return (
        (pl.ds(0, begin), pairs[:middle]),
        (pl.ds(begin, features - begin), pairs[middle:]),
    )


def norm_stats(values):
    average = jnp.mean(values, axis=-1, keepdims=True)
    centered = values - average
    variance = jnp.mean(centered * centered, axis=-1, keepdims=True)
    scale = lax.rsqrt(variance + 1e-05)
    return centered * scale, scale


def norm_back(values, gain, grad):
    xhat, scale = norm_stats(values)
    scaled = grad * gain
    part = scale * (
        scaled
        - jnp.mean(scaled, axis=-1, keepdims=True)
        - xhat * jnp.mean(scaled * xhat, axis=-1, keepdims=True)
    )
    return part, jnp.sum(grad * xhat, axis=0, keepdims=True)


def gelu_tanh(values):
    inner = 0.7978845608028654 * (values + 0.044715 * values * values * values)
    return 0.5 * values * (1.0 + jnp.tanh(inner))


def gelu_slope(values):
    square = values * values
    bent = jnp.tanh(0.7978845608028654 * values * (1.0 + 0.044715 * square))
    slope = 0.7978845608028654 * (1.0 + 3.0 * 0.044715 * square)
    return 0.5 * (1.0 + bent) + 0.5 * values * (1.0 - bent * bent) * slope


def pick_copies(layer, mine, theirs, target, sem):
    def start():
        mine_here = lax.axis_index("section") == layer

        @pl.when(mine_here)
        def _():
            pltpu.make_async_copy(mine, target, sem).start()

        @pl.when(jnp.logical_not(mine_here))
        def _():
            pltpu.make_async_copy(theirs, target, sem).start()

    def wait():
        pltpu.make_async_copy(mine, target, sem).wait()

    return start, wait


def pair_columns(features):
    width = 2 * HEAD_DIM
    return [
        (start, min(width, features - start)) for start in range(0, features, width)
    ]


def head_masks(width):
    lanes = lax.broadcasted_iota(jnp.int32, (1, width), 1)
    if width == HEAD_DIM:
        return [None]
    return [lanes < HEAD_DIM, lanes >= HEAD_DIM]


def masked(values, mask):
    return values if mask is None else jnp.where(mask, values, jnp.zeros_like(values))


def plain_copy(src, target, sem):
    copy = functools.partial(pltpu.make_async_copy, src, target, sem)
    return lambda: copy().start(), lambda: copy().wait()


def forward_kernel(layer, features, *refs):
    take = iter(refs)

    def some(count):
        return [next(take) for _ in range(count)]

    (x_ref, bias_ref, gains_ref, at_full, up_mine, up_theirs, down_mine, down_theirs) = some(8)
    shard_ref = next(take) if layer == 0 else None
    (y_ref, middle_ref, one_ref, query_ref, key_ref, value_ref, mixed_ref, two_ref, act_ref,
     hidden_ref) = some(10)
    next_ref = next(take) if layer == 0 else None
    (at_w, up_w, down_w, weight_sems_, parts, landing, passing, arrived,
     key_send, key_recv, value_send, value_recv, two_send, two_recv, sum_send, sum_recv) = some(16)
    ring = Ring("x")
    me = ring.me
    fetches = [
        plain_copy(at_full.at[which], at_w.at[which], weight_sems_.at[which]) for which in range(4)
    ]
    fetches.append(pick_copies(layer, up_mine, up_theirs, up_w, weight_sems_.at[4]))
    fetches.append(pick_copies(layer, down_mine, down_theirs, down_w, weight_sems_.at[5]))
    for which in (1, 2, 0, 3, 4, 5):
        fetches[which][0]()
    if layer == 0:
        following = WeightGather(1, shard_ref, next_ref, (0, 144, 80, 64), some(13))
        greet_all()
    else:
        greet(ring.to_right, ring.to_left)

    def steps(*names):
        if layer == 0:
            following.steps(*names)

    rows = x_ref.shape[0]
    inputs = x_ref[...].astype(F32)
    xhat, _ = norm_stats(inputs)
    one_ref[...] = (xhat * gains_ref[0:1, :]).astype(LOW)
    normed_one = one_ref[...]
    groups = head_groups(features)
    keys, values = [], []
    fetches[1][1]()
    fetches[2][1]()
    for which, (columns, _) in enumerate(groups):
        key_ref[me, :, columns] = dot_nn(normed_one, at_w[1, :, columns]).astype(LOW)
        keys.append(
            row_gather(ring, key_ref, (key_send.at[which], key_recv.at[which]), columns)
        )
        if which == 0:
            keys[0].start()
        value_ref[me, :, columns] = dot_nn(normed_one, at_w[2, :, columns]).astype(LOW)
        values.append(
            row_gather(ring, value_ref, (value_send.at[which], value_recv.at[which]), columns)
        )
        if which == 0:
            values[0].start()
            steps("start")
    fetches[0][1]()
    query_ref[...] = dot_nn(normed_one, at_w[0]).astype(LOW)
    keys[0].relay()
    values[0].relay()
    keys[1].start()
    values[1].start()
    steps("first_relay")
    bias = bias_ref[...]

    def attend(begin, width):
        columns = pl.ds(begin, width)
        queries = query_ref[:, columns]
        key_block = key_ref[:, :, columns].reshape(4 * rows, width)
        value_block = value_ref[:, :, columns].reshape(4 * rows, width)
        mixed = None
        for mask in head_masks(width):
            scores = dot_nt(masked(queries, mask), key_block) * 0.125 + bias
            raised = jnp.exp(scores - jnp.max(scores, axis=-1, keepdims=True))
            probs = raised * (1.0 / jnp.sum(raised, axis=-1, keepdims=True))
            own = dot_nn(probs.astype(LOW), value_block)
            mixed = own if mixed is None else jnp.where(mask, own, mixed)
        mixed_ref[:, columns] = mixed.astype(LOW)

    for which, (_, pairs) in enumerate(groups):
        keys[which].wait_all()
        values[which].wait_all()
        for count, (begin, width) in enumerate(pairs):
            attend(begin, width)
            if which == 0 and count == 2:
                keys[1].relay()
                values[1].relay()
                steps("second")
    fetches[3][1]()
    middle_ref[...] = x_ref[...].astype(F32) + dot_nn(mixed_ref[...], at_w[3])
    xhat, _ = norm_stats(middle_ref[...])
    two_ref[me] = (xhat * gains_ref[1:2, :]).astype(LOW)
    tokens = row_gather(ring, two_ref, (two_send, two_recv))
    tokens.start()
    fetches[4][1]()
    fetches[5][1]()
    sums = row_scatter(ring, parts, landing, passing, arrived, (sum_send, sum_recv))

    def feed(block):
        act_ref[block] = dot_nn(two_ref[block], up_w[...])
        hidden_ref[block] = gelu_tanh(act_ref[block]).astype(LOW)
        parts[block] = dot_nn(hidden_ref[block], down_w[...]).astype(LOW)

    feed(me)
    tokens.relay()
    tokens.wait_left()
    feed(ring.left)
    tokens.wait_right()
    feed(ring.right)
    sums.start_near()
    tokens.wait_opposite()
    feed(ring.opposite)
    sums.start_far()
    sums.relay()
    steps("second_relay")
    y_ref[...] = (middle_ref[...] + row_total(sums)).astype(LOW)
    for gather in keys + values:
        gather.finish()
    tokens.finish()
    sums.finish()
    if layer == 0:
        following.end()


def scatter_scratch(rows, features):
    return [
        pltpu.VMEM((4, rows, features), LOW),
        pltpu.VMEM((2, rows // 2, features), LOW),
        pltpu.VMEM((2, rows // 2, features), LOW),
        pltpu.VMEM((2, rows, features), LOW),
    ]


def weight_scratch(features, hidden, matrices=4):
    shape = (features, features) if matrices == 1 else (matrices, features, features)
    return [
        pltpu.VMEM(shape, LOW),
        pltpu.VMEM((features, hidden), LOW),
        pltpu.VMEM((hidden, features), LOW),
        pltpu.SemaphoreType.DMA((6,)),
    ]


def in_vmem():
    return pl.BlockSpec(memory_space=pltpu.VMEM)


def anywhere():
    return pl.BlockSpec(memory_space=pl.ANY)


def forward_layer(layer, x, bias, gains, attention, feed, shard=()):
    rows, features = x.shape
    hidden = feed[0].shape[1]
    out_shape = (
        jax.ShapeDtypeStruct((rows, features), LOW),
        jax.ShapeDtypeStruct((rows, features), F32),
        jax.ShapeDtypeStruct((rows, features), LOW),
        jax.ShapeDtypeStruct((rows, features), LOW),
        jax.ShapeDtypeStruct((4, rows, features), LOW),
        jax.ShapeDtypeStruct((4, rows, features), LOW),
        jax.ShapeDtypeStruct((rows, features), LOW),
        jax.ShapeDtypeStruct((4, rows, features), LOW),
        jax.ShapeDtypeStruct((4, rows, hidden), F32),
        jax.ShapeDtypeStruct((4, rows, hidden), LOW),
    )
    following = (
        (jax.ShapeDtypeStruct((4, 4, features // 4, features), LOW),) if layer == 0 else ()
    )
    return pl.pallas_call(
        functools.partial(forward_kernel, layer, features),
        out_shape=out_shape + following,
        in_specs=[in_vmem()] * 3 + [anywhere()] * 5 + [in_vmem()] * len(shard),
        out_specs=[in_vmem()] * len(out_shape) + [anywhere()] * len(following),
        scratch_shapes=weight_scratch(features, hidden)
        + scatter_scratch(rows, features)
        + [pltpu.SemaphoreType.DMA((2, 6))] * 4
        + [pltpu.SemaphoreType.DMA((6,))] * 4
        + (weight_sems() if layer == 0 else []),
        compiler_params=pltpu.CompilerParams(
            collective_id=layer, has_side_effects=True, vmem_limit_bytes=56 * 2**20
        ),
        cost_estimate=pl.CostEstimate(
            flops=3 * 10**9, bytes_accessed=24 * 10**6, transcendentals=10**6
        ),
        name=f"layer_forward_{layer}",
    )(x, bias, gains, attention, *feed, *shard)


def backward_kernel(layer, features, *refs):
    take = iter(refs)

    def some(count):
        return [next(take) for _ in range(count)]

    (x_ref, dy_ref, bias_ref, gains_ref, middle_ref, query_ref, key_ref, value_ref, act_ref,
     at_full, up_mine, up_theirs, down_mine, down_theirs) = some(14)
    operands = some(12) if layer == 0 else None
    (dx_ref, gain_ref, out_ref, pre_ref, branch_ref, dquery_ref, dkey_ref, dvalue_ref) = some(8)
    results = some(4) if layer == 0 else None
    (at_w, up_w, down_w, weight_sems, parts, landing, passing, arrived, parts_b, landing_b,
     passing_b, arrived_b, parts_c, landing_c, passing_c, arrived_c, mixed_grad, kept_grad,
     out_send, out_recv, sum_send, sum_recv, key_send, key_recv, value_send, value_recv) = some(26)
    extra = layer == 0
    if extra:
        (two, pre, hidden, out_all, one, mixed, dq, dk, dv, branch, two_own, hidden_own) = operands
        feed_out, feed_given, feed_own_out, kept = results
        feed_one = FeedSum(features, (two, pre, hidden, out_all), feed_out, take)
        feed_own = FeedSum(
            features, (two_own, pre_ref, hidden_own, out_ref), feed_own_out, take
        )
        across = AcrossSum(features, (one, mixed, dq, dk, dv, branch), kept, take)
        given = hand_over(1, feed_out, feed_given, feed_one.end_sems)
    ring = Ring("x")
    me = ring.me
    fetches = [
        plain_copy(at_full.at[which], target, weight_sems.at[which])
        for which, target in enumerate((up_w, down_w, at_w, at_w))
    ]
    fetches.append(pick_copies(layer, up_mine, up_theirs, up_w, weight_sems.at[4]))
    fetches.append(pick_copies(layer, down_mine, down_theirs, down_w, weight_sems.at[5]))
    for which in (5, 4, 3):
        fetches[which][0]()
    rows = x_ref.shape[0]
    out_ref[me] = dy_ref[...]
    if not extra:
        greet(ring.to_right, ring.to_left)
    else:
        greet_all()
    grads = row_gather(ring, out_ref, (out_send, out_recv))
    grads.start()
    if extra:
        across.inputs.start()
        feed_one.inputs.start()
    sums = row_scatter(ring, parts, landing, passing, arrived, (sum_send, sum_recv))
    fetches[5][1]()
    fetches[4][1]()

    def feed(block):
        hidden_grad = dot_nt(out_ref[block], down_w[...])
        pre_ref[block] = (hidden_grad * gelu_slope(act_ref[block])).astype(LOW)
        parts[block] = dot_nt(pre_ref[block], up_w[...]).astype(LOW)

    feed(me)
    grads.relay()
    if extra:
        across.products(0)
        feed_one.products()
    grads.wait_left()
    feed(ring.left)
    grads.wait_right()
    feed(ring.right)
    sums.start_near()
    grads.wait_opposite()
    feed(ring.opposite)
    sums.start_far()
    for which in (0, 1):
        fetches[which][0]()
    if extra:
        feed_own.inputs.start()
        feed_one.run("relay")
    sums.relay()
    if extra:
        across.products(1)
    middle_part, gain_two = norm_back(middle_ref[...], gains_ref[1:2, :], row_total(sums))
    gain_ref[1:2, :] = gain_two
    middle_grad = dy_ref[...].astype(F32) + middle_part
    kept_grad[...] = middle_grad
    branch_ref[...] = middle_grad.astype(LOW)
    fetches[3][1]()
    mixed_grad[...] = dot_nt(branch_ref[...], at_w[...]).astype(LOW)
    fetches[2][0]()
    bias = bias_ref[...]
    groups = head_groups(features)
    dkeys = [
        row_scatter(ring, parts_b, landing_b, passing_b, arrived_b,
                    (key_send.at[which], key_recv.at[which]), columns)
        for which, (columns, _) in enumerate(groups)
    ]
    dvalues = [
        row_scatter(ring, parts_c, landing_c, passing_c, arrived_c,
                    (value_send.at[which], value_recv.at[which]), columns)
        for which, (columns, _) in enumerate(groups)
    ]

    def send_pair(which):
        for scatter in (dkeys[which], dvalues[which]):
            scatter.start_far()
        for scatter in (dkeys[which], dvalues[which]):
            scatter.start_near()

    def relay_pair(which):
        for scatter in (dkeys[which], dvalues[which]):
            scatter.relay()

    for count, (begin, width) in enumerate(pair_columns(features)):
        columns = pl.ds(begin, width)
        queries = query_ref[:, columns]
        outer = mixed_grad[:, columns]
        key_block = key_ref[:, :, columns].reshape(4 * rows, width)
        value_block = value_ref[:, :, columns].reshape(4 * rows, width)
        dquery = dkey = dvalue = None
        for mask in head_masks(width):
            query_one, outer_one = masked(queries, mask), masked(outer, mask)
            scores = dot_nt(key_block, query_one) * 0.125 + bias
            raised = jnp.exp(scores - jnp.max(scores, axis=0, keepdims=True))
            probs = raised * (1.0 / jnp.sum(raised, axis=0, keepdims=True))
            probs_grad = dot_nt(value_block, outer_one)
            mean = jnp.sum(probs * probs_grad, axis=0, keepdims=True)
            score_grad = (probs * (probs_grad - mean)).astype(LOW)
            own_query = dot_tn(score_grad, key_block)
            own_key = dot_nn(score_grad, query_one)
            own_value = dot_nn(probs.astype(LOW), outer_one)
            if dquery is None:
                dquery, dkey, dvalue = own_query, own_key, own_value
            else:
                dquery = jnp.where(mask, own_query, dquery)
                dkey, dvalue = dkey + own_key, dvalue + own_value
        dquery_ref[:, columns] = (dquery * 0.125).astype(LOW)
        parts_b[:, :, columns] = (dkey * 0.125).astype(LOW).reshape(4, rows, width)
        parts_c[:, :, columns] = dvalue.astype(LOW).reshape(4, rows, width)
        if begin + width == groups[0][0].size:
            send_pair(0)
        if extra and count == 1:
            feed_one.run("middle")
            across.relay(0)
        if extra and count == 4:
            feed_own.products()
            feed_one.run("middle_relay")
        if extra and count == 7:
            feed_own.run("relay")
    relay_pair(0)
    send_pair(1)
    for which in (0, 1, 2):
        fetches[which][1]()
    one_grad = dot_nt(dquery_ref[...], up_w[...])
    if extra:
        feed_one.run("end")
    relay_pair(1)
    if extra:
        across.relay(1)
        feed_own.run("middle")
        feed_one.run("end_relay")
    for which, (columns, _) in enumerate(groups):
        dkey_ref[:, columns] = row_total(dkeys[which]).astype(LOW)
    one_grad = one_grad + dot_nt(dkey_ref[...], down_w[...])
    if extra:
        across.keep(0)
        feed_own.run("middle_relay")
    for which, (columns, _) in enumerate(groups):
        dvalue_ref[:, columns] = row_total(dvalues[which]).astype(LOW)
    one_grad = one_grad + dot_nt(dvalue_ref[...], at_w[...])
    inputs_part, gain_one = norm_back(x_ref[...].astype(F32), gains_ref[0:1, :], one_grad)
    gain_ref[0:1, :] = gain_one
    dx_ref[...] = (kept_grad[...] + inputs_part).astype(LOW)
    if extra:
        feed_one.run("wait")
        given[0]()
        feed_own.run("end")
        across.keep(1)
        feed_own.run("end_relay")
        feed_one.finish()
        across.finish()
        given[1]()
        feed_own.run("wait")
        feed_own.finish()
    grads.finish()
    sums.finish()
    for scatter in dkeys + dvalues:
        scatter.finish()


def greet_all(far=False):
    rings = [Ring(axis) for axis in ("x", "y", "z")]
    greet(
        *[ring.to_right for ring in rings], *[ring.to_left for ring in rings], sibling(),
        *[ring.to_opposite for ring in rings[1:] if far],
    )


def backward_layer(layer, x, dy, bias, gains, middle, query, key, value, act, attention, feed,
                   operands=()):
    rows, features = x.shape
    hidden = feed[0].shape[1]
    out_shape = (
        jax.ShapeDtypeStruct((rows, features), LOW),
        jax.ShapeDtypeStruct((2, features), F32),
        jax.ShapeDtypeStruct((4, rows, features), LOW),
        jax.ShapeDtypeStruct((4, rows, hidden), LOW),
        jax.ShapeDtypeStruct((rows, features), LOW),
        jax.ShapeDtypeStruct((rows, features), LOW),
        jax.ShapeDtypeStruct((rows, features), LOW),
        jax.ShapeDtypeStruct((rows, features), LOW),
    )
    sums = feed_output(features) * 3 + kept_output(features) if layer == 0 else ()
    return pl.pallas_call(
        functools.partial(backward_kernel, layer, features),
        out_shape=out_shape + sums,
        in_specs=[in_vmem()] * 9 + [anywhere()] * (5 + len(operands)),
        out_specs=[in_vmem()] * len(out_shape) + [anywhere()] * 3 * (len(sums) // 4)
        + [in_vmem()] * (len(sums) // 4),
        scratch_shapes=weight_scratch(features, hidden, 1)
        + scatter_scratch(rows, features) * 3
        + [pltpu.VMEM((rows, features), LOW), pltpu.VMEM((rows, features), F32)]
        + [pltpu.SemaphoreType.DMA((6,))] * 4
        + [pltpu.SemaphoreType.DMA((2, 6))] * 4
        + (
            feed_scratch(features, rows) * 2 + across_scratch(features, rows)
            if layer == 0
            else []
        ),
        compiler_params=pltpu.CompilerParams(
            collective_id=2 + layer, has_side_effects=True, vmem_limit_bytes=62 * 2**20
        ),
        cost_estimate=pl.CostEstimate(
            flops=4 * 10**9, bytes_accessed=24 * 10**6, transcendentals=10**6
        ),
        name=f"layer_backward_{layer}",
    )(x, dy, bias, gains, middle, query, key, value, act, attention, *feed, *operands)


class WeightGather:
    def __init__(self, layer, shard, full, split, sems):
        self.layer, self.full = layer, full
        self.owner = lax.axis_index("section") == layer
        local_sems, pair_sems = sems[0], sems[11:13]
        rings = [tuple(sems[which : which + 2]) for which in (1, 3, 5, 7, 9)]
        x_ring, y_ring, z_ring = Ring("x"), Ring("y"), Ring("z")
        self.y_ring, self.z_ring = y_ring, z_ring
        x_rows, y_rows, y_first, z_first = split
        z_rows = shard.shape[1] - x_rows - y_rows
        z_begin = x_rows + y_rows
        self.with_x = x_rows > 0
        all_x, all_y, all_z = pl.ds(0, x_rows), pl.ds(x_rows, y_rows), pl.ds(z_begin, z_rows)
        self.all_x, self.all_y, self.all_z = all_x, all_y, all_z
        y_half = (pl.ds(x_rows, y_first), pl.ds(x_rows + y_first, y_rows - y_first))
        z_half = (pl.ds(z_begin, z_first), pl.ds(z_begin + z_first, z_rows - z_first))
        me_x, me_y, me_z = x_ring.me, y_ring.me, z_ring.me
        self.pair, self.pair_sems = sibling(), pair_sems

        def local(which):
            src, dst = (
                lambda: (shard.at[me_y, all_y], full.at[me_y, me_x, all_y]),
                lambda: (shard.at[me_z, all_z], full.at[me_z, me_x, all_z]),
                lambda: (shard.at[:, all_x], full.at[:, me_x, all_x]),
            )[which]()
            return pltpu.make_async_copy(src, dst, local_sems.at[which])

        self.local = local
        self.first_y = Gather(
            x_ring,
            lambda block, half: full.at[me_y, block, y_half[half]],
            rings[0],
            lambda half: shard.at[me_y, y_half[half]],
        )
        self.first_z = Gather(
            x_ring,
            lambda block, half: full.at[me_z, block, z_half[half]],
            rings[1],
            lambda half: shard.at[me_z, z_half[half]],
        )
        self.along_x = Gather(
            x_ring,
            lambda block, half: full.at[pl.ds(2 * half, 2), block, all_x],
            rings[2],
            lambda half: shard.at[pl.ds(2 * half, 2), all_x],
        )
        self.along_y = Gather(
            y_ring, lambda block, half: full.at[block, pl.ds(2 * half, 2), all_y], rings[3]
        )
        self.along_z = Gather(
            z_ring, lambda block, half: full.at[block, pl.ds(2 * half, 2), all_z], rings[4]
        )

    def hand(self, which):
        y_ring, z_ring = self.y_ring, self.z_ring
        if which == 2:
            region = (slice(None), slice(None), self.all_x)
        elif which in (0, 3, 5, 7):
            block = {0: y_ring.me, 3: y_ring.left, 5: y_ring.right, 7: y_ring.opposite}[which]
            region = (block, slice(None), self.all_y)
        else:
            block = {1: z_ring.me, 4: z_ring.left, 6: z_ring.right, 8: z_ring.opposite}[which]
            region = (block, slice(None), self.all_z)
        part = self.full.at[region]
        return remote(part, part, self.pair_sems, which, self.pair)

    def handed(self):
        return [which for which in range(9) if which != 2 or self.with_x]

    def start(self):
        self.first_y.start()
        self.first_z.start()
        for which in (0, 1, 2) if self.with_x else (0, 1):
            self.local(which).start()

    def first_relay(self):
        self.first_y.relay()
        self.first_z.relay()
        if self.with_x:
            self.along_x.start()

    def second(self):
        self.first_y.wait_all()
        self.local(0).wait()
        self.along_y.start()
        self.hand(0).start()
        self.first_z.wait_all()
        self.local(1).wait()
        self.along_z.start()
        self.hand(1).start()

    def second_relay(self):
        if self.with_x:
            self.along_x.relay()
        self.along_y.relay()
        self.along_z.relay()

    def last(self):
        if self.with_x:
            self.along_x.wait_all()
            self.local(2).wait()
            self.hand(2).start()
        for which, (gather, wait) in enumerate(
            (gather, wait)
            for wait in ("wait_left", "wait_right", "wait_opposite")
            for gather in (self.along_y, self.along_z)
        ):
            getattr(gather, wait)()
            self.hand(3 + which).start()

    def finish(self):
        for which in self.handed():
            self.hand(which).wait_send()
        for gather in (self.first_y, self.first_z, self.along_y, self.along_z):
            gather.finish()
        if self.with_x:
            self.along_x.finish()

    def receive(self):
        for which in self.handed():
            self.hand(which).wait_recv()

    def steps(self, *names):
        @pl.when(self.owner)
        def _():
            for name in names:
                getattr(self, name)()

    def end(self):
        self.steps("last", "finish")

        @pl.when(jnp.logical_not(self.owner))
        def _():
            self.receive()


def weight_sems():
    dma = pltpu.SemaphoreType.DMA
    return [dma((3,))] + [dma((6,))] * 10 + [dma((9,))] * 2


def weights_kernel(shard_ref, gain_ref, full_ref, gain_mine, gain_theirs, *sems):
    gain_local, gain_send, gain_recv = sems[13:]
    weights = WeightGather(0, shard_ref, full_ref, (64, 112, 64, 48), sems[:13])
    x_ring = Ring("x")
    mine_x, pair = x_ring.me, sibling()
    greet_all()

    def gain_copy(which, block, src=None):
        part = gain_mine.at[block]
        target = x_ring.to_left if which == 1 else x_ring.to_right
        return remote(part if src is None else src, part, (gain_send, gain_recv), which, target)

    gain_keep = pltpu.make_async_copy(gain_ref, gain_mine.at[mine_x], gain_local.at[0])
    weights.steps("start")
    gain_keep.start()
    gain_copy(0, mine_x, gain_ref).start()
    gain_copy(1, mine_x, gain_ref).start()
    weights.steps("first_relay")
    gain_copy(0, x_ring.left).wait_recv()
    gain_copy(2, x_ring.left).start()
    weights.steps("second")
    gain_copy(1, x_ring.right).wait_recv()
    gain_copy(2, x_ring.opposite).wait_recv()
    gain_keep.wait()
    gains = remote(gain_mine, gain_theirs, (gain_send, gain_recv), 3, pair)
    gains.start()
    weights.steps("second_relay")
    weights.end()
    gains.wait()
    for which in range(3):
        gain_copy(which, mine_x).wait_send()


def gather_weights(shard, gain):
    mats, share, features = shard.shape
    gains = jax.ShapeDtypeStruct((4,) + gain.shape, LOW)
    dma = pltpu.SemaphoreType.DMA
    return pl.pallas_call(
        weights_kernel,
        out_shape=(jax.ShapeDtypeStruct((mats, 4, share, features), LOW), gains, gains),
        in_specs=[in_vmem()] * 2,
        out_specs=[anywhere()] * 3,
        scratch_shapes=weight_sems() + [dma((1,)), dma((4,)), dma((4,))],
        compiler_params=pltpu.CompilerParams(collective_id=4, has_side_effects=True),
        cost_estimate=pl.CostEstimate(flops=0, bytes_accessed=30 * 10**6, transcendentals=0),
        name="gather_weights",
    )(shard, gain)


class SmallSum:
    def __init__(self, ring, slots, sems):
        self.ring, self.slots, self.sems = ring, slots, sems

    def copy(self, which, block):
        target = self.ring.to_left if which == 1 else self.ring.to_right
        part = self.slots.at[block]
        return remote(part, part, self.sems, which, target)

    def start(self):
        self.copy(0, self.ring.me).start()
        self.copy(1, self.ring.me).start()

    def relay(self):
        self.copy(0, self.ring.left).wait_recv()
        self.copy(2, self.ring.left).start()

    def result(self):
        self.copy(1, self.ring.right).wait_recv()
        self.copy(2, self.ring.opposite).wait_recv()
        return (self.slots[0] + self.slots[1]) + (self.slots[2] + self.slots[3])

    def finish(self):
        for which in range(3):
            self.copy(which, self.ring.me).wait_send()


class PlaneSum:
    def __init__(self, near, far, source, out, size, first, scratch, sems, keep, direct=False,
                 base=0):
        if direct:
            self.arrived, self.mid, self.done = scratch
        else:
            self.landing, self.passing, self.arrived, self.mid, self.done = scratch
        self.direct, self.base = direct, base
        self.out, self.size, self.near, self.far, self.keep = out, size, near, far, keep
        self.halves = ((0, first), (first, size - first))

        def rows(block, half):
            begin, count = (0, size) if half is None else self.halves[half]
            return pl.ds(pl.multiple_of(base + block * size + begin, 16), count)

        def half_rows(half):
            return pl.ds(0, size) if half is None else pl.ds(*self.halves[half])

        self.half_rows = half_rows
        def part(block, half):
            return source.at[rows(block, half)]

        if direct:
            self.scatter = DirectScatter(near, part, lambda side: self.arrived.at[side], sems[0])
        else:
            self.scatter = Scatter(
                near,
                part,
                lambda half: self.landing.at[half_rows(half)],
                lambda half: self.passing.at[half_rows(half)],
                lambda side, half: self.arrived.at[side, half_rows(half)],
                sems[0],
            )
        kind = DirectGather if direct else Gather
        self.gather = kind(far, lambda block, half: self.mid.at[block, half_rows(half)], sems[1])
        self.spread = kind(
            near,
            lambda block, half: out.at[rows(block, half)],
            sems[2],
            lambda half: self.done.at[half_rows(half)],
        )

    def start(self):
        self.scatter.start_far()
        self.scatter.start_near()

    def relay(self):
        self.scatter.relay()

    def middle(self):
        self.scatter.wait()
        if self.direct:
            self.mid[self.far.me] = self.scatter.whole().astype(LOW)
        else:
            for half in range(2):
                self.mid[self.far.me, self.half_rows(half)] = self.scatter.total(half).astype(LOW)
        self.gather.start()

    def middle_relay(self):
        self.gather.relay()

    def own(self):
        place = pl.ds(
            pl.multiple_of(self.base + self.near.me * self.size, 16), self.size
        )
        return pltpu.make_async_copy(self.done, self.out.at[place], self.keep)

    def end(self):
        self.gather.wait_all()
        four = [self.mid[block].astype(F32) for block in range(4)]
        self.done[...] = ((four[0] + four[1]) + (four[2] + four[3])).astype(LOW)
        self.spread.start()
        self.own().start()

    def end_relay(self):
        self.spread.relay()

    def wait(self):
        self.spread.wait_all()
        self.own().wait()

    def finish(self):
        self.scatter.finish()
        self.gather.finish()
        self.spread.finish()


FEED_BLOCK, AT_BLOCK = 144, 80


def feed_output(features):
    return (jax.ShapeDtypeStruct((2, 4 * FEED_BLOCK, features), LOW),)


def kept_output(features):
    return (jax.ShapeDtypeStruct((2, 4 * AT_BLOCK, features), LOW),)


def plane_scratch(size, features, direct=False):
    dma = pltpu.SemaphoreType.DMA

    def low(*shape):
        return pltpu.VMEM(shape + (features,), LOW)

    if direct:
        return [low(3, size), low(4, size), low(size)] + [dma((3,))] * 6
    return [low(size), low(size), low(2, size), low(4, size), low(size)] + [dma((6,))] * 6


def feed_scratch(features, rows):
    dma = pltpu.SemaphoreType.DMA
    return (
        [pltpu.VMEM((2, 2, 4, rows, features), LOW), pltpu.VMEM((2, 4 * FEED_BLOCK, features), LOW)]
        + plane_scratch(FEED_BLOCK, features) * 2
        + [dma((2,)), dma((2,)), dma((2,)), dma((2,)), dma((1,)), dma((1,))]
    )


def across_scratch(features, rows):
    share = features // 4
    dma = pltpu.SemaphoreType.DMA

    def low(*shape):
        return pltpu.VMEM(shape + (features,), LOW)

    return (
        [low(2, 2, rows), low(2, 2, rows), low(2, features)]
        + ([low(share), low(share), low(2, share)] + [dma((6,))] * 2) * 2
        + [dma((4,)), dma((4,)), dma((4,))]
    )


WIDE_PIECES = ((0, 0, 80, 48, 0), (1, 0, 80, 48, 1))
FINE_PIECES = ((0, 0, 48, 32, 0), (0, 192, 32, 16, 1), (1, 0, 48, 32, 1), (1, 192, 32, 16, 0))


def attention_scratch(features, pieces, direct):
    dma = pltpu.SemaphoreType.DMA
    scratch = []
    for piece in pieces:
        scratch += plane_scratch(piece[2], features, direct)
    return scratch + [dma((len(pieces),)), dma((2,)), dma((2,))]


def take_planes(take, count, direct=False):
    planes = []
    for _ in range(count):
        scratch = [next(take) for _ in range(3 if direct else 5)]
        sems = [next(take) for _ in range(6)]
        planes.append((scratch, [tuple(sems[i : i + 2]) for i in (0, 2, 4)]))
    return planes


def hand_over(layer, src, dst, sems, which=0):
    section = lax.axis_index("section")
    copy = functools.partial(remote, src, dst, sems, which, sibling())

    def start():
        @pl.when(section != layer)
        def _():
            copy().start()

    def wait():
        @pl.when(section != layer)
        def _():
            copy().wait_send()

        @pl.when(section == layer)
        def _():
            copy().wait_recv()

    return start, wait


class SwappedInputs:
    def __init__(self, zero, other, targets, local_sems, swap):
        self.zero, self.other, self.targets = zero, other, targets
        self.local_sems, self.swap, self.pair = local_sems, swap, sibling()

    def copies(self, first, which):
        own, sent = (self.zero, self.other) if first else (self.other, self.zero)
        target = self.targets[which]
        return (
            lambda: pltpu.make_async_copy(own[which], target.at[0], self.local_sems.at[which]),
            lambda: remote(sent[which], target.at[1], self.swap, which, self.pair),
        )

    def start(self):
        section = lax.axis_index("section")
        for first in (True, False):

            @pl.when(section == (0 if first else 1))
            def _(first=first):
                for which in range(len(self.targets)):
                    self.copies(first, which)[1]().start()
                for which in range(len(self.targets)):
                    self.copies(first, which)[0]().start()

    def wait(self, whiches):
        for which in whiches:
            keep, send = self.copies(True, which)
            keep().wait()
            send().wait_recv()

    def finish(self):
        for which in range(len(self.targets)):
            self.copies(True, which)[1]().wait_send()


class AttentionSum:
    def __init__(self, layer, kept, results, take, pieces, direct):
        out, other = results
        planes = take_planes(take, len(pieces), direct)
        keep, send, recv = [next(take) for _ in range(3)]
        y_ring, z_ring = Ring("y"), Ring("z")
        orders = ((y_ring, z_ring), (z_ring, y_ring))
        self.pieces = pieces
        self.planes = [
            PlaneSum(
                *orders[order], kept.at[matrix], out.at[matrix], size, first, *planes[which],
                keep.at[which], direct, base,
            )
            for which, (matrix, base, size, first, order) in enumerate(pieces)
        ]
        self.given = [
            hand_over(layer, out.at[which], other.at[which], (send, recv), which)
            for which in range(2)
        ]

    def run(self, name, matrix=None):
        for plane, piece in zip(self.planes, self.pieces):
            if matrix is None or piece[0] == matrix:
                getattr(plane, name)()

    def hand(self, matrix):
        self.run("wait", matrix)
        self.given[matrix][0]()

    def finish(self):
        self.run("finish")
        for given in self.given:
            given[1]()


class FeedSum:
    def __init__(self, features, operands, out, take):
        two, pre, hidden, out_all = operands
        self.features = features
        self.feed_in, self.feed_sum = next(take), next(take)
        planes = take_planes(take, 2)
        local_sems, swap_send, swap_recv, keep, end_send, end_recv = [
            next(take) for _ in range(6)
        ]
        self.end_sems = (end_send, end_recv)
        self.inputs = SwappedInputs(
            (two, pre), (hidden, out_all), (self.feed_in.at[0], self.feed_in.at[1]), local_sems,
            (swap_send, swap_recv),
        )
        y_ring, z_ring = Ring("y"), Ring("z")
        orders = ((y_ring, z_ring), (z_ring, y_ring))
        self.planes = [
            PlaneSum(
                *orders[which], self.feed_sum.at[which], out.at[which], FEED_BLOCK, 80,
                *planes[which], keep.at[which],
            )
            for which in range(2)
        ]

    def products(self):
        self.inputs.wait((0, 1))
        features, whole = self.features, 4 * FEED_BLOCK
        right = self.feed_in[1].reshape(-1, features)
        for begin in range(0, features, 256):
            count = min(256, features - begin)
            left = self.feed_in[0, :, :, :, pl.ds(begin, count)].reshape(-1, count)
            product = dot_tn(left, right).astype(LOW)
            first = max(0, min(count, whole - begin))
            if first:
                self.feed_sum[0, pl.ds(begin, first)] = product[:first]
            if first < count:
                self.feed_sum[1, pl.ds(begin + first - whole, count - first)] = product[first:]
        spare = 2 * whole - features
        self.feed_sum[1, pl.ds(whole - spare, spare)] = jnp.zeros((spare, features), LOW)
        self.run("start")

    def run(self, name):
        for plane in self.planes:
            getattr(plane, name)()

    def finish(self):
        self.inputs.finish()
        self.run("finish")


class AcrossSum:
    def __init__(self, features, operands, kept, take):
        one, mixed, dq, dk, dv, branch = operands
        self.features, self.share, self.kept = features, features // 4, kept
        share = self.share
        self.at_left, self.at_right, self.at_sum = [next(take) for _ in range(3)]
        self.halves = halves = ((0, 144), (144, share - 144))
        x_ring = Ring("x")
        self.across = []
        for which in range(2):
            landing, passing, arrived, send, recv = [next(take) for _ in range(5)]

            def part(block, half, which=which):
                begin, count = halves[half]
                row = pl.multiple_of(block * share + begin, 16)
                return self.at_sum.at[which, pl.ds(row, count)]

            def cut(ref):
                return lambda half: ref.at[pl.ds(*halves[half])]

            self.across.append(
                Scatter(
                    x_ring, part, cut(landing), cut(passing),
                    lambda side, half, arrived=arrived: arrived.at[side, pl.ds(*halves[half])],
                    (send, recv),
                )
            )
        local_sems, swap_send, swap_recv = [next(take) for _ in range(3)]
        self.inputs = SwappedInputs(
            (one, dq, one, dk),
            (one, dv, mixed, branch),
            (self.at_left.at[0], self.at_right.at[0], self.at_left.at[1], self.at_right.at[1]),
            local_sems,
            (swap_send, swap_recv),
        )

    def products(self, which):
        self.inputs.wait((2 * which, 2 * which + 1))
        features = self.features
        right = self.at_right[which].reshape(-1, features)
        for begin in range(0, features, 256):
            count = min(256, features - begin)
            left = self.at_left[which, :, :, pl.ds(begin, count)].reshape(-1, count)
            self.at_sum[which, pl.ds(begin, count)] = dot_tn(left, right).astype(LOW)
        self.across[which].start_far()

    def relay(self, which):
        self.across[which].relay()
        self.across[which].start_near()

    def keep(self, which):
        across = self.across[which]
        across.wait()
        for half in range(2):
            self.kept[which, pl.ds(*self.halves[half])] = across.total(half).astype(LOW)
        spare = 4 * AT_BLOCK - self.share
        self.kept[which, pl.ds(self.share, spare)] = jnp.zeros((spare, self.features), LOW)

    def finish(self):
        self.inputs.finish()
        for across in self.across:
            across.finish()


def gradient_kernel(features, *refs):
    take = iter(refs)

    def some(count):
        return [next(take) for _ in range(count)]

    operands = some(6)
    y_a, y_b, dx_a, dx_b, feed_zero, gain_in, kept_one = some(7)
    (feed_given,), at_zero, at_one = some(1), some(2), some(2)
    act_out, grad_out, gain_out = some(3)
    (kept_zero,) = some(1)
    sums = AcrossSum(features, operands, kept_zero, take)
    zero = AttentionSum(0, kept_zero, at_zero, take, FINE_PIECES, True)
    one = AttentionSum(1, kept_one, at_one, take, WIDE_PIECES, False)
    (gain_pair, gain_x, gain_y, gain_z, gain_send, gain_recv, last_send, last_recv, keep_sems,
     feed_send, feed_recv) = some(11)
    x_ring, y_ring, z_ring = Ring("x"), Ring("y"), Ring("z")
    pair, section = sibling(), lax.axis_index("section")
    greet_all(far=True)
    sums.inputs.start()
    feed = hand_over(0, feed_zero, feed_given, (feed_send, feed_recv))

    def last_copies(y, dx):
        return (
            remote(y, act_out.at[section], (last_send, last_recv), 0, pair),
            remote(dx, grad_out.at[section], (last_send, last_recv), 1, pair),
        )

    def keep_copies(y, dx):
        return (
            pltpu.make_async_copy(y, act_out.at[section], keep_sems.at[0]),
            pltpu.make_async_copy(dx, grad_out.at[section], keep_sems.at[1]),
        )

    @pl.when(section == 0)
    def _():
        for copy in last_copies(y_b, dx_b) + keep_copies(y_a, dx_a):
            copy.start()

    @pl.when(section == 1)
    def _():
        for copy in last_copies(y_a, dx_a) + keep_copies(y_b, dx_b):
            copy.start()

    gain_pair[0] = gain_in[...]
    swap_gain = remote(gain_pair.at[0], gain_pair.at[1], (gain_send, gain_recv), 9, pair)
    swap_gain.start()
    one.run("start")
    sums.products(0)
    sums.products(1)
    feed[0]()
    swap_gain.wait()
    gain_x[x_ring.me] = gain_pair[0] + gain_pair[1]
    small = [
        SmallSum(ring, slots, (gain_send.at[pl.ds(3 * i, 3)], gain_recv.at[pl.ds(3 * i, 3)]))
        for i, (ring, slots) in enumerate(((x_ring, gain_x), (y_ring, gain_y), (z_ring, gain_z)))
    ]
    small[0].start()
    one.run("relay")
    sums.relay(0)
    small[0].relay()
    one.run("middle")
    gain_y[y_ring.me] = small[0].result()
    small[1].start()
    one.run("middle_relay")
    small[1].relay()
    sums.keep(0)
    sums.relay(1)
    zero.run("start", 0)
    one.run("end")
    gain_z[z_ring.me] = small[1].result()
    small[2].start()
    zero.run("middle", 0)
    one.run("end_relay")
    small[2].relay()
    zero.run("end", 0)
    gain_out[...] = small[2].result()
    sums.keep(1)
    zero.run("start", 1)
    one.hand(0)
    one.hand(1)
    zero.hand(0)
    zero.run("middle", 1)
    zero.run("end", 1)
    zero.hand(1)
    zero.finish()
    one.finish()
    sums.finish()
    feed[1]()
    for each in small:
        each.finish()
    for copy in last_copies(y_a, dx_a) + keep_copies(y_a, dx_a):
        copy.wait()


def sum_gradients(features, rows, operands, last, gain, kept):
    dma = pltpu.SemaphoreType.DMA
    small = [pltpu.VMEM((4, 8, features), F32)] * 3
    return pl.pallas_call(
        functools.partial(gradient_kernel, features),
        out_shape=feed_output(features)
        + kept_output(features) * 4
        + (
            jax.ShapeDtypeStruct((2, rows, features), LOW),
            jax.ShapeDtypeStruct((2, rows, features), LOW),
            jax.ShapeDtypeStruct((8, features), F32),
        ),
        in_specs=[anywhere()] * 11 + [in_vmem()] * 2,
        out_specs=[anywhere()] * 7 + [in_vmem()],
        scratch_shapes=[pltpu.VMEM((2, 4 * AT_BLOCK, features), LOW)]
        + across_scratch(features, rows)
        + attention_scratch(features, FINE_PIECES, True)
        + attention_scratch(features, WIDE_PIECES, False)
        + [pltpu.VMEM((2, 8, features), F32)]
        + small
        + [dma((10,)), dma((10,)), dma((2,)), dma((2,)), dma((2,)), dma((1,)), dma((1,))],
        compiler_params=pltpu.CompilerParams(
            collective_id=5, has_side_effects=True, vmem_limit_bytes=60 * 2**20
        ),
        cost_estimate=pl.CostEstimate(
            flops=3 * 10**9, bytes_accessed=60 * 10**6, transcendentals=0
        ),
        name="sum_gradients",
    )(*operands, *last, gain, kept)


def doc_numbers(lengths, positions):
    doc_ends = jnp.cumsum(lengths)
    return jnp.sum((positions[:, None] >= doc_ends[None, :]).astype(jnp.int32), axis=1)


def swapped(block):
    return lax.ppermute(block, "section", [(0, 1), (1, 0)])


def body(tokens, cotangent, doc_lengths, norm_gains, w_qkv, w_out, w_up, w_down):
    batches, rows, features = tokens.shape
    share = w_qkv.shape[1]
    seq_rows = rows * lax.axis_size("tensor")
    section = lax.axis_index("section")
    is_first = section == 0

    def choose(zero_side, one_side):
        return jnp.where(is_first, zero_side, one_side)

    own_tokens = lax.dynamic_index_in_dim(tokens, section, 0, keepdims=False)
    own_cotangent = lax.dynamic_index_in_dim(cotangent, section, 0, keepdims=False)
    lengths = lax.dynamic_index_in_dim(doc_lengths, section, 0, keepdims=False)
    own_places = lax.axis_index("tensor") * rows + jnp.arange(rows, dtype=jnp.int32)
    all_places = jnp.arange(seq_rows, dtype=jnp.int32)
    own_docs = doc_numbers(lengths, own_places)
    all_docs = doc_numbers(lengths, all_places)
    allowed = (all_places[None, :] <= own_places[:, None]) & (
        all_docs[None, :] == own_docs[:, None]
    )
    bias = jnp.where(allowed, 0.0, -1e30).astype(F32)
    bias_turned = bias.T

    feed = (w_up[0], swapped(w_up[0]), w_down[0], swapped(w_down[0]))
    shard = jnp.stack(
        [w_qkv[0, :, :features], w_qkv[0, :, features : 2 * features], w_qkv[0, :, 2 * features :],
         w_out[0]]
    )
    gain_shard = jnp.pad(norm_gains[0], ((0, 14), (0, 0)))
    at_zero, gain_mine, gain_theirs = gather_weights(shard, gain_shard)
    attention = [at_zero.reshape(4, features, features), None]

    def whole_gains(block):
        return block[:, :2].transpose(1, 0, 2).reshape(2, features).astype(F32)

    gain_mine, gain_theirs = whole_gains(gain_mine), whole_gains(gain_theirs)
    gains = (choose(gain_mine, gain_theirs), choose(gain_theirs, gain_mine))

    inputs = own_tokens
    saved = []
    for layer in range(2):
        results = forward_layer(
            layer, inputs, bias, gains[layer], attention[layer], feed,
            (shard,) if layer == 0 else (),
        )
        if layer == 0:
            attention[1] = results[10].reshape(4, features, features)
        saved.append((inputs,) + tuple(results[:10]))
        inputs = results[0]

    grad = own_cotangent
    gain_grads, input_grads, operands = [None, None], [None, None], ()
    for layer in (1, 0):
        (x, _, middle, normed_one, query, key, value, mixed, normed_two, act, hidden) = saved[layer]
        results = backward_layer(
            layer, x, grad, bias_turned, gains[layer], middle, query, key, value, act,
            attention[layer], feed, operands + (saved[0][8], saved[0][10]) if layer == 0 else (),
        )
        (grad, gain_grads[layer], out_all, pre_grad, branch, dquery, dkey, dvalue) = results[:8]
        input_grads[layer] = grad
        operands = (
            normed_two, pre_grad, hidden, out_all, normed_one, mixed, dquery, dkey, dvalue, branch,
        )
    feed_one, feed_one_given, feed_zero, kept_one = results[8:]
    gain_rows = jnp.concatenate(gain_grads + [jnp.zeros((4, features), F32)], axis=0)
    (feed_zero_given, at_zero, at_zero_given, at_one, at_one_given, activations, input_grads,
     gain_total) = sum_gradients(
        features, rows, operands[4:], (saved[0][1], saved[1][1], *input_grads, feed_zero),
        gain_rows, kept_one,
    )
    gain_own = lax.dynamic_slice(
        gain_total, (2 * section, lax.axis_index("tensor") * share), (2, share)
    )

    def whole(block):
        return block.reshape(-1, features)[:features].astype(F32)[None]

    first_half = choose(at_zero, at_one_given)[:, :share].astype(F32)
    other_half = choose(at_zero_given, at_one)[:, :share].astype(F32)
    grad_qkv = jnp.concatenate([first_half[0], first_half[1], other_half[0]], axis=1)
    return (
        activations[None],
        input_grads[None],
        gain_own[None],
        grad_qkv[None],
        other_half[1][None],
        whole(choose(feed_zero, feed_one_given)),
        whole(choose(feed_zero_given, feed_one)),
    )


def solution(mesh):
    placed = (
        P("dp", "tensor", None),
        P("dp", "tensor", None),
        P("dp", None),
        P("section", None, "tensor"),
        P("section", "tensor", None),
        P("section", "tensor", None),
        P("section", None, "tensor"),
        P("section", "tensor", None),
    )
    return jax.shard_map(
        body,
        mesh=mesh,
        in_specs=placed,
        out_specs=(
            P("section", "dp", "tensor", None),
            P("section", "dp", "tensor", None),
            P("section", None, "tensor"),
            P("section", "tensor", None),
            P("section", "tensor", None),
            P("section", None, "tensor"),
            P("section", "tensor", None),
        ),
        check_vma=False,
    )
```

```python
import functools
import jax
import jax.numpy as jnp
from jax import lax
from jax.experimental import pallas as pl
from jax.experimental.pallas import tpu as pltpu
from jax.sharding import PartitionSpec as P

HEAD_DIM = 64
LOW = jnp.bfloat16
F32 = jnp.float32
MESH = pl.DeviceIdType.MESH


def dot_nn(left, right):
    return lax.dot_general(left, right, (((1,), (0,)), ((), ())), preferred_element_type=F32)


def dot_nt(left, right):
    return lax.dot_general(left, right, (((1,), (1,)), ((), ())), preferred_element_type=F32)


def dot_tn(left, right):
    return lax.dot_general(left, right, (((0,), (0,)), ((), ())), preferred_element_type=F32)


class Ring:
    def __init__(self, axis):
        whole = lax.axis_index("dp")
        rest = None
        if axis == "x":
            self.me = lax.axis_index("tensor")
        elif axis == "y":
            self.me, rest = lax.rem(whole, 4), lax.div(whole, 4) * 4
        else:
            self.me, rest = lax.div(whole, 4), lax.rem(whole, 4)
        self.right = lax.rem(self.me + 1, 4)
        self.left = lax.rem(self.me + 3, 4)
        self.opposite = lax.rem(self.me + 2, 4)

        def device(place):
            if axis == "x":
                return {"tensor": place}
            if axis == "y":
                return {"dp": rest + place}
            return {"dp": place * 4 + rest}

        self.to_right, self.to_left = device(self.right), device(self.left)
        self.to_opposite = device(self.opposite)


def sibling():
    return {"section": 1 - lax.axis_index("section")}


def greet(*targets):
    barrier = pltpu.get_barrier_semaphore()
    for target in targets:
        pl.semaphore_signal(barrier, inc=1, device_id=target, device_id_type=MESH)
    pl.semaphore_wait(barrier, len(targets))


def remote(src, dst, sems, which, target):
    return pltpu.make_async_remote_copy(
        src_ref=src,
        dst_ref=dst,
        send_sem=sems[0].at[which],
        recv_sem=sems[1].at[which],
        device_id=target,
        device_id_type=MESH,
    )


class Gather:
    def __init__(self, ring, slot, sems, own=None):
        self.ring, self.slot, self.sems = ring, slot, sems
        self.own = own if own is not None else lambda half: slot(ring.me, half)

    def copy(self, which, arriving=False):
        ring = self.ring
        half = (0, 1, 1, 0, 0, 1)[which]
        goes_right = which in (0, 2, 4)
        target = ring.to_right if goes_right else ring.to_left
        if which < 4:
            source_block = ring.left if goes_right else ring.right
            if not arriving:
                return remote(self.own(half), self.slot(ring.me, half), self.sems, which, target)
        else:
            source_block = ring.opposite
            if not arriving:
                handed = self.slot(ring.left if goes_right else ring.right, half)
                return remote(handed, handed, self.sems, which, target)
        part = self.slot(source_block, half)
        return remote(part, part, self.sems, which, target)

    def start(self):
        for which in range(4):
            self.copy(which).start()

    def relay(self):
        for which in (0, 1):
            self.copy(which, arriving=True).wait_recv()
            self.copy(which + 4).start()

    def wait_left(self):
        self.copy(2, arriving=True).wait_recv()

    def wait_right(self):
        self.copy(3, arriving=True).wait_recv()

    def wait_opposite(self):
        self.copy(4, arriving=True).wait_recv()
        self.copy(5, arriving=True).wait_recv()

    def wait_all(self):
        self.wait_left()
        self.wait_right()
        self.wait_opposite()

    def finish(self):
        for which in range(6):
            self.copy(which).wait_send()


class Scatter:
    def __init__(self, ring, part, landing, passing, arrived, sems):
        self.ring, self.part, self.landing, self.passing = ring, part, landing, passing
        self.arrived, self.sems = arrived, sems

    def copy(self, which):
        ring = self.ring
        half = (0, 1, 1, 0, 0, 1)[which]
        goes_right = which in (0, 2, 4)
        if which < 2:
            src, dst = self.part(ring.opposite, half), self.landing(half)
        else:
            dst = self.arrived(0 if goes_right else 1, half)
            if which < 4:
                src = self.part(ring.right if goes_right else ring.left, half)
            else:
                src = self.passing(half)
        return remote(src, dst, self.sems, which, ring.to_right if goes_right else ring.to_left)

    def start_near(self):
        self.copy(2).start()
        self.copy(3).start()

    def start_far(self):
        self.copy(0).start()
        self.copy(1).start()

    def relay(self):
        for half, block in ((0, self.ring.right), (1, self.ring.left)):
            self.copy(half).wait_recv()
            added = self.part(block, half)[...].astype(F32) + self.landing(half)[...].astype(F32)
            self.passing(half)[...] = added.astype(LOW)
            self.copy(half + 4).start()

    def wait(self):
        for which in (2, 3, 4, 5):
            self.copy(which).wait_recv()

    def total(self, half):
        return (
            self.part(self.ring.me, half)[...].astype(F32)
            + self.arrived(0, half)[...].astype(F32)
            + self.arrived(1, half)[...].astype(F32)
        )

    def finish(self):
        for which in range(6):
            self.copy(which).wait_send()


class DirectGather:
    def __init__(self, ring, slot, sems, own=None):
        self.ring, self.slot, self.sems = ring, slot, sems
        self.own = own if own is not None else lambda half: slot(ring.me, half)

    def copy(self, which):
        target = (self.ring.to_right, self.ring.to_left, self.ring.to_opposite)[which]
        return remote(self.own(None), self.slot(self.ring.me, None), self.sems, which, target)

    def start(self):
        for which in (2, 0, 1):
            self.copy(which).start()

    def relay(self):
        pass

    def wait_all(self):
        for which, block in enumerate((self.ring.left, self.ring.right, self.ring.opposite)):
            part = self.slot(block, None)
            remote(part, part, self.sems, which, self.ring.to_right).wait_recv()

    def finish(self):
        for which in range(3):
            self.copy(which).wait_send()


class DirectScatter:
    def __init__(self, ring, part, arrived, sems):
        self.ring, self.part, self.arrived, self.sems = ring, part, arrived, sems

    def copy(self, which):
        ring = self.ring
        block = (ring.right, ring.left, ring.opposite)[which]
        target = (ring.to_right, ring.to_left, ring.to_opposite)[which]
        return remote(self.part(block, None), self.arrived(which), self.sems, which, target)

    def start_far(self):
        self.copy(2).start()

    def start_near(self):
        self.copy(0).start()
        self.copy(1).start()

    def relay(self):
        pass

    def wait(self):
        for which in range(3):
            self.copy(which).wait_recv()

    def whole(self):
        near = self.arrived(0)[...].astype(F32) + self.arrived(1)[...].astype(F32)
        own = self.part(self.ring.me, None)[...].astype(F32)
        return (own + near) + self.arrived(2)[...].astype(F32)

    def finish(self):
        for which in range(3):
            self.copy(which).wait_send()


def row_gather(ring, full, sems, columns=slice(None)):
    half = full.shape[1] // 2
    return Gather(
        ring, lambda block, which: full.at[block, pl.ds(which * half, half), columns], sems
    )


def row_scatter(ring, parts, landing, passing, arrived, sems, columns=slice(None)):
    half = parts.shape[1] // 2

    def rows(which):
        return pl.ds(which * half, half)

    return Scatter(
        ring,
        lambda block, which: parts.at[block, rows(which), columns],
        lambda which: landing.at[which, :, columns],
        lambda which: passing.at[which, :, columns],
        lambda side, which: arrived.at[side, rows(which), columns],
        sems,
    )


def row_total(scatter):
    scatter.wait()
    return jnp.concatenate([scatter.total(0), scatter.total(1)], axis=0)


def head_groups(features):
    pairs = pair_columns(features)
    middle = (len(pairs) + 1) // 2
    begin = pairs[middle][0]
    return (
        (pl.ds(0, begin), pairs[:middle]),
        (pl.ds(begin, features - begin), pairs[middle:]),
    )


def norm_stats(values):
    average = jnp.mean(values, axis=-1, keepdims=True)
    centered = values - average
    variance = jnp.mean(centered * centered, axis=-1, keepdims=True)
    scale = lax.rsqrt(variance + 1e-05)
    return centered * scale, scale


def norm_back(values, gain, grad):
    xhat, scale = norm_stats(values)
    scaled = grad * gain
    part = scale * (
        scaled
        - jnp.mean(scaled, axis=-1, keepdims=True)
        - xhat * jnp.mean(scaled * xhat, axis=-1, keepdims=True)
    )
    return part, jnp.sum(grad * xhat, axis=0, keepdims=True)


def gelu_tanh(values):
    inner = 0.7978845608028654 * (values + 0.044715 * values * values * values)
    return 0.5 * values * (1.0 + jnp.tanh(inner))


def gelu_slope(values):
    square = values * values
    bent = jnp.tanh(0.7978845608028654 * values * (1.0 + 0.044715 * square))
    slope = 0.7978845608028654 * (1.0 + 3.0 * 0.044715 * square)
    return 0.5 * (1.0 + bent) + 0.5 * values * (1.0 - bent * bent) * slope


def pick_copies(layer, mine, theirs, target, sem):
    def start():
        mine_here = lax.axis_index("section") == layer

        @pl.when(mine_here)
        def _():
            pltpu.make_async_copy(mine, target, sem).start()

        @pl.when(jnp.logical_not(mine_here))
        def _():
            pltpu.make_async_copy(theirs, target, sem).start()

    def wait():
        pltpu.make_async_copy(mine, target, sem).wait()

    return start, wait


def pair_columns(features):
    width = 2 * HEAD_DIM
    return [
        (start, min(width, features - start)) for start in range(0, features, width)
    ]


def head_masks(width):
    lanes = lax.broadcasted_iota(jnp.int32, (1, width), 1)
    if width == HEAD_DIM:
        return [None]
    return [lanes < HEAD_DIM, lanes >= HEAD_DIM]


def masked(values, mask):
    return values if mask is None else jnp.where(mask, values, jnp.zeros_like(values))


def attention_weights(layer, mine, theirs, target, sems):
    return [
        pick_copies(layer, mine.at[which], theirs.at[which], target.at[which], sems.at[which])
        for which in range(4)
    ]


def forward_kernel(
    layer, features, x_ref, bias_ref, gains_ref, at_mine, at_theirs, up_mine, up_theirs, down_mine,
    down_theirs, y_ref, middle_ref, one_ref, query_ref, key_ref, value_ref, mixed_ref, two_ref,
    act_ref, hidden_ref, at_w, up_w, down_w, weight_sems, parts, landing, passing, arrived,
    key_send, key_recv, value_send, value_recv, two_send, two_recv, sum_send, sum_recv,
):
    ring = Ring("x")
    me = ring.me
    fetches = attention_weights(layer, at_mine, at_theirs, at_w, weight_sems)
    fetches.append(pick_copies(layer, up_mine, up_theirs, up_w, weight_sems.at[4]))
    fetches.append(pick_copies(layer, down_mine, down_theirs, down_w, weight_sems.at[5]))
    for which in (1, 2, 0, 3, 4, 5):
        fetches[which][0]()
    greet(ring.to_right, ring.to_left)
    rows = x_ref.shape[0]
    inputs = x_ref[...].astype(F32)
    xhat, _ = norm_stats(inputs)
    one_ref[...] = (xhat * gains_ref[0:1, :]).astype(LOW)
    normed_one = one_ref[...]
    groups = head_groups(features)
    keys, values = [], []
    fetches[1][1]()
    fetches[2][1]()
    for which, (columns, _) in enumerate(groups):
        key_ref[me, :, columns] = dot_nn(normed_one, at_w[1, :, columns]).astype(LOW)
        keys.append(
            row_gather(ring, key_ref, (key_send.at[which], key_recv.at[which]), columns)
        )
        if which == 0:
            keys[0].start()
        value_ref[me, :, columns] = dot_nn(normed_one, at_w[2, :, columns]).astype(LOW)
        values.append(
            row_gather(ring, value_ref, (value_send.at[which], value_recv.at[which]), columns)
        )
        if which == 0:
            values[0].start()
    fetches[0][1]()
    query_ref[...] = dot_nn(normed_one, at_w[0]).astype(LOW)
    keys[0].relay()
    values[0].relay()
    keys[1].start()
    values[1].start()
    bias = bias_ref[...]

    def attend(begin, width):
        columns = pl.ds(begin, width)
        queries = query_ref[:, columns]
        key_block = key_ref[:, :, columns].reshape(4 * rows, width)
        value_block = value_ref[:, :, columns].reshape(4 * rows, width)
        mixed = None
        for mask in head_masks(width):
            scores = dot_nt(masked(queries, mask), key_block) * 0.125 + bias
            raised = jnp.exp(scores - jnp.max(scores, axis=-1, keepdims=True))
            probs = raised * (1.0 / jnp.sum(raised, axis=-1, keepdims=True))
            own = dot_nn(probs.astype(LOW), value_block)
            mixed = own if mixed is None else jnp.where(mask, own, mixed)
        mixed_ref[:, columns] = mixed.astype(LOW)

    for which, (_, pairs) in enumerate(groups):
        keys[which].wait_all()
        values[which].wait_all()
        for count, (begin, width) in enumerate(pairs):
            attend(begin, width)
            if which == 0 and count == 2:
                keys[1].relay()
                values[1].relay()
    fetches[3][1]()
    middle_ref[...] = x_ref[...].astype(F32) + dot_nn(mixed_ref[...], at_w[3])
    xhat, _ = norm_stats(middle_ref[...])
    two_ref[me] = (xhat * gains_ref[1:2, :]).astype(LOW)
    tokens = row_gather(ring, two_ref, (two_send, two_recv))
    tokens.start()
    fetches[4][1]()
    fetches[5][1]()
    sums = row_scatter(ring, parts, landing, passing, arrived, (sum_send, sum_recv))

    def feed(block):
        act_ref[block] = dot_nn(two_ref[block], up_w[...])
        hidden_ref[block] = gelu_tanh(act_ref[block]).astype(LOW)
        parts[block] = dot_nn(hidden_ref[block], down_w[...]).astype(LOW)

    feed(me)
    tokens.relay()
    tokens.wait_left()
    feed(ring.left)
    tokens.wait_right()
    feed(ring.right)
    sums.start_near()
    tokens.wait_opposite()
    feed(ring.opposite)
    sums.start_far()
    sums.relay()
    y_ref[...] = (middle_ref[...] + row_total(sums)).astype(LOW)
    for gather in keys + values:
        gather.finish()
    tokens.finish()
    sums.finish()


def scatter_scratch(rows, features):
    return [
        pltpu.VMEM((4, rows, features), LOW),
        pltpu.VMEM((2, rows // 2, features), LOW),
        pltpu.VMEM((2, rows // 2, features), LOW),
        pltpu.VMEM((2, rows, features), LOW),
    ]


def weight_scratch(features, hidden, matrices=4):
    shape = (features, features) if matrices == 1 else (matrices, features, features)
    return [
        pltpu.VMEM(shape, LOW),
        pltpu.VMEM((features, hidden), LOW),
        pltpu.VMEM((hidden, features), LOW),
        pltpu.SemaphoreType.DMA((6,)),
    ]


def in_vmem():
    return pl.BlockSpec(memory_space=pltpu.VMEM)


def anywhere():
    return pl.BlockSpec(memory_space=pl.ANY)


def forward_layer(layer, x, bias, gains, attention, feed):
    rows, features = x.shape
    hidden = feed[0].shape[1]
    out_shape = (
        jax.ShapeDtypeStruct((rows, features), LOW),
        jax.ShapeDtypeStruct((rows, features), F32),
        jax.ShapeDtypeStruct((rows, features), LOW),
        jax.ShapeDtypeStruct((rows, features), LOW),
        jax.ShapeDtypeStruct((4, rows, features), LOW),
        jax.ShapeDtypeStruct((4, rows, features), LOW),
        jax.ShapeDtypeStruct((rows, features), LOW),
        jax.ShapeDtypeStruct((4, rows, features), LOW),
        jax.ShapeDtypeStruct((4, rows, hidden), F32),
        jax.ShapeDtypeStruct((4, rows, hidden), LOW),
    )
    return pl.pallas_call(
        functools.partial(forward_kernel, layer, features),
        out_shape=out_shape,
        in_specs=[in_vmem()] * 3 + [anywhere()] * 6,
        out_specs=[in_vmem()] * len(out_shape),
        scratch_shapes=weight_scratch(features, hidden)
        + scatter_scratch(rows, features)
        + [pltpu.SemaphoreType.DMA((2, 6))] * 4
        + [pltpu.SemaphoreType.DMA((6,))] * 4,
        compiler_params=pltpu.CompilerParams(
            collective_id=layer, has_side_effects=True, vmem_limit_bytes=56 * 2**20
        ),
        cost_estimate=pl.CostEstimate(
            flops=3 * 10**9, bytes_accessed=24 * 10**6, transcendentals=10**6
        ),
        name=f"layer_forward_{layer}",
    )(x, bias, gains, *attention, *feed)


def backward_kernel(layer, features, *refs):
    take = iter(refs)

    def some(count):
        return [next(take) for _ in range(count)]

    (x_ref, dy_ref, bias_ref, gains_ref, middle_ref, query_ref, key_ref, value_ref, act_ref,
     at_mine, at_theirs, up_mine, up_theirs, down_mine, down_theirs) = some(15)
    operands = some(12) if layer == 0 else None
    (dx_ref, gain_ref, out_ref, pre_ref, branch_ref, dquery_ref, dkey_ref, dvalue_ref) = some(8)
    results = some(4) if layer == 0 else None
    (at_w, up_w, down_w, weight_sems, parts, landing, passing, arrived, parts_b, landing_b,
     passing_b, arrived_b, parts_c, landing_c, passing_c, arrived_c, mixed_grad, kept_grad,
     out_send, out_recv, sum_send, sum_recv, key_send, key_recv, value_send, value_recv) = some(26)
    extra = layer == 0
    if extra:
        (two, pre, hidden, out_all, one, mixed, dq, dk, dv, branch, two_own, hidden_own) = operands
        feed_out, feed_given, feed_own_out, kept = results
        feed_one = FeedSum(features, (two, pre, hidden, out_all), feed_out, take)
        feed_own = FeedSum(
            features, (two_own, pre_ref, hidden_own, out_ref), feed_own_out, take
        )
        across = AcrossSum(features, (one, mixed, dq, dk, dv, branch), kept, take)
        given = hand_over(1, feed_out, feed_given, feed_one.end_sems)
    ring = Ring("x")
    me = ring.me
    fetches = [
        pick_copies(layer, at_mine.at[which], at_theirs.at[which], target, weight_sems.at[which])
        for which, target in enumerate((up_w, down_w, at_w, at_w))
    ]
    fetches.append(pick_copies(layer, up_mine, up_theirs, up_w, weight_sems.at[4]))
    fetches.append(pick_copies(layer, down_mine, down_theirs, down_w, weight_sems.at[5]))
    for which in (5, 4, 3):
        fetches[which][0]()
    rows = x_ref.shape[0]
    out_ref[me] = dy_ref[...]
    if not extra:
        greet(ring.to_right, ring.to_left)
    else:
        greet_all()
    grads = row_gather(ring, out_ref, (out_send, out_recv))
    grads.start()
    if extra:
        across.inputs.start()
        feed_one.inputs.start()
    sums = row_scatter(ring, parts, landing, passing, arrived, (sum_send, sum_recv))
    fetches[5][1]()
    fetches[4][1]()

    def feed(block):
        hidden_grad = dot_nt(out_ref[block], down_w[...])
        pre_ref[block] = (hidden_grad * gelu_slope(act_ref[block])).astype(LOW)
        parts[block] = dot_nt(pre_ref[block], up_w[...]).astype(LOW)

    feed(me)
    grads.relay()
    if extra:
        across.products(0)
        feed_one.products()
    grads.wait_left()
    feed(ring.left)
    grads.wait_right()
    feed(ring.right)
    sums.start_near()
    grads.wait_opposite()
    feed(ring.opposite)
    sums.start_far()
    for which in (0, 1):
        fetches[which][0]()
    if extra:
        feed_own.inputs.start()
        feed_one.run("relay")
    sums.relay()
    if extra:
        across.products(1)
    middle_part, gain_two = norm_back(middle_ref[...], gains_ref[1:2, :], row_total(sums))
    gain_ref[1:2, :] = gain_two
    middle_grad = dy_ref[...].astype(F32) + middle_part
    kept_grad[...] = middle_grad
    branch_ref[...] = middle_grad.astype(LOW)
    fetches[3][1]()
    mixed_grad[...] = dot_nt(branch_ref[...], at_w[...]).astype(LOW)
    fetches[2][0]()
    bias = bias_ref[...]
    groups = head_groups(features)
    dkeys = [
        row_scatter(ring, parts_b, landing_b, passing_b, arrived_b,
                    (key_send.at[which], key_recv.at[which]), columns)
        for which, (columns, _) in enumerate(groups)
    ]
    dvalues = [
        row_scatter(ring, parts_c, landing_c, passing_c, arrived_c,
                    (value_send.at[which], value_recv.at[which]), columns)
        for which, (columns, _) in enumerate(groups)
    ]

    def send_pair(which):
        for scatter in (dkeys[which], dvalues[which]):
            scatter.start_far()
        for scatter in (dkeys[which], dvalues[which]):
            scatter.start_near()

    def relay_pair(which):
        for scatter in (dkeys[which], dvalues[which]):
            scatter.relay()

    for count, (begin, width) in enumerate(pair_columns(features)):
        columns = pl.ds(begin, width)
        queries = query_ref[:, columns]
        outer = mixed_grad[:, columns]
        key_block = key_ref[:, :, columns].reshape(4 * rows, width)
        value_block = value_ref[:, :, columns].reshape(4 * rows, width)
        dquery = dkey = dvalue = None
        for mask in head_masks(width):
            query_one, outer_one = masked(queries, mask), masked(outer, mask)
            scores = dot_nt(key_block, query_one) * 0.125 + bias
            raised = jnp.exp(scores - jnp.max(scores, axis=0, keepdims=True))
            probs = raised * (1.0 / jnp.sum(raised, axis=0, keepdims=True))
            probs_grad = dot_nt(value_block, outer_one)
            mean = jnp.sum(probs * probs_grad, axis=0, keepdims=True)
            score_grad = (probs * (probs_grad - mean)).astype(LOW)
            own_query = dot_tn(score_grad, key_block)
            own_key = dot_nn(score_grad, query_one)
            own_value = dot_nn(probs.astype(LOW), outer_one)
            if dquery is None:
                dquery, dkey, dvalue = own_query, own_key, own_value
            else:
                dquery = jnp.where(mask, own_query, dquery)
                dkey, dvalue = dkey + own_key, dvalue + own_value
        dquery_ref[:, columns] = (dquery * 0.125).astype(LOW)
        parts_b[:, :, columns] = (dkey * 0.125).astype(LOW).reshape(4, rows, width)
        parts_c[:, :, columns] = dvalue.astype(LOW).reshape(4, rows, width)
        if begin + width == groups[0][0].size:
            send_pair(0)
        if extra and count == 1:
            feed_one.run("middle")
            across.relay(0)
        if extra and count == 4:
            feed_own.products()
            feed_one.run("middle_relay")
        if extra and count == 7:
            feed_own.run("relay")
    relay_pair(0)
    send_pair(1)
    for which in (0, 1, 2):
        fetches[which][1]()
    one_grad = dot_nt(dquery_ref[...], up_w[...])
    if extra:
        feed_one.run("end")
    relay_pair(1)
    if extra:
        across.relay(1)
        feed_own.run("middle")
        feed_one.run("end_relay")
    for which, (columns, _) in enumerate(groups):
        dkey_ref[:, columns] = row_total(dkeys[which]).astype(LOW)
    one_grad = one_grad + dot_nt(dkey_ref[...], down_w[...])
    if extra:
        across.keep(0)
        feed_own.run("middle_relay")
    for which, (columns, _) in enumerate(groups):
        dvalue_ref[:, columns] = row_total(dvalues[which]).astype(LOW)
    one_grad = one_grad + dot_nt(dvalue_ref[...], at_w[...])
    inputs_part, gain_one = norm_back(x_ref[...].astype(F32), gains_ref[0:1, :], one_grad)
    gain_ref[0:1, :] = gain_one
    dx_ref[...] = (kept_grad[...] + inputs_part).astype(LOW)
    if extra:
        feed_one.run("wait")
        given[0]()
        feed_own.run("end")
        across.keep(1)
        feed_own.run("end_relay")
        feed_one.finish()
        across.finish()
        given[1]()
        feed_own.run("wait")
        feed_own.finish()
    grads.finish()
    sums.finish()
    for scatter in dkeys + dvalues:
        scatter.finish()


def greet_all(far=False):
    rings = [Ring(axis) for axis in ("x", "y", "z")]
    greet(
        *[ring.to_right for ring in rings], *[ring.to_left for ring in rings], sibling(),
        *[ring.to_opposite for ring in rings[1:] if far],
    )


def backward_layer(layer, x, dy, bias, gains, middle, query, key, value, act, attention, feed,
                   operands=()):
    rows, features = x.shape
    hidden = feed[0].shape[1]
    out_shape = (
        jax.ShapeDtypeStruct((rows, features), LOW),
        jax.ShapeDtypeStruct((2, features), F32),
        jax.ShapeDtypeStruct((4, rows, features), LOW),
        jax.ShapeDtypeStruct((4, rows, hidden), LOW),
        jax.ShapeDtypeStruct((rows, features), LOW),
        jax.ShapeDtypeStruct((rows, features), LOW),
        jax.ShapeDtypeStruct((rows, features), LOW),
        jax.ShapeDtypeStruct((rows, features), LOW),
    )
    sums = feed_output(features) * 3 + kept_output(features) if layer == 0 else ()
    return pl.pallas_call(
        functools.partial(backward_kernel, layer, features),
        out_shape=out_shape + sums,
        in_specs=[in_vmem()] * 9 + [anywhere()] * (6 + len(operands)),
        out_specs=[in_vmem()] * len(out_shape) + [anywhere()] * 3 * (len(sums) // 4)
        + [in_vmem()] * (len(sums) // 4),
        scratch_shapes=weight_scratch(features, hidden, 1)
        + scatter_scratch(rows, features) * 3
        + [pltpu.VMEM((rows, features), LOW), pltpu.VMEM((rows, features), F32)]
        + [pltpu.SemaphoreType.DMA((6,))] * 4
        + [pltpu.SemaphoreType.DMA((2, 6))] * 4
        + (
            feed_scratch(features, rows) * 2 + across_scratch(features, rows)
            if layer == 0
            else []
        ),
        compiler_params=pltpu.CompilerParams(
            collective_id=2 + layer, has_side_effects=True, vmem_limit_bytes=62 * 2**20
        ),
        cost_estimate=pl.CostEstimate(
            flops=4 * 10**9, bytes_accessed=24 * 10**6, transcendentals=10**6
        ),
        name=f"layer_backward_{layer}",
    )(x, dy, bias, gains, middle, query, key, value, act, *attention, *feed, *operands)


X_ROWS, Y_ROWS = 96, 96


def weights_kernel(
    shard_ref, gain_ref, mine_ref, theirs_ref, gain_mine, gain_theirs, local_sems, x_send, x_recv,
    yx_send, yx_recv, zx_send, zx_recv, y_send, y_recv, z_send, z_recv, gain_send, gain_recv,
    pair_send, pair_recv,
):
    x_ring, y_ring, z_ring = Ring("x"), Ring("y"), Ring("z")
    mine_y, mine_z, mine_x = y_ring.me, z_ring.me, x_ring.me
    share = shard_ref.shape[1]
    y_begin, z_begin = X_ROWS, X_ROWS + Y_ROWS
    z_rows = share - z_begin
    all_x, all_y, all_z = pl.ds(0, X_ROWS), pl.ds(y_begin, Y_ROWS), pl.ds(z_begin, z_rows)
    y_half = (pl.ds(y_begin, 48), pl.ds(y_begin + 48, Y_ROWS - 48))
    z_half = (pl.ds(z_begin, 48), pl.ds(z_begin + 48, z_rows - 48))
    pair = sibling()
    greet(
        x_ring.to_right, x_ring.to_left, y_ring.to_right, y_ring.to_left, z_ring.to_right,
        z_ring.to_left, pair,
    )
    locals_ = [
        pltpu.make_async_copy(
            shard_ref.at[mine_y, all_y], mine_ref.at[mine_y, mine_x, all_y], local_sems.at[0]
        ),
        pltpu.make_async_copy(
            shard_ref.at[mine_z, all_z], mine_ref.at[mine_z, mine_x, all_z], local_sems.at[1]
        ),
        pltpu.make_async_copy(
            shard_ref.at[:, all_x], mine_ref.at[:, mine_x, all_x], local_sems.at[2]
        ),
        pltpu.make_async_copy(gain_ref, gain_mine.at[mine_x], local_sems.at[3]),
    ]
    first_y = Gather(
        x_ring,
        lambda block, half: mine_ref.at[mine_y, block, y_half[half]],
        (yx_send, yx_recv),
        lambda half: shard_ref.at[mine_y, y_half[half]],
    )
    first_z = Gather(
        x_ring,
        lambda block, half: mine_ref.at[mine_z, block, z_half[half]],
        (zx_send, zx_recv),
        lambda half: shard_ref.at[mine_z, z_half[half]],
    )
    along_x = Gather(
        x_ring,
        lambda block, half: mine_ref.at[pl.ds(2 * half, 2), block, all_x],
        (x_send, x_recv),
        lambda half: shard_ref.at[pl.ds(2 * half, 2), all_x],
    )
    along_y = Gather(
        y_ring,
        lambda block, half: mine_ref.at[block, pl.ds(2 * half, 2), all_y],
        (y_send, y_recv),
    )
    along_z = Gather(
        z_ring,
        lambda block, half: mine_ref.at[block, pl.ds(2 * half, 2), all_z],
        (z_send, z_recv),
    )

    def gain_copy(which, block, src=None):
        part = gain_mine.at[block]
        target = x_ring.to_left if which == 1 else x_ring.to_right
        return remote(part if src is None else src, part, (gain_send, gain_recv), which, target)

    def hand(which, region):
        return remote(mine_ref.at[region], theirs_ref.at[region], (pair_send, pair_recv), which, pair)

    handed = []

    def hand_on(which, region):
        copy = hand(which, region)
        copy.start()
        handed.append(copy)

    first_y.start()
    first_z.start()
    for copy in locals_:
        copy.start()
    gain_copy(0, mine_x, gain_ref).start()
    gain_copy(1, mine_x, gain_ref).start()
    first_y.relay()
    first_z.relay()
    along_x.start()
    first_y.wait_all()
    locals_[0].wait()
    along_y.start()
    hand_on(0, (mine_y, slice(None), all_y))
    first_z.wait_all()
    locals_[1].wait()
    along_z.start()
    hand_on(1, (mine_z, slice(None), all_z))
    gain_copy(0, x_ring.left).wait_recv()
    gain_copy(2, x_ring.left).start()
    along_x.relay()
    along_y.relay()
    along_z.relay()
    along_x.wait_all()
    locals_[2].wait()
    hand_on(2, (slice(None), slice(None), all_x))
    along_y.wait_left()
    hand_on(3, (y_ring.left, slice(None), all_y))
    along_z.wait_left()
    hand_on(4, (z_ring.left, slice(None), all_z))
    along_y.wait_right()
    hand_on(5, (y_ring.right, slice(None), all_y))
    along_z.wait_right()
    hand_on(6, (z_ring.right, slice(None), all_z))
    gain_copy(1, x_ring.right).wait_recv()
    gain_copy(2, x_ring.opposite).wait_recv()
    locals_[3].wait()
    gains = remote(gain_mine, gain_theirs, (pair_send, pair_recv), 9, pair)
    gains.start()
    along_y.wait_opposite()
    hand_on(7, (y_ring.opposite, slice(None), all_y))
    along_z.wait_opposite()
    hand_on(8, (z_ring.opposite, slice(None), all_z))
    for copy in handed + [gains]:
        copy.wait()
    for which in range(3):
        gain_copy(which, mine_x).wait_send()
    for gather in (first_y, first_z, along_x, along_y, along_z):
        gather.finish()


def gather_weights(shard, gain):
    mats, share, features = shard.shape
    full = jax.ShapeDtypeStruct((mats, 4, share, features), LOW)
    gains = jax.ShapeDtypeStruct((4,) + gain.shape, LOW)
    return pl.pallas_call(
        weights_kernel,
        out_shape=(full, full, gains, gains),
        in_specs=[in_vmem()] * 2,
        out_specs=[anywhere()] * 4,
        scratch_shapes=[pltpu.SemaphoreType.DMA((4,))]
        + [pltpu.SemaphoreType.DMA((6,))] * 10
        + [pltpu.SemaphoreType.DMA((3,))] * 2
        + [pltpu.SemaphoreType.DMA((10,))] * 2,
        compiler_params=pltpu.CompilerParams(collective_id=4, has_side_effects=True),
        cost_estimate=pl.CostEstimate(flops=0, bytes_accessed=60 * 10**6, transcendentals=0),
        name="gather_weights",
    )(shard, gain)


class SmallSum:
    def __init__(self, ring, slots, sems):
        self.ring, self.slots, self.sems = ring, slots, sems

    def copy(self, which, block):
        target = self.ring.to_left if which == 1 else self.ring.to_right
        part = self.slots.at[block]
        return remote(part, part, self.sems, which, target)

    def start(self):
        self.copy(0, self.ring.me).start()
        self.copy(1, self.ring.me).start()

    def relay(self):
        self.copy(0, self.ring.left).wait_recv()
        self.copy(2, self.ring.left).start()

    def result(self):
        self.copy(1, self.ring.right).wait_recv()
        self.copy(2, self.ring.opposite).wait_recv()
        return (self.slots[0] + self.slots[1]) + (self.slots[2] + self.slots[3])

    def finish(self):
        for which in range(3):
            self.copy(which, self.ring.me).wait_send()


class PlaneSum:
    def __init__(self, near, far, source, out, size, first, scratch, sems, keep, direct=False,
                 base=0):
        if direct:
            self.arrived, self.mid, self.done = scratch
        else:
            self.landing, self.passing, self.arrived, self.mid, self.done = scratch
        self.direct, self.base = direct, base
        self.out, self.size, self.near, self.far, self.keep = out, size, near, far, keep
        self.halves = ((0, first), (first, size - first))

        def rows(block, half):
            begin, count = (0, size) if half is None else self.halves[half]
            return pl.ds(pl.multiple_of(base + block * size + begin, 16), count)

        def half_rows(half):
            return pl.ds(0, size) if half is None else pl.ds(*self.halves[half])

        self.half_rows = half_rows
        def part(block, half):
            return source.at[rows(block, half)]

        if direct:
            self.scatter = DirectScatter(near, part, lambda side: self.arrived.at[side], sems[0])
        else:
            self.scatter = Scatter(
                near,
                part,
                lambda half: self.landing.at[half_rows(half)],
                lambda half: self.passing.at[half_rows(half)],
                lambda side, half: self.arrived.at[side, half_rows(half)],
                sems[0],
            )
        kind = DirectGather if direct else Gather
        self.gather = kind(far, lambda block, half: self.mid.at[block, half_rows(half)], sems[1])
        self.spread = kind(
            near,
            lambda block, half: out.at[rows(block, half)],
            sems[2],
            lambda half: self.done.at[half_rows(half)],
        )

    def start(self):
        self.scatter.start_far()
        self.scatter.start_near()

    def relay(self):
        self.scatter.relay()

    def middle(self):
        self.scatter.wait()
        if self.direct:
            self.mid[self.far.me] = self.scatter.whole().astype(LOW)
        else:
            for half in range(2):
                self.mid[self.far.me, self.half_rows(half)] = self.scatter.total(half).astype(LOW)
        self.gather.start()

    def middle_relay(self):
        self.gather.relay()

    def own(self):
        place = pl.ds(
            pl.multiple_of(self.base + self.near.me * self.size, 16), self.size
        )
        return pltpu.make_async_copy(self.done, self.out.at[place], self.keep)

    def end(self):
        self.gather.wait_all()
        four = [self.mid[block].astype(F32) for block in range(4)]
        self.done[...] = ((four[0] + four[1]) + (four[2] + four[3])).astype(LOW)
        self.spread.start()
        self.own().start()

    def end_relay(self):
        self.spread.relay()

    def wait(self):
        self.spread.wait_all()
        self.own().wait()

    def finish(self):
        self.scatter.finish()
        self.gather.finish()
        self.spread.finish()


FEED_BLOCK, AT_BLOCK = 144, 80


def feed_output(features):
    return (jax.ShapeDtypeStruct((2, 4 * FEED_BLOCK, features), LOW),)


def kept_output(features):
    return (jax.ShapeDtypeStruct((2, 4 * AT_BLOCK, features), LOW),)


def plane_scratch(size, features, direct=False):
    dma = pltpu.SemaphoreType.DMA

    def low(*shape):
        return pltpu.VMEM(shape + (features,), LOW)

    if direct:
        return [low(3, size), low(4, size), low(size)] + [dma((3,))] * 6
    return [low(size), low(size), low(2, size), low(4, size), low(size)] + [dma((6,))] * 6


def feed_scratch(features, rows):
    dma = pltpu.SemaphoreType.DMA
    return (
        [pltpu.VMEM((2, 2, 4, rows, features), LOW), pltpu.VMEM((2, 4 * FEED_BLOCK, features), LOW)]
        + plane_scratch(FEED_BLOCK, features) * 2
        + [dma((2,)), dma((2,)), dma((2,)), dma((2,)), dma((1,)), dma((1,))]
    )


def across_scratch(features, rows):
    share = features // 4
    dma = pltpu.SemaphoreType.DMA

    def low(*shape):
        return pltpu.VMEM(shape + (features,), LOW)

    return (
        [low(2, 2, rows), low(2, 2, rows), low(2, features)]
        + ([low(share), low(share), low(2, share)] + [dma((6,))] * 2) * 2
        + [dma((4,)), dma((4,)), dma((4,))]
    )


WIDE_PIECES = ((0, 0, 80, 48, 0), (1, 0, 80, 48, 1))
FINE_PIECES = ((0, 0, 48, 32, 0), (0, 192, 32, 16, 1), (1, 0, 48, 32, 1), (1, 192, 32, 16, 0))


def attention_scratch(features, pieces, direct):
    dma = pltpu.SemaphoreType.DMA
    scratch = []
    for piece in pieces:
        scratch += plane_scratch(piece[2], features, direct)
    return scratch + [dma((len(pieces),)), dma((2,)), dma((2,))]


def take_planes(take, count, direct=False):
    planes = []
    for _ in range(count):
        scratch = [next(take) for _ in range(3 if direct else 5)]
        sems = [next(take) for _ in range(6)]
        planes.append((scratch, [tuple(sems[i : i + 2]) for i in (0, 2, 4)]))
    return planes


def hand_over(layer, src, dst, sems, which=0):
    section = lax.axis_index("section")
    copy = functools.partial(remote, src, dst, sems, which, sibling())

    def start():
        @pl.when(section != layer)
        def _():
            copy().start()

    def wait():
        @pl.when(section != layer)
        def _():
            copy().wait_send()

        @pl.when(section == layer)
        def _():
            copy().wait_recv()

    return start, wait


class SwappedInputs:
    def __init__(self, zero, other, targets, local_sems, swap):
        self.zero, self.other, self.targets = zero, other, targets
        self.local_sems, self.swap, self.pair = local_sems, swap, sibling()

    def copies(self, first, which):
        own, sent = (self.zero, self.other) if first else (self.other, self.zero)
        target = self.targets[which]
        return (
            lambda: pltpu.make_async_copy(own[which], target.at[0], self.local_sems.at[which]),
            lambda: remote(sent[which], target.at[1], self.swap, which, self.pair),
        )

    def start(self):
        section = lax.axis_index("section")
        for first in (True, False):

            @pl.when(section == (0 if first else 1))
            def _(first=first):
                for which in range(len(self.targets)):
                    self.copies(first, which)[1]().start()
                for which in range(len(self.targets)):
                    self.copies(first, which)[0]().start()

    def wait(self, whiches):
        for which in whiches:
            keep, send = self.copies(True, which)
            keep().wait()
            send().wait_recv()

    def finish(self):
        for which in range(len(self.targets)):
            self.copies(True, which)[1]().wait_send()


class AttentionSum:
    def __init__(self, layer, kept, results, take, pieces, direct):
        out, other = results
        planes = take_planes(take, len(pieces), direct)
        keep, send, recv = [next(take) for _ in range(3)]
        y_ring, z_ring = Ring("y"), Ring("z")
        orders = ((y_ring, z_ring), (z_ring, y_ring))
        self.pieces = pieces
        self.planes = [
            PlaneSum(
                *orders[order], kept.at[matrix], out.at[matrix], size, first, *planes[which],
                keep.at[which], direct, base,
            )
            for which, (matrix, base, size, first, order) in enumerate(pieces)
        ]
        self.given = [
            hand_over(layer, out.at[which], other.at[which], (send, recv), which)
            for which in range(2)
        ]

    def run(self, name, matrix=None):
        for plane, piece in zip(self.planes, self.pieces):
            if matrix is None or piece[0] == matrix:
                getattr(plane, name)()

    def hand(self, matrix):
        self.run("wait", matrix)
        self.given[matrix][0]()

    def finish(self):
        self.run("finish")
        for given in self.given:
            given[1]()


class FeedSum:
    def __init__(self, features, operands, out, take):
        two, pre, hidden, out_all = operands
        self.features = features
        self.feed_in, self.feed_sum = next(take), next(take)
        planes = take_planes(take, 2)
        local_sems, swap_send, swap_recv, keep, end_send, end_recv = [
            next(take) for _ in range(6)
        ]
        self.end_sems = (end_send, end_recv)
        self.inputs = SwappedInputs(
            (two, pre), (hidden, out_all), (self.feed_in.at[0], self.feed_in.at[1]), local_sems,
            (swap_send, swap_recv),
        )
        y_ring, z_ring = Ring("y"), Ring("z")
        orders = ((y_ring, z_ring), (z_ring, y_ring))
        self.planes = [
            PlaneSum(
                *orders[which], self.feed_sum.at[which], out.at[which], FEED_BLOCK, 80,
                *planes[which], keep.at[which],
            )
            for which in range(2)
        ]

    def products(self):
        self.inputs.wait((0, 1))
        features, whole = self.features, 4 * FEED_BLOCK
        right = self.feed_in[1].reshape(-1, features)
        for begin in range(0, features, 256):
            count = min(256, features - begin)
            left = self.feed_in[0, :, :, :, pl.ds(begin, count)].reshape(-1, count)
            product = dot_tn(left, right).astype(LOW)
            first = max(0, min(count, whole - begin))
            if first:
                self.feed_sum[0, pl.ds(begin, first)] = product[:first]
            if first < count:
                self.feed_sum[1, pl.ds(begin + first - whole, count - first)] = product[first:]
        spare = 2 * whole - features
        self.feed_sum[1, pl.ds(whole - spare, spare)] = jnp.zeros((spare, features), LOW)
        self.run("start")

    def run(self, name):
        for plane in self.planes:
            getattr(plane, name)()

    def finish(self):
        self.inputs.finish()
        self.run("finish")


class AcrossSum:
    def __init__(self, features, operands, kept, take):
        one, mixed, dq, dk, dv, branch = operands
        self.features, self.share, self.kept = features, features // 4, kept
        share = self.share
        self.at_left, self.at_right, self.at_sum = [next(take) for _ in range(3)]
        self.halves = halves = ((0, 144), (144, share - 144))
        x_ring = Ring("x")
        self.across = []
        for which in range(2):
            landing, passing, arrived, send, recv = [next(take) for _ in range(5)]

            def part(block, half, which=which):
                begin, count = halves[half]
                row = pl.multiple_of(block * share + begin, 16)
                return self.at_sum.at[which, pl.ds(row, count)]

            def cut(ref):
                return lambda half: ref.at[pl.ds(*halves[half])]

            self.across.append(
                Scatter(
                    x_ring, part, cut(landing), cut(passing),
                    lambda side, half, arrived=arrived: arrived.at[side, pl.ds(*halves[half])],
                    (send, recv),
                )
            )
        local_sems, swap_send, swap_recv = [next(take) for _ in range(3)]
        self.inputs = SwappedInputs(
            (one, dq, one, dk),
            (one, dv, mixed, branch),
            (self.at_left.at[0], self.at_right.at[0], self.at_left.at[1], self.at_right.at[1]),
            local_sems,
            (swap_send, swap_recv),
        )

    def products(self, which):
        self.inputs.wait((2 * which, 2 * which + 1))
        features = self.features
        right = self.at_right[which].reshape(-1, features)
        for begin in range(0, features, 256):
            count = min(256, features - begin)
            left = self.at_left[which, :, :, pl.ds(begin, count)].reshape(-1, count)
            self.at_sum[which, pl.ds(begin, count)] = dot_tn(left, right).astype(LOW)
        self.across[which].start_far()

    def relay(self, which):
        self.across[which].relay()
        self.across[which].start_near()

    def keep(self, which):
        across = self.across[which]
        across.wait()
        for half in range(2):
            self.kept[which, pl.ds(*self.halves[half])] = across.total(half).astype(LOW)
        spare = 4 * AT_BLOCK - self.share
        self.kept[which, pl.ds(self.share, spare)] = jnp.zeros((spare, self.features), LOW)

    def finish(self):
        self.inputs.finish()
        for across in self.across:
            across.finish()


def gradient_kernel(features, *refs):
    take = iter(refs)

    def some(count):
        return [next(take) for _ in range(count)]

    operands = some(6)
    y_a, y_b, dx_a, dx_b, feed_zero, gain_in, kept_one = some(7)
    (feed_given,), at_zero, at_one = some(1), some(2), some(2)
    act_out, grad_out, gain_out = some(3)
    (kept_zero,) = some(1)
    sums = AcrossSum(features, operands, kept_zero, take)
    zero = AttentionSum(0, kept_zero, at_zero, take, FINE_PIECES, True)
    one = AttentionSum(1, kept_one, at_one, take, WIDE_PIECES, False)
    (gain_pair, gain_x, gain_y, gain_z, gain_send, gain_recv, last_send, last_recv, keep_sems,
     feed_send, feed_recv) = some(11)
    x_ring, y_ring, z_ring = Ring("x"), Ring("y"), Ring("z")
    pair, section = sibling(), lax.axis_index("section")
    greet_all(far=True)
    sums.inputs.start()
    feed = hand_over(0, feed_zero, feed_given, (feed_send, feed_recv))

    def last_copies(y, dx):
        return (
            remote(y, act_out.at[section], (last_send, last_recv), 0, pair),
            remote(dx, grad_out.at[section], (last_send, last_recv), 1, pair),
        )

    def keep_copies(y, dx):
        return (
            pltpu.make_async_copy(y, act_out.at[section], keep_sems.at[0]),
            pltpu.make_async_copy(dx, grad_out.at[section], keep_sems.at[1]),
        )

    @pl.when(section == 0)
    def _():
        for copy in last_copies(y_b, dx_b) + keep_copies(y_a, dx_a):
            copy.start()

    @pl.when(section == 1)
    def _():
        for copy in last_copies(y_a, dx_a) + keep_copies(y_b, dx_b):
            copy.start()

    gain_pair[0] = gain_in[...]
    swap_gain = remote(gain_pair.at[0], gain_pair.at[1], (gain_send, gain_recv), 9, pair)
    swap_gain.start()
    one.run("start")
    sums.products(0)
    sums.products(1)
    feed[0]()
    swap_gain.wait()
    gain_x[x_ring.me] = gain_pair[0] + gain_pair[1]
    small = [
        SmallSum(ring, slots, (gain_send.at[pl.ds(3 * i, 3)], gain_recv.at[pl.ds(3 * i, 3)]))
        for i, (ring, slots) in enumerate(((x_ring, gain_x), (y_ring, gain_y), (z_ring, gain_z)))
    ]
    small[0].start()
    one.run("relay")
    sums.relay(0)
    small[0].relay()
    one.run("middle")
    gain_y[y_ring.me] = small[0].result()
    small[1].start()
    one.run("middle_relay")
    small[1].relay()
    sums.keep(0)
    sums.relay(1)
    zero.run("start", 0)
    one.run("end")
    gain_z[z_ring.me] = small[1].result()
    small[2].start()
    zero.run("middle", 0)
    one.run("end_relay")
    small[2].relay()
    zero.run("end", 0)
    gain_out[...] = small[2].result()
    sums.keep(1)
    zero.run("start", 1)
    one.hand(0)
    one.hand(1)
    zero.hand(0)
    zero.run("middle", 1)
    zero.run("end", 1)
    zero.hand(1)
    zero.finish()
    one.finish()
    sums.finish()
    feed[1]()
    for each in small:
        each.finish()
    for copy in last_copies(y_a, dx_a) + keep_copies(y_a, dx_a):
        copy.wait()


def sum_gradients(features, rows, operands, last, gain, kept):
    dma = pltpu.SemaphoreType.DMA
    small = [pltpu.VMEM((4, 8, features), F32)] * 3
    return pl.pallas_call(
        functools.partial(gradient_kernel, features),
        out_shape=feed_output(features)
        + kept_output(features) * 4
        + (
            jax.ShapeDtypeStruct((2, rows, features), LOW),
            jax.ShapeDtypeStruct((2, rows, features), LOW),
            jax.ShapeDtypeStruct((8, features), F32),
        ),
        in_specs=[anywhere()] * 11 + [in_vmem()] * 2,
        out_specs=[anywhere()] * 7 + [in_vmem()],
        scratch_shapes=[pltpu.VMEM((2, 4 * AT_BLOCK, features), LOW)]
        + across_scratch(features, rows)
        + attention_scratch(features, FINE_PIECES, True)
        + attention_scratch(features, WIDE_PIECES, False)
        + [pltpu.VMEM((2, 8, features), F32)]
        + small
        + [dma((10,)), dma((10,)), dma((2,)), dma((2,)), dma((2,)), dma((1,)), dma((1,))],
        compiler_params=pltpu.CompilerParams(
            collective_id=5, has_side_effects=True, vmem_limit_bytes=60 * 2**20
        ),
        cost_estimate=pl.CostEstimate(
            flops=3 * 10**9, bytes_accessed=60 * 10**6, transcendentals=0
        ),
        name="sum_gradients",
    )(*operands, *last, gain, kept)


def widen_kernel(features, share, *refs):
    (feed_zero, feed_zero_given, feed_one, feed_one_given, at_zero, at_zero_given, at_one,
     at_one_given, up_ref, down_ref, qkv_ref, out_ref, up_in, down_in, first_in, other_in,
     up_wide, down_wide, qkv_wide, out_wide, in_sems, out_sems) = refs
    section = lax.axis_index("section")
    targets = (up_in, down_in, first_in, other_in)
    sources = (
        (feed_zero, feed_zero_given, at_zero, at_zero_given),
        (feed_one_given, feed_one, at_one_given, at_one),
    )

    def fetch(which, side):
        return pltpu.make_async_copy(sources[side][which], targets[which], in_sems.at[which])

    for side in range(2):

        @pl.when(section == side)
        def _(side=side):
            for which in range(4):
                fetch(which, side).start()

    outs = [
        pltpu.make_async_copy(src, dst, out_sems.at[which])
        for which, (src, dst) in enumerate(
            ((up_wide, up_ref), (down_wide, down_ref), (qkv_wide, qkv_ref), (out_wide, out_ref))
        )
    ]
    whole = 4 * FEED_BLOCK
    for which, wide in ((0, up_wide), (1, down_wide)):
        fetch(which, 0).wait()
        wide[pl.ds(0, whole)] = targets[which][0].astype(F32)
        wide[pl.ds(whole, features - whole)] = targets[which][1, : features - whole].astype(F32)
        outs[which].start()
    fetch(2, 0).wait()
    fetch(3, 0).wait()
    qkv_wide[...] = jnp.concatenate(
        [first_in[0, :share], first_in[1, :share], other_in[0, :share]], axis=1
    ).astype(F32)
    outs[2].start()
    out_wide[...] = other_in[1, :share].astype(F32)
    outs[3].start()
    for copy in outs:
        copy.wait()


def widen(features, share, *sums):
    def wide(*shape):
        return jax.ShapeDtypeStruct(shape, F32)

    shapes = (
        wide(features, features), wide(features, features), wide(share, 3 * features),
        wide(share, features),
    )
    return pl.pallas_call(
        functools.partial(widen_kernel, features, share),
        out_shape=shapes,
        in_specs=[anywhere()] * 8,
        out_specs=[anywhere()] * 4,
        scratch_shapes=[pltpu.VMEM((2, 4 * FEED_BLOCK, features), LOW)] * 2
        + [pltpu.VMEM((2, 4 * AT_BLOCK, features), LOW)] * 2
        + [pltpu.VMEM(shape.shape, F32) for shape in shapes]
        + [pltpu.SemaphoreType.DMA((4,))] * 2,
        compiler_params=pltpu.CompilerParams(vmem_limit_bytes=40 * 2**20),
        cost_estimate=pl.CostEstimate(
            flops=0, bytes_accessed=24 * 10**6, transcendentals=0
        ),
        name="widen",
    )(*sums)


def doc_numbers(lengths, positions):
    doc_ends = jnp.cumsum(lengths)
    return jnp.sum((positions[:, None] >= doc_ends[None, :]).astype(jnp.int32), axis=1)


def swapped(block):
    return lax.ppermute(block, "section", [(0, 1), (1, 0)])


def body(tokens, cotangent, doc_lengths, norm_gains, w_qkv, w_out, w_up, w_down):
    batches, rows, features = tokens.shape
    share = w_qkv.shape[1]
    seq_rows = rows * lax.axis_size("tensor")
    section = lax.axis_index("section")
    is_first = section == 0

    def choose(zero_side, one_side):
        return jnp.where(is_first, zero_side, one_side)

    own_tokens = lax.dynamic_index_in_dim(tokens, section, 0, keepdims=False)
    own_cotangent = lax.dynamic_index_in_dim(cotangent, section, 0, keepdims=False)
    lengths = lax.dynamic_index_in_dim(doc_lengths, section, 0, keepdims=False)
    own_places = lax.axis_index("tensor") * rows + jnp.arange(rows, dtype=jnp.int32)
    all_places = jnp.arange(seq_rows, dtype=jnp.int32)
    own_docs = doc_numbers(lengths, own_places)
    all_docs = doc_numbers(lengths, all_places)
    allowed = (all_places[None, :] <= own_places[:, None]) & (
        all_docs[None, :] == own_docs[:, None]
    )
    bias = jnp.where(allowed, 0.0, -1e30).astype(F32)
    bias_turned = bias.T

    feed = (w_up[0], swapped(w_up[0]), w_down[0], swapped(w_down[0]))
    shard = jnp.stack(
        [w_qkv[0, :, :features], w_qkv[0, :, features : 2 * features], w_qkv[0, :, 2 * features :],
         w_out[0]]
    )
    gain_shard = jnp.pad(norm_gains[0], ((0, 14), (0, 0)))
    at_mine, at_theirs, gain_mine, gain_theirs = gather_weights(shard, gain_shard)
    attention = (
        at_mine.reshape(4, features, features), at_theirs.reshape(4, features, features)
    )

    def whole_gains(block):
        return block[:, :2].transpose(1, 0, 2).reshape(2, features).astype(F32)

    gain_mine, gain_theirs = whole_gains(gain_mine), whole_gains(gain_theirs)
    gains = (choose(gain_mine, gain_theirs), choose(gain_theirs, gain_mine))

    inputs = own_tokens
    saved = []
    for layer in range(2):
        results = forward_layer(layer, inputs, bias, gains[layer], attention, feed)
        saved.append((inputs,) + tuple(results))
        inputs = results[0]

    grad = own_cotangent
    gain_grads, input_grads, operands = [None, None], [None, None], ()
    for layer in (1, 0):
        (x, _, middle, normed_one, query, key, value, mixed, normed_two, act, hidden) = saved[layer]
        results = backward_layer(
            layer, x, grad, bias_turned, gains[layer], middle, query, key, value, act,
            attention, feed, operands + (saved[0][8], saved[0][10]) if layer == 0 else (),
        )
        (grad, gain_grads[layer], out_all, pre_grad, branch, dquery, dkey, dvalue) = results[:8]
        input_grads[layer] = grad
        operands = (
            normed_two, pre_grad, hidden, out_all, normed_one, mixed, dquery, dkey, dvalue, branch,
        )
    feed_one, feed_one_given, feed_zero, kept_one = results[8:]
    gain_rows = jnp.concatenate(gain_grads + [jnp.zeros((4, features), F32)], axis=0)
    (feed_zero_given, at_zero, at_zero_given, at_one, at_one_given, activations, input_grads,
     gain_total) = sum_gradients(
        features, rows, operands[4:], (saved[0][1], saved[1][1], *input_grads, feed_zero),
        gain_rows, kept_one,
    )
    gain_own = lax.dynamic_slice(
        gain_total, (2 * section, lax.axis_index("tensor") * share), (2, share)
    )

    grad_up, grad_down, grad_qkv, grad_out = widen(
        features, share, feed_zero, feed_zero_given, feed_one, feed_one_given, at_zero,
        at_zero_given, at_one, at_one_given,
    )
    return (
        activations[None],
        input_grads[None],
        gain_own[None],
        grad_qkv[None],
        grad_out[None],
        grad_up[None],
        grad_down[None],
    )


def solution(mesh):
    placed = (
        P("dp", "tensor", None),
        P("dp", "tensor", None),
        P("dp", None),
        P("section", None, "tensor"),
        P("section", "tensor", None),
        P("section", "tensor", None),
        P("section", None, "tensor"),
        P("section", "tensor", None),
    )
    return jax.shard_map(
        body,
        mesh=mesh,
        in_specs=placed,
        out_specs=(
            P("section", "dp", "tensor", None),
            P("section", "dp", "tensor", None),
            P("section", None, "tensor"),
            P("section", "tensor", None),
            P("section", "tensor", None),
            P("section", None, "tensor"),
            P("section", "tensor", None),
        ),
        check_vma=False,
    )
```

```python
import functools
import jax
import jax.numpy as jnp
from jax import lax
from jax.experimental import pallas as pl
from jax.experimental.pallas import tpu as pltpu
from jax.sharding import PartitionSpec as P

HEAD_DIM = 64
LOW = jnp.bfloat16
F32 = jnp.float32
MESH = pl.DeviceIdType.MESH


def dot_nn(left, right):
    return lax.dot_general(left, right, (((1,), (0,)), ((), ())), preferred_element_type=F32)


def dot_nt(left, right):
    return lax.dot_general(left, right, (((1,), (1,)), ((), ())), preferred_element_type=F32)


def dot_tn(left, right):
    return lax.dot_general(left, right, (((0,), (0,)), ((), ())), preferred_element_type=F32)


class Ring:
    def __init__(self, axis):
        whole = lax.axis_index("dp")
        rest = None
        if axis == "x":
            self.me = lax.axis_index("tensor")
        elif axis == "y":
            self.me, rest = lax.rem(whole, 4), lax.div(whole, 4) * 4
        else:
            self.me, rest = lax.div(whole, 4), lax.rem(whole, 4)
        self.right = lax.rem(self.me + 1, 4)
        self.left = lax.rem(self.me + 3, 4)
        self.opposite = lax.rem(self.me + 2, 4)

        def device(place):
            if axis == "x":
                return {"tensor": place}
            if axis == "y":
                return {"dp": rest + place}
            return {"dp": place * 4 + rest}

        self.to_right, self.to_left = device(self.right), device(self.left)
        self.to_opposite = device(self.opposite)


def sibling():
    return {"section": 1 - lax.axis_index("section")}


def greet(*targets):
    barrier = pltpu.get_barrier_semaphore()
    for target in targets:
        pl.semaphore_signal(barrier, inc=1, device_id=target, device_id_type=MESH)
    pl.semaphore_wait(barrier, len(targets))


def remote(src, dst, sems, which, target):
    return pltpu.make_async_remote_copy(
        src_ref=src,
        dst_ref=dst,
        send_sem=sems[0].at[which],
        recv_sem=sems[1].at[which],
        device_id=target,
        device_id_type=MESH,
    )


class Gather:
    def __init__(self, ring, slot, sems, own=None):
        self.ring, self.slot, self.sems = ring, slot, sems
        self.own = own if own is not None else lambda half: slot(ring.me, half)

    def copy(self, which, arriving=False):
        ring = self.ring
        half = (0, 1, 1, 0, 0, 1)[which]
        goes_right = which in (0, 2, 4)
        target = ring.to_right if goes_right else ring.to_left
        if which < 4:
            source_block = ring.left if goes_right else ring.right
            if not arriving:
                return remote(self.own(half), self.slot(ring.me, half), self.sems, which, target)
        else:
            source_block = ring.opposite
            if not arriving:
                handed = self.slot(ring.left if goes_right else ring.right, half)
                return remote(handed, handed, self.sems, which, target)
        part = self.slot(source_block, half)
        return remote(part, part, self.sems, which, target)

    def start(self):
        for which in range(4):
            self.copy(which).start()

    def relay(self):
        for which in (0, 1):
            self.copy(which, arriving=True).wait_recv()
            self.copy(which + 4).start()

    def wait_left(self):
        self.copy(2, arriving=True).wait_recv()

    def wait_right(self):
        self.copy(3, arriving=True).wait_recv()

    def wait_opposite(self):
        self.copy(4, arriving=True).wait_recv()
        self.copy(5, arriving=True).wait_recv()

    def wait_all(self):
        self.wait_left()
        self.wait_right()
        self.wait_opposite()

    def finish(self):
        for which in range(6):
            self.copy(which).wait_send()


class Scatter:
    def __init__(self, ring, part, landing, passing, arrived, sems):
        self.ring, self.part, self.landing, self.passing = ring, part, landing, passing
        self.arrived, self.sems = arrived, sems

    def copy(self, which):
        ring = self.ring
        half = (0, 1, 1, 0, 0, 1)[which]
        goes_right = which in (0, 2, 4)
        if which < 2:
            src, dst = self.part(ring.opposite, half), self.landing(half)
        else:
            dst = self.arrived(0 if goes_right else 1, half)
            if which < 4:
                src = self.part(ring.right if goes_right else ring.left, half)
            else:
                src = self.passing(half)
        return remote(src, dst, self.sems, which, ring.to_right if goes_right else ring.to_left)

    def start_near(self):
        self.copy(2).start()
        self.copy(3).start()

    def start_far(self):
        self.copy(0).start()
        self.copy(1).start()

    def relay(self):
        for half, block in ((0, self.ring.right), (1, self.ring.left)):
            self.copy(half).wait_recv()
            added = self.part(block, half)[...].astype(F32) + self.landing(half)[...].astype(F32)
            self.passing(half)[...] = added.astype(LOW)
            self.copy(half + 4).start()

    def wait(self):
        for which in (2, 3, 4, 5):
            self.copy(which).wait_recv()

    def total(self, half):
        return (
            self.part(self.ring.me, half)[...].astype(F32)
            + self.arrived(0, half)[...].astype(F32)
            + self.arrived(1, half)[...].astype(F32)
        )

    def finish(self):
        for which in range(6):
            self.copy(which).wait_send()


class DirectGather:
    def __init__(self, ring, slot, sems, own=None):
        self.ring, self.slot, self.sems = ring, slot, sems
        self.own = own if own is not None else lambda half: slot(ring.me, half)

    def copy(self, which):
        target = (self.ring.to_right, self.ring.to_left, self.ring.to_opposite)[which]
        return remote(self.own(None), self.slot(self.ring.me, None), self.sems, which, target)

    def start(self):
        for which in (2, 0, 1):
            self.copy(which).start()

    def relay(self):
        pass

    def wait_all(self):
        for which, block in enumerate((self.ring.left, self.ring.right, self.ring.opposite)):
            part = self.slot(block, None)
            remote(part, part, self.sems, which, self.ring.to_right).wait_recv()

    def finish(self):
        for which in range(3):
            self.copy(which).wait_send()


class DirectScatter:
    def __init__(self, ring, part, arrived, sems):
        self.ring, self.part, self.arrived, self.sems = ring, part, arrived, sems

    def copy(self, which):
        ring = self.ring
        block = (ring.right, ring.left, ring.opposite)[which]
        target = (ring.to_right, ring.to_left, ring.to_opposite)[which]
        return remote(self.part(block, None), self.arrived(which), self.sems, which, target)

    def start_far(self):
        self.copy(2).start()

    def start_near(self):
        self.copy(0).start()
        self.copy(1).start()

    def relay(self):
        pass

    def wait(self):
        for which in range(3):
            self.copy(which).wait_recv()

    def whole(self):
        near = self.arrived(0)[...].astype(F32) + self.arrived(1)[...].astype(F32)
        own = self.part(self.ring.me, None)[...].astype(F32)
        return (own + near) + self.arrived(2)[...].astype(F32)

    def finish(self):
        for which in range(3):
            self.copy(which).wait_send()


def row_gather(ring, full, sems, columns=slice(None)):
    half = full.shape[1] // 2
    return Gather(
        ring, lambda block, which: full.at[block, pl.ds(which * half, half), columns], sems
    )


def row_scatter(ring, parts, landing, passing, arrived, sems, columns=slice(None)):
    half = parts.shape[1] // 2

    def rows(which):
        return pl.ds(which * half, half)

    return Scatter(
        ring,
        lambda block, which: parts.at[block, rows(which), columns],
        lambda which: landing.at[which, :, columns],
        lambda which: passing.at[which, :, columns],
        lambda side, which: arrived.at[side, rows(which), columns],
        sems,
    )


def row_total(scatter):
    scatter.wait()
    return jnp.concatenate([scatter.total(0), scatter.total(1)], axis=0)


def head_groups(features):
    pairs = pair_columns(features)
    middle = (len(pairs) + 1) // 2
    begin = pairs[middle][0]
    return (
        (pl.ds(0, begin), pairs[:middle]),
        (pl.ds(begin, features - begin), pairs[middle:]),
    )


def norm_stats(values):
    average = jnp.mean(values, axis=-1, keepdims=True)
    centered = values - average
    variance = jnp.mean(centered * centered, axis=-1, keepdims=True)
    scale = lax.rsqrt(variance + 1e-05)
    return centered * scale, scale


def norm_back(values, gain, grad):
    xhat, scale = norm_stats(values)
    scaled = grad * gain
    part = scale * (
        scaled
        - jnp.mean(scaled, axis=-1, keepdims=True)
        - xhat * jnp.mean(scaled * xhat, axis=-1, keepdims=True)
    )
    return part, jnp.sum(grad * xhat, axis=0, keepdims=True)


def gelu_tanh(values):
    inner = 0.7978845608028654 * (values + 0.044715 * values * values * values)
    return 0.5 * values * (1.0 + jnp.tanh(inner))


def gelu_slope(values):
    square = values * values
    bent = jnp.tanh(0.7978845608028654 * values * (1.0 + 0.044715 * square))
    slope = 0.7978845608028654 * (1.0 + 3.0 * 0.044715 * square)
    return 0.5 * (1.0 + bent) + 0.5 * values * (1.0 - bent * bent) * slope


def pick_copies(layer, mine, theirs, target, sem):
    def start():
        mine_here = lax.axis_index("section") == layer

        @pl.when(mine_here)
        def _():
            pltpu.make_async_copy(mine, target, sem).start()

        @pl.when(jnp.logical_not(mine_here))
        def _():
            pltpu.make_async_copy(theirs, target, sem).start()

    def wait():
        pltpu.make_async_copy(mine, target, sem).wait()

    return start, wait


def pair_columns(features):
    width = 2 * HEAD_DIM
    return [
        (start, min(width, features - start)) for start in range(0, features, width)
    ]


def head_masks(width):
    lanes = lax.broadcasted_iota(jnp.int32, (1, width), 1)
    if width == HEAD_DIM:
        return [None]
    return [lanes < HEAD_DIM, lanes >= HEAD_DIM]


def masked(values, mask):
    return values if mask is None else jnp.where(mask, values, jnp.zeros_like(values))


def attention_weights(layer, mine, theirs, target, sems):
    return [
        pick_copies(layer, mine.at[which], theirs.at[which], target.at[which], sems.at[which])
        for which in range(4)
    ]


def forward_kernel(
    layer, features, x_ref, bias_ref, gains_ref, at_mine, at_theirs, up_mine, up_theirs, down_mine,
    down_theirs, y_ref, middle_ref, one_ref, query_ref, key_ref, value_ref, mixed_ref, two_ref,
    act_ref, hidden_ref, at_w, up_w, down_w, weight_sems, parts, landing, passing, arrived,
    key_send, key_recv, value_send, value_recv, two_send, two_recv, sum_send, sum_recv,
):
    ring = Ring("x")
    me = ring.me
    fetches = attention_weights(layer, at_mine, at_theirs, at_w, weight_sems)
    fetches.append(pick_copies(layer, up_mine, up_theirs, up_w, weight_sems.at[4]))
    fetches.append(pick_copies(layer, down_mine, down_theirs, down_w, weight_sems.at[5]))
    for which in (1, 2, 0, 3, 4, 5):
        fetches[which][0]()
    greet(ring.to_right, ring.to_left)
    rows = x_ref.shape[0]
    inputs = x_ref[...].astype(F32)
    xhat, _ = norm_stats(inputs)
    one_ref[...] = (xhat * gains_ref[0:1, :]).astype(LOW)
    normed_one = one_ref[...]
    groups = head_groups(features)
    keys, values = [], []
    fetches[1][1]()
    fetches[2][1]()
    for which, (columns, _) in enumerate(groups):
        key_ref[me, :, columns] = dot_nn(normed_one, at_w[1, :, columns]).astype(LOW)
        keys.append(
            row_gather(ring, key_ref, (key_send.at[which], key_recv.at[which]), columns)
        )
        if which == 0:
            keys[0].start()
        value_ref[me, :, columns] = dot_nn(normed_one, at_w[2, :, columns]).astype(LOW)
        values.append(
            row_gather(ring, value_ref, (value_send.at[which], value_recv.at[which]), columns)
        )
        if which == 0:
            values[0].start()
    fetches[0][1]()
    query_ref[...] = dot_nn(normed_one, at_w[0]).astype(LOW)
    keys[0].relay()
    values[0].relay()
    keys[1].start()
    values[1].start()
    bias = bias_ref[...]

    def attend(begin, width):
        columns = pl.ds(begin, width)
        queries = query_ref[:, columns]
        key_block = key_ref[:, :, columns].reshape(4 * rows, width)
        value_block = value_ref[:, :, columns].reshape(4 * rows, width)
        mixed = None
        for mask in head_masks(width):
            scores = dot_nt(masked(queries, mask), key_block) * 0.125 + bias
            raised = jnp.exp(scores - jnp.max(scores, axis=-1, keepdims=True))
            probs = raised * (1.0 / jnp.sum(raised, axis=-1, keepdims=True))
            own = dot_nn(probs.astype(LOW), value_block)
            mixed = own if mixed is None else jnp.where(mask, own, mixed)
        mixed_ref[:, columns] = mixed.astype(LOW)

    for which, (_, pairs) in enumerate(groups):
        keys[which].wait_all()
        values[which].wait_all()
        for count, (begin, width) in enumerate(pairs):
            attend(begin, width)
            if which == 0 and count == 2:
                keys[1].relay()
                values[1].relay()
    fetches[3][1]()
    middle_ref[...] = x_ref[...].astype(F32) + dot_nn(mixed_ref[...], at_w[3])
    xhat, _ = norm_stats(middle_ref[...])
    two_ref[me] = (xhat * gains_ref[1:2, :]).astype(LOW)
    tokens = row_gather(ring, two_ref, (two_send, two_recv))
    tokens.start()
    fetches[4][1]()
    fetches[5][1]()
    sums = row_scatter(ring, parts, landing, passing, arrived, (sum_send, sum_recv))

    def feed(block):
        act_ref[block] = dot_nn(two_ref[block], up_w[...])
        hidden_ref[block] = gelu_tanh(act_ref[block]).astype(LOW)
        parts[block] = dot_nn(hidden_ref[block], down_w[...]).astype(LOW)

    feed(me)
    tokens.relay()
    tokens.wait_left()
    feed(ring.left)
    tokens.wait_right()
    feed(ring.right)
    sums.start_near()
    tokens.wait_opposite()
    feed(ring.opposite)
    sums.start_far()
    sums.relay()
    y_ref[...] = (middle_ref[...] + row_total(sums)).astype(LOW)
    for gather in keys + values:
        gather.finish()
    tokens.finish()
    sums.finish()


def scatter_scratch(rows, features):
    return [
        pltpu.VMEM((4, rows, features), LOW),
        pltpu.VMEM((2, rows // 2, features), LOW),
        pltpu.VMEM((2, rows // 2, features), LOW),
        pltpu.VMEM((2, rows, features), LOW),
    ]


def weight_scratch(features, hidden, matrices=4):
    shape = (features, features) if matrices == 1 else (matrices, features, features)
    return [
        pltpu.VMEM(shape, LOW),
        pltpu.VMEM((features, hidden), LOW),
        pltpu.VMEM((hidden, features), LOW),
        pltpu.SemaphoreType.DMA((6,)),
    ]


def in_vmem():
    return pl.BlockSpec(memory_space=pltpu.VMEM)


def anywhere():
    return pl.BlockSpec(memory_space=pl.ANY)


def forward_layer(layer, x, bias, gains, attention, feed):
    rows, features = x.shape
    hidden = feed[0].shape[1]
    out_shape = (
        jax.ShapeDtypeStruct((rows, features), LOW),
        jax.ShapeDtypeStruct((rows, features), F32),
        jax.ShapeDtypeStruct((rows, features), LOW),
        jax.ShapeDtypeStruct((rows, features), LOW),
        jax.ShapeDtypeStruct((4, rows, features), LOW),
        jax.ShapeDtypeStruct((4, rows, features), LOW),
        jax.ShapeDtypeStruct((rows, features), LOW),
        jax.ShapeDtypeStruct((4, rows, features), LOW),
        jax.ShapeDtypeStruct((4, rows, hidden), F32),
        jax.ShapeDtypeStruct((4, rows, hidden), LOW),
    )
    return pl.pallas_call(
        functools.partial(forward_kernel, layer, features),
        out_shape=out_shape,
        in_specs=[in_vmem()] * 3 + [anywhere()] * 6,
        out_specs=[in_vmem()] * len(out_shape),
        scratch_shapes=weight_scratch(features, hidden)
        + scatter_scratch(rows, features)
        + [pltpu.SemaphoreType.DMA((2, 6))] * 4
        + [pltpu.SemaphoreType.DMA((6,))] * 4,
        compiler_params=pltpu.CompilerParams(
            collective_id=layer, has_side_effects=True, vmem_limit_bytes=56 * 2**20
        ),
        cost_estimate=pl.CostEstimate(
            flops=3 * 10**9, bytes_accessed=24 * 10**6, transcendentals=10**6
        ),
        name=f"layer_forward_{layer}",
    )(x, bias, gains, *attention, *feed)


def backward_kernel(layer, features, *refs):
    take = iter(refs)

    def some(count):
        return [next(take) for _ in range(count)]

    (x_ref, dy_ref, bias_ref, gains_ref, middle_ref, query_ref, key_ref, value_ref, act_ref,
     at_mine, at_theirs, up_mine, up_theirs, down_mine, down_theirs) = some(15)
    operands = some(12) if layer == 0 else None
    (dx_ref, gain_ref, out_ref, pre_ref, branch_ref, dquery_ref, dkey_ref, dvalue_ref) = some(8)
    results = some(4) if layer == 0 else None
    (at_w, up_w, down_w, weight_sems, parts, landing, passing, arrived, parts_b, landing_b,
     passing_b, arrived_b, parts_c, landing_c, passing_c, arrived_c, mixed_grad, kept_grad,
     out_send, out_recv, sum_send, sum_recv, key_send, key_recv, value_send, value_recv) = some(26)
    extra = layer == 0
    if extra:
        (two, pre, hidden, out_all, one, mixed, dq, dk, dv, branch, two_own, hidden_own) = operands
        feed_out, feed_given, feed_own_out, kept = results
        feed_one = FeedSum(features, (two, pre, hidden, out_all), feed_out, take)
        feed_own = FeedSum(
            features, (two_own, pre_ref, hidden_own, out_ref), feed_own_out, take
        )
        across = AcrossSum(features, (one, mixed, dq, dk, dv, branch), kept, take)
        given = hand_over(1, feed_out, feed_given, feed_one.end_sems)
    ring = Ring("x")
    me = ring.me
    fetches = [
        pick_copies(layer, at_mine.at[which], at_theirs.at[which], target, weight_sems.at[which])
        for which, target in enumerate((up_w, down_w, at_w, at_w))
    ]
    fetches.append(pick_copies(layer, up_mine, up_theirs, up_w, weight_sems.at[4]))
    fetches.append(pick_copies(layer, down_mine, down_theirs, down_w, weight_sems.at[5]))
    for which in (5, 4, 3):
        fetches[which][0]()
    rows = x_ref.shape[0]
    out_ref[me] = dy_ref[...]
    if not extra:
        greet(ring.to_right, ring.to_left)
    else:
        greet_all()
    grads = row_gather(ring, out_ref, (out_send, out_recv))
    grads.start()
    if extra:
        across.inputs.start()
        feed_one.inputs.start()
    sums = row_scatter(ring, parts, landing, passing, arrived, (sum_send, sum_recv))
    fetches[5][1]()
    fetches[4][1]()

    def feed(block):
        hidden_grad = dot_nt(out_ref[block], down_w[...])
        pre_ref[block] = (hidden_grad * gelu_slope(act_ref[block])).astype(LOW)
        parts[block] = dot_nt(pre_ref[block], up_w[...]).astype(LOW)

    feed(me)
    grads.relay()
    if extra:
        across.products(0)
        feed_one.products()
    grads.wait_left()
    feed(ring.left)
    grads.wait_right()
    feed(ring.right)
    sums.start_near()
    grads.wait_opposite()
    feed(ring.opposite)
    sums.start_far()
    for which in (0, 1):
        fetches[which][0]()
    if extra:
        feed_own.inputs.start()
        feed_one.run("relay")
    sums.relay()
    if extra:
        across.products(1)
    middle_part, gain_two = norm_back(middle_ref[...], gains_ref[1:2, :], row_total(sums))
    gain_ref[1:2, :] = gain_two
    middle_grad = dy_ref[...].astype(F32) + middle_part
    kept_grad[...] = middle_grad
    branch_ref[...] = middle_grad.astype(LOW)
    fetches[3][1]()
    mixed_grad[...] = dot_nt(branch_ref[...], at_w[...]).astype(LOW)
    fetches[2][0]()
    bias = bias_ref[...]
    groups = head_groups(features)
    dkeys = [
        row_scatter(ring, parts_b, landing_b, passing_b, arrived_b,
                    (key_send.at[which], key_recv.at[which]), columns)
        for which, (columns, _) in enumerate(groups)
    ]
    dvalues = [
        row_scatter(ring, parts_c, landing_c, passing_c, arrived_c,
                    (value_send.at[which], value_recv.at[which]), columns)
        for which, (columns, _) in enumerate(groups)
    ]

    def send_pair(which):
        for scatter in (dkeys[which], dvalues[which]):
            scatter.start_far()
        for scatter in (dkeys[which], dvalues[which]):
            scatter.start_near()

    def relay_pair(which):
        for scatter in (dkeys[which], dvalues[which]):
            scatter.relay()

    for count, (begin, width) in enumerate(pair_columns(features)):
        columns = pl.ds(begin, width)
        queries = query_ref[:, columns]
        outer = mixed_grad[:, columns]
        key_block = key_ref[:, :, columns].reshape(4 * rows, width)
        value_block = value_ref[:, :, columns].reshape(4 * rows, width)
        dquery = dkey = dvalue = None
        for mask in head_masks(width):
            query_one, outer_one = masked(queries, mask), masked(outer, mask)
            scores = dot_nt(key_block, query_one) * 0.125 + bias
            raised = jnp.exp(scores - jnp.max(scores, axis=0, keepdims=True))
            probs = raised * (1.0 / jnp.sum(raised, axis=0, keepdims=True))
            probs_grad = dot_nt(value_block, outer_one)
            mean = jnp.sum(probs * probs_grad, axis=0, keepdims=True)
            score_grad = (probs * (probs_grad - mean)).astype(LOW)
            own_query = dot_tn(score_grad, key_block)
            own_key = dot_nn(score_grad, query_one)
            own_value = dot_nn(probs.astype(LOW), outer_one)
            if dquery is None:
                dquery, dkey, dvalue = own_query, own_key, own_value
            else:
                dquery = jnp.where(mask, own_query, dquery)
                dkey, dvalue = dkey + own_key, dvalue + own_value
        dquery_ref[:, columns] = (dquery * 0.125).astype(LOW)
        parts_b[:, :, columns] = (dkey * 0.125).astype(LOW).reshape(4, rows, width)
        parts_c[:, :, columns] = dvalue.astype(LOW).reshape(4, rows, width)
        if begin + width == groups[0][0].size:
            send_pair(0)
        if extra and count == 1:
            feed_one.run("middle")
            across.relay(0)
        if extra and count == 4:
            feed_own.products()
            feed_one.run("middle_relay")
        if extra and count == 7:
            feed_own.run("relay")
    relay_pair(0)
    send_pair(1)
    for which in (0, 1, 2):
        fetches[which][1]()
    one_grad = dot_nt(dquery_ref[...], up_w[...])
    if extra:
        feed_one.run("end")
    relay_pair(1)
    if extra:
        across.relay(1)
        feed_own.run("middle")
        feed_one.run("end_relay")
    for which, (columns, _) in enumerate(groups):
        dkey_ref[:, columns] = row_total(dkeys[which]).astype(LOW)
    one_grad = one_grad + dot_nt(dkey_ref[...], down_w[...])
    if extra:
        across.keep(0)
        feed_own.run("middle_relay")
    for which, (columns, _) in enumerate(groups):
        dvalue_ref[:, columns] = row_total(dvalues[which]).astype(LOW)
    one_grad = one_grad + dot_nt(dvalue_ref[...], at_w[...])
    inputs_part, gain_one = norm_back(x_ref[...].astype(F32), gains_ref[0:1, :], one_grad)
    gain_ref[0:1, :] = gain_one
    dx_ref[...] = (kept_grad[...] + inputs_part).astype(LOW)
    if extra:
        feed_one.run("wait")
        given[0]()
        feed_own.run("end")
        across.keep(1)
        feed_own.run("end_relay")
        feed_one.finish()
        across.finish()
        given[1]()
        feed_own.run("wait")
        feed_own.finish()
    grads.finish()
    sums.finish()
    for scatter in dkeys + dvalues:
        scatter.finish()


def greet_all(far=False):
    rings = [Ring(axis) for axis in ("x", "y", "z")]
    greet(
        *[ring.to_right for ring in rings], *[ring.to_left for ring in rings], sibling(),
        *[ring.to_opposite for ring in rings[1:] if far],
    )


def backward_layer(layer, x, dy, bias, gains, middle, query, key, value, act, attention, feed,
                   operands=()):
    rows, features = x.shape
    hidden = feed[0].shape[1]
    out_shape = (
        jax.ShapeDtypeStruct((rows, features), LOW),
        jax.ShapeDtypeStruct((2, features), F32),
        jax.ShapeDtypeStruct((4, rows, features), LOW),
        jax.ShapeDtypeStruct((4, rows, hidden), LOW),
        jax.ShapeDtypeStruct((rows, features), LOW),
        jax.ShapeDtypeStruct((rows, features), LOW),
        jax.ShapeDtypeStruct((rows, features), LOW),
        jax.ShapeDtypeStruct((rows, features), LOW),
    )
    sums = feed_output(features) * 3 + kept_output(features) if layer == 0 else ()
    return pl.pallas_call(
        functools.partial(backward_kernel, layer, features),
        out_shape=out_shape + sums,
        in_specs=[in_vmem()] * 9 + [anywhere()] * (6 + len(operands)),
        out_specs=[in_vmem()] * len(out_shape) + [anywhere()] * 3 * (len(sums) // 4)
        + [in_vmem()] * (len(sums) // 4),
        scratch_shapes=weight_scratch(features, hidden, 1)
        + scatter_scratch(rows, features) * 3
        + [pltpu.VMEM((rows, features), LOW), pltpu.VMEM((rows, features), F32)]
        + [pltpu.SemaphoreType.DMA((6,))] * 4
        + [pltpu.SemaphoreType.DMA((2, 6))] * 4
        + (
            feed_scratch(features, rows) * 2 + across_scratch(features, rows)
            if layer == 0
            else []
        ),
        compiler_params=pltpu.CompilerParams(
            collective_id=2 + layer, has_side_effects=True, vmem_limit_bytes=62 * 2**20
        ),
        cost_estimate=pl.CostEstimate(
            flops=4 * 10**9, bytes_accessed=24 * 10**6, transcendentals=10**6
        ),
        name=f"layer_backward_{layer}",
    )(x, dy, bias, gains, middle, query, key, value, act, *attention, *feed, *operands)


X_ROWS, Y_ROWS = 64, 112


def weights_kernel(
    shard_ref, gain_ref, mine_ref, theirs_ref, gain_mine, gain_theirs, local_sems, x_send, x_recv,
    yx_send, yx_recv, zx_send, zx_recv, y_send, y_recv, z_send, z_recv, gain_send, gain_recv,
    pair_send, pair_recv,
):
    x_ring, y_ring, z_ring = Ring("x"), Ring("y"), Ring("z")
    mine_y, mine_z, mine_x = y_ring.me, z_ring.me, x_ring.me
    share = shard_ref.shape[1]
    y_begin, z_begin = X_ROWS, X_ROWS + Y_ROWS
    z_rows = share - z_begin
    all_x, all_y, all_z = pl.ds(0, X_ROWS), pl.ds(y_begin, Y_ROWS), pl.ds(z_begin, z_rows)
    y_half = (pl.ds(y_begin, 48), pl.ds(y_begin + 48, Y_ROWS - 48))
    z_half = (pl.ds(z_begin, 48), pl.ds(z_begin + 48, z_rows - 48))
    pair = sibling()
    greet(
        x_ring.to_right, x_ring.to_left, y_ring.to_right, y_ring.to_left, z_ring.to_right,
        z_ring.to_left, pair,
    )
    locals_ = [
        pltpu.make_async_copy(
            shard_ref.at[mine_y, all_y], mine_ref.at[mine_y, mine_x, all_y], local_sems.at[0]
        ),
        pltpu.make_async_copy(
            shard_ref.at[mine_z, all_z], mine_ref.at[mine_z, mine_x, all_z], local_sems.at[1]
        ),
        pltpu.make_async_copy(
            shard_ref.at[:, all_x], mine_ref.at[:, mine_x, all_x], local_sems.at[2]
        ),
        pltpu.make_async_copy(gain_ref, gain_mine.at[mine_x], local_sems.at[3]),
    ]
    first_y = Gather(
        x_ring,
        lambda block, half: mine_ref.at[mine_y, block, y_half[half]],
        (yx_send, yx_recv),
        lambda half: shard_ref.at[mine_y, y_half[half]],
    )
    first_z = Gather(
        x_ring,
        lambda block, half: mine_ref.at[mine_z, block, z_half[half]],
        (zx_send, zx_recv),
        lambda half: shard_ref.at[mine_z, z_half[half]],
    )
    along_x = Gather(
        x_ring,
        lambda block, half: mine_ref.at[pl.ds(2 * half, 2), block, all_x],
        (x_send, x_recv),
        lambda half: shard_ref.at[pl.ds(2 * half, 2), all_x],
    )
    along_y = Gather(
        y_ring,
        lambda block, half: mine_ref.at[block, pl.ds(2 * half, 2), all_y],
        (y_send, y_recv),
    )
    along_z = Gather(
        z_ring,
        lambda block, half: mine_ref.at[block, pl.ds(2 * half, 2), all_z],
        (z_send, z_recv),
    )

    def gain_copy(which, block, src=None):
        part = gain_mine.at[block]
        target = x_ring.to_left if which == 1 else x_ring.to_right
        return remote(part if src is None else src, part, (gain_send, gain_recv), which, target)

    def hand(which, region):
        return remote(mine_ref.at[region], theirs_ref.at[region], (pair_send, pair_recv), which, pair)

    handed = []

    def hand_on(which, region):
        copy = hand(which, region)
        copy.start()
        handed.append(copy)

    first_y.start()
    first_z.start()
    for copy in locals_:
        copy.start()
    gain_copy(0, mine_x, gain_ref).start()
    gain_copy(1, mine_x, gain_ref).start()
    first_y.relay()
    first_z.relay()
    along_x.start()
    first_y.wait_all()
    locals_[0].wait()
    along_y.start()
    hand_on(0, (mine_y, slice(None), all_y))
    first_z.wait_all()
    locals_[1].wait()
    along_z.start()
    hand_on(1, (mine_z, slice(None), all_z))
    gain_copy(0, x_ring.left).wait_recv()
    gain_copy(2, x_ring.left).start()
    along_x.relay()
    along_y.relay()
    along_z.relay()
    along_x.wait_all()
    locals_[2].wait()
    hand_on(2, (slice(None), slice(None), all_x))
    along_y.wait_left()
    hand_on(3, (y_ring.left, slice(None), all_y))
    along_z.wait_left()
    hand_on(4, (z_ring.left, slice(None), all_z))
    along_y.wait_right()
    hand_on(5, (y_ring.right, slice(None), all_y))
    along_z.wait_right()
    hand_on(6, (z_ring.right, slice(None), all_z))
    gain_copy(1, x_ring.right).wait_recv()
    gain_copy(2, x_ring.opposite).wait_recv()
    locals_[3].wait()
    gains = remote(gain_mine, gain_theirs, (pair_send, pair_recv), 9, pair)
    gains.start()
    along_y.wait_opposite()
    hand_on(7, (y_ring.opposite, slice(None), all_y))
    along_z.wait_opposite()
    hand_on(8, (z_ring.opposite, slice(None), all_z))
    for copy in handed + [gains]:
        copy.wait()
    for which in range(3):
        gain_copy(which, mine_x).wait_send()
    for gather in (first_y, first_z, along_x, along_y, along_z):
        gather.finish()


def gather_weights(shard, gain):
    mats, share, features = shard.shape
    full = jax.ShapeDtypeStruct((mats, 4, share, features), LOW)
    gains = jax.ShapeDtypeStruct((4,) + gain.shape, LOW)
    return pl.pallas_call(
        weights_kernel,
        out_shape=(full, full, gains, gains),
        in_specs=[in_vmem()] * 2,
        out_specs=[anywhere()] * 4,
        scratch_shapes=[pltpu.SemaphoreType.DMA((4,))]
        + [pltpu.SemaphoreType.DMA((6,))] * 10
        + [pltpu.SemaphoreType.DMA((3,))] * 2
        + [pltpu.SemaphoreType.DMA((10,))] * 2,
        compiler_params=pltpu.CompilerParams(collective_id=4, has_side_effects=True),
        cost_estimate=pl.CostEstimate(flops=0, bytes_accessed=60 * 10**6, transcendentals=0),
        name="gather_weights",
    )(shard, gain)


class SmallSum:
    def __init__(self, ring, slots, sems):
        self.ring, self.slots, self.sems = ring, slots, sems

    def copy(self, which, block):
        target = self.ring.to_left if which == 1 else self.ring.to_right
        part = self.slots.at[block]
        return remote(part, part, self.sems, which, target)

    def start(self):
        self.copy(0, self.ring.me).start()
        self.copy(1, self.ring.me).start()

    def relay(self):
        self.copy(0, self.ring.left).wait_recv()
        self.copy(2, self.ring.left).start()

    def result(self):
        self.copy(1, self.ring.right).wait_recv()
        self.copy(2, self.ring.opposite).wait_recv()
        return (self.slots[0] + self.slots[1]) + (self.slots[2] + self.slots[3])

    def finish(self):
        for which in range(3):
            self.copy(which, self.ring.me).wait_send()


class PlaneSum:
    def __init__(self, near, far, source, out, size, first, scratch, sems, keep, direct=False,
                 base=0):
        if direct:
            self.arrived, self.mid, self.done = scratch
        else:
            self.landing, self.passing, self.arrived, self.mid, self.done = scratch
        self.direct, self.base = direct, base
        self.out, self.size, self.near, self.far, self.keep = out, size, near, far, keep
        self.halves = ((0, first), (first, size - first))

        def rows(block, half):
            begin, count = (0, size) if half is None else self.halves[half]
            return pl.ds(pl.multiple_of(base + block * size + begin, 16), count)

        def half_rows(half):
            return pl.ds(0, size) if half is None else pl.ds(*self.halves[half])

        self.half_rows = half_rows
        def part(block, half):
            return source.at[rows(block, half)]

        if direct:
            self.scatter = DirectScatter(near, part, lambda side: self.arrived.at[side], sems[0])
        else:
            self.scatter = Scatter(
                near,
                part,
                lambda half: self.landing.at[half_rows(half)],
                lambda half: self.passing.at[half_rows(half)],
                lambda side, half: self.arrived.at[side, half_rows(half)],
                sems[0],
            )
        kind = DirectGather if direct else Gather
        self.gather = kind(far, lambda block, half: self.mid.at[block, half_rows(half)], sems[1])
        self.spread = kind(
            near,
            lambda block, half: out.at[rows(block, half)],
            sems[2],
            lambda half: self.done.at[half_rows(half)],
        )

    def start(self):
        self.scatter.start_far()
        self.scatter.start_near()

    def relay(self):
        self.scatter.relay()

    def middle(self):
        self.scatter.wait()
        if self.direct:
            self.mid[self.far.me] = self.scatter.whole().astype(LOW)
        else:
            for half in range(2):
                self.mid[self.far.me, self.half_rows(half)] = self.scatter.total(half).astype(LOW)
        self.gather.start()

    def middle_relay(self):
        self.gather.relay()

    def own(self):
        place = pl.ds(
            pl.multiple_of(self.base + self.near.me * self.size, 16), self.size
        )
        return pltpu.make_async_copy(self.done, self.out.at[place], self.keep)

    def end(self):
        self.gather.wait_all()
        four = [self.mid[block].astype(F32) for block in range(4)]
        self.done[...] = ((four[0] + four[1]) + (four[2] + four[3])).astype(LOW)
        self.spread.start()
        self.own().start()

    def end_relay(self):
        self.spread.relay()

    def wait(self):
        self.spread.wait_all()
        self.own().wait()

    def finish(self):
        self.scatter.finish()
        self.gather.finish()
        self.spread.finish()


FEED_BLOCK, AT_BLOCK = 144, 80


def feed_output(features):
    return (jax.ShapeDtypeStruct((2, 4 * FEED_BLOCK, features), LOW),)


def kept_output(features):
    return (jax.ShapeDtypeStruct((2, 4 * AT_BLOCK, features), LOW),)


def plane_scratch(size, features, direct=False):
    dma = pltpu.SemaphoreType.DMA

    def low(*shape):
        return pltpu.VMEM(shape + (features,), LOW)

    if direct:
        return [low(3, size), low(4, size), low(size)] + [dma((3,))] * 6
    return [low(size), low(size), low(2, size), low(4, size), low(size)] + [dma((6,))] * 6


def feed_scratch(features, rows):
    dma = pltpu.SemaphoreType.DMA
    return (
        [pltpu.VMEM((2, 2, 4, rows, features), LOW), pltpu.VMEM((2, 4 * FEED_BLOCK, features), LOW)]
        + plane_scratch(FEED_BLOCK, features) * 2
        + [dma((2,)), dma((2,)), dma((2,)), dma((2,)), dma((1,)), dma((1,))]
    )


def across_scratch(features, rows):
    share = features // 4
    dma = pltpu.SemaphoreType.DMA

    def low(*shape):
        return pltpu.VMEM(shape + (features,), LOW)

    return (
        [low(2, 2, rows), low(2, 2, rows), low(2, features)]
        + ([low(share), low(share), low(2, share)] + [dma((6,))] * 2) * 2
        + [dma((4,)), dma((4,)), dma((4,))]
    )


WIDE_PIECES = ((0, 0, 80, 48, 0), (1, 0, 80, 48, 1))
FINE_PIECES = ((0, 0, 48, 32, 0), (0, 192, 32, 16, 1), (1, 0, 48, 32, 1), (1, 192, 32, 16, 0))


def attention_scratch(features, pieces, direct):
    dma = pltpu.SemaphoreType.DMA
    scratch = []
    for piece in pieces:
        scratch += plane_scratch(piece[2], features, direct)
    return scratch + [dma((len(pieces),)), dma((2,)), dma((2,))]


def take_planes(take, count, direct=False):
    planes = []
    for _ in range(count):
        scratch = [next(take) for _ in range(3 if direct else 5)]
        sems = [next(take) for _ in range(6)]
        planes.append((scratch, [tuple(sems[i : i + 2]) for i in (0, 2, 4)]))
    return planes


def hand_over(layer, src, dst, sems, which=0):
    section = lax.axis_index("section")
    copy = functools.partial(remote, src, dst, sems, which, sibling())

    def start():
        @pl.when(section != layer)
        def _():
            copy().start()

    def wait():
        @pl.when(section != layer)
        def _():
            copy().wait_send()

        @pl.when(section == layer)
        def _():
            copy().wait_recv()

    return start, wait


class SwappedInputs:
    def __init__(self, zero, other, targets, local_sems, swap):
        self.zero, self.other, self.targets = zero, other, targets
        self.local_sems, self.swap, self.pair = local_sems, swap, sibling()

    def copies(self, first, which):
        own, sent = (self.zero, self.other) if first else (self.other, self.zero)
        target = self.targets[which]
        return (
            lambda: pltpu.make_async_copy(own[which], target.at[0], self.local_sems.at[which]),
            lambda: remote(sent[which], target.at[1], self.swap, which, self.pair),
        )

    def start(self):
        section = lax.axis_index("section")
        for first in (True, False):

            @pl.when(section == (0 if first else 1))
            def _(first=first):
                for which in range(len(self.targets)):
                    self.copies(first, which)[1]().start()
                for which in range(len(self.targets)):
                    self.copies(first, which)[0]().start()

    def wait(self, whiches):
        for which in whiches:
            keep, send = self.copies(True, which)
            keep().wait()
            send().wait_recv()

    def finish(self):
        for which in range(len(self.targets)):
            self.copies(True, which)[1]().wait_send()


class AttentionSum:
    def __init__(self, layer, kept, results, take, pieces, direct):
        out, other = results
        planes = take_planes(take, len(pieces), direct)
        keep, send, recv = [next(take) for _ in range(3)]
        y_ring, z_ring = Ring("y"), Ring("z")
        orders = ((y_ring, z_ring), (z_ring, y_ring))
        self.pieces = pieces
        self.planes = [
            PlaneSum(
                *orders[order], kept.at[matrix], out.at[matrix], size, first, *planes[which],
                keep.at[which], direct, base,
            )
            for which, (matrix, base, size, first, order) in enumerate(pieces)
        ]
        self.given = [
            hand_over(layer, out.at[which], other.at[which], (send, recv), which)
            for which in range(2)
        ]

    def run(self, name, matrix=None):
        for plane, piece in zip(self.planes, self.pieces):
            if matrix is None or piece[0] == matrix:
                getattr(plane, name)()

    def hand(self, matrix):
        self.run("wait", matrix)
        self.given[matrix][0]()

    def finish(self):
        self.run("finish")
        for given in self.given:
            given[1]()


class FeedSum:
    def __init__(self, features, operands, out, take):
        two, pre, hidden, out_all = operands
        self.features = features
        self.feed_in, self.feed_sum = next(take), next(take)
        planes = take_planes(take, 2)
        local_sems, swap_send, swap_recv, keep, end_send, end_recv = [
            next(take) for _ in range(6)
        ]
        self.end_sems = (end_send, end_recv)
        self.inputs = SwappedInputs(
            (two, pre), (hidden, out_all), (self.feed_in.at[0], self.feed_in.at[1]), local_sems,
            (swap_send, swap_recv),
        )
        y_ring, z_ring = Ring("y"), Ring("z")
        orders = ((y_ring, z_ring), (z_ring, y_ring))
        self.planes = [
            PlaneSum(
                *orders[which], self.feed_sum.at[which], out.at[which], FEED_BLOCK, 80,
                *planes[which], keep.at[which],
            )
            for which in range(2)
        ]

    def products(self):
        self.inputs.wait((0, 1))
        features, whole = self.features, 4 * FEED_BLOCK
        right = self.feed_in[1].reshape(-1, features)
        for begin in range(0, features, 256):
            count = min(256, features - begin)
            left = self.feed_in[0, :, :, :, pl.ds(begin, count)].reshape(-1, count)
            product = dot_tn(left, right).astype(LOW)
            first = max(0, min(count, whole - begin))
            if first:
                self.feed_sum[0, pl.ds(begin, first)] = product[:first]
            if first < count:
                self.feed_sum[1, pl.ds(begin + first - whole, count - first)] = product[first:]
        spare = 2 * whole - features
        self.feed_sum[1, pl.ds(whole - spare, spare)] = jnp.zeros((spare, features), LOW)
        self.run("start")

    def run(self, name):
        for plane in self.planes:
            getattr(plane, name)()

    def finish(self):
        self.inputs.finish()
        self.run("finish")


class AcrossSum:
    def __init__(self, features, operands, kept, take):
        one, mixed, dq, dk, dv, branch = operands
        self.features, self.share, self.kept = features, features // 4, kept
        share = self.share
        self.at_left, self.at_right, self.at_sum = [next(take) for _ in range(3)]
        self.halves = halves = ((0, 144), (144, share - 144))
        x_ring = Ring("x")
        self.across = []
        for which in range(2):
            landing, passing, arrived, send, recv = [next(take) for _ in range(5)]

            def part(block, half, which=which):
                begin, count = halves[half]
                row = pl.multiple_of(block * share + begin, 16)
                return self.at_sum.at[which, pl.ds(row, count)]

            def cut(ref):
                return lambda half: ref.at[pl.ds(*halves[half])]

            self.across.append(
                Scatter(
                    x_ring, part, cut(landing), cut(passing),
                    lambda side, half, arrived=arrived: arrived.at[side, pl.ds(*halves[half])],
                    (send, recv),
                )
            )
        local_sems, swap_send, swap_recv = [next(take) for _ in range(3)]
        self.inputs = SwappedInputs(
            (one, dq, one, dk),
            (one, dv, mixed, branch),
            (self.at_left.at[0], self.at_right.at[0], self.at_left.at[1], self.at_right.at[1]),
            local_sems,
            (swap_send, swap_recv),
        )

    def products(self, which):
        self.inputs.wait((2 * which, 2 * which + 1))
        features = self.features
        right = self.at_right[which].reshape(-1, features)
        for begin in range(0, features, 256):
            count = min(256, features - begin)
            left = self.at_left[which, :, :, pl.ds(begin, count)].reshape(-1, count)
            self.at_sum[which, pl.ds(begin, count)] = dot_tn(left, right).astype(LOW)
        self.across[which].start_far()

    def relay(self, which):
        self.across[which].relay()
        self.across[which].start_near()

    def keep(self, which):
        across = self.across[which]
        across.wait()
        for half in range(2):
            self.kept[which, pl.ds(*self.halves[half])] = across.total(half).astype(LOW)
        spare = 4 * AT_BLOCK - self.share
        self.kept[which, pl.ds(self.share, spare)] = jnp.zeros((spare, self.features), LOW)

    def finish(self):
        self.inputs.finish()
        for across in self.across:
            across.finish()


def gradient_kernel(features, *refs):
    take = iter(refs)

    def some(count):
        return [next(take) for _ in range(count)]

    operands = some(6)
    y_a, y_b, dx_a, dx_b, feed_zero, gain_in, kept_one = some(7)
    (feed_given,), at_zero, at_one = some(1), some(2), some(2)
    act_out, grad_out, gain_out = some(3)
    (kept_zero,) = some(1)
    sums = AcrossSum(features, operands, kept_zero, take)
    zero = AttentionSum(0, kept_zero, at_zero, take, FINE_PIECES, True)
    one = AttentionSum(1, kept_one, at_one, take, WIDE_PIECES, False)
    (gain_pair, gain_x, gain_y, gain_z, gain_send, gain_recv, last_send, last_recv, keep_sems,
     feed_send, feed_recv) = some(11)
    x_ring, y_ring, z_ring = Ring("x"), Ring("y"), Ring("z")
    pair, section = sibling(), lax.axis_index("section")
    greet_all(far=True)
    sums.inputs.start()
    feed = hand_over(0, feed_zero, feed_given, (feed_send, feed_recv))

    def last_copies(y, dx):
        return (
            remote(y, act_out.at[section], (last_send, last_recv), 0, pair),
            remote(dx, grad_out.at[section], (last_send, last_recv), 1, pair),
        )

    def keep_copies(y, dx):
        return (
            pltpu.make_async_copy(y, act_out.at[section], keep_sems.at[0]),
            pltpu.make_async_copy(dx, grad_out.at[section], keep_sems.at[1]),
        )

    @pl.when(section == 0)
    def _():
        for copy in last_copies(y_b, dx_b) + keep_copies(y_a, dx_a):
            copy.start()

    @pl.when(section == 1)
    def _():
        for copy in last_copies(y_a, dx_a) + keep_copies(y_b, dx_b):
            copy.start()

    gain_pair[0] = gain_in[...]
    swap_gain = remote(gain_pair.at[0], gain_pair.at[1], (gain_send, gain_recv), 9, pair)
    swap_gain.start()
    one.run("start")
    sums.products(0)
    sums.products(1)
    feed[0]()
    swap_gain.wait()
    gain_x[x_ring.me] = gain_pair[0] + gain_pair[1]
    small = [
        SmallSum(ring, slots, (gain_send.at[pl.ds(3 * i, 3)], gain_recv.at[pl.ds(3 * i, 3)]))
        for i, (ring, slots) in enumerate(((x_ring, gain_x), (y_ring, gain_y), (z_ring, gain_z)))
    ]
    small[0].start()
    one.run("relay")
    sums.relay(0)
    small[0].relay()
    one.run("middle")
    gain_y[y_ring.me] = small[0].result()
    small[1].start()
    one.run("middle_relay")
    small[1].relay()
    sums.keep(0)
    sums.relay(1)
    zero.run("start", 0)
    one.run("end")
    gain_z[z_ring.me] = small[1].result()
    small[2].start()
    zero.run("middle", 0)
    one.run("end_relay")
    small[2].relay()
    zero.run("end", 0)
    gain_out[...] = small[2].result()
    sums.keep(1)
    zero.run("start", 1)
    one.hand(0)
    one.hand(1)
    zero.hand(0)
    zero.run("middle", 1)
    zero.run("end", 1)
    zero.hand(1)
    zero.finish()
    one.finish()
    sums.finish()
    feed[1]()
    for each in small:
        each.finish()
    for copy in last_copies(y_a, dx_a) + keep_copies(y_a, dx_a):
        copy.wait()


def sum_gradients(features, rows, operands, last, gain, kept):
    dma = pltpu.SemaphoreType.DMA
    small = [pltpu.VMEM((4, 8, features), F32)] * 3
    return pl.pallas_call(
        functools.partial(gradient_kernel, features),
        out_shape=feed_output(features)
        + kept_output(features) * 4
        + (
            jax.ShapeDtypeStruct((2, rows, features), LOW),
            jax.ShapeDtypeStruct((2, rows, features), LOW),
            jax.ShapeDtypeStruct((8, features), F32),
        ),
        in_specs=[anywhere()] * 11 + [in_vmem()] * 2,
        out_specs=[anywhere()] * 7 + [in_vmem()],
        scratch_shapes=[pltpu.VMEM((2, 4 * AT_BLOCK, features), LOW)]
        + across_scratch(features, rows)
        + attention_scratch(features, FINE_PIECES, True)
        + attention_scratch(features, WIDE_PIECES, False)
        + [pltpu.VMEM((2, 8, features), F32)]
        + small
        + [dma((10,)), dma((10,)), dma((2,)), dma((2,)), dma((2,)), dma((1,)), dma((1,))],
        compiler_params=pltpu.CompilerParams(
            collective_id=5, has_side_effects=True, vmem_limit_bytes=60 * 2**20
        ),
        cost_estimate=pl.CostEstimate(
            flops=3 * 10**9, bytes_accessed=60 * 10**6, transcendentals=0
        ),
        name="sum_gradients",
    )(*operands, *last, gain, kept)


def widen_kernel(features, share, *refs):
    (feed_zero, feed_zero_given, feed_one, feed_one_given, at_zero, at_zero_given, at_one,
     at_one_given, up_ref, down_ref, qkv_ref, out_ref, up_in, down_in, first_in, other_in,
     up_wide, down_wide, qkv_wide, out_wide, in_sems, out_sems) = refs
    section = lax.axis_index("section")
    targets = (up_in, down_in, first_in, other_in)
    sources = (
        (feed_zero, feed_zero_given, at_zero, at_zero_given),
        (feed_one_given, feed_one, at_one_given, at_one),
    )

    def fetch(which, side):
        return pltpu.make_async_copy(sources[side][which], targets[which], in_sems.at[which])

    for side in range(2):

        @pl.when(section == side)
        def _(side=side):
            for which in range(4):
                fetch(which, side).start()

    outs = [
        pltpu.make_async_copy(src, dst, out_sems.at[which])
        for which, (src, dst) in enumerate(
            ((up_wide, up_ref), (down_wide, down_ref), (qkv_wide, qkv_ref), (out_wide, out_ref))
        )
    ]
    whole = 4 * FEED_BLOCK
    for which, wide in ((0, up_wide), (1, down_wide)):
        fetch(which, 0).wait()
        wide[pl.ds(0, whole)] = targets[which][0].astype(F32)
        wide[pl.ds(whole, features - whole)] = targets[which][1, : features - whole].astype(F32)
        outs[which].start()
    fetch(2, 0).wait()
    fetch(3, 0).wait()
    qkv_wide[...] = jnp.concatenate(
        [first_in[0, :share], first_in[1, :share], other_in[0, :share]], axis=1
    ).astype(F32)
    outs[2].start()
    out_wide[...] = other_in[1, :share].astype(F32)
    outs[3].start()
    for copy in outs:
        copy.wait()


def widen(features, share, *sums):
    def wide(*shape):
        return jax.ShapeDtypeStruct(shape, F32)

    shapes = (
        wide(features, features), wide(features, features), wide(share, 3 * features),
        wide(share, features),
    )
    return pl.pallas_call(
        functools.partial(widen_kernel, features, share),
        out_shape=shapes,
        in_specs=[anywhere()] * 8,
        out_specs=[anywhere()] * 4,
        scratch_shapes=[pltpu.VMEM((2, 4 * FEED_BLOCK, features), LOW)] * 2
        + [pltpu.VMEM((2, 4 * AT_BLOCK, features), LOW)] * 2
        + [pltpu.VMEM(shape.shape, F32) for shape in shapes]
        + [pltpu.SemaphoreType.DMA((4,))] * 2,
        compiler_params=pltpu.CompilerParams(vmem_limit_bytes=62 * 2**20),
        cost_estimate=pl.CostEstimate(
            flops=0, bytes_accessed=24 * 10**6, transcendentals=0
        ),
        name="widen",
    )(*sums)


def doc_numbers(lengths, positions):
    doc_ends = jnp.cumsum(lengths)
    return jnp.sum((positions[:, None] >= doc_ends[None, :]).astype(jnp.int32), axis=1)


def swapped(block):
    return lax.ppermute(block, "section", [(0, 1), (1, 0)])


def body(tokens, cotangent, doc_lengths, norm_gains, w_qkv, w_out, w_up, w_down):
    batches, rows, features = tokens.shape
    share = w_qkv.shape[1]
    seq_rows = rows * lax.axis_size("tensor")
    section = lax.axis_index("section")
    is_first = section == 0

    def choose(zero_side, one_side):
        return jnp.where(is_first, zero_side, one_side)

    own_tokens = lax.dynamic_index_in_dim(tokens, section, 0, keepdims=False)
    own_cotangent = lax.dynamic_index_in_dim(cotangent, section, 0, keepdims=False)
    lengths = lax.dynamic_index_in_dim(doc_lengths, section, 0, keepdims=False)
    own_places = lax.axis_index("tensor") * rows + jnp.arange(rows, dtype=jnp.int32)
    all_places = jnp.arange(seq_rows, dtype=jnp.int32)
    own_docs = doc_numbers(lengths, own_places)
    all_docs = doc_numbers(lengths, all_places)
    allowed = (all_places[None, :] <= own_places[:, None]) & (
        all_docs[None, :] == own_docs[:, None]
    )
    bias = jnp.where(allowed, 0.0, -1e30).astype(F32)
    bias_turned = bias.T

    feed = (w_up[0], swapped(w_up[0]), w_down[0], swapped(w_down[0]))
    shard = jnp.stack(
        [w_qkv[0, :, :features], w_qkv[0, :, features : 2 * features], w_qkv[0, :, 2 * features :],
         w_out[0]]
    )
    gain_shard = jnp.pad(norm_gains[0], ((0, 14), (0, 0)))
    at_mine, at_theirs, gain_mine, gain_theirs = gather_weights(shard, gain_shard)
    attention = (
        at_mine.reshape(4, features, features), at_theirs.reshape(4, features, features)
    )

    def whole_gains(block):
        return block[:, :2].transpose(1, 0, 2).reshape(2, features).astype(F32)

    gain_mine, gain_theirs = whole_gains(gain_mine), whole_gains(gain_theirs)
    gains = (choose(gain_mine, gain_theirs), choose(gain_theirs, gain_mine))

    inputs = own_tokens
    saved = []
    for layer in range(2):
        results = forward_layer(layer, inputs, bias, gains[layer], attention, feed)
        saved.append((inputs,) + tuple(results))
        inputs = results[0]

    grad = own_cotangent
    gain_grads, input_grads, operands = [None, None], [None, None], ()
    for layer in (1, 0):
        (x, _, middle, normed_one, query, key, value, mixed, normed_two, act, hidden) = saved[layer]
        results = backward_layer(
            layer, x, grad, bias_turned, gains[layer], middle, query, key, value, act,
            attention, feed, operands + (saved[0][8], saved[0][10]) if layer == 0 else (),
        )
        (grad, gain_grads[layer], out_all, pre_grad, branch, dquery, dkey, dvalue) = results[:8]
        input_grads[layer] = grad
        operands = (
            normed_two, pre_grad, hidden, out_all, normed_one, mixed, dquery, dkey, dvalue, branch,
        )
    feed_one, feed_one_given, feed_zero, kept_one = results[8:]
    gain_rows = jnp.concatenate(gain_grads + [jnp.zeros((4, features), F32)], axis=0)
    (feed_zero_given, at_zero, at_zero_given, at_one, at_one_given, activations, input_grads,
     gain_total) = sum_gradients(
        features, rows, operands[4:], (saved[0][1], saved[1][1], *input_grads, feed_zero),
        gain_rows, kept_one,
    )
    gain_own = lax.dynamic_slice(
        gain_total, (2 * section, lax.axis_index("tensor") * share), (2, share)
    )

    grad_up, grad_down, grad_qkv, grad_out = widen(
        features, share, feed_zero, feed_zero_given, feed_one, feed_one_given, at_zero,
        at_zero_given, at_one, at_one_given,
    )
    return (
        activations[None],
        input_grads[None],
        gain_own[None],
        grad_qkv[None],
        grad_out[None],
        grad_up[None],
        grad_down[None],
    )


def solution(mesh):
    placed = (
        P("dp", "tensor", None),
        P("dp", "tensor", None),
        P("dp", None),
        P("section", None, "tensor"),
        P("section", "tensor", None),
        P("section", "tensor", None),
        P("section", None, "tensor"),
        P("section", "tensor", None),
    )
    return jax.shard_map(
        body,
        mesh=mesh,
        in_specs=placed,
        out_specs=(
            P("section", "dp", "tensor", None),
            P("section", "dp", "tensor", None),
            P("section", None, "tensor"),
            P("section", "tensor", None),
            P("section", "tensor", None),
            P("section", None, "tensor"),
            P("section", "tensor", None),
        ),
        check_vma=False,
    )
```
